32 devices in a mesh: grp: 2 (over x), term: 16 (over z, y, core).
Axes of the slice: x: 2, y: 2, z: 4, core: 2. Of those that a mesh axis runs over, the one named last changes fastest.
Arguments:
- wavefunction: bfloat16 [6, 512, 512], P('grp', 'term'), parts along dimension 0
- diagonal: bfloat16 [6, 512, 512], P('grp', 'term'), parts along dimension 0, may hold values from 1 to 10
- left_blocks: bfloat16 [256, 512, 512], P(('grp', 'term')), parts along dimension 0, may hold values from -0.25 to 0.25
- right_blocks: bfloat16 [256, 512, 512], P(('grp', 'term')), parts along dimension 0, may hold values from -0.09375 to 0.09375
- block_source: int32 [256], P(('grp', 'term')), parts along dimension 0, may hold values from 0 to 2
- block_target: int32 [256], P(('grp', 'term')), parts along dimension 0, may hold values from 0 to 2
- live_count: int32 [32], P(('grp', 'term')), parts along dimension 0, may hold values from 1 to 8, as said below
Outputs:
- first_image: float32 [6, 512, 512], P('grp', 'term'), parts along dimension 0
- second_vector: float32 [6, 512, 512], P('grp', 'term'), parts along dimension 0
- second_image: float32 [6, 512, 512], P('grp', 'term'), parts along dimension 0
The draws below stay inside these ranges and needn't reach their ends.
There are 2 independent parts, one for each index of `grp`. The reference program is written for one: setup_inputs(seed, part) draws one part's arguments, and reference() takes and returns one part's arrays. A program takes and returns all parts, laid end to end along the dimension named above; each array names one. Nothing has to cross between parts.
Inputs may be any that keep to these rules, and one draw needn't show every extreme that they name: A device's used slots are its first live_count slots; some device uses all 8 in every draw.
All inputs are finite; a program needn't handle non-finite values.
Results may differ from the reference program's by a relative error of at most 0.0032.
Values may be sent and summed in bfloat16 or wider, within the bound.
No kernel may reach another device: no remote copies, remote signals or barrier semaphores. Data moves between devices by JAX's collectives and lax.ppermute only.
A program may use at most 64 MiB of HBM per device.

```python
import math
import jax
import jax.numpy as jnp
from jax import lax

SECTOR_DIM = 512
SECTORS = 3
BLOCKS_DEV = 8
BLOCKS = 128
N_TERM = 16


def draw_wavefunction(key, part):
    key = jax.random.fold_in(key, 11)
    key_base, key_rows, key_cols = jax.random.split(key, 3)
    base = jax.random.normal(key_base, (SECTORS, SECTOR_DIM, SECTOR_DIM), jnp.float32)
    spread = math.log(10.0)
    row_scale = jnp.exp(jax.random.uniform(key_rows, (SECTORS, SECTOR_DIM, 1), jnp.float32) * spread)
    col_scale = jnp.exp(jax.random.uniform(key_cols, (SECTORS, 1, SECTOR_DIM), jnp.float32) * spread)
    rising = 1.0 + 2.0 * jnp.arange(SECTOR_DIM, dtype=jnp.float32).reshape(1, SECTOR_DIM, 1) / (SECTOR_DIM - 1)
    return (base * row_scale * col_scale * rising).astype(jnp.bfloat16)


def draw_live_count(key, part):
    key = jax.random.fold_in(key, 23)
    key_counts, key_pick = jax.random.split(key)
    counts = jax.random.randint(key_counts, (N_TERM,), 1, BLOCKS_DEV + 1, jnp.int32)
    chosen = jax.random.randint(key_pick, (), 0, N_TERM, jnp.int32)
    return counts.at[chosen].set(BLOCKS_DEV)


def plant(values, rng, smallest, largest):
    extent = values.shape
    spot = [jax.random.randint(jax.random.fold_in(rng, axis), (), 0, extent[axis]) for axis in range(len(extent))]
    values = values.at[tuple(spot)].set(smallest)
    longest = extent.index(max(extent))
    spot[longest] = (spot[longest] + 1) % extent[longest]
    return values.at[tuple(spot)].set(largest)


def levels(rng, extent, pieces, low, top_value):
    loudness = 1.0
    for dim, shards_of in pieces:
        steps = jax.random.uniform(jax.random.fold_in(jax.random.fold_in(rng, 6), dim), (shards_of,), jnp.float32, low / len(pieces), top_value / len(pieces))
        loudness = loudness * jnp.repeat(jnp.exp(steps), extent[dim] // shards_of).reshape((-1,) + (1,) * (len(extent) - 1 - dim))
    return loudness


def centred(rng, dims, width, limit, shards=(), held_as=jnp.bfloat16):
    drawn = jax.random.normal(rng, dims, jnp.float32) * width
    if len(shards) > 0:
        drawn = levels(rng, dims, shards, -0.22, 0.18) * drawn
    return jnp.clip(drawn, min=-limit, max=limit).astype(held_as)


def setup_inputs(seed: int = 0, part: int = 0) -> dict:
    arg_keys = jax.random.split(jax.random.key(seed), 8)
    part_splits = jax.random.split(jax.random.fold_in(arg_keys[7], part), 8)
    wavefunction = draw_wavefunction(jax.random.fold_in(jax.random.fold_in(arg_keys[7], part), 71), part)
    diagonal = jnp.clip(jnp.exp(math.log(10.0) - 2.3025851 * jax.random.uniform(part_splits[1], (SECTORS, SECTOR_DIM, SECTOR_DIM), jnp.float32) ** levels(part_splits[1], (SECTORS, SECTOR_DIM, SECTOR_DIM), ((1, 16),), -0.2, 0.2)), 1.0, 10.0).astype(jnp.bfloat16)
    left_blocks = centred(part_splits[2], (BLOCKS, SECTOR_DIM, SECTOR_DIM), SECTOR_DIM ** -0.5, 0.25, ((0, 16),))
    right_blocks = centred(part_splits[3], (BLOCKS, SECTOR_DIM, SECTOR_DIM), (SECTOR_DIM * 8) ** -0.5, 0.09375, ((0, 16),))
    block_source = plant(jax.random.randint(part_splits[4], (BLOCKS,), 0, SECTORS), jax.random.fold_in(part_splits[4], 1), 0, SECTORS - 1).astype(jnp.int32)
    block_target = plant(jax.random.randint(part_splits[5], (BLOCKS,), 0, SECTORS), jax.random.fold_in(part_splits[5], 1), 0, SECTORS - 1).astype(jnp.int32)
    live_count = draw_live_count(jax.random.fold_in(jax.random.fold_in(arg_keys[7], part), 71), part)
    return dict(wavefunction=wavefunction, diagonal=diagonal, left_blocks=left_blocks, right_blocks=right_blocks, block_source=block_source, block_target=block_target, live_count=live_count)


def apply_blocks(field_rounded, left_blocks, right_blocks, block_source, block_target, used_flags):
    zeroed = jnp.zeros(field_rounded.shape, jnp.float32)

    def add_block(running, entry):
        left_op, right_op, source, target, used = entry

        def live_block(current):
            piece = lax.dynamic_index_in_dim(field_rounded, source, 0, keepdims=False)
            product = jnp.dot(left_op, piece, preferred_element_type=jnp.float32).astype(jnp.bfloat16)
            term_value = jnp.dot(product, right_op.T, preferred_element_type=jnp.float32)
            before = lax.dynamic_index_in_dim(current, target, 0, keepdims=False)
            return lax.dynamic_update_index_in_dim(current, before + term_value, target, 0)
        return (lax.cond(used, live_block, lambda current: current, running), None)
    result, _ = lax.scan(add_block, zeroed, (left_blocks, right_blocks, block_source, block_target, used_flags))
    return result

def reference(wavefunction, diagonal, left_blocks, right_blocks, block_source, block_target, live_count):
    used_flags = jnp.arange(BLOCKS, dtype=jnp.int32) % BLOCKS_DEV < jnp.repeat(live_count, BLOCKS_DEV)
    entries = float(SECTORS * SECTOR_DIM * SECTOR_DIM)
    wave_float = wavefunction.astype(jnp.float32)
    diag_float = diagonal.astype(jnp.float32)
    scale = jnp.sqrt(jnp.sum(wave_float * wave_float) / entries)
    start = wave_float / scale
    first_image = apply_blocks(start.astype(jnp.bfloat16), left_blocks, right_blocks, block_source, block_target, used_flags) + diag_float * start
    ritz_value = jnp.sum(start * first_image) / entries
    correction = (first_image - ritz_value * start) / jnp.maximum(jnp.abs(diag_float - ritz_value), 1.0)
    correlation = jnp.sum(start * correction) / entries
    projected = correction - correlation * start
    second_vector = projected / jnp.sqrt(jnp.sum(projected * projected) / entries)
    second_image = apply_blocks(second_vector.astype(jnp.bfloat16), left_blocks, right_blocks, block_source, block_target, used_flags) + diag_float * second_vector
    return (first_image, second_vector, second_image)
```

```python
import functools

import jax
import jax.numpy as jnp
from jax import lax
from jax.experimental import pallas as pl
from jax.experimental.pallas import tpu as pltpu
from jax.sharding import PartitionSpec as P

VMEM = pl.BlockSpec(memory_space=pltpu.VMEM)
SMEM = pl.BlockSpec(memory_space=pltpu.SMEM)
ANY = pl.BlockSpec(memory_space=pl.ANY)
PARAMS = pltpu.CompilerParams(vmem_limit_bytes=48 * 1024 * 1024)


def fold(values):
    sectors, rows, width = values.shape
    summed = jnp.sum(values.reshape(sectors * rows // 8, 8, width), axis=0)
    return sum(summed[:, k * 128 : (k + 1) * 128] for k in range(width // 128))


def blocks_kernel(
    normalize, kept, rows, entries, sources, targets, live, offsets, *refs
):
    pieces = len(kept)
    field_refs, (left_hbm, right_hbm) = refs[:pieces], refs[pieces : pieces + 2]
    outs = refs[pieces + 2 :]
    keep_ref, send_ref, dot_ref, scale_ref = outs[:4]
    left, right, field, total, left_sem, right_sem = outs[4:]
    slots = left.shape[0]
    used = live[0]

    def copies(slot):
        return (
            pltpu.make_async_copy(left_hbm.at[slot], left.at[slot], left_sem.at[slot]),
            pltpu.make_async_copy(right_hbm.at[slot], right.at[slot], right_sem.at[slot]),
        )

    for slot in range(slots):

        @pl.when(slot < used)
        def _():
            for copy in copies(slot):
                copy.start()

    total[...] = jnp.zeros_like(total)
    if normalize:
        square = jnp.zeros((8, 128), jnp.float32)
        for ref in field_refs:
            value = ref[...].astype(jnp.float32)
            square += fold(value * value)
        scale = jnp.sqrt(jnp.sum(square) / entries)
    else:
        scale = jnp.float32(1.0)
    scale_ref[0] = scale
    for index, ref in enumerate(field_refs):
        place = pl.ds(pl.multiple_of(offsets[index], rows), rows)
        if normalize:
            field[:, place, :] = (ref[...].astype(jnp.float32) / scale).astype(jnp.bfloat16)
        else:
            field[:, place, :] = ref[...]

    def add_block(slot, carry):
        for copy in copies(slot):
            copy.wait()
        product = jnp.dot(
            left[slot], field[sources[slot]], preferred_element_type=jnp.float32
        ).astype(jnp.bfloat16)
        total[targets[slot]] += lax.dot_general(
            product, right[slot], (((1,), (1,)), ((), ())), preferred_element_type=jnp.float32
        )
        return carry

    lax.fori_loop(0, used, add_block, 0)

    dot = jnp.zeros((8, 128), jnp.float32)
    n_keep = n_send = 0
    for index, ref in enumerate(field_refs):
        place = pl.ds(pl.multiple_of(offsets[index], rows), rows)
        value = total[:, place, :]
        if normalize:
            dot += fold(value * ref[...].astype(jnp.float32))
        if kept[index]:
            keep_ref[n_keep] = value
            n_keep += 1
        else:
            send_ref[n_send] = value.astype(jnp.bfloat16)
            n_send += 1
    dot_ref[...] = dot / scale


def apply_blocks(pieces, kept, offsets, left, right, sources, targets, live, normalize, entries):
    sectors, rows, width = pieces[0].shape
    order = left.shape[1]
    slots = left.shape[0]
    n_keep = sum(kept)
    n_send = max(len(kept) - n_keep, 1)
    return pl.pallas_call(
        functools.partial(blocks_kernel, normalize, kept, rows, entries),
        grid_spec=pltpu.PrefetchScalarGridSpec(
            num_scalar_prefetch=4,
            in_specs=[VMEM] * len(pieces) + [ANY, ANY],
            out_specs=[VMEM, VMEM, VMEM, SMEM],
            scratch_shapes=[
                pltpu.VMEM(left.shape, left.dtype),
                pltpu.VMEM(right.shape, right.dtype),
                pltpu.VMEM((sectors, order, width), jnp.bfloat16),
                pltpu.VMEM((sectors, order, width), jnp.float32),
                pltpu.SemaphoreType.DMA((slots,)),
                pltpu.SemaphoreType.DMA((slots,)),
            ],
        ),
        out_shape=[
            jax.ShapeDtypeStruct((n_keep, sectors, rows, width), jnp.float32),
            jax.ShapeDtypeStruct((n_send, sectors, rows, width), jnp.bfloat16),
            jax.ShapeDtypeStruct((8, 128), jnp.float32),
            jax.ShapeDtypeStruct((1,), jnp.float32),
        ],
        compiler_params=PARAMS,
        cost_estimate=pl.CostEstimate(
            flops=4 * slots * order * order * width,
            bytes_accessed=4 * slots * order * order,
            transcendentals=0,
        ),
    )(sources, targets, live, offsets, *pieces, left, right)


def pair_kernel(keep_ref, other_ref, own_ref, *send_refs):
    own_ref[...] = keep_ref[0] + other_ref[0].astype(jnp.float32)
    for index, ref in enumerate(send_refs):
        value = keep_ref[index + 1] + other_ref[index + 1].astype(jnp.float32)
        ref[...] = value.astype(jnp.bfloat16)


def pair_sums(keep, other):
    count, *shape = keep.shape
    return pl.pallas_call(
        pair_kernel,
        in_specs=[VMEM, VMEM],
        out_specs=[VMEM] * count,
        out_shape=[jax.ShapeDtypeStruct(shape, jnp.float32)]
        + [jax.ShapeDtypeStruct(shape, jnp.bfloat16)] * (count - 1),
        compiler_params=PARAMS,
    )(keep, other)


def add_parts(own_ref, part_refs):
    value = own_ref[...]
    for ref in part_refs:
        value = value + ref[...].astype(jnp.float32)
    return value


def step_kernel(entries, ritz_ref, scale_ref, wave_ref, diag_ref, own_ref, *refs):
    *part_refs, first_ref, terms_ref, correction_ref, rounded_ref, dots_ref = refs
    start = wave_ref[...].astype(jnp.float32) / scale_ref[0]
    diag = diag_ref[...].astype(jnp.float32)
    ritz = jnp.sum(ritz_ref[...]) / entries
    terms = add_parts(own_ref, part_refs)
    first = terms + diag * start
    correction = (first - ritz * start) / jnp.maximum(jnp.abs(diag - ritz), 1.0)
    first_ref[...] = first
    terms_ref[...] = terms
    correction_ref[...] = correction
    rounded_ref[...] = correction.astype(jnp.bfloat16)
    dots_ref[0] = fold(start * correction)
    dots_ref[1] = fold(correction * correction)


def davidson_step(ritz, scale, wave, diag, own, parts, entries):
    full = jax.ShapeDtypeStruct(wave.shape, jnp.float32)
    return pl.pallas_call(
        functools.partial(step_kernel, entries),
        in_specs=[VMEM, SMEM] + [VMEM] * (3 + len(parts)),
        out_specs=[VMEM] * 5,
        out_shape=[
            full,
            full,
            full,
            jax.ShapeDtypeStruct(wave.shape, jnp.bfloat16),
            jax.ShapeDtypeStruct((2, 8, 128), jnp.float32),
        ],
        compiler_params=PARAMS,
    )(ritz, scale, wave, diag, own, *parts)


def finish_kernel(
    entries, dots_ref, scale_ref, wave_ref, diag_ref, terms_ref, correction_ref, own_ref, *refs
):
    *part_refs, vector_ref, image_ref = refs
    start = wave_ref[...].astype(jnp.float32) / scale_ref[0]
    along = jnp.sum(dots_ref[0]) / entries
    norm = jnp.sqrt(jnp.sum(dots_ref[1]) / entries - along * along)
    second = (correction_ref[...] - along * start) / norm
    vector_ref[...] = second
    image = (add_parts(own_ref, part_refs) - along * terms_ref[...]) / norm
    image_ref[...] = image + diag_ref[...].astype(jnp.float32) * second


def finish(dots, scale, wave, diag, terms, correction, own, parts, entries):
    full = jax.ShapeDtypeStruct(wave.shape, jnp.float32)
    return pl.pallas_call(
        functools.partial(finish_kernel, entries),
        in_specs=[VMEM, SMEM] + [VMEM] * (5 + len(parts)),
        out_specs=[VMEM] * 2,
        out_shape=[full, full],
        compiler_params=PARAMS,
    )(dots, scale, wave, diag, terms, correction, own, *parts)


class DirectPlan:
    def __init__(self, rows):
        self.rows = rows
        me = lax.axis_index("term")
        offsets, self.kept = [], []
        for dc in range(2):
            for dz in range(4):
                for dy in range(2):
                    z, y, c = (me // 4 - dz + 4) % 4, (me // 2 % 2 + dy) % 2, (me % 2 + dc) % 2
                    offsets.append(((z * 2 + y) * 2 + c) * rows)
                    self.kept.append(dc == 0)
        self.offsets = jnp.stack(offsets).astype(jnp.int32)

    @staticmethod
    def shift(value, dz, dy, dc):
        pairs = []
        for index in range(16):
            z, y, c = index // 4, index // 2 % 2, index % 2
            pairs.append((index, (((z + dz) % 4) * 2 + (y + dy) % 2) * 2 + (c + dc) % 2))
        return lax.ppermute(value, "term", pairs)

    def gather(self, own):
        along_z = [own] + [self.shift(own, dz, 0, 0) for dz in (1, 2, 3)]
        chips = []
        for piece in along_z:
            chips += [piece, self.shift(piece, 0, 1, 0)]
        return chips + [self.shift(piece, 0, 0, 1) for piece in chips]

    def scatter(self, keep, send):
        other = self.shift(send, 0, 0, 1)
        own, *sums = pair_sums(keep, other)
        parts = []
        for index, value in enumerate(sums):
            dz, dy = (index + 1) // 2, (index + 1) % 2
            parts.append(self.shift(value, (4 - dz) % 4, dy, 0))
        return own, parts


class WholePlan:
    def __init__(self):
        self.kept = [True]
        self.offsets = jnp.zeros((1,), jnp.int32)

    def gather(self, own):
        return [lax.all_gather(own, "term", axis=1, tiled=True)]

    def scatter(self, keep, send):
        return lax.psum_scatter(keep[0], "term", scatter_dimension=1, tiled=True), []


def on_device(
    wavefunction, diagonal, left_blocks, right_blocks, block_source, block_target, live_count
):
    devices = lax.axis_size("term")
    sectors, rows, width = wavefunction.shape
    entries = float(sectors * rows * devices * width)
    plan = DirectPlan(rows) if devices == 16 else WholePlan()
    blocks = (left_blocks, right_blocks, block_source, block_target, live_count)

    def apply(pieces, normalize):
        keep, send, dot, scale = apply_blocks(
            pieces, plan.kept, plan.offsets, *blocks, normalize, entries
        )
        return (*plan.scatter(keep, send), dot, scale)

    own, parts, dot, scale = apply(plan.gather(wavefunction), True)
    start = wavefunction.astype(jnp.float32) / scale[0]
    dot = dot + fold(diagonal.astype(jnp.float32) * start * start)
    ritz = lax.psum(dot, "term")
    first_image, terms, correction, rounded, dots = davidson_step(
        ritz, scale, wavefunction, diagonal, own, parts, entries
    )
    dots = lax.psum(dots, "term")
    own, parts, _, _ = apply(plan.gather(rounded), False)
    second_vector, second_image = finish(
        dots, scale, wavefunction, diagonal, terms, correction, own, parts, entries
    )
    return (first_image, second_vector, second_image)


def solution(mesh):
    placed = (
        P("grp", "term", None),
        P("grp", "term", None),
        P(("grp", "term"), None, None),
        P(("grp", "term"), None, None),
        P(("grp", "term")),
        P(("grp", "term")),
        P(("grp", "term")),
    )
    return jax.shard_map(
        on_device,
        mesh=mesh,
        in_specs=placed,
        out_specs=(P("grp", "term", None), P("grp", "term", None), P("grp", "term", None)),
        check_vma=False,
    )
```

```python
import functools

import jax
import jax.numpy as jnp
from jax import lax
from jax.experimental import pallas as pl
from jax.experimental.pallas import tpu as pltpu
from jax.sharding import PartitionSpec as P

VMEM = pl.BlockSpec(memory_space=pltpu.VMEM)
SMEM = pl.BlockSpec(memory_space=pltpu.SMEM)
HBM = pl.BlockSpec(memory_space=pltpu.HBM)
PARAMS = pltpu.CompilerParams(vmem_limit_bytes=48 * 1024 * 1024)
HALF = 16
LANES = 128


def fold(value):
    rows, width = value.shape
    summed = jnp.sum(value.reshape(rows // 8, 8, width), axis=0)
    return sum(summed[:, k * 128 : (k + 1) * 128] for k in range(width // 128))


def fold_all(value):
    return sum(fold(value[s]) for s in range(value.shape[0]))


def message_shape(sectors, rows, width):
    return (HALF, sectors * (rows // HALF) * width + LANES)


def write_scalar(ref, index, scalar):
    whole = jnp.full((HALF, LANES), scalar, jnp.float32)
    high = whole.astype(jnp.bfloat16).astype(jnp.float32)
    rest = whole - high
    middle = rest.astype(jnp.bfloat16).astype(jnp.float32)
    low = rest - middle
    row = lax.broadcasted_iota(jnp.int32, whole.shape, 0)
    lane = lax.broadcasted_iota(jnp.int32, whole.shape, 1)
    value = jnp.where(row == 0, high, jnp.where(row == 1, middle, jnp.where(row == 2, low, 0.0)))
    value = jnp.where(lane == 0, value, 0.0)
    ref[index, :, ref.shape[2] - LANES :] = value.astype(jnp.bfloat16)


def read_scalar(ref, indices):
    return jnp.sum(
        sum(ref[i, :, ref.shape[2] - LANES :].astype(jnp.float32) for i in indices)
    )


def write_piece(ref, index, sector, value):
    rows, width = value.shape
    for h in range(rows // HALF):
        at = (sector * (rows // HALF) + h) * width
        ref[index, :, at : at + width] = value[h * HALF : (h + 1) * HALF].astype(jnp.bfloat16)


def read_piece(ref, index, sector, rows, width):
    parts = []
    for h in range(rows // HALF):
        at = (sector * (rows // HALF) + h) * width
        parts.append(ref[index, :, at : at + width].astype(jnp.float32))
    return jnp.concatenate(parts, axis=0)


def position(me_ref):
    me = me_ref[0]
    return me // 4, me // 2 % 2, me % 2


def blocks_kernel(first, direct, rows, entries, me_ref, *refs):
    n_field = 2 if direct else 1
    field_refs, refs = refs[:n_field], refs[n_field:]
    if first:
        (wave_ref, diag_ref), refs = refs[:2], refs[2:]
    else:
        (scale_ref, wave_ref, correction_ref, dots_ref), refs = refs[:4], refs[4:]
    ints_hbm, (left_hbm, right_hbm), refs = refs[:3], refs[3:5], refs[5:]
    keep_ref, send_ref, dot_ref, out_ref = refs[:4]
    left, right, field, total, sources, targets, live, left_sem, right_sem, int_sem = refs[4:]
    slots, width = left.shape[0], total.shape[2]
    sectors = total.shape[0]
    in_messages = direct and not first

    int_copies = [
        pltpu.make_async_copy(src, dst, int_sem.at[k])
        for k, (src, dst) in enumerate(zip(ints_hbm, (sources, targets, live)))
    ]
    for copy in int_copies:
        copy.start()

    def copies(slot):
        return (
            pltpu.make_async_copy(left_hbm.at[slot], left.at[slot], left_sem.at[slot]),
            pltpu.make_async_copy(right_hbm.at[slot], right.at[slot], right_sem.at[slot]),
        )

    for slot in range(slots):
        for copy in copies(slot):
            copy.start()

    core = me_ref[0] % 2
    pieces = []
    for k, ref in enumerate(field_refs):
        for i in range(ref.shape[0]):
            at = pl.multiple_of((i * 2 + (core + k) % 2) * rows, rows) if direct else 0
            for s in range(sectors):
                if in_messages:
                    read = functools.partial(read_piece, ref, i, s, rows, width)
                else:
                    read = lambda ref=ref, i=i, s=s: ref[i, s].astype(jnp.float32)
                pieces.append((k, i, s, pl.ds(at, rows), read))

    total[...] = jnp.zeros_like(total)
    dot = jnp.zeros((8, 128), jnp.float32)
    if first:
        for *_, read in pieces:
            value = read()
            dot += fold(value * value)
        scale = jnp.sqrt(jnp.sum(dot) / entries)
        out_ref[0] = scale
        for _, _, s, place, read in pieces:
            field[s, place, :] = (read() / scale).astype(jnp.bfloat16)
    else:
        for _, _, s, place, read in pieces:
            field[s, place, :] = read().astype(jnp.bfloat16)

    for copy in int_copies:
        copy.wait()
    used = live[0]

    def add_block(slot, carry):
        for copy in copies(slot):
            copy.wait()

        @pl.when(slot < used)
        def _():
            product = jnp.dot(
                left[slot], field[sources[slot]], preferred_element_type=jnp.float32
            ).astype(jnp.bfloat16)
            total[targets[slot]] += lax.dot_general(
                product, right[slot], (((1,), (1,)), ((), ())), preferred_element_type=jnp.float32
            )

        return carry

    lax.fori_loop(0, slots, add_block, 0)

    dot = jnp.zeros((8, 128), jnp.float32)
    for k, i, s, place, read in pieces:
        value = total[s, place, :]
        if first:
            dot += fold(value * read())
        if k == 0:
            keep_ref[i, s] = value
        else:
            write_piece(send_ref, i, s, value)
    if first:
        start = wave_ref[...].astype(jnp.float32) / scale
        dot = dot / scale + fold_all(diag_ref[...].astype(jnp.float32) * start * start)
    else:
        if direct:
            count = field_refs[0].shape[0]
            along = sum(read_scalar(ref, range(count)) for ref in field_refs) / entries
        else:
            along = jnp.sum(dots_ref[...]) / entries
        out_ref[0] = along
        start = wave_ref[...].astype(jnp.float32) / scale_ref[0]
        projected = correction_ref[...] - along * start
        dot = fold_all(projected * projected)
    dot_ref[...] = dot
    if direct:
        scalar = jnp.sum(dot)
        for i in range(send_ref.shape[0]):
            write_scalar(send_ref, i, scalar)


def apply_blocks(me, fields, own, blocks, first, entries):
    left, right, *ints = blocks
    slots, order, width = left.shape
    sectors = own[0 if first else 1].shape[0]
    direct = len(fields) == 2
    rows = own[0 if first else 1].shape[1] if direct else order
    count = fields[0].shape[0]
    if direct:
        kept = (count, sectors, rows, width)
        sent = (count,) + message_shape(sectors, rows, width)
    else:
        kept, sent = (1, sectors, order, width), (1, HALF, LANES)
    own_specs = [VMEM, VMEM] if first else [SMEM, VMEM, VMEM, VMEM]
    return pl.pallas_call(
        functools.partial(blocks_kernel, first, direct, rows, entries),
        in_specs=[SMEM] + [VMEM] * len(fields) + own_specs + [HBM] * 5,
        out_specs=[VMEM, VMEM, VMEM, SMEM],
        scratch_shapes=[
            pltpu.VMEM(left.shape, left.dtype),
            pltpu.VMEM(right.shape, right.dtype),
            pltpu.VMEM((sectors, order, width), jnp.bfloat16),
            pltpu.VMEM((sectors, order, width), jnp.float32),
            pltpu.SMEM((slots,), jnp.int32),
            pltpu.SMEM((slots,), jnp.int32),
            pltpu.SMEM((1,), jnp.int32),
            pltpu.SemaphoreType.DMA((slots,)),
            pltpu.SemaphoreType.DMA((slots,)),
            pltpu.SemaphoreType.DMA((3,)),
        ],
        out_shape=[
            jax.ShapeDtypeStruct(kept, jnp.float32),
            jax.ShapeDtypeStruct(sent, jnp.bfloat16),
            jax.ShapeDtypeStruct((8, 128), jnp.float32),
            jax.ShapeDtypeStruct((1,), jnp.float32),
        ],
        compiler_params=PARAMS,
        cost_estimate=pl.CostEstimate(
            flops=4 * slots * order * order * width,
            bytes_accessed=4 * slots * order * order,
            transcendentals=0,
        ),
    )(me, *fields, *own, *ints, left, right)


def core_kernel(me_ref, keep_ref, other_ref, dot_ref, kept_ref, send_ref, sum_ref):
    _, y, _ = position(me_ref)
    sectors, rows, width = keep_ref.shape[1:]
    scalar = jnp.sum(dot_ref[...]) + read_scalar(other_ref, [0])
    sum_ref[0] = scalar
    for z in range(kept_ref.shape[0]):
        mine, theirs = z * 2 + y, z * 2 + 1 - y
        for s in range(sectors):
            kept_ref[z, s] = keep_ref[mine, s] + read_piece(other_ref, mine, s, rows, width)
            value = keep_ref[theirs, s] + read_piece(other_ref, theirs, s, rows, width)
            write_piece(send_ref, z, s, value)
        write_scalar(send_ref, z, scalar)


def add_core(me, keep, other, dot):
    count, *piece = keep.shape
    return pl.pallas_call(
        core_kernel,
        in_specs=[SMEM, VMEM, VMEM, VMEM],
        out_specs=[VMEM, VMEM, SMEM],
        out_shape=[
            jax.ShapeDtypeStruct((count // 2, *piece), jnp.float32),
            jax.ShapeDtypeStruct((count // 2, *message_shape(*piece)), jnp.bfloat16),
            jax.ShapeDtypeStruct((1,), jnp.float32),
        ],
        compiler_params=PARAMS,
    )(me, keep, other, dot)


def row_kernel(keep_ref, other_ref, sum_ref, send_ref):
    sectors, rows, width = keep_ref.shape[1:]
    scalar = sum_ref[0] + read_scalar(other_ref, [0])
    for z in range(keep_ref.shape[0]):
        for s in range(sectors):
            value = keep_ref[z, s] + read_piece(other_ref, z, s, rows, width)
            write_piece(send_ref, z, s, value)
        write_scalar(send_ref, z, scalar)


def add_row(keep, other, summed):
    return pl.pallas_call(
        row_kernel,
        in_specs=[VMEM, VMEM, SMEM],
        out_specs=VMEM,
        out_shape=jax.ShapeDtypeStruct(other.shape, jnp.bfloat16),
        compiler_params=PARAMS,
    )(keep, other, summed)


def own_terms(direct, refs, sector, rows, width):
    if not direct:
        return refs[0][sector]
    ref = refs[0]
    return sum(read_piece(ref, i, sector, rows, width) for i in range(ref.shape[0]))


def own_scalar(direct, refs):
    return read_scalar(refs[0], range(refs[0].shape[0])) if direct else jnp.sum(refs[1][...])


def step_kernel(direct, entries, scale_ref, wave_ref, diag_ref, *refs):
    n_in = 1 if direct else 2
    ins, (first_ref, terms_ref, correction_ref, rounded_ref, dots_ref) = refs[:n_in], refs[n_in:]
    sectors, rows, width = wave_ref.shape
    ritz = own_scalar(direct, ins) / entries
    dots = jnp.zeros((8, 128), jnp.float32)
    for s in range(sectors):
        start = wave_ref[s].astype(jnp.float32) / scale_ref[0]
        diag = diag_ref[s].astype(jnp.float32)
        terms = own_terms(direct, ins, s, rows, width)
        first = terms + diag * start
        correction = (first - ritz * start) / jnp.maximum(jnp.abs(diag - ritz), 1.0)
        first_ref[s] = first
        terms_ref[s] = terms
        correction_ref[s] = correction
        dots += fold(start * correction)
        if direct:
            for i in range(rounded_ref.shape[0]):
                write_piece(rounded_ref, i, s, correction)
        else:
            rounded_ref[s] = correction.astype(jnp.bfloat16)
    dots_ref[...] = dots
    if direct:
        scalar = jnp.sum(dots)
        for i in range(rounded_ref.shape[0]):
            write_scalar(rounded_ref, i, scalar)


def davidson_step(scale, wave, diag, ins, entries, copies):
    full = jax.ShapeDtypeStruct(wave.shape, jnp.float32)
    direct = len(ins) == 1
    rounded = (copies, *message_shape(*wave.shape)) if direct else wave.shape
    return pl.pallas_call(
        functools.partial(step_kernel, direct, entries),
        in_specs=[SMEM, VMEM, VMEM] + [VMEM] * len(ins),
        out_specs=[VMEM] * 5,
        out_shape=[
            full,
            full,
            full,
            jax.ShapeDtypeStruct(rounded, jnp.bfloat16),
            jax.ShapeDtypeStruct((8, 128), jnp.float32),
        ],
        compiler_params=PARAMS,
    )(scale, wave, diag, *ins)


def finish_kernel(
    direct, entries, along_ref, scale_ref, wave_ref, diag_ref, terms_ref, correction_ref, *refs
):
    *ins, vector_ref, image_ref = refs
    sectors, rows, width = wave_ref.shape
    along = along_ref[0]
    norm = jnp.sqrt(own_scalar(direct, ins) / entries)
    for s in range(sectors):
        start = wave_ref[s].astype(jnp.float32) / scale_ref[0]
        second = (correction_ref[s] - along * start) / norm
        vector_ref[s] = second
        image = (own_terms(direct, ins, s, rows, width) - along * terms_ref[s]) / norm
        image_ref[s] = image + diag_ref[s].astype(jnp.float32) * second


def finish(along, scale, wave, diag, terms, correction, ins, entries):
    full = jax.ShapeDtypeStruct(wave.shape, jnp.float32)
    return pl.pallas_call(
        functools.partial(finish_kernel, len(ins) == 1, entries),
        in_specs=[SMEM, SMEM] + [VMEM] * (4 + len(ins)),
        out_specs=[VMEM] * 2,
        out_shape=[full, full],
        compiler_params=PARAMS,
    )(along, scale, wave, diag, terms, correction, *ins)


def flip(value, bit):
    return lax.ppermute(value, "term", [(i, i ^ bit) for i in range(16)])


class DirectPlan:
    copies = 8

    def gather(self, copies):
        groups = [[chip * 2 + c for chip in range(8)] for c in range(2)]
        mine = lax.all_to_all(copies, "term", 0, 0, axis_index_groups=groups)
        return [mine, flip(mine, 1)]

    def gather_first(self, own):
        return self.gather(jnp.broadcast_to(own[None], (self.copies, *own.shape)))

    def scatter(self, me, keep, send, dot):
        keep, send, summed = add_core(me, keep, flip(send, 1), dot)
        sums = add_row(keep, flip(send, 2), summed)
        groups = [[z * 4 + y * 2 + c for z in range(4)] for y in range(2) for c in range(2)]
        return [lax.all_to_all(sums, "term", 0, 0, axis_index_groups=groups)]


class WholePlan:
    copies = 1

    def gather(self, own):
        return [lax.all_gather(own, "term", axis=1, tiled=True)[None]]

    gather_first = gather

    def scatter(self, me, keep, send, dot):
        rows = lax.psum_scatter(keep[0], "term", scatter_dimension=1, tiled=True)
        return [rows, lax.psum(dot, "term")]


def on_device(
    wavefunction, diagonal, left_blocks, right_blocks, block_source, block_target, live_count
):
    devices = lax.axis_size("term")
    sectors, rows, width = wavefunction.shape
    entries = float(sectors * rows * devices * width)
    plan = DirectPlan() if devices == 16 else WholePlan()
    direct = devices == 16
    me = lax.axis_index("term").astype(jnp.int32).reshape(1)
    blocks = (left_blocks, right_blocks, block_source, block_target, live_count)

    fields = plan.gather_first(wavefunction)
    own = (wavefunction, diagonal)
    keep, send, dot, scale = apply_blocks(me, fields, own, blocks, True, entries)
    ins = plan.scatter(me, keep, send, dot)
    first_image, terms, correction, rounded, dots = davidson_step(
        scale, wavefunction, diagonal, ins, entries, plan.copies
    )
    fields = plan.gather(rounded)
    if not direct:
        dots = lax.psum(dots, "term")
    own = (scale, wavefunction, correction, dots)
    keep, send, dot, along = apply_blocks(me, fields, own, blocks, False, entries)
    ins = plan.scatter(me, keep, send, dot)
    second_vector, second_image = finish(
        along, scale, wavefunction, diagonal, terms, correction, ins, entries
    )
    return (first_image, second_vector, second_image)


def solution(mesh):
    placed = (
        P("grp", "term", None),
        P("grp", "term", None),
        P(("grp", "term"), None, None),
        P(("grp", "term"), None, None),
        P(("grp", "term")),
        P(("grp", "term")),
        P(("grp", "term")),
    )
    return jax.shard_map(
        on_device,
        mesh=mesh,
        in_specs=placed,
        out_specs=(P("grp", "term", None), P("grp", "term", None), P("grp", "term", None)),
        check_vma=False,
    )
```

```python
import functools

import jax
import jax.numpy as jnp
from jax import lax
from jax.experimental import pallas as pl
from jax.experimental.pallas import tpu as pltpu
from jax.sharding import PartitionSpec as P

VMEM = pl.BlockSpec(memory_space=pltpu.VMEM)
SMEM = pl.BlockSpec(memory_space=pltpu.SMEM)
HBM = pl.BlockSpec(memory_space=pltpu.HBM)
PARAMS = pltpu.CompilerParams(vmem_limit_bytes=48 * 1024 * 1024)
HALF = 16
LANES = 128


def fold(value):
    rows, width = value.shape
    summed = jnp.sum(value.reshape(rows // 8, 8, width), axis=0)
    return sum(summed[:, k * 128 : (k + 1) * 128] for k in range(width // 128))


def fold_all(value):
    return sum(fold(value[s]) for s in range(value.shape[0]))


def message_shape(sectors, rows, width):
    return (HALF, sectors * (rows // HALF) * width + LANES)


def write_lanes(ref, lanes):
    whole = jnp.broadcast_to(lanes, (HALF, LANES))
    high = whole.astype(jnp.bfloat16).astype(jnp.float32)
    rest = whole - high
    middle = rest.astype(jnp.bfloat16).astype(jnp.float32)
    low = rest - middle
    row = lax.broadcasted_iota(jnp.int32, whole.shape, 0)
    value = jnp.where(row == 0, high, jnp.where(row == 1, middle, jnp.where(row == 2, low, 0.0)))
    ref[:, ref.shape[1] - LANES :] = value.astype(jnp.bfloat16)


def read_lanes(ref):
    return jnp.sum(ref[:, ref.shape[1] - LANES :].astype(jnp.float32), axis=0, keepdims=True)


def message_parts(sectors, rows, width):
    for s in range(sectors):
        for h in range(rows // HALF):
            at = (s * (rows // HALF) + h) * width
            yield s, h * HALF, slice(at, at + width)


def chip_at(place):
    place = lax.rem(place + 8, 8)
    return jnp.where(place < 4, 2 * place, 15 - 2 * place)


def ring_place(me):
    chip, core = me // 2, me % 2
    place = jnp.where(chip % 2 == 0, chip // 2, (15 - chip) // 2)
    return place, core


def ahead(me, distance, half, core=None):
    place, own = ring_place(me)
    core = own if core is None else core
    return chip_at(place + (1 - 2 * core) * distance) * 2 + half


CHAIN = ((4, True), (3, True), (3, False), (2, True), (2, False), (1, True), (1, False), (0, True))


def chain_devices(me, core):
    return [ahead(me, d, core if own else 1 - core, core) for d, own in CHAIN]


def gathered_devices(me):
    core = me % 2
    devices = []
    for sign, mine in ((-1, core), (1, 1 - core)):
        devices.append(ahead(me, 0, mine))
        for d in (1, 2, 3):
            devices += [ahead(me, sign * d, mine), ahead(me, sign * d, 1 - mine)]
        devices.append(ahead(me, 4, mine))
    return devices


def blocks_kernel(first, direct, rows, entries, me_ref, *refs):
    n_field = 16 if direct else 1
    field_refs, refs = refs[:n_field], refs[n_field:]
    if first:
        (wave_ref, diag_ref), refs = refs[:2], refs[2:]
    else:
        (scale_ref, wave_ref, correction_ref, dots_ref), refs = refs[:4], refs[4:]
    ints_hbm, (left_hbm, right_hbm), refs = refs[:3], refs[3:5], refs[5:]
    keep_ref, near_ref, far_ref, dot_ref, out_ref = refs[:5]
    left, right, field, total, sources, targets, live, left_sem, right_sem, int_sem = refs[5:]
    slots, width = left.shape[0], total.shape[2]
    sectors = total.shape[0]

    int_copies = [
        pltpu.make_async_copy(src, dst, int_sem.at[k])
        for k, (src, dst) in enumerate(zip(ints_hbm, (sources, targets, live)))
    ]
    for copy in int_copies:
        copy.start()

    def copies(slot):
        return (
            pltpu.make_async_copy(left_hbm.at[slot], left.at[slot], left_sem.at[slot]),
            pltpu.make_async_copy(right_hbm.at[slot], right.at[slot], right_sem.at[slot]),
        )

    for slot in range(slots):
        for copy in copies(slot):
            copy.start()

    me = me_ref[0]
    pieces = []
    owners = gathered_devices(me) if direct else [0]
    for ref, owner in zip(field_refs, owners):
        at = pl.multiple_of(owner * rows, rows) if direct else 0
        if direct and not first:
            for s, row, lanes in message_parts(sectors, rows, width):
                pieces.append((ref, (slice(None), lanes), s, pl.ds(at + row, HALF)))
        else:
            for s in range(sectors):
                pieces.append((ref, (s,), s, pl.ds(at, rows if direct else field.shape[1])))

    total[...] = jnp.zeros_like(total)
    dot = jnp.zeros((8, 128), jnp.float32)
    if first:
        for ref, part, _, _ in pieces:
            value = ref[part].astype(jnp.float32)
            dot += fold(value * value)
        scale = jnp.sqrt(jnp.sum(dot) / entries)
        out_ref[0] = scale
        for ref, part, s, place in pieces:
            field[s, place, :] = (ref[part].astype(jnp.float32) / scale).astype(jnp.bfloat16)
    else:
        for ref, part, s, place in pieces:
            field[s, place, :] = ref[part]

    for copy in int_copies:
        copy.wait()
    used = live[0]

    def add_block(slot, carry):
        for copy in copies(slot):
            copy.wait()

        @pl.when(slot < used)
        def _():
            product = jnp.dot(
                left[slot], field[sources[slot]], preferred_element_type=jnp.float32
            ).astype(jnp.bfloat16)
            total[targets[slot]] += lax.dot_general(
                product, right[slot], (((1,), (1,)), ((), ())), preferred_element_type=jnp.float32
            )

        return carry

    lax.fori_loop(0, slots, add_block, 0)

    dot = jnp.zeros((8, 128), jnp.float32)
    if first:
        for ref, part, s, place in pieces:
            dot += fold(total[s, place, :] * ref[part].astype(jnp.float32))
        start = wave_ref[...].astype(jnp.float32) / scale
        dot = dot / scale + fold_all(diag_ref[...].astype(jnp.float32) * start * start)
    else:
        if direct:
            along = jnp.sum(sum(read_lanes(ref) for ref in field_refs)) / entries
        else:
            along = jnp.sum(dots_ref[...]) / entries
        out_ref[0] = along
        start = wave_ref[...].astype(jnp.float32) / scale_ref[0]
        projected = correction_ref[...] - along * start
        dot = fold_all(projected * projected)
    dot_ref[...] = dot
    if not direct:
        keep_ref[0] = total[...]
        return
    lanes = jnp.sum(dot, axis=0, keepdims=True)
    core = me % 2
    for k, owner in enumerate(chain_devices(me, core)):
        at = pl.multiple_of(owner * rows, rows)
        for s in range(sectors):
            keep_ref[k, s] = total[s, pl.ds(at, rows), :]
    for k, owner in enumerate(chain_devices(me, 1 - core)):
        at = pl.multiple_of(owner * rows, rows)
        ref = near_ref.at[k] if k < near_ref.shape[0] else far_ref.at[k - near_ref.shape[0]]
        for s, row, part in message_parts(sectors, rows, width):
            ref[:, part] = total[s, pl.ds(at + row, HALF), :].astype(jnp.bfloat16)
        write_lanes(ref, lanes)


def apply_blocks(me, fields, own, blocks, first, entries):
    left, right, *ints = blocks
    slots, order, width = left.shape
    sectors, rows, _ = own[0 if first else 1].shape
    direct = len(fields) == 16
    if direct:
        kept, message = (8, sectors, rows, width), message_shape(sectors, rows, width)
    else:
        kept, message = (1, sectors, order, width), (HALF, LANES)
    own_specs = [VMEM, VMEM] if first else [SMEM, VMEM, VMEM, VMEM]
    return pl.pallas_call(
        functools.partial(blocks_kernel, first, direct, rows, entries),
        in_specs=[SMEM] + [VMEM] * len(fields) + own_specs + [HBM] * 5,
        out_specs=[VMEM, VMEM, VMEM, VMEM, SMEM],
        scratch_shapes=[
            pltpu.VMEM(left.shape, left.dtype),
            pltpu.VMEM(right.shape, right.dtype),
            pltpu.VMEM((sectors, order, width), jnp.bfloat16),
            pltpu.VMEM((sectors, order, width), jnp.float32),
            pltpu.SMEM((slots,), jnp.int32),
            pltpu.SMEM((slots,), jnp.int32),
            pltpu.SMEM((1,), jnp.int32),
            pltpu.SemaphoreType.DMA((slots,)),
            pltpu.SemaphoreType.DMA((slots,)),
            pltpu.SemaphoreType.DMA((3,)),
        ],
        out_shape=[
            jax.ShapeDtypeStruct(kept, jnp.float32),
            jax.ShapeDtypeStruct((3, *message), jnp.bfloat16),
            jax.ShapeDtypeStruct((5, *message), jnp.bfloat16),
            jax.ShapeDtypeStruct((8, 128), jnp.float32),
            jax.ShapeDtypeStruct((1,), jnp.float32),
        ],
        compiler_params=PARAMS,
        cost_estimate=pl.CostEstimate(
            flops=4 * slots * order * order * width,
            bytes_accessed=4 * slots * order * order,
            transcendentals=0,
        ),
    )(me, *fields, *own, *ints, left, right)


def chain_kernel(links, keep_ref, other_ref, dot_ref, *refs):
    n_in = sum(arrived for _, _, arrived in links)
    arrived_refs, out_refs = list(refs[:n_in]), refs[n_in:]
    sectors, rows, width = keep_ref.shape[1:]
    for (k, other, arrived), out_ref in zip(links, out_refs):
        arrived_ref = arrived_refs.pop(0) if arrived else None
        for s, row, part in message_parts(sectors, rows, width):
            value = keep_ref[k, s, row : row + HALF, :]
            value += other_ref[other, :, part].astype(jnp.float32)
            if arrived:
                value += arrived_ref[:, part].astype(jnp.float32)
            out_ref[:, part] = value.astype(jnp.bfloat16)
        lanes = jnp.sum(dot_ref[...], axis=0, keepdims=True) + read_lanes(other_ref.at[other])
        if arrived:
            lanes += read_lanes(arrived_ref)
        write_lanes(out_ref, lanes)


def chain(links, keep, other, dot, *arrived):
    out = [jax.ShapeDtypeStruct(other.shape[1:], jnp.bfloat16)] * len(links)
    return pl.pallas_call(
        functools.partial(chain_kernel, links),
        in_specs=[VMEM] * (3 + len(arrived)),
        out_specs=[VMEM] * len(links),
        out_shape=out,
        compiler_params=PARAMS,
    )(keep, other, dot, *arrived)


def own_terms(direct, refs, sector):
    if not direct:
        return refs[0][sector]
    keep_ref, other_ref, _, *arrived_refs = refs
    own = keep_ref.shape[0] - 1
    parts = []
    for s, row, part in message_parts(*keep_ref.shape[1:]):
        if s == sector:
            value = keep_ref[own, s, row : row + HALF, :]
            value += other_ref[other_ref.shape[0] - 1, :, part].astype(jnp.float32)
            for ref in arrived_refs:
                value += ref[:, part].astype(jnp.float32)
            parts.append(value)
    return jnp.concatenate(parts, axis=0)


def own_scalar(direct, refs):
    if not direct:
        return jnp.sum(refs[1][...])
    _, other_ref, dot_ref, *arrived_refs = refs
    lanes = jnp.sum(dot_ref[...], axis=0, keepdims=True)
    lanes += read_lanes(other_ref.at[other_ref.shape[0] - 1])
    return jnp.sum(lanes + sum(read_lanes(ref) for ref in arrived_refs))


def step_kernel(direct, entries, scale_ref, wave_ref, diag_ref, *refs):
    n_in = 5 if direct else 2
    ins, (first_ref, terms_ref, correction_ref, rounded_ref, dots_ref) = refs[:n_in], refs[n_in:]
    sectors, rows, width = wave_ref.shape
    ritz = own_scalar(direct, ins) / entries
    dots = jnp.zeros((8, 128), jnp.float32)
    for s in range(sectors):
        start = wave_ref[s].astype(jnp.float32) / scale_ref[0]
        diag = diag_ref[s].astype(jnp.float32)
        terms = own_terms(direct, ins, s)
        first = terms + diag * start
        correction = (first - ritz * start) / jnp.maximum(jnp.abs(diag - ritz), 1.0)
        first_ref[s] = first
        terms_ref[s] = terms
        correction_ref[s] = correction
        dots += fold(start * correction)
        if direct:
            for t, row, part in message_parts(sectors, rows, width):
                if t == s:
                    rounded_ref[:, part] = correction[row : row + HALF].astype(jnp.bfloat16)
        else:
            rounded_ref[s] = correction.astype(jnp.bfloat16)
    dots_ref[...] = dots
    if direct:
        write_lanes(rounded_ref, jnp.sum(dots, axis=0, keepdims=True))


def davidson_step(scale, wave, diag, ins, entries):
    full = jax.ShapeDtypeStruct(wave.shape, jnp.float32)
    direct = len(ins) == 5
    rounded = message_shape(*wave.shape) if direct else wave.shape
    return pl.pallas_call(
        functools.partial(step_kernel, direct, entries),
        in_specs=[SMEM, VMEM, VMEM] + [VMEM] * len(ins),
        out_specs=[VMEM] * 5,
        out_shape=[
            full,
            full,
            full,
            jax.ShapeDtypeStruct(rounded, jnp.bfloat16),
            jax.ShapeDtypeStruct((8, 128), jnp.float32),
        ],
        compiler_params=PARAMS,
    )(scale, wave, diag, *ins)


def finish_kernel(
    direct, entries, along_ref, scale_ref, wave_ref, diag_ref, terms_ref, correction_ref, *refs
):
    *ins, vector_ref, image_ref = refs
    sectors, rows, width = wave_ref.shape
    along = along_ref[0]
    norm = jnp.sqrt(own_scalar(direct, ins) / entries)
    for s in range(sectors):
        start = wave_ref[s].astype(jnp.float32) / scale_ref[0]
        second = (correction_ref[s] - along * start) / norm
        vector_ref[s] = second
        image = (own_terms(direct, ins, s) - along * terms_ref[s]) / norm
        image_ref[s] = image + diag_ref[s].astype(jnp.float32) * second


def finish(along, scale, wave, diag, terms, correction, ins, entries):
    full = jax.ShapeDtypeStruct(wave.shape, jnp.float32)
    return pl.pallas_call(
        functools.partial(finish_kernel, len(ins) == 5, entries),
        in_specs=[SMEM, SMEM] + [VMEM] * (4 + len(ins)),
        out_specs=[VMEM] * 2,
        out_shape=[full, full],
        compiler_params=PARAMS,
    )(along, scale, wave, diag, terms, correction, *ins)


def flip(value):
    return lax.ppermute(value, "term", [(i, i ^ 1) for i in range(16)])


def hop(value):
    order = [0, 2, 4, 6, 7, 5, 3, 1]
    pairs = []
    for place in range(8):
        for core, step in ((0, 1), (1, 7)):
            pairs.append((order[place] * 2 + core, order[(place + step) % 8] * 2 + core))
    return lax.ppermute(value, "term", pairs)


class RingPlan:
    def gather(self, own):
        partner = flip(own)
        mine, theirs = [own], [partner]
        one, two = own, partner
        for _ in range(3):
            one = hop(one)
            two = hop(two)
            mine += [one, two]
            theirs += [flip(one), flip(two)]
        one = hop(one)
        return mine + [one] + theirs + [flip(one)]

    def scatter(self, keep, near, far, dot):
        near = flip(near)
        near, far = lax.optimization_barrier((near, far))
        far = flip(far)
        one, two = chain(((0, 0, False), (2, 2, False)), keep, near, dot)
        one = hop(one)
        two = hop(two)
        (one,) = chain(((1, 1, True),), keep, near, dot, one)
        one = hop(one)
        (two,) = chain(((4, 1, True),), keep, far, dot, two)
        two = hop(two)
        (one,) = chain(((3, 0, True),), keep, far, dot, one)
        one = hop(one)
        (two,) = chain(((6, 3, True),), keep, far, dot, two)
        two = hop(two)
        (one,) = chain(((5, 2, True),), keep, far, dot, one)
        one = hop(one)
        return [keep, far, dot, one, flip(two)]


class WholePlan:
    def gather(self, own):
        return [lax.all_gather(own, "term", axis=1, tiled=True)]

    def scatter(self, keep, near, far, dot):
        rows = lax.psum_scatter(keep[0], "term", scatter_dimension=1, tiled=True)
        return [rows, lax.psum(dot, "term")]


def on_device(
    wavefunction, diagonal, left_blocks, right_blocks, block_source, block_target, live_count
):
    devices = lax.axis_size("term")
    sectors, rows, width = wavefunction.shape
    entries = float(sectors * rows * devices * width)
    plan = RingPlan() if devices == 16 else WholePlan()
    me = lax.axis_index("term").astype(jnp.int32).reshape(1)
    blocks = (left_blocks, right_blocks, block_source, block_target, live_count)

    own = (wavefunction, diagonal)
    *terms, scale = apply_blocks(me, plan.gather(wavefunction), own, blocks, True, entries)
    first_image, terms, correction, rounded, dots = davidson_step(
        scale, wavefunction, diagonal, plan.scatter(*terms), entries
    )
    fields = plan.gather(rounded)
    if devices != 16:
        dots = lax.psum(dots, "term")
    own = (scale, wavefunction, correction, dots)
    *second_terms, along = apply_blocks(me, fields, own, blocks, False, entries)
    second_vector, second_image = finish(
        along, scale, wavefunction, diagonal, terms, correction, plan.scatter(*second_terms), entries
    )
    return (first_image, second_vector, second_image)


def solution(mesh):
    placed = (
        P("grp", "term", None),
        P("grp", "term", None),
        P(("grp", "term"), None, None),
        P(("grp", "term"), None, None),
        P(("grp", "term")),
        P(("grp", "term")),
        P(("grp", "term")),
    )
    return jax.shard_map(
        on_device,
        mesh=mesh,
        in_specs=placed,
        out_specs=(P("grp", "term", None), P("grp", "term", None), P("grp", "term", None)),
        check_vma=False,
    )
```

```python
import functools

import jax
import jax.numpy as jnp
from jax import lax
from jax.experimental import pallas as pl
from jax.experimental.pallas import tpu as pltpu
from jax.sharding import PartitionSpec as P

VMEM = pl.BlockSpec(memory_space=pltpu.VMEM)
SMEM = pl.BlockSpec(memory_space=pltpu.SMEM)
HBM = pl.BlockSpec(memory_space=pltpu.HBM)
PARAMS = pltpu.CompilerParams(vmem_limit_bytes=48 * 1024 * 1024)
HALF = 16
LANES = 128


def fold(value):
    rows, width = value.shape
    summed = jnp.sum(value.reshape(rows // 8, 8, width), axis=0)
    return sum(summed[:, k * 128 : (k + 1) * 128] for k in range(width // 128))


def fold_all(value):
    return sum(fold(value[s]) for s in range(value.shape[0]))


def message_shape(sectors, rows, width):
    return (HALF, sectors * (rows // HALF) * width + LANES)


def write_lanes(ref, lanes):
    whole = jnp.broadcast_to(lanes, (HALF, LANES))
    high = whole.astype(jnp.bfloat16).astype(jnp.float32)
    rest = whole - high
    middle = rest.astype(jnp.bfloat16).astype(jnp.float32)
    low = rest - middle
    row = lax.broadcasted_iota(jnp.int32, whole.shape, 0)
    value = jnp.where(row == 0, high, jnp.where(row == 1, middle, jnp.where(row == 2, low, 0.0)))
    ref[:, ref.shape[1] - LANES :] = value.astype(jnp.bfloat16)


def read_lanes(ref):
    return jnp.sum(ref[:, ref.shape[1] - LANES :].astype(jnp.float32), axis=0, keepdims=True)


def message_parts(sectors, rows, width):
    for s in range(sectors):
        for h in range(rows // HALF):
            at = (s * (rows // HALF) + h) * width
            yield s, h * HALF, slice(at, at + width)


def chip_at(place):
    place = lax.rem(place + 8, 8)
    return jnp.where(place < 4, 2 * place, 15 - 2 * place)


def ring_place(me):
    chip, core = me // 2, me % 2
    place = jnp.where(chip % 2 == 0, chip // 2, (15 - chip) // 2)
    return place, core


def ahead(me, distance, half, core=None):
    place, own = ring_place(me)
    core = own if core is None else core
    return chip_at(place + (1 - 2 * core) * distance) * 2 + half


CHAIN = ((4, True), (3, True), (3, False), (2, True), (2, False), (1, True), (1, False), (0, True))


def chain_devices(me, core):
    return [ahead(me, d, core if own else 1 - core, core) for d, own in CHAIN]


def gathered_devices(me):
    core = me % 2
    devices = []
    for sign, mine in ((-1, core), (1, 1 - core)):
        devices += [ahead(me, 0, mine), ahead(me, sign, mine)]
        for d in (1, 2, 3):
            devices += [ahead(me, sign * (d + 1), mine), ahead(me, sign * d, 1 - mine)]
    return devices


def is_pair(ref, raw):
    return len(ref.shape) == (4 if raw else 3)


def blocks_kernel(first, direct, rows, entries, me_ref, *refs):
    n_field = 10 if direct else 1
    field_refs, refs = refs[:n_field], refs[n_field:]
    if direct:
        views = []
        for ref in field_refs:
            views += [ref.at[k] for k in range(ref.shape[0])] if is_pair(ref, first) else [ref]
        field_refs = views
    if first:
        square_ref, *refs = refs
    else:
        (scale_ref, wave_ref, correction_ref, dots_ref), refs = refs[:4], refs[4:]
    (sources, targets, live), (left_hbm, right_hbm), refs = refs[:3], refs[3:5], refs[5:]
    keep_ref, near_ref, far_ref, dot_ref, out_ref = refs[:5]
    left, right, field, total, left_sem, right_sem = refs[5:]
    slots, width = left.shape[0], total.shape[2]
    sectors = total.shape[0]

    def copies(slot):
        return (
            pltpu.make_async_copy(left_hbm.at[slot], left.at[slot], left_sem.at[slot]),
            pltpu.make_async_copy(right_hbm.at[slot], right.at[slot], right_sem.at[slot]),
        )

    for slot in range(slots):
        for copy in copies(slot):
            copy.start()

    me = me_ref[0]
    pieces = []
    owners = gathered_devices(me) if direct else [0]
    for ref, owner in zip(field_refs, owners):
        at = pl.multiple_of(owner * rows, rows) if direct else 0
        if direct and not first:
            for s, row, lanes in message_parts(sectors, rows, width):
                pieces.append((ref, (slice(None), lanes), s, pl.ds(at + row, HALF)))
        else:
            for s in range(sectors):
                pieces.append((ref, (s,), s, pl.ds(at, rows if direct else field.shape[1])))

    total[...] = jnp.zeros_like(total)
    dot = jnp.zeros((8, 128), jnp.float32)
    if first:
        for ref, part, _, _ in pieces:
            value = ref[part].astype(jnp.float32)
            dot += fold(value * value)
        scale = jnp.sqrt(jnp.sum(dot) / entries)
        out_ref[0] = scale
        for ref, part, s, place in pieces:
            field[s, place, :] = (ref[part].astype(jnp.float32) / scale).astype(jnp.bfloat16)
    else:
        for ref, part, s, place in pieces:
            field[s, place, :] = ref[part]

    used = live[0]

    def add_block(slot, carry):
        for copy in copies(slot):
            copy.wait()

        @pl.when(slot < used)
        def _():
            product = jnp.dot(
                left[slot], field[sources[slot]], preferred_element_type=jnp.float32
            ).astype(jnp.bfloat16)
            total[targets[slot]] += lax.dot_general(
                product, right[slot], (((1,), (1,)), ((), ())), preferred_element_type=jnp.float32
            )

        return carry

    lax.fori_loop(0, slots, add_block, 0)

    dot = jnp.zeros((8, 128), jnp.float32)
    if first:
        for ref, part, s, place in pieces:
            dot += fold(total[s, place, :] * ref[part].astype(jnp.float32))
        dot = dot / scale + square_ref[...] / scale / scale
    else:
        if direct:
            along = jnp.sum(sum(read_lanes(ref) for ref in field_refs)) / entries
        else:
            along = jnp.sum(dots_ref[...]) / entries
        out_ref[0] = along
        start = wave_ref[...].astype(jnp.float32) / scale_ref[0]
        projected = correction_ref[...] - along * start
        dot = fold_all(projected * projected)
    dot_ref[...] = dot
    if not direct:
        keep_ref[0] = total[...]
        return
    lanes = jnp.sum(dot, axis=0, keepdims=True)
    core = me % 2
    for k, owner in enumerate(chain_devices(me, core)):
        at = pl.multiple_of(owner * rows, rows)
        for s in range(sectors):
            keep_ref[k, s] = total[s, pl.ds(at, rows), :]
    for k, owner in enumerate(chain_devices(me, 1 - core)):
        at = pl.multiple_of(owner * rows, rows)
        ref = near_ref.at[k] if k < near_ref.shape[0] else far_ref.at[k - near_ref.shape[0]]
        for s, row, part in message_parts(sectors, rows, width):
            ref[:, part] = total[s, pl.ds(at + row, HALF), :].astype(jnp.bfloat16)
        write_lanes(ref, lanes)


def apply_blocks(me, fields, own, blocks, first, entries):
    left, right, *ints = blocks
    slots, order, width = left.shape
    direct = len(fields) == 10
    sectors = fields[0].shape[0] if first or not direct else own[1].shape[0]
    rows = fields[0].shape[1] if first else own[1].shape[1]
    if direct:
        kept, message = (8, sectors, rows, width), message_shape(sectors, rows, width)
    else:
        kept, message = (1, sectors, order, width), (HALF, LANES)
    own_specs = [VMEM] if first else [SMEM, VMEM, VMEM, VMEM]
    return pl.pallas_call(
        functools.partial(blocks_kernel, first, direct, rows, entries),
        in_specs=[SMEM] + [VMEM] * len(fields) + own_specs + [SMEM] * 3 + [HBM] * 2,
        out_specs=[VMEM, VMEM, VMEM, VMEM, SMEM],
        scratch_shapes=[
            pltpu.VMEM(left.shape, left.dtype),
            pltpu.VMEM(right.shape, right.dtype),
            pltpu.VMEM((sectors, order, width), jnp.bfloat16),
            pltpu.VMEM((sectors, order, width), jnp.float32),
            pltpu.SemaphoreType.DMA((slots,)),
            pltpu.SemaphoreType.DMA((slots,)),
        ],
        out_shape=[
            jax.ShapeDtypeStruct(kept, jnp.float32),
            jax.ShapeDtypeStruct((1, *message), jnp.bfloat16),
            jax.ShapeDtypeStruct((7, *message), jnp.bfloat16),
            jax.ShapeDtypeStruct((8, 128), jnp.float32),
            jax.ShapeDtypeStruct((1,), jnp.float32),
        ],
        compiler_params=PARAMS,
        cost_estimate=pl.CostEstimate(
            flops=4 * slots * order * order * width,
            bytes_accessed=4 * slots * order * order,
            transcendentals=0,
        ),
    )(me, *fields, *own, *ints, left, right)


def chain_kernel(links, keep_ref, other_ref, dot_ref, *refs):
    *arrived_refs, out_ref = refs
    sectors, rows, width = keep_ref.shape[1:]
    for place, (k, other, arrived) in enumerate(links):
        arrived_ref = arrived_refs[0].at[place] if arrived else None
        for s, row, part in message_parts(sectors, rows, width):
            value = keep_ref[k, s, row : row + HALF, :]
            value += other_ref[other, :, part].astype(jnp.float32)
            if arrived:
                value += arrived_ref[:, part].astype(jnp.float32)
            out_ref[place, :, part] = value.astype(jnp.bfloat16)
        lanes = jnp.sum(dot_ref[...], axis=0, keepdims=True) + read_lanes(other_ref.at[other])
        if arrived:
            lanes += read_lanes(arrived_ref)
        write_lanes(out_ref.at[place], lanes)


def chain(links, keep, other, dot, *arrived):
    return pl.pallas_call(
        functools.partial(chain_kernel, links),
        in_specs=[VMEM] * (3 + len(arrived)),
        out_specs=VMEM,
        out_shape=jax.ShapeDtypeStruct((len(links), *other.shape[1:]), jnp.bfloat16),
        compiler_params=PARAMS,
    )(keep, other, dot, *arrived)


def pair_kernel(one_ref, two_ref, out_ref):
    out_ref[0] = one_ref[...]
    out_ref[1] = two_ref[...]


def pair(one, two):
    return pl.pallas_call(
        pair_kernel,
        in_specs=[VMEM, VMEM],
        out_specs=VMEM,
        out_shape=jax.ShapeDtypeStruct((2, *one.shape), one.dtype),
        compiler_params=PARAMS,
    )(one, two)


def second_kernel(both_ref, out_ref):
    out_ref[...] = both_ref[1]


def second(both):
    return pl.pallas_call(
        second_kernel,
        in_specs=[VMEM],
        out_specs=VMEM,
        out_shape=jax.ShapeDtypeStruct(both.shape[1:], both.dtype),
        compiler_params=PARAMS,
    )(both)


def prepare_kernel(wave_ref, diag_ref, *refs):
    (source_ref, target_ref, live_ref, _), outs = refs[:4], refs[4:]
    own_ref, square_ref, source_out, target_out, live_out = outs
    own_ref[...] = wave_ref[...]
    wave = wave_ref[...].astype(jnp.float32)
    square_ref[...] = fold_all(diag_ref[...].astype(jnp.float32) * wave * wave)
    for k in range(source_ref.shape[0]):
        source_out[k] = source_ref[k]
        target_out[k] = target_ref[k]
    live_out[0] = live_ref[0]


def prepare(wave, diag, ints, after):
    return pl.pallas_call(
        prepare_kernel,
        in_specs=[VMEM, VMEM, SMEM, SMEM, SMEM, HBM],
        out_specs=[VMEM, VMEM, SMEM, SMEM, SMEM],
        out_shape=[
            jax.ShapeDtypeStruct(wave.shape, wave.dtype),
            jax.ShapeDtypeStruct((8, 128), jnp.float32),
            *(jax.ShapeDtypeStruct(i.shape, i.dtype) for i in ints),
        ],
        compiler_params=PARAMS,
    )(wave, diag, *ints, after)


def own_terms(direct, refs, sector):
    if not direct:
        return refs[0][sector]
    keep_ref, other_ref, _, ours_ref, theirs_ref = refs
    own = keep_ref.shape[0] - 1
    parts = []
    for s, row, part in message_parts(*keep_ref.shape[1:]):
        if s == sector:
            value = keep_ref[own, s, row : row + HALF, :]
            value += other_ref[other_ref.shape[0] - 1, :, part].astype(jnp.float32)
            value += ours_ref[0, :, part].astype(jnp.float32)
            value += theirs_ref[:, part].astype(jnp.float32)
            parts.append(value)
    return jnp.concatenate(parts, axis=0)


def own_scalar(direct, refs):
    if not direct:
        return jnp.sum(refs[1][...])
    _, other_ref, dot_ref, ours_ref, theirs_ref = refs
    lanes = jnp.sum(dot_ref[...], axis=0, keepdims=True)
    lanes += read_lanes(other_ref.at[other_ref.shape[0] - 1])
    return jnp.sum(lanes + read_lanes(ours_ref.at[0]) + read_lanes(theirs_ref))


def step_kernel(direct, entries, scale_ref, wave_ref, diag_ref, *refs):
    n_in = 5 if direct else 2
    ins, (first_ref, terms_ref, correction_ref, rounded_ref, dots_ref) = refs[:n_in], refs[n_in:]
    sectors, rows, width = wave_ref.shape
    ritz = own_scalar(direct, ins) / entries
    dots = jnp.zeros((8, 128), jnp.float32)
    for s in range(sectors):
        start = wave_ref[s].astype(jnp.float32) / scale_ref[0]
        diag = diag_ref[s].astype(jnp.float32)
        terms = own_terms(direct, ins, s)
        first = terms + diag * start
        correction = (first - ritz * start) / jnp.maximum(jnp.abs(diag - ritz), 1.0)
        first_ref[s] = first
        terms_ref[s] = terms
        correction_ref[s] = correction
        dots += fold(start * correction)
        if direct:
            for t, row, part in message_parts(sectors, rows, width):
                if t == s:
                    rounded_ref[:, part] = correction[row : row + HALF].astype(jnp.bfloat16)
        else:
            rounded_ref[s] = correction.astype(jnp.bfloat16)
    dots_ref[...] = dots
    if direct:
        write_lanes(rounded_ref, jnp.sum(dots, axis=0, keepdims=True))


def davidson_step(scale, wave, diag, ins, entries):
    full = jax.ShapeDtypeStruct(wave.shape, jnp.float32)
    direct = len(ins) == 5
    rounded = message_shape(*wave.shape) if direct else wave.shape
    return pl.pallas_call(
        functools.partial(step_kernel, direct, entries),
        in_specs=[SMEM, VMEM, VMEM] + [VMEM] * len(ins),
        out_specs=[VMEM] * 5,
        out_shape=[
            full,
            full,
            full,
            jax.ShapeDtypeStruct(rounded, jnp.bfloat16),
            jax.ShapeDtypeStruct((8, 128), jnp.float32),
        ],
        compiler_params=PARAMS,
    )(scale, wave, diag, *ins)


def finish_kernel(
    direct, entries, along_ref, scale_ref, wave_ref, diag_ref, terms_ref, correction_ref, *refs
):
    *ins, vector_ref, image_ref = refs
    sectors, rows, width = wave_ref.shape
    along = along_ref[0]
    norm = jnp.sqrt(own_scalar(direct, ins) / entries)
    for s in range(sectors):
        start = wave_ref[s].astype(jnp.float32) / scale_ref[0]
        second = (correction_ref[s] - along * start) / norm
        vector_ref[s] = second
        image = (own_terms(direct, ins, s) - along * terms_ref[s]) / norm
        image_ref[s] = image + diag_ref[s].astype(jnp.float32) * second


def finish(along, scale, wave, diag, terms, correction, ins, entries):
    full = jax.ShapeDtypeStruct(wave.shape, jnp.float32)
    return pl.pallas_call(
        functools.partial(finish_kernel, len(ins) == 5, entries),
        in_specs=[SMEM, SMEM] + [VMEM] * (4 + len(ins)),
        out_specs=[VMEM] * 2,
        out_shape=[full, full],
        compiler_params=PARAMS,
    )(along, scale, wave, diag, terms, correction, *ins)


def flip(value):
    return lax.ppermute(value, "term", [(i, i ^ 1) for i in range(16)])


def hop(value):
    order = [0, 2, 4, 6, 7, 5, 3, 1]
    pairs = []
    for place in range(8):
        for core, step in ((0, 1), (1, 7)):
            pairs.append((order[place] * 2 + core, order[(place + step) % 8] * 2 + core))
    return lax.ppermute(value, "term", pairs)


class RingPlan:
    def gather(self, own, meanwhile=None):
        arrived = hop(own)
        partner = flip(own)
        both = pair(arrived, partner)
        beside = None if meanwhile is None else meanwhile(both)
        mine, theirs = [own, arrived], [partner, flip(arrived)]
        for step in range(3):
            both = hop(both)
            if step == 1 and beside is not None:
                both, beside = lax.optimization_barrier((both, beside))
                mine[0] = beside[0]
            mine.append(both)
            theirs.append(flip(both))
        return mine + theirs, beside

    def scatter(self, keep, near, far, dot):
        near = flip(near)
        near, far = lax.optimization_barrier((near, far))
        far = flip(far)
        message = hop(chain(((0, 0, False),), keep, near, dot))
        message = hop(chain(((1, 0, True), (2, 1, False)), keep, far, dot, message))
        message = hop(chain(((3, 2, True), (4, 3, True)), keep, far, dot, message))
        message = hop(chain(((5, 4, True), (6, 5, True)), keep, far, dot, message))
        return [keep, far, dot, message, flip(second(message))]


class WholePlan:
    def gather(self, own, meanwhile=None):
        whole = lax.all_gather(own, "term", axis=1, tiled=True)
        return [whole], None if meanwhile is None else meanwhile(own)

    def scatter(self, keep, near, far, dot):
        rows = lax.psum_scatter(keep[0], "term", scatter_dimension=1, tiled=True)
        return [rows, lax.psum(dot, "term")]


def on_device(
    wavefunction, diagonal, left_blocks, right_blocks, block_source, block_target, live_count
):
    devices = lax.axis_size("term")
    sectors, rows, width = wavefunction.shape
    entries = float(sectors * rows * devices * width)
    plan = RingPlan() if devices == 16 else WholePlan()
    me = lax.axis_index("term").astype(jnp.int32).reshape(1)
    ints = (block_source, block_target, live_count)

    beside = functools.partial(prepare, wavefunction, diagonal, ints)
    fields, (_, square, *ints) = plan.gather(wavefunction, beside)
    blocks = (left_blocks, right_blocks, *ints)
    *terms, scale = apply_blocks(me, fields, (square,), blocks, True, entries)
    first_image, terms, correction, rounded, dots = davidson_step(
        scale, wavefunction, diagonal, plan.scatter(*terms), entries
    )
    fields, _ = plan.gather(rounded)
    if devices != 16:
        dots = lax.psum(dots, "term")
    own = (scale, wavefunction, correction, dots)
    *second_terms, along = apply_blocks(me, fields, own, blocks, False, entries)
    second_vector, second_image = finish(
        along, scale, wavefunction, diagonal, terms, correction, plan.scatter(*second_terms), entries
    )
    return (first_image, second_vector, second_image)


def solution(mesh):
    placed = (
        P("grp", "term", None),
        P("grp", "term", None),
        P(("grp", "term"), None, None),
        P(("grp", "term"), None, None),
        P(("grp", "term")),
        P(("grp", "term")),
        P(("grp", "term")),
    )
    return jax.shard_map(
        on_device,
        mesh=mesh,
        in_specs=placed,
        out_specs=(P("grp", "term", None), P("grp", "term", None), P("grp", "term", None)),
        check_vma=False,
    )
```

```python
import functools

import jax
import jax.numpy as jnp
from jax import lax
from jax.experimental import pallas as pl
from jax.experimental.pallas import tpu as pltpu
from jax.sharding import PartitionSpec as P

VMEM = pl.BlockSpec(memory_space=pltpu.VMEM)
SMEM = pl.BlockSpec(memory_space=pltpu.SMEM)
HBM = pl.BlockSpec(memory_space=pltpu.HBM)
PARAMS = pltpu.CompilerParams(vmem_limit_bytes=48 * 1024 * 1024)
HALF = 16
LANES = 128


def fold(value):
    rows, width = value.shape
    summed = jnp.sum(value.reshape(rows // 8, 8, width), axis=0)
    return sum(summed[:, k * 128 : (k + 1) * 128] for k in range(width // 128))


def fold_all(value):
    return sum(fold(value[s]) for s in range(value.shape[0]))


def message_shape(sectors, rows, width):
    return (HALF, rows // HALF * sectors * width + LANES)


def quarter_shapes(sectors, width):
    return (HALF, sectors * width + LANES), (HALF, sectors * width)


def lanes_at(ref):
    lanes = ref.shape[1] - LANES
    first = lanes if lanes % 1024 else lanes // 2
    return slice(first, first + LANES)


def write_lanes(ref, lanes):
    whole = jnp.broadcast_to(lanes, (HALF, LANES))
    high = whole.astype(jnp.bfloat16).astype(jnp.float32)
    rest = whole - high
    middle = rest.astype(jnp.bfloat16).astype(jnp.float32)
    low = rest - middle
    row = lax.broadcasted_iota(jnp.int32, whole.shape, 0)
    value = jnp.where(row == 0, high, jnp.where(row == 1, middle, jnp.where(row == 2, low, 0.0)))
    ref[:, lanes_at(ref)] = value.astype(jnp.bfloat16)


def read_lanes(ref):
    return jnp.sum(ref[:, lanes_at(ref)].astype(jnp.float32), axis=0, keepdims=True)


def message_parts(sectors, rows, width):
    for h in range(rows // HALF):
        for s in range(sectors):
            at = (h * sectors + s) * width + (LANES if h else 0)
            yield s, h * HALF, slice(at, at + width)


def quarter_parts(sectors, width):
    for s in range(sectors):
        yield s, slice(s * width, (s + 1) * width)


def chip_at(place):
    place = lax.rem(place + 8, 8)
    return jnp.where(place < 4, 2 * place, 15 - 2 * place)


def ring_place(me):
    chip, core = me // 2, me % 2
    place = jnp.where(chip % 2 == 0, chip // 2, (15 - chip) // 2)
    return place, core


def ahead(me, distance, half, core=None):
    place, own = ring_place(me)
    core = own if core is None else core
    return chip_at(place + (1 - 2 * core) * distance) * 2 + half


CHAIN = ((4, True), (3, True), (3, False), (2, True), (2, False), (1, True), (1, False), (0, True))


def chain_devices(me, core):
    return [ahead(me, d, core if own else 1 - core, core) for d, own in CHAIN]


def gathered_devices(me):
    core = me % 2
    devices = []
    for sign, mine in ((-1, core), (1, 1 - core)):
        devices += [ahead(me, 0, mine), ahead(me, sign, mine)]
        for d in (1, 2, 3):
            devices += [ahead(me, sign * (d + 1), mine), ahead(me, sign * d, 1 - mine)]
    return devices


def blocks_kernel(first, direct, rows, entries, me_ref, *refs):
    n_field = 10 if direct else 1
    field_refs, refs = refs[:n_field], refs[n_field:]
    if direct:
        views = []
        for ref in field_refs:
            views += [ref.at[k] for k in range(ref.shape[0])] if len(ref.shape) == 3 else [ref]
        field_refs = views
    if first:
        square_ref, *refs = refs
    else:
        (scale_ref, wave_ref, correction_ref, dots_ref), refs = refs[:4], refs[4:]
    (sources, targets, live), (left_hbm, right_hbm), refs = refs[:3], refs[3:5], refs[5:]
    keep_ref, near_ref, far_ref, dot_ref, out_ref = refs[:5]
    left, right, field, total, left_sem, right_sem = refs[5:]
    slots, width = left.shape[0], total.shape[2]
    sectors = total.shape[0]

    def copies(slot):
        return (
            pltpu.make_async_copy(left_hbm.at[slot], left.at[slot], left_sem.at[slot]),
            pltpu.make_async_copy(right_hbm.at[slot], right.at[slot], right_sem.at[slot]),
        )

    for slot in range(slots):
        for copy in copies(slot):
            copy.start()

    me = me_ref[0]
    pieces = []
    owners = gathered_devices(me) if direct else [0]
    for ref, owner in zip(field_refs, owners):
        at = pl.multiple_of(owner * rows, rows) if direct else 0
        if direct:
            for s, row, lanes in message_parts(sectors, rows, width):
                pieces.append((ref, (slice(None), lanes), s, pl.ds(at + row, HALF)))
        else:
            for s in range(sectors):
                pieces.append((ref, (s,), s, pl.ds(at, field.shape[1])))

    total[...] = jnp.zeros_like(total)
    dot = jnp.zeros((8, 128), jnp.float32)
    if first:
        for ref, part, _, _ in pieces:
            value = ref[part].astype(jnp.float32)
            dot += fold(value * value)
        scale = jnp.sqrt(jnp.sum(dot) / entries)
        out_ref[0] = scale
        inverse = 1.0 / scale
        for ref, part, s, place in pieces:
            field[s, place, :] = (ref[part].astype(jnp.float32) * inverse).astype(jnp.bfloat16)
    else:
        for ref, part, s, place in pieces:
            field[s, place, :] = ref[part]

    used = live[0]

    def add_block(slot, carry):
        for copy in copies(slot):
            copy.wait()

        @pl.when(slot < used)
        def _():
            product = jnp.dot(
                left[slot], field[sources[slot]], preferred_element_type=jnp.float32
            ).astype(jnp.bfloat16)
            total[targets[slot]] += lax.dot_general(
                product, right[slot], (((1,), (1,)), ((), ())), preferred_element_type=jnp.float32
            )

        return carry

    lax.fori_loop(0, slots, add_block, 0)

    dot = jnp.zeros((8, 128), jnp.float32)
    if first:
        for ref, part, s, place in pieces:
            dot += fold(total[s, place, :] * ref[part].astype(jnp.float32))
        dot = dot / scale + square_ref[...] / scale / scale
    else:
        if direct:
            along = jnp.sum(sum(read_lanes(ref) for ref in field_refs)) / entries
        else:
            along = jnp.sum(dots_ref[...]) / entries
        out_ref[0] = along
        start = wave_ref[...].astype(jnp.float32) / scale_ref[0]
        projected = correction_ref[...] - along * start
        dot = fold_all(projected * projected)
    dot_ref[...] = dot
    if not direct:
        keep_ref[0] = total[...]
        return
    lanes = jnp.sum(dot, axis=0, keepdims=True)
    core = me % 2
    for k, owner in enumerate(chain_devices(me, core)):
        at = pl.multiple_of(owner * rows, rows)
        for s in range(sectors):
            keep_ref[k, s] = total[s, pl.ds(at, rows), :]
    for k, owner in enumerate(chain_devices(me, 1 - core)):
        at = pl.multiple_of(owner * rows, rows)
        ref = near_ref.at[k] if k < near_ref.shape[0] else far_ref.at[k - near_ref.shape[0]]
        for s, row, part in message_parts(sectors, rows, width):
            ref[:, part] = total[s, pl.ds(at + row, HALF), :].astype(jnp.bfloat16)
        write_lanes(ref, lanes)


def apply_blocks(me, fields, own, blocks, shape, first, entries):
    left, right, *ints = blocks
    slots, order, width = left.shape
    direct = len(fields) == 10
    sectors, rows, _ = shape
    if direct:
        kept, message = (8, sectors, rows, width), message_shape(sectors, rows, width)
    else:
        kept, message = (1, sectors, order, width), (HALF, LANES)
    own_specs = [VMEM] if first else [SMEM, VMEM, VMEM, VMEM]
    return pl.pallas_call(
        functools.partial(blocks_kernel, first, direct, rows, entries),
        in_specs=[SMEM] + [VMEM] * len(fields) + own_specs + [SMEM] * 3 + [HBM] * 2,
        out_specs=[VMEM, VMEM, VMEM, VMEM, SMEM],
        scratch_shapes=[
            pltpu.VMEM(left.shape, left.dtype),
            pltpu.VMEM(right.shape, right.dtype),
            pltpu.VMEM((sectors, order, width), jnp.bfloat16),
            pltpu.VMEM((sectors, order, width), jnp.float32),
            pltpu.SemaphoreType.DMA((slots,)),
            pltpu.SemaphoreType.DMA((slots,)),
        ],
        out_shape=[
            jax.ShapeDtypeStruct(kept, jnp.float32),
            jax.ShapeDtypeStruct((1, *message), jnp.bfloat16),
            jax.ShapeDtypeStruct((7, *message), jnp.bfloat16),
            jax.ShapeDtypeStruct((8, 128), jnp.float32),
            jax.ShapeDtypeStruct((1,), jnp.float32),
        ],
        compiler_params=PARAMS,
        cost_estimate=pl.CostEstimate(
            flops=4 * slots * order * order * width,
            bytes_accessed=4 * slots * order * order,
            transcendentals=0,
        ),
    )(me, *fields, *own, *ints, left, right)


def chain_kernel(k, other, h, keep_ref, other_ref, dot_ref, *refs):
    *arrived_refs, out_ref = refs
    sectors, rows, width = keep_ref.shape[1:]
    places = [p for p in message_parts(sectors, rows, width) if p[1] == h * HALF]
    for (s, row, part), (_, lanes) in zip(places, quarter_parts(sectors, width)):
        value = keep_ref[k, s, row : row + HALF, :]
        value += other_ref[other, :, part].astype(jnp.float32)
        for ref in arrived_refs:
            value += ref[:, lanes].astype(jnp.float32)
        out_ref[:, lanes] = value.astype(jnp.bfloat16)
    if h == 0:
        lanes = jnp.sum(dot_ref[...], axis=0, keepdims=True) + read_lanes(other_ref.at[other])
        for ref in arrived_refs:
            lanes += read_lanes(ref)
        write_lanes(out_ref, lanes)


def chain(k, other, h, keep, terms, dot, *arrived):
    sectors, _, width = keep.shape[1:]
    return pl.pallas_call(
        functools.partial(chain_kernel, k, other, h),
        in_specs=[VMEM] * (3 + len(arrived)),
        out_specs=VMEM,
        out_shape=jax.ShapeDtypeStruct(quarter_shapes(sectors, width)[h], jnp.bfloat16),
        compiler_params=PARAMS,
    )(keep, terms, dot, *arrived)


def pack_kernel(*refs):
    *quarter_refs, out_ref = refs
    for k in range(len(quarter_refs) // 2):
        first = quarter_refs[2 * k].shape[1]
        out_ref[k, :, :first] = quarter_refs[2 * k][...]
        out_ref[k, :, first:] = quarter_refs[2 * k + 1][...]


def pack(*quarters):
    lanes = quarters[0].shape[1] + quarters[1].shape[1]
    return pl.pallas_call(
        pack_kernel,
        in_specs=[VMEM] * len(quarters),
        out_specs=VMEM,
        out_shape=jax.ShapeDtypeStruct((len(quarters) // 2, HALF, lanes), jnp.bfloat16),
        compiler_params=PARAMS,
    )(*quarters)


def split_kernel(whole_ref, one_ref, two_ref):
    first = one_ref.shape[1]
    one_ref[...] = whole_ref[:, :first]
    two_ref[...] = whole_ref[:, first:]


def split(whole, sectors, width):
    return pl.pallas_call(
        split_kernel,
        in_specs=[VMEM],
        out_specs=[VMEM] * 2,
        out_shape=[jax.ShapeDtypeStruct(q, whole.dtype) for q in quarter_shapes(sectors, width)],
        compiler_params=PARAMS,
    )(whole)


def message_kernel(wave_ref, whole_ref, one_ref, two_ref):
    sectors, rows, width = wave_ref.shape
    first = one_ref.shape[1]
    for s, row, part in message_parts(sectors, rows, width):
        value = wave_ref[s, row : row + HALF, :]
        whole_ref[:, part] = value
        if row == 0:
            one_ref[:, part] = value
        else:
            two_ref[:, part.start - first : part.stop - first] = value
    for ref in (whole_ref, one_ref):
        write_lanes(ref, jnp.zeros((1, LANES), jnp.float32))


def as_message(wave):
    sectors, rows, width = wave.shape
    shapes = (message_shape(sectors, rows, width), *quarter_shapes(sectors, width))
    return pl.pallas_call(
        message_kernel,
        in_specs=[VMEM],
        out_specs=[VMEM] * 3,
        out_shape=[jax.ShapeDtypeStruct(q, wave.dtype) for q in shapes],
        compiler_params=PARAMS,
    )(wave)


def prepare_kernel(wave_ref, diag_ref, *refs):
    (source_ref, target_ref, live_ref, _), outs = refs[:4], refs[4:]
    square_ref, source_out, target_out, live_out = outs
    wave = wave_ref[...].astype(jnp.float32)
    square_ref[...] = fold_all(diag_ref[...].astype(jnp.float32) * wave * wave)
    for k in range(source_ref.shape[0]):
        source_out[k] = source_ref[k]
        target_out[k] = target_ref[k]
    live_out[0] = live_ref[0]


def prepare(wave, diag, ints, after):
    return pl.pallas_call(
        prepare_kernel,
        in_specs=[VMEM, VMEM, SMEM, SMEM, SMEM, HBM],
        out_specs=[VMEM, SMEM, SMEM, SMEM],
        out_shape=[
            jax.ShapeDtypeStruct((8, 128), jnp.float32),
            *(jax.ShapeDtypeStruct(i.shape, i.dtype) for i in ints),
        ],
        compiler_params=PARAMS,
    )(wave, diag, *ints, after)


def own_terms(direct, refs, sector):
    if not direct:
        return refs[0][sector]
    keep_ref, other_ref, _, *arrived_refs = refs
    own, width = keep_ref.shape[0] - 1, keep_ref.shape[3]
    parts = []
    for s, row, part in message_parts(*keep_ref.shape[1:]):
        if s == sector:
            value = keep_ref[own, s, row : row + HALF, :]
            value += other_ref[other_ref.shape[0] - 1, :, part].astype(jnp.float32)
            lanes = slice(s * width, (s + 1) * width)
            for ref in arrived_refs[row // HALF :: 2]:
                value += ref[:, lanes].astype(jnp.float32)
            parts.append(value)
    return jnp.concatenate(parts, axis=0)


def own_scalar(direct, refs):
    if not direct:
        return jnp.sum(refs[1][...])
    _, other_ref, dot_ref, *arrived_refs = refs
    lanes = jnp.sum(dot_ref[...], axis=0, keepdims=True)
    lanes += read_lanes(other_ref.at[other_ref.shape[0] - 1])
    return jnp.sum(lanes + sum(read_lanes(ref) for ref in arrived_refs[::2]))


def step_kernel(direct, entries, scale_ref, wave_ref, diag_ref, *refs):
    n_in = 7 if direct else 2
    ins, outs = refs[:n_in], refs[n_in:]
    first_ref, terms_ref, correction_ref, dots_ref, *rounded_refs = outs
    sectors, rows, width = wave_ref.shape
    ritz = own_scalar(direct, ins) / entries
    dots = jnp.zeros((8, 128), jnp.float32)
    for s in range(sectors):
        start = wave_ref[s].astype(jnp.float32) / scale_ref[0]
        diag = diag_ref[s].astype(jnp.float32)
        terms = own_terms(direct, ins, s)
        first = terms + diag * start
        correction = (first - ritz * start) / jnp.maximum(jnp.abs(diag - ritz), 1.0)
        first_ref[s] = first
        terms_ref[s] = terms
        correction_ref[s] = correction
        dots += fold(start * correction)
        if direct:
            for t, row, part in message_parts(sectors, rows, width):
                if t == s:
                    value = correction[row : row + HALF].astype(jnp.bfloat16)
                    rounded_refs[0][:, part] = value
                    lanes = slice(s * width, (s + 1) * width)
                    rounded_refs[1 + row // HALF][:, lanes] = value
        else:
            rounded_refs[0][s] = correction.astype(jnp.bfloat16)
    dots_ref[...] = dots
    if direct:
        for ref in rounded_refs[:2]:
            write_lanes(ref, jnp.sum(dots, axis=0, keepdims=True))


def davidson_step(scale, wave, diag, ins, entries):
    full = jax.ShapeDtypeStruct(wave.shape, jnp.float32)
    direct = len(ins) == 7
    sectors, rows, width = wave.shape
    rounded = [wave.shape]
    if direct:
        rounded = [message_shape(sectors, rows, width), *quarter_shapes(sectors, width)]
    return pl.pallas_call(
        functools.partial(step_kernel, direct, entries),
        in_specs=[SMEM, VMEM, VMEM] + [VMEM] * len(ins),
        out_specs=[VMEM] * (4 + len(rounded)),
        out_shape=[
            full,
            full,
            full,
            jax.ShapeDtypeStruct((8, 128), jnp.float32),
            *(jax.ShapeDtypeStruct(shape, jnp.bfloat16) for shape in rounded),
        ],
        compiler_params=PARAMS,
    )(scale, wave, diag, *ins)


def finish_kernel(
    direct, entries, along_ref, scale_ref, wave_ref, diag_ref, terms_ref, correction_ref, *refs
):
    *ins, vector_ref, image_ref = refs
    sectors, rows, width = wave_ref.shape
    along = along_ref[0]
    norm = jnp.sqrt(own_scalar(direct, ins) / entries)
    for s in range(sectors):
        start = wave_ref[s].astype(jnp.float32) / scale_ref[0]
        second = (correction_ref[s] - along * start) / norm
        vector_ref[s] = second
        image = (own_terms(direct, ins, s) - along * terms_ref[s]) / norm
        image_ref[s] = image + diag_ref[s].astype(jnp.float32) * second


def finish(along, scale, wave, diag, terms, correction, ins, entries):
    full = jax.ShapeDtypeStruct(wave.shape, jnp.float32)
    return pl.pallas_call(
        functools.partial(finish_kernel, len(ins) == 7, entries),
        in_specs=[SMEM, SMEM] + [VMEM] * (4 + len(ins)),
        out_specs=[VMEM] * 2,
        out_shape=[full, full],
        compiler_params=PARAMS,
    )(along, scale, wave, diag, terms, correction, *ins)


def flip(value):
    return lax.ppermute(value, "term", [(i, i ^ 1) for i in range(16)])


def hop(value):
    order = [0, 2, 4, 6, 7, 5, 3, 1]
    pairs = []
    for place in range(8):
        for core, step in ((0, 1), (1, 7)):
            pairs.append((order[place] * 2 + core, order[(place + step) % 8] * 2 + core))
    return lax.ppermute(value, "term", pairs)


class RingPlan:
    def __init__(self, shape):
        self.sectors, _, self.width = shape

    def message(self, wave):
        return as_message(wave)

    def gather(self, message, meanwhile=None):
        own, *one = message
        one = [hop(q) for q in one]
        partner = flip(own)
        two = split(partner, self.sectors, self.width)
        arrived = pack(*one)
        beside = None if meanwhile is None else meanwhile(arrived)
        mine, theirs = [own, arrived], [partner, flip(arrived)]
        for step in range(3):
            one = [hop(q) for q in one]
            two = [hop(q) for q in two]
            if step == 1 and beside is not None:
                two[1], beside = lax.optimization_barrier((two[1], beside))
            arrived = pack(*one, *two)
            mine.append(arrived)
            theirs.append(flip(arrived))
        return mine + theirs, beside

    def scatter(self, keep, near, far, dot):
        near = flip(near)
        near, far = lax.optimization_barrier((near, far))
        far = flip(far)
        one = [hop(chain(0, 0, h, keep, near, dot)) for h in (0, 1)]
        two = []
        for k in (1, 3, 5):
            arrived = zip((0, 1), one)
            one = [hop(chain(k, k - 1, h, keep, far, dot, q)) for h, q in arrived]
            arrived = zip((0, 1), two) if two else ((0,), (1,))
            two = [hop(chain(k + 1, k, h, keep, far, dot, *q)) for h, *q in arrived]
        return [keep, far, dot, *one, *(flip(q) for q in two)]


class WholePlan:
    def __init__(self, shape):
        pass

    def message(self, wave):
        return [wave]

    def gather(self, message, meanwhile=None):
        (own,) = message
        whole = lax.all_gather(own, "term", axis=1, tiled=True)
        return [whole], None if meanwhile is None else meanwhile(own)

    def scatter(self, keep, near, far, dot):
        rows = lax.psum_scatter(keep[0], "term", scatter_dimension=1, tiled=True)
        return [rows, lax.psum(dot, "term")]


def on_device(
    wavefunction, diagonal, left_blocks, right_blocks, block_source, block_target, live_count
):
    devices = lax.axis_size("term")
    sectors, rows, width = wavefunction.shape
    entries = float(sectors * rows * devices * width)
    plan = (RingPlan if devices == 16 else WholePlan)(wavefunction.shape)
    me = lax.axis_index("term").astype(jnp.int32).reshape(1)
    ints = (block_source, block_target, live_count)

    beside = functools.partial(prepare, wavefunction, diagonal, ints)
    fields, (square, *ints) = plan.gather(plan.message(wavefunction), beside)
    blocks = (left_blocks, right_blocks, *ints)
    *terms, scale = apply_blocks(
        me, fields, (square,), blocks, wavefunction.shape, True, entries
    )
    first_image, terms, correction, dots, *rounded = davidson_step(
        scale, wavefunction, diagonal, plan.scatter(*terms), entries
    )
    fields, _ = plan.gather(rounded)
    if devices != 16:
        dots = lax.psum(dots, "term")
    own = (scale, wavefunction, correction, dots)
    *second_terms, along = apply_blocks(
        me, fields, own, blocks, wavefunction.shape, False, entries
    )
    second_vector, second_image = finish(
        along, scale, wavefunction, diagonal, terms, correction, plan.scatter(*second_terms), entries
    )
    return (first_image, second_vector, second_image)


def solution(mesh):
    placed = (
        P("grp", "term", None),
        P("grp", "term", None),
        P(("grp", "term"), None, None),
        P(("grp", "term"), None, None),
        P(("grp", "term")),
        P(("grp", "term")),
        P(("grp", "term")),
    )
    return jax.shard_map(
        on_device,
        mesh=mesh,
        in_specs=placed,
        out_specs=(P("grp", "term", None), P("grp", "term", None), P("grp", "term", None)),
        check_vma=False,
    )
```

```python
import functools

import jax
import jax.numpy as jnp
from jax import lax
from jax.experimental import pallas as pl
from jax.experimental.pallas import tpu as pltpu
from jax.sharding import PartitionSpec as P

VMEM = pl.BlockSpec(memory_space=pltpu.VMEM)
SMEM = pl.BlockSpec(memory_space=pltpu.SMEM)
HBM = pl.BlockSpec(memory_space=pltpu.HBM)
PARAMS = pltpu.CompilerParams(vmem_limit_bytes=32 * 1024 * 1024)
HALF = 16
LANES = 128


def fold(value):
    rows, width = value.shape
    summed = jnp.sum(value.reshape(rows // 8, 8, width), axis=0)
    return sum(summed[:, k * 128 : (k + 1) * 128] for k in range(width // 128))


def down(value):
    return jnp.sum(value, axis=0, keepdims=True)


def halves(rows, width, start=0):
    for h in range(rows // HALF):
        yield h * HALF, slice(start + h * width, start + (h + 1) * width)


def write_lanes(ref, at, lanes):
    whole = jnp.broadcast_to(lanes, (HALF, LANES))
    high = whole.astype(jnp.bfloat16).astype(jnp.float32)
    rest = whole - high
    middle = rest.astype(jnp.bfloat16).astype(jnp.float32)
    low = rest - middle
    row = lax.broadcasted_iota(jnp.int32, whole.shape, 0)
    value = jnp.where(row == 0, high, jnp.where(row == 1, middle, jnp.where(row == 2, low, 0.0)))
    ref[:, at : at + LANES] = value.astype(jnp.bfloat16)


def read_lanes(ref, at):
    return down(ref[:, at : at + LANES].astype(jnp.float32))


def chip_at(place):
    place = lax.rem(place + 8, 8)
    return jnp.where(place < 4, 2 * place, 15 - 2 * place)


def ring_place(me):
    chip, core = me // 2, me % 2
    place = jnp.where(chip % 2 == 0, chip // 2, (15 - chip) // 2)
    return place, core


def ahead(me, distance, half, core=None):
    place, own = ring_place(me)
    core = own if core is None else core
    return chip_at(place + (1 - 2 * core) * distance) * 2 + half


CHAIN = ((4, True), (3, True), (3, False), (2, True), (2, False), (1, True), (1, False), (0, True))


def chain_device(me, core, k):
    distance, own = CHAIN[k]
    return ahead(me, distance, core if own else 1 - core, core)


def gathered_devices(me):
    core = me % 2
    devices = []
    for sign, mine in ((-1, core), (1, 1 - core)):
        devices += [ahead(me, 0, mine), ahead(me, sign, mine)]
        for d in (1, 2, 3):
            devices += [ahead(me, sign * (d + 1), mine), ahead(me, sign * d, 1 - mine)]
    return devices


def message_kernel(wave_ref, *out_refs):
    sectors, rows, width = wave_ref.shape
    for s in range(sectors):
        for row, part in halves(rows, width):
            out_refs[s][0, :, part] = wave_ref[s, row : row + HALF, :]


def as_messages(wave):
    sectors, rows, width = wave.shape
    shape = (1, HALF, rows // HALF * width)
    return pl.pallas_call(
        message_kernel,
        in_specs=[VMEM],
        out_specs=[VMEM] * sectors,
        out_shape=[jax.ShapeDtypeStruct(shape, wave.dtype)] * sectors,
        compiler_params=PARAMS,
    )(wave)


def pair_kernel(one_ref, two_ref, out_ref):
    out_ref[0] = one_ref[0]
    out_ref[1] = two_ref[0]


def pair(one, two):
    return pl.pallas_call(
        pair_kernel,
        in_specs=[VMEM, VMEM],
        out_specs=VMEM,
        out_shape=jax.ShapeDtypeStruct((2, *one.shape[1:]), one.dtype),
        compiler_params=PARAMS,
    )(one, two)


def pack_kernel(*refs):
    *in_refs, out_ref = refs
    at = 0
    for ref in in_refs:
        for k in range(ref.shape[0]):
            out_ref[at, :, : ref.shape[2]] = ref[k]
            at += 1


def pack(*messages):
    lanes = max(m.shape[2] for m in messages)
    count = sum(m.shape[0] for m in messages)
    return pl.pallas_call(
        pack_kernel,
        in_specs=[VMEM] * len(messages),
        out_specs=VMEM,
        out_shape=jax.ShapeDtypeStruct((count, HALF, lanes), messages[0].dtype),
        compiler_params=PARAMS,
    )(*messages)


def prepare_kernel(diag_ref, _, *refs):
    *wave_refs, square_ref = refs
    sectors, rows, width = diag_ref.shape
    square = jnp.zeros((8, 128), jnp.float32)
    for s in range(sectors):
        for row, part in halves(rows, width):
            wave = wave_refs[s][0, :, part].astype(jnp.float32)
            square += fold(diag_ref[s, row : row + HALF, :].astype(jnp.float32) * wave * wave)
    square_ref[...] = square


def prepare(diag, waves, after):
    return pl.pallas_call(
        prepare_kernel,
        in_specs=[VMEM, HBM] + [VMEM] * len(waves),
        out_specs=VMEM,
        out_shape=jax.ShapeDtypeStruct((8, 128), jnp.float32),
        compiler_params=PARAMS,
    )(diag, after, *waves)


def blocks_kernel(first, sectors, rows, entries, me_ref, ints_ref, *refs):
    packed_ref, refs = refs[0], refs[1:]
    views = []
    for s in range(sectors):
        mine, (partner, last), refs = refs[:5], refs[5:7], refs[7:]
        view = [ref.at[k] for ref in mine for k in range(ref.shape[0])]
        view += [partner.at[0], *(packed_ref.at[s * 5 + k] for k in range(5)), last.at[0], last.at[1]]
        views.append(view)
    if first:
        (square_ref,), refs = refs[:1], refs[1:]
    else:
        (scale_ref, wave_ref), corrections, refs = refs[:2], refs[2 : 2 + sectors], refs[2 + sectors :]
    left_hbm, right_hbm, *refs = refs
    total, near_ref, far_ref, dot_ref, out_ref, left, right, field, left_sem, right_sem = refs
    slots, width = left.shape[0], total.shape[2]
    data = rows // HALF * width

    def copies(slot):
        return (
            pltpu.make_async_copy(left_hbm.at[slot], left.at[slot], left_sem.at[slot]),
            pltpu.make_async_copy(right_hbm.at[slot], right.at[slot], right_sem.at[slot]),
        )

    for slot in range(slots):
        for copy in copies(slot):
            copy.start()

    me = me_ref[0]
    pieces = []
    for k, owner in enumerate(gathered_devices(me)):
        for s in range(sectors):
            ref = views[s][k]
            for row, part in halves(rows, width):
                at = pl.ds(pl.multiple_of(owner * rows + row, HALF), HALF)
                pieces.append((ref, part, s, at))

    total[...] = jnp.zeros_like(total)
    if first:
        dot = jnp.zeros((8, 128), jnp.float32)
        for ref, part, _, _ in pieces:
            value = ref[:, part].astype(jnp.float32)
            dot += fold(value * value)
        scale = jnp.sqrt(jnp.sum(dot) / entries)
        out_ref[0] = scale
        inverse = 1.0 / scale
        for ref, part, s, at in pieces:
            field[s, at, :] = (ref[:, part].astype(jnp.float32) * inverse).astype(jnp.bfloat16)
    else:
        for ref, part, s, at in pieces:
            field[s, at, :] = ref[:, part]

    used = ints_ref[2 * slots]

    def add_pair(step, carry):
        one, two = 2 * step, 2 * step + 1
        for slot in (one, two):
            for copy in copies(slot):
                copy.wait()

        @pl.when(one < used)
        def _():
            products = [
                jnp.dot(
                    left[slot], field[ints_ref[slot]], preferred_element_type=jnp.float32
                ).astype(jnp.bfloat16)
                for slot in (one, two)
            ]
            products[1] = jnp.where(two < used, products[1], jnp.zeros_like(products[1]))
            for slot, product in zip((one, two), products):
                total[ints_ref[slots + slot]] += lax.dot_general(
                    product,
                    right[slot],
                    (((1,), (1,)), ((), ())),
                    preferred_element_type=jnp.float32,
                )

        return carry

    lax.fori_loop(0, slots // 2, add_pair, 0)

    dot = jnp.zeros((8, 128), jnp.float32)
    if first:
        for ref, part, s, at in pieces:
            dot += fold(total[s, at, :] * ref[:, part].astype(jnp.float32))
        dot = dot * inverse + square_ref[...] * inverse * inverse
    else:
        lanes = sum(read_lanes(view, data) for view in views[sectors - 1])
        along = jnp.sum(lanes) / entries
        out_ref[0] = along
        for s in range(sectors):
            start = wave_ref[s].astype(jnp.float32) / scale_ref[0]
            projected = corrections[s][...] - along * start
            dot += fold(projected * projected)
    dot_ref[...] = dot
    lanes = down(dot)
    core = me % 2
    for k in range(len(CHAIN)):
        owner = chain_device(me, 1 - core, k)
        ref = near_ref.at[k] if k < near_ref.shape[0] else far_ref.at[k - near_ref.shape[0]]
        for s in range(sectors):
            for row, part in halves(rows, width, s * data):
                at = pl.ds(pl.multiple_of(owner * rows + row, HALF), HALF)
                ref[:, part] = total[s, at, :].astype(jnp.bfloat16)
        write_lanes(ref, sectors * data, lanes)


def apply_blocks(me, ints, fields, packed, own, left, right, shape, first, entries):
    slots, order, width = left.shape
    sectors, rows, _ = shape
    piece = (HALF, sectors * (rows // HALF) * width + LANES)
    pieces = [packed]
    for mine, partner, last in fields:
        pieces += [*mine, partner, last]
    own_specs = [VMEM] if first else [SMEM] + [VMEM] * (1 + sectors)
    return pl.pallas_call(
        functools.partial(blocks_kernel, first, sectors, rows, entries),
        in_specs=[SMEM, SMEM] + [VMEM] * len(pieces) + own_specs + [HBM] * 2,
        out_specs=[VMEM, VMEM, VMEM, VMEM, SMEM],
        scratch_shapes=[
            pltpu.VMEM(left.shape, left.dtype),
            pltpu.VMEM(right.shape, right.dtype),
            pltpu.VMEM((sectors, order, width), jnp.bfloat16),
            pltpu.SemaphoreType.DMA((slots,)),
            pltpu.SemaphoreType.DMA((slots,)),
        ],
        out_shape=[
            jax.ShapeDtypeStruct((sectors, order, width), jnp.float32),
            jax.ShapeDtypeStruct((1, *piece), jnp.bfloat16),
            jax.ShapeDtypeStruct((len(CHAIN) - 1, *piece), jnp.bfloat16),
            jax.ShapeDtypeStruct((8, 128), jnp.float32),
            jax.ShapeDtypeStruct((1,), jnp.float32),
        ],
        compiler_params=PARAMS,
        cost_estimate=pl.CostEstimate(
            flops=4 * slots * order * order * width,
            bytes_accessed=4 * slots * order * order,
            transcendentals=0,
        ),
    )(me, ints, *pieces, *own, left, right)


def chip_terms(me, core, k, s, rows, row, part, total, other):
    at = pl.multiple_of(chain_device(me, core, k) * rows + row, HALF)
    return total[s, pl.ds(at, HALF), :] + other[:, part].astype(jnp.float32)


def chain_kernel(links, s, rows, me_ref, total_ref, dot_ref, *refs):
    n_other = max(other for _, other, _, _ in links) + 1
    other_refs, (*arrived_refs, out_ref) = refs[:n_other], refs[n_other:]
    sectors, _, width = total_ref.shape
    data = rows // HALF * width
    me = me_ref[0]
    for place, (k, which, index, arrived) in enumerate(links):
        other = other_refs[which].at[index]
        for row, lanes in halves(rows, width):
            part = slice(s * data + lanes.start, s * data + lanes.stop)
            value = chip_terms(me, me % 2, k, s, rows, row, part, total_ref, other)
            if arrived:
                value += arrived_refs[0][place, :, lanes].astype(jnp.float32)
            out_ref[place, :, lanes] = value.astype(jnp.bfloat16)
        if s == 0:
            lanes = down(dot_ref[...]) + read_lanes(other, sectors * data)
            if arrived:
                lanes += read_lanes(arrived_refs[0].at[place], data)
            write_lanes(out_ref.at[place], data, lanes)


def chain(links, s, rows, me, total, dot, others, *arrived):
    width = total.shape[2]
    lanes = rows // HALF * width + (LANES if s == 0 else 0)
    n_other = max(other for _, other, _, _ in links) + 1
    return pl.pallas_call(
        functools.partial(chain_kernel, links, s, rows),
        in_specs=[SMEM] + [VMEM] * (2 + n_other + len(arrived)),
        out_specs=VMEM,
        out_shape=jax.ShapeDtypeStruct((len(links), HALF, lanes), jnp.bfloat16),
        compiler_params=PARAMS,
    )(me, total, dot, *others[:n_other], *arrived)


def own_terms(me, s, rows, total_ref, far_ref, ours_ref, theirs_ref):
    width = total_ref.shape[2]
    data = rows // HALF * width
    last = len(CHAIN) - 1
    values = []
    for row, lanes in halves(rows, width):
        part = slice(s * data + lanes.start, s * data + lanes.stop)
        value = chip_terms(me, me % 2, last, s, rows, row, part, total_ref, far_ref.at[last - 1])
        value += ours_ref[0, :, lanes].astype(jnp.float32)
        value += theirs_ref[1, :, lanes].astype(jnp.float32)
        values.append(value)
    return jnp.concatenate(values, axis=0)


def own_scalar(sectors, rows, dot_ref, total_ref, far_ref, ours_ref, theirs_ref):
    data = rows // HALF * total_ref.shape[2]
    lanes = down(dot_ref[...]) + read_lanes(far_ref.at[len(CHAIN) - 2], sectors * data)
    lanes += read_lanes(ours_ref.at[0], data) + read_lanes(theirs_ref.at[1], data)
    return jnp.sum(lanes)


def step_kernel(s, entries, me_ref, scale_ref, wave_ref, diag_ref, dot_ref, *refs):
    *sums, extra_ref, terms_ref, correction_ref, message_ref, dots_ref, ritz_ref = refs
    sectors, rows, width = wave_ref.shape
    if s == 0:
        ritz = own_scalar(sectors, rows, dot_ref, *sums) / entries
    else:
        ritz = extra_ref[0]
    ritz_ref[0] = ritz
    start = wave_ref[s].astype(jnp.float32) * (1.0 / scale_ref[0])
    diag = diag_ref[s].astype(jnp.float32)
    terms = own_terms(me_ref[0], s, rows, *sums)
    first = terms + diag * start
    correction = (first - ritz * start) / jnp.maximum(jnp.abs(diag - ritz), 1.0)
    terms_ref[...] = terms
    correction_ref[...] = correction
    dots = fold(start * correction)
    if s > 0:
        dots += dot_ref[...]
    dots_ref[...] = dots
    for row, part in halves(rows, width):
        message_ref[0, :, part] = correction[row : row + HALF].astype(jnp.bfloat16)
    if s == sectors - 1:
        write_lanes(message_ref.at[0], rows // HALF * width, down(dots))


def davidson_step(s, me, scale, wave, diag, dot, sums, extra, entries):
    sectors, rows, width = wave.shape
    lanes = rows // HALF * width + (LANES if s == sectors - 1 else 0)
    return pl.pallas_call(
        functools.partial(step_kernel, s, entries),
        in_specs=[SMEM, SMEM] + [VMEM] * 7 + [SMEM],
        out_specs=[VMEM] * 4 + [SMEM],
        out_shape=[
            jax.ShapeDtypeStruct((rows, width), jnp.float32),
            jax.ShapeDtypeStruct((rows, width), jnp.float32),
            jax.ShapeDtypeStruct((1, HALF, lanes), jnp.bfloat16),
            jax.ShapeDtypeStruct((8, 128), jnp.float32),
            jax.ShapeDtypeStruct((1,), jnp.float32),
        ],
        compiler_params=PARAMS,
    )(me, scale, wave, diag, dot, *sums, extra)


def finish_kernel(entries, me_ref, along_ref, scale_ref, wave_ref, diag_ref, dot_ref, *refs):
    first_ref, vector_ref, image_ref = refs[-3:]
    sectors, rows, width = wave_ref.shape
    terms, corrections, refs = refs[:sectors], refs[sectors : 2 * sectors], refs[2 * sectors : -3]
    total_ref, far_ref, *arrived = refs
    along = along_ref[0]
    square = own_scalar(sectors, rows, dot_ref, total_ref, far_ref, arrived[0], arrived[1])
    inverse = 1.0 / jnp.sqrt(square / entries)
    start_scale = 1.0 / scale_ref[0]
    for s in range(sectors):
        start = wave_ref[s].astype(jnp.float32) * start_scale
        diag = diag_ref[s].astype(jnp.float32)
        first_ref[s] = terms[s][...] + diag * start
        second = (corrections[s][...] - along * start) * inverse
        vector_ref[s] = second
        image = own_terms(me_ref[0], s, rows, total_ref, far_ref, *arrived[2 * s : 2 * s + 2])
        image_ref[s] = (image - along * terms[s][...]) * inverse + diag * second


def finish(me, along, scale, wave, diag, dot, terms, corrections, total, far, arrived, entries):
    full = jax.ShapeDtypeStruct(wave.shape, jnp.float32)
    operands = (wave, diag, dot, *terms, *corrections, total, far, *arrived)
    return pl.pallas_call(
        functools.partial(finish_kernel, entries),
        in_specs=[SMEM] * 3 + [VMEM] * len(operands),
        out_specs=[VMEM] * 3,
        out_shape=[full] * 3,
        compiler_params=PARAMS,
    )(me, along, scale, *operands)


def flip(value):
    return lax.ppermute(value, "term", [(i, i ^ 1) for i in range(16)])


def hop(value):
    order = [0, 2, 4, 6, 7, 5, 3, 1]
    pairs = []
    for place in range(8):
        for core, step in ((0, 1), (1, 7)):
            pairs.append((order[place] * 2 + core, order[(place + step) % 8] * 2 + core))
    return lax.ppermute(value, "term", pairs)


def gather(own):
    partner = [flip(m) for m in own]
    arrived = [hop(m) for m in own]
    rounds = [arrived]
    arrived = [hop(pair(m, p)) for m, p in zip(arrived, partner)]
    rounds.append(arrived)
    for _ in range(2):
        arrived = [hop(m) for m in arrived]
        rounds.append(arrived)
    sectors = len(own)
    packed = flip(pack(*(rounds[k][s] for s in range(sectors) for k in range(3))))
    last = [flip(m) for m in arrived]
    fields = []
    for s in range(sectors):
        mine = [own[s], *(r[s] for r in rounds)]
        fields.append((mine, partner[s], last[s]))
    return fields, packed


def scatter(me, rows, total, near, far, dot):
    sectors = total.shape[0]
    near = flip(near)
    near, far = lax.optimization_barrier((near, far))
    far = flip(far)
    others = (near, far)
    links = ((0, 0, 0, False),)
    arrived = [hop(chain(links, s, rows, me, total, dot, others)) for s in range(sectors)]
    for k in (1, 3, 5):
        links = ((k, 1, k - 1, True), (k + 1, 1, k, k > 1))
        arrived = [
            hop(chain(links, s, rows, me, total, dot, others, m)) for s, m in enumerate(arrived)
        ]
    return far, [(m, flip(m)) for m in arrived]


def on_ring(
    wavefunction, diagonal, left_blocks, right_blocks, block_source, block_target, live_count
):
    sectors, rows, width = wavefunction.shape
    entries = float(sectors * rows * lax.axis_size("term") * width)
    me = lax.axis_index("term").astype(jnp.int32).reshape(1)
    ints = jnp.concatenate([block_source, block_target, live_count])
    blocks = (left_blocks, right_blocks, wavefunction.shape)

    waves = as_messages(wavefunction)
    fields, packed = gather(waves)
    square = prepare(diagonal, waves, fields[0][0][1])
    total, near, far, dot, scale = apply_blocks(
        me, ints, fields, packed, (square,), *blocks, True, entries
    )
    far, arrived = scatter(me, rows, total, near, far, dot)
    terms, corrections, messages = [], [], []
    ritz, dots = scale, dot
    for s in range(sectors):
        sums = (total, far, *arrived[s])
        term, correction, message, dots, ritz = davidson_step(
            s, me, scale, wavefunction, diagonal, dots, sums, ritz, entries
        )
        terms.append(term)
        corrections.append(correction)
        messages.append(message)
    fields, packed = gather(messages)
    own = (scale, wavefunction, *corrections)
    total, near, far, dot, along = apply_blocks(
        me, ints, fields, packed, own, *blocks, False, entries
    )
    far, arrived = scatter(me, rows, total, near, far, dot)
    arrived = [m for both in arrived for m in both]
    return tuple(
        finish(
            me, along, scale, wavefunction, diagonal, dot, terms, corrections, total, far, arrived,
            entries,
        )
    )


def block_loop(field_rounded, left_ops, right_ops, sources, targets, last_slot, partial_sum):

    def add_block(slot_index, running):
        left_op = lax.dynamic_index_in_dim(left_ops, slot_index, 0, keepdims=False)
        right_op = lax.dynamic_index_in_dim(right_ops, slot_index, 0, keepdims=False)
        source = lax.dynamic_index_in_dim(sources, slot_index, 0, keepdims=False)
        target = lax.dynamic_index_in_dim(targets, slot_index, 0, keepdims=False)
        piece = lax.dynamic_index_in_dim(field_rounded, source, 0, keepdims=False)
        product = jnp.dot(left_op, piece, preferred_element_type=jnp.float32).astype(jnp.bfloat16)
        term_value = jnp.dot(product, right_op.T, preferred_element_type=jnp.float32)
        before = lax.dynamic_index_in_dim(running, target, 0, keepdims=False)
        return lax.dynamic_update_index_in_dim(running, before + term_value, target, 0)

    return lax.fori_loop(0, last_slot, add_block, partial_sum)


def on_any(
    wavefunction, diagonal, left_blocks, right_blocks, block_source, block_target, live_count
):
    devices = lax.axis_size("term")
    position = lax.axis_index("term")
    row_count = wavefunction.shape[1]
    sector_count = wavefunction.shape[0]
    width = wavefunction.shape[2]
    entries = float(sector_count * row_count * devices * width)
    own_count = live_count[0]
    diag_own = diagonal.astype(jnp.float32)
    whole_wave = lax.all_gather(wavefunction, "term", axis=1, tiled=True).astype(jnp.float32)
    scale = jnp.sqrt(jnp.sum(whole_wave * whole_wave) / entries)
    start_whole = whole_wave / scale
    empty_sum = jnp.zeros(start_whole.shape, jnp.float32)
    first_terms = block_loop(
        start_whole.astype(jnp.bfloat16),
        left_blocks,
        right_blocks,
        block_source,
        block_target,
        own_count,
        empty_sum,
    )
    row_start = position * row_count
    whole_diag = lax.all_gather(diagonal, "term", axis=1, tiled=True).astype(jnp.float32)
    first_whole = lax.psum(first_terms, "term") + whole_diag * start_whole
    ritz_value = jnp.sum(start_whole * first_whole) / entries
    correction = (first_whole - ritz_value * start_whole) / jnp.maximum(
        jnp.abs(whole_diag - ritz_value), 1.0
    )
    correlation = jnp.sum(start_whole * correction) / entries
    projected = correction - correlation * start_whole
    second_whole = projected / jnp.sqrt(jnp.sum(projected * projected) / entries)
    first_image = lax.dynamic_slice_in_dim(first_whole, row_start, row_count, 1)
    second_vector = lax.dynamic_slice_in_dim(second_whole, row_start, row_count, 1)
    second_rounded = second_whole.astype(jnp.bfloat16)
    second_terms = block_loop(
        second_rounded, left_blocks, right_blocks, block_source, block_target, own_count, empty_sum
    )
    second_image = (
        lax.psum_scatter(second_terms, "term", scatter_dimension=1, tiled=True)
        + diag_own * second_vector
    )
    return (first_image, second_vector, second_image)


def solution(mesh):
    placed = (
        P("grp", "term", None),
        P("grp", "term", None),
        P(("grp", "term"), None, None),
        P(("grp", "term"), None, None),
        P(("grp", "term")),
        P(("grp", "term")),
        P(("grp", "term")),
    )
    on_device = on_ring if mesh.shape["term"] == 16 else on_any
    return jax.shard_map(
        on_device,
        mesh=mesh,
        in_specs=placed,
        out_specs=(P("grp", "term", None), P("grp", "term", None), P("grp", "term", None)),
        check_vma=False,
    )
```

```python
import functools

import jax
import jax.numpy as jnp
from jax import lax
from jax.experimental import pallas as pl
from jax.experimental.pallas import tpu as pltpu
from jax.sharding import PartitionSpec as P

VMEM = pl.BlockSpec(memory_space=pltpu.VMEM)
SMEM = pl.BlockSpec(memory_space=pltpu.SMEM)
HBM = pl.BlockSpec(memory_space=pltpu.HBM)
PARAMS = pltpu.CompilerParams(vmem_limit_bytes=48 * 1024 * 1024)
HALF = 16
LANES = 128


def fold(value):
    rows, width = value.shape
    summed = jnp.sum(value.reshape(rows // 8, 8, width), axis=0)
    return sum(summed[:, k * 128 : (k + 1) * 128] for k in range(width // 128))


def down(value):
    return jnp.sum(value, axis=0, keepdims=True)


def halves(rows, width, start=0):
    for h in range(rows // HALF):
        yield h * HALF, slice(start + h * width, start + (h + 1) * width)


def write_lanes(ref, at, lanes):
    whole = jnp.broadcast_to(lanes, (HALF, LANES))
    high = whole.astype(jnp.bfloat16).astype(jnp.float32)
    rest = whole - high
    middle = rest.astype(jnp.bfloat16).astype(jnp.float32)
    low = rest - middle
    row = lax.broadcasted_iota(jnp.int32, whole.shape, 0)
    value = jnp.where(row == 0, high, jnp.where(row == 1, middle, jnp.where(row == 2, low, 0.0)))
    ref[:, at : at + LANES] = value.astype(jnp.bfloat16)


def read_lanes(ref, at):
    return down(ref[:, at : at + LANES].astype(jnp.float32))


def chip_at(place):
    place = lax.rem(place + 8, 8)
    return jnp.where(place < 4, 2 * place, 15 - 2 * place)


def ring_place(me):
    chip, core = me // 2, me % 2
    place = jnp.where(chip % 2 == 0, chip // 2, (15 - chip) // 2)
    return place, core


def ahead(me, distance, half, core=None):
    place, own = ring_place(me)
    core = own if core is None else core
    return chip_at(place + (1 - 2 * core) * distance) * 2 + half


ROUNDS = 4


def sent_devices(me, core):
    devices = []
    for k in range(ROUNDS):
        for half in (core, 1 - core):
            devices.append(ahead(me, ROUNDS - 1 - k + core, half, core))
    return devices


def gathered_devices(me):
    core = me % 2
    devices = [ahead(me, 0, core), ahead(me, 0, 1 - core)]
    for k in (1, 2, 3):
        devices += [ahead(me, -k, core), ahead(me, -k, 1 - core)]
        devices += [ahead(me, k, 1 - core), ahead(me, k, core)]
    return devices + [ahead(me, 4, 1), ahead(me, 4, 0)]


def message_parts(sectors, rows, width):
    for s in range(sectors):
        for row, part in halves(rows, width, s * (rows // HALF) * width):
            yield s, row, part


def message_shape(sectors, rows, width):
    return (HALF, rows // HALF * sectors * width + LANES)


def prepare_kernel(wave_ref, diag_ref, _, own_ref, square_ref):
    own_ref[...] = wave_ref[...]
    square = jnp.zeros((8, 128), jnp.float32)
    for s in range(wave_ref.shape[0]):
        wave = wave_ref[s].astype(jnp.float32)
        square += fold(diag_ref[s].astype(jnp.float32) * wave * wave)
    square_ref[...] = square


def prepare(wave, diag, after):
    return pl.pallas_call(
        prepare_kernel,
        in_specs=[VMEM, VMEM, HBM],
        out_specs=[VMEM, VMEM],
        out_shape=[
            jax.ShapeDtypeStruct(wave.shape, wave.dtype),
            jax.ShapeDtypeStruct((8, 128), jnp.float32),
        ],
        compiler_params=PARAMS,
    )(wave, diag, after)


def blocks_kernel(first, shape, entries, me_ref, ints_ref, *refs):
    sectors, rows, width = shape
    field_refs, refs = refs[:18], refs[18:]
    if first:
        square_ref, *refs = refs
    else:
        scale_ref, wave_ref, correction_ref, *refs = refs
    left_hbm, right_hbm, *refs = refs
    total, near_ref, far_ref, dot_ref, out_ref, left, right, field, left_sem, right_sem = refs
    slots = left.shape[0]

    def copies(slot):
        return (
            pltpu.make_async_copy(left_hbm.at[slot], left.at[slot], left_sem.at[slot]),
            pltpu.make_async_copy(right_hbm.at[slot], right.at[slot], right_sem.at[slot]),
        )

    for slot in range(slots):
        for copy in copies(slot):
            copy.start()

    me = me_ref[0]
    core = me % 2

    def read(k, part):
        if k < 14:
            return field_refs[k][part]
        return jnp.where(core == 1, field_refs[k][part], field_refs[k + 2][part])

    pieces = []
    for k, owner in enumerate(gathered_devices(me)):
        at = pl.multiple_of(owner * rows, rows)
        if first:
            for s in range(sectors):
                pieces.append((k, (s,), s, pl.ds(at, rows)))
        else:
            for s, row, part in message_parts(sectors, rows, width):
                pieces.append((k, (slice(None), part), s, pl.ds(at + row, HALF)))

    total[...] = jnp.zeros_like(total)
    if first:
        dot = jnp.zeros((8, 128), jnp.float32)
        for k, part, _, _ in pieces:
            value = read(k, part).astype(jnp.float32)
            dot += fold(value * value)
        scale = jnp.sqrt(jnp.sum(dot) / entries)
        inverse = 1.0 / scale
        out_ref[...] = jnp.full(out_ref.shape, scale, jnp.float32)
        for k, part, s, at in pieces:
            field[s, at, :] = (read(k, part).astype(jnp.float32) * inverse).astype(jnp.bfloat16)
    else:
        for k, part, s, at in pieces:
            field[s, at, :] = read(k, part)

    used = ints_ref[2 * slots]

    def add_pair(step, carry):
        one, two = 2 * step, 2 * step + 1
        for slot in (one, two):
            for copy in copies(slot):
                copy.wait()

        @pl.when(one < used)
        def _():
            products = [
                jnp.dot(
                    left[slot], field[ints_ref[slot]], preferred_element_type=jnp.float32
                ).astype(jnp.bfloat16)
                for slot in (one, two)
            ]
            products[1] = jnp.where(two < used, products[1], jnp.zeros_like(products[1]))
            for slot, product in zip((one, two), products):
                total[ints_ref[slots + slot]] += lax.dot_general(
                    product,
                    right[slot],
                    (((1,), (1,)), ((), ())),
                    preferred_element_type=jnp.float32,
                )

        return carry

    lax.fori_loop(0, slots // 2, add_pair, 0)

    dot = jnp.zeros((8, 128), jnp.float32)
    if first:
        for k, part, s, at in pieces:
            dot += fold(total[s, at, :] * read(k, part).astype(jnp.float32))
        dot = dot * inverse + square_ref[...] * inverse * inverse
    else:
        at = message_shape(*shape)[1] - LANES
        lanes = sum(
            read(k, (slice(None), slice(at, at + LANES))).astype(jnp.float32) for k in range(16)
        )
        along = jnp.sum(lanes) / entries
        out_ref[...] = jnp.full(out_ref.shape, along, jnp.float32)
        inverse = 1.0 / scale_ref[0:1, 0:1]
        for s in range(sectors):
            projected = correction_ref[s] - along * (wave_ref[s].astype(jnp.float32) * inverse)
            dot += fold(projected * projected)
    dot_ref[...] = dot
    lanes = down(dot)
    for k, owner in enumerate(sent_devices(me, 1 - core)):
        at = pl.multiple_of(owner * rows, rows)
        ref = near_ref.at[k] if k < near_ref.shape[0] else far_ref.at[k - near_ref.shape[0]]
        for s, row, part in message_parts(*shape):
            ref[:, part] = total[s, pl.ds(at + row, HALF), :].astype(jnp.bfloat16)
        write_lanes(ref, ref.shape[1] - LANES, lanes)


def apply_blocks(me, ints, fields, own, left, right, shape, first, entries):
    slots, order, width = left.shape
    sectors = shape[0]
    message = message_shape(*shape)
    return pl.pallas_call(
        functools.partial(blocks_kernel, first, shape, entries),
        in_specs=[SMEM, SMEM] + [VMEM] * (len(fields) + len(own)) + [HBM] * 2,
        out_specs=[VMEM] * 5,
        scratch_shapes=[
            pltpu.VMEM(left.shape, left.dtype),
            pltpu.VMEM(right.shape, right.dtype),
            pltpu.VMEM((sectors, order, width), jnp.bfloat16),
            pltpu.SemaphoreType.DMA((slots,)),
            pltpu.SemaphoreType.DMA((slots,)),
        ],
        out_shape=[
            jax.ShapeDtypeStruct((sectors, order, width), jnp.float32),
            jax.ShapeDtypeStruct((2, *message), jnp.bfloat16),
            jax.ShapeDtypeStruct((2 * ROUNDS - 2, *message), jnp.bfloat16),
            jax.ShapeDtypeStruct((8, 128), jnp.float32),
            jax.ShapeDtypeStruct((8, 128), jnp.float32),
        ],
        compiler_params=PARAMS,
        cost_estimate=pl.CostEstimate(
            flops=4 * slots * order * order * width,
            bytes_accessed=4 * slots * order * order,
            transcendentals=0,
        ),
    )(me, ints, *fields, *own, left, right)


def chain_kernel(shape, k, index, me_ref, total_ref, dot_ref, other_ref, *refs):
    *arrived_refs, out_ref = refs
    _, rows, _ = shape
    me = me_ref[0]
    start = pl.multiple_of(sent_devices(me, me % 2)[k] * rows, rows)
    for s, row, part in message_parts(*shape):
        value = total_ref[s, pl.ds(start + row, HALF), :]
        value += other_ref[index, :, part].astype(jnp.float32)
        for ref in arrived_refs:
            value += ref[:, part].astype(jnp.float32)
        out_ref[:, part] = value.astype(jnp.bfloat16)
    at = out_ref.shape[1] - LANES
    lanes = down(dot_ref[...]) + read_lanes(other_ref.at[index], at)
    for ref in arrived_refs:
        lanes += read_lanes(ref, at)
    write_lanes(out_ref, at, lanes)


def chain(shape, k, index, me, total, dot, other, *arrived):
    return pl.pallas_call(
        functools.partial(chain_kernel, shape, k, index),
        in_specs=[SMEM] + [VMEM] * (3 + len(arrived)),
        out_specs=VMEM,
        out_shape=jax.ShapeDtypeStruct(message_shape(*shape), jnp.bfloat16),
        compiler_params=PARAMS,
    )(me, total, dot, other, *arrived)


def pick_kernel(me_ref, even_ref, odd_ref, out_ref):
    out_ref[...] = jnp.where(me_ref[0] % 2 == 0, even_ref[...], odd_ref[...])


def pick(me, even, odd):
    return pl.pallas_call(
        pick_kernel,
        in_specs=[SMEM, VMEM, VMEM],
        out_specs=VMEM,
        out_shape=jax.ShapeDtypeStruct(even.shape, even.dtype),
        compiler_params=PARAMS,
    )(me, even, odd)


def own_terms(shape, sector, ours, theirs):
    values = []
    for s, _, part in message_parts(*shape):
        if s == sector:
            values.append(ours[:, part].astype(jnp.float32) + theirs[:, part].astype(jnp.float32))
    return jnp.concatenate(values, axis=0)


def own_scalar(ours, theirs):
    at = ours.shape[1] - LANES
    return jnp.sum(read_lanes(ours, at) + read_lanes(theirs, at))


def step_kernel(entries, scale_ref, wave_ref, diag_ref, ours_ref, theirs_ref, *refs):
    first_ref, terms_ref, correction_ref, message_ref = refs
    shape = wave_ref.shape
    ritz = own_scalar(ours_ref, theirs_ref) / entries
    inverse = 1.0 / scale_ref[0:1, 0:1]
    dots = jnp.zeros((8, 128), jnp.float32)
    for s in range(shape[0]):
        start = wave_ref[s].astype(jnp.float32) * inverse
        diag = diag_ref[s].astype(jnp.float32)
        terms = own_terms(shape, s, ours_ref, theirs_ref)
        first = terms + diag * start
        correction = (first - ritz * start) / jnp.maximum(jnp.abs(diag - ritz), 1.0)
        first_ref[s] = first
        terms_ref[s] = terms
        correction_ref[s] = correction
        dots += fold(start * correction)
        for t, row, part in message_parts(*shape):
            if t == s:
                message_ref[:, part] = correction[row : row + HALF].astype(jnp.bfloat16)
    write_lanes(message_ref, message_ref.shape[1] - LANES, down(dots))


def davidson_step(scale, wave, diag, sums, entries):
    full = jax.ShapeDtypeStruct(wave.shape, jnp.float32)
    return pl.pallas_call(
        functools.partial(step_kernel, entries),
        in_specs=[VMEM] * 5,
        out_specs=[VMEM] * 4,
        out_shape=[full, full, full, jax.ShapeDtypeStruct(message_shape(*wave.shape), jnp.bfloat16)],
        compiler_params=PARAMS,
    )(scale, wave, diag, *sums)


def finish_kernel(entries, along_ref, scale_ref, wave_ref, diag_ref, *refs):
    terms_ref, correction_ref, ours_ref, theirs_ref, vector_ref, image_ref = refs
    shape = wave_ref.shape
    along = along_ref[0:1, 0:1]
    norm = jnp.sqrt(jnp.full((1, 1), own_scalar(ours_ref, theirs_ref) / entries, jnp.float32))
    inverse = 1.0 / norm
    start_scale = 1.0 / scale_ref[0:1, 0:1]
    for s in range(shape[0]):
        start = wave_ref[s].astype(jnp.float32) * start_scale
        second = (correction_ref[s] - along * start) * inverse
        vector_ref[s] = second
        image = (own_terms(shape, s, ours_ref, theirs_ref) - along * terms_ref[s]) * inverse
        image_ref[s] = image + diag_ref[s].astype(jnp.float32) * second


def finish(along, scale, wave, diag, terms, correction, sums, entries):
    full = jax.ShapeDtypeStruct(wave.shape, jnp.float32)
    return pl.pallas_call(
        functools.partial(finish_kernel, entries),
        in_specs=[VMEM] * 8,
        out_specs=[VMEM] * 2,
        out_shape=[full, full],
        compiler_params=PARAMS,
    )(along, scale, wave, diag, terms, correction, *sums)


def flip(value):
    return lax.ppermute(value, "term", [(i, i ^ 1) for i in range(16)])


def down_core(value):
    return lax.ppermute(value, "term", [(i, i - 1) for i in range(1, 16, 2)])


def hop(value, cores=(0, 1)):
    order = [0, 2, 4, 6, 7, 5, 3, 1]
    pairs = []
    for place in range(8):
        for core in cores:
            there = order[(place + 1 - 2 * core) % 8]
            pairs.append((order[place] * 2 + core, there * 2 + core))
    return lax.ppermute(value, "term", pairs)


def gather(own):
    one, two = own, flip(own)
    pieces = [one, two]
    for _ in (1, 2, 3):
        one, two = hop(one), hop(two)
        pieces += [one, two, flip(one), flip(two)]
    one, two = hop(one, (1,)), hop(two, (1,))
    return pieces + [one, two, down_core(one), down_core(two)], two


def scatter(shape, me, total, near, far, dot):
    near = flip(near)
    near, far = lax.optimization_barrier((near, far))
    far = flip(far)
    one = hop(chain(shape, 0, 0, me, total, dot, near))
    two = hop(chain(shape, 1, 1, me, total, dot, near))
    for k in (2, 4):
        one = hop(chain(shape, k, k - 2, me, total, dot, far, one))
        two = hop(chain(shape, k + 1, k - 1, me, total, dot, far, two))
    one = chain(shape, 6, 4, me, total, dot, far, one)
    two = chain(shape, 7, 5, me, total, dot, far, two)
    one = pick(me, one, hop(one, (1,)))
    two = pick(me, two, hop(two, (1,)))
    return one, flip(two)


def on_ring(
    wavefunction, diagonal, left_blocks, right_blocks, block_source, block_target, live_count
):
    shape = wavefunction.shape
    sectors, rows, width = shape
    entries = float(sectors * rows * lax.axis_size("term") * width)
    me = lax.axis_index("term").astype(jnp.int32).reshape(1)
    ints = jnp.concatenate([block_source, block_target, live_count])
    blocks = (left_blocks, right_blocks, shape)

    fields, last = gather(wavefunction)
    fields[0], square = prepare(wavefunction, diagonal, last)
    total, near, far, dot, scale = apply_blocks(me, ints, fields, (square,), *blocks, True, entries)
    first_image, terms, correction, message = davidson_step(
        scale, wavefunction, diagonal, scatter(shape, me, total, near, far, dot), entries
    )
    fields, _ = gather(message)
    own = (scale, wavefunction, correction)
    total, near, far, dot, along = apply_blocks(me, ints, fields, own, *blocks, False, entries)
    second_vector, second_image = finish(
        along, scale, wavefunction, diagonal, terms, correction,
        scatter(shape, me, total, near, far, dot), entries,
    )
    return (first_image, second_vector, second_image)


def block_loop(field_rounded, left_ops, right_ops, sources, targets, last_slot, partial_sum):

    def add_block(slot_index, running):
        left_op = lax.dynamic_index_in_dim(left_ops, slot_index, 0, keepdims=False)
        right_op = lax.dynamic_index_in_dim(right_ops, slot_index, 0, keepdims=False)
        source = lax.dynamic_index_in_dim(sources, slot_index, 0, keepdims=False)
        target = lax.dynamic_index_in_dim(targets, slot_index, 0, keepdims=False)
        piece = lax.dynamic_index_in_dim(field_rounded, source, 0, keepdims=False)
        product = jnp.dot(left_op, piece, preferred_element_type=jnp.float32).astype(jnp.bfloat16)
        term_value = jnp.dot(product, right_op.T, preferred_element_type=jnp.float32)
        before = lax.dynamic_index_in_dim(running, target, 0, keepdims=False)
        return lax.dynamic_update_index_in_dim(running, before + term_value, target, 0)

    return lax.fori_loop(0, last_slot, add_block, partial_sum)


def on_any(
    wavefunction, diagonal, left_blocks, right_blocks, block_source, block_target, live_count
):
    devices = lax.axis_size("term")
    position = lax.axis_index("term")
    row_count = wavefunction.shape[1]
    sector_count = wavefunction.shape[0]
    width = wavefunction.shape[2]
    entries = float(sector_count * row_count * devices * width)
    own_count = live_count[0]
    diag_own = diagonal.astype(jnp.float32)
    whole_wave = lax.all_gather(wavefunction, "term", axis=1, tiled=True).astype(jnp.float32)
    scale = jnp.sqrt(jnp.sum(whole_wave * whole_wave) / entries)
    start_whole = whole_wave / scale
    empty_sum = jnp.zeros(start_whole.shape, jnp.float32)
    first_terms = block_loop(
        start_whole.astype(jnp.bfloat16),
        left_blocks,
        right_blocks,
        block_source,
        block_target,
        own_count,
        empty_sum,
    )
    row_start = position * row_count
    whole_diag = lax.all_gather(diagonal, "term", axis=1, tiled=True).astype(jnp.float32)
    first_whole = lax.psum(first_terms, "term") + whole_diag * start_whole
    ritz_value = jnp.sum(start_whole * first_whole) / entries
    correction = (first_whole - ritz_value * start_whole) / jnp.maximum(
        jnp.abs(whole_diag - ritz_value), 1.0
    )
    correlation = jnp.sum(start_whole * correction) / entries
    projected = correction - correlation * start_whole
    second_whole = projected / jnp.sqrt(jnp.sum(projected * projected) / entries)
    first_image = lax.dynamic_slice_in_dim(first_whole, row_start, row_count, 1)
    second_vector = lax.dynamic_slice_in_dim(second_whole, row_start, row_count, 1)
    second_rounded = second_whole.astype(jnp.bfloat16)
    second_terms = block_loop(
        second_rounded, left_blocks, right_blocks, block_source, block_target, own_count, empty_sum
    )
    second_image = (
        lax.psum_scatter(second_terms, "term", scatter_dimension=1, tiled=True)
        + diag_own * second_vector
    )
    return (first_image, second_vector, second_image)


def solution(mesh):
    placed = (
        P("grp", "term", None),
        P("grp", "term", None),
        P(("grp", "term"), None, None),
        P(("grp", "term"), None, None),
        P(("grp", "term")),
        P(("grp", "term")),
        P(("grp", "term")),
    )
    on_device = on_ring if mesh.shape["term"] == 16 else on_any
    return jax.shard_map(
        on_device,
        mesh=mesh,
        in_specs=placed,
        out_specs=(P("grp", "term", None), P("grp", "term", None), P("grp", "term", None)),
        check_vma=False,
    )
```

```python
import functools

import jax
import jax.numpy as jnp
from jax import lax
from jax.experimental import pallas as pl
from jax.experimental.pallas import tpu as pltpu
from jax.sharding import PartitionSpec as P

VMEM = pl.BlockSpec(memory_space=pltpu.VMEM)
SMEM = pl.BlockSpec(memory_space=pltpu.SMEM)
HBM = pl.BlockSpec(memory_space=pltpu.HBM)
PARAMS = pltpu.CompilerParams(vmem_limit_bytes=48 * 1024 * 1024)
HALF = 16
LANES = 128


def fold(value):
    rows, width = value.shape
    summed = jnp.sum(value.reshape(rows // 8, 8, width), axis=0)
    return sum(summed[:, k * 128 : (k + 1) * 128] for k in range(width // 128))


def down(value):
    return jnp.sum(value, axis=0, keepdims=True)


def halves(rows, width, start=0):
    for h in range(rows // HALF):
        yield h * HALF, slice(start + h * width, start + (h + 1) * width)


def write_lanes(ref, at, lanes):
    whole = jnp.broadcast_to(lanes, (HALF, LANES))
    high = whole.astype(jnp.bfloat16).astype(jnp.float32)
    rest = whole - high
    middle = rest.astype(jnp.bfloat16).astype(jnp.float32)
    low = rest - middle
    row = lax.broadcasted_iota(jnp.int32, whole.shape, 0)
    value = jnp.where(row == 0, high, jnp.where(row == 1, middle, jnp.where(row == 2, low, 0.0)))
    ref[:, at : at + LANES] = value.astype(jnp.bfloat16)


def read_lanes(ref, at):
    return down(ref[:, at : at + LANES].astype(jnp.float32))


def chip_at(place):
    place = lax.rem(place + 8, 8)
    return jnp.where(place < 4, 2 * place, 15 - 2 * place)


def ring_place(me):
    chip, core = me // 2, me % 2
    place = jnp.where(chip % 2 == 0, chip // 2, (15 - chip) // 2)
    return place, core


def ahead(me, distance, half, core=None):
    place, own = ring_place(me)
    core = own if core is None else core
    return chip_at(place + (1 - 2 * core) * distance) * 2 + half


ROUNDS = 4


def sent_devices(me, core):
    devices = []
    for k in range(ROUNDS):
        for half in (core, 1 - core):
            devices.append(ahead(me, ROUNDS - 1 - k + core, half, core))
    return devices


def gathered_devices(me):
    core = me % 2
    devices = [ahead(me, 0, core), ahead(me, 0, 1 - core)]
    for k in (1, 2, 3):
        devices += [ahead(me, -k, core), ahead(me, -k, 1 - core)]
        devices += [ahead(me, k, 1 - core), ahead(me, k, core)]
    return devices + [ahead(me, 4, 1), ahead(me, 4, 0)]


def message_parts(sectors, rows, width):
    for s in range(sectors):
        for row, part in halves(rows, width, s * (rows // HALF) * width):
            yield s, row, part


def message_shape(sectors, rows, width):
    return (HALF, rows // HALF * sectors * width + LANES)


def prepare_kernel(wave_ref, diag_ref, _, own_ref, square_ref):
    own_ref[...] = wave_ref[...]
    square = jnp.zeros((8, 128), jnp.float32)
    for s in range(wave_ref.shape[0]):
        wave = wave_ref[s].astype(jnp.float32)
        square += fold(diag_ref[s].astype(jnp.float32) * wave * wave)
    square_ref[...] = square


def prepare(wave, diag, after):
    return pl.pallas_call(
        prepare_kernel,
        in_specs=[VMEM, VMEM, HBM],
        out_specs=[VMEM, VMEM],
        out_shape=[
            jax.ShapeDtypeStruct(wave.shape, wave.dtype),
            jax.ShapeDtypeStruct((8, 128), jnp.float32),
        ],
        compiler_params=PARAMS,
    )(wave, diag, after)


def blocks_kernel(first, shape, entries, me_ref, ints_ref, *refs):
    sectors, rows, width = shape
    field_refs, refs = refs[:18], refs[18:]
    if first:
        square_ref, *refs = refs
    else:
        scale_ref, wave_ref, correction_ref, *refs = refs
    left_hbm, right_hbm, *refs = refs
    total, near_ref, far_ref, dot_ref, out_ref, left, right, field, left_sem, right_sem = refs
    slots = left.shape[0]

    def copies(slot):
        return (
            pltpu.make_async_copy(left_hbm.at[slot], left.at[slot], left_sem.at[slot]),
            pltpu.make_async_copy(right_hbm.at[slot], right.at[slot], right_sem.at[slot]),
        )

    for slot in range(slots):
        for copy in copies(slot):
            copy.start()

    me = me_ref[0]
    core = me % 2

    def read(k, part):
        if k < 14:
            return field_refs[k][part]
        return jnp.where(core == 1, field_refs[k][part], field_refs[k + 2][part])

    pieces = []
    for k, owner in enumerate(gathered_devices(me)):
        at = pl.multiple_of(owner * rows, rows)
        if first:
            for s in range(sectors):
                pieces.append((k, (s,), s, pl.ds(at, rows)))
        else:
            for s, row, part in message_parts(sectors, rows, width):
                pieces.append((k, (slice(None), part), s, pl.ds(at + row, HALF)))

    total[...] = jnp.zeros_like(total)
    if first:
        dot = jnp.zeros((8, 128), jnp.float32)
        for k, part, _, _ in pieces:
            value = read(k, part).astype(jnp.float32)
            dot += fold(value * value)
        scale = jnp.sqrt(jnp.sum(dot) / entries)
        inverse = 1.0 / scale
        out_ref[...] = jnp.full(out_ref.shape, scale, jnp.float32)
        for k, part, s, at in pieces:
            field[s, at, :] = (read(k, part).astype(jnp.float32) * inverse).astype(jnp.bfloat16)
    else:
        for k, part, s, at in pieces:
            field[s, at, :] = read(k, part)

    used = ints_ref[2 * slots]

    def add_pair(step, carry):
        one, two = 2 * step, 2 * step + 1
        for slot in (one, two):
            for copy in copies(slot):
                copy.wait()

        @pl.when(one < used)
        def _():
            products = [
                jnp.dot(
                    left[slot], field[ints_ref[slot]], preferred_element_type=jnp.float32
                ).astype(jnp.bfloat16)
                for slot in (one, two)
            ]
            products[1] = jnp.where(two < used, products[1], jnp.zeros_like(products[1]))
            for slot, product in zip((one, two), products):
                total[ints_ref[slots + slot]] += lax.dot_general(
                    product,
                    right[slot],
                    (((1,), (1,)), ((), ())),
                    preferred_element_type=jnp.float32,
                )

        return carry

    lax.fori_loop(0, slots // 2, add_pair, 0)

    dot = jnp.zeros((8, 128), jnp.float32)
    if first:
        for k, part, s, at in pieces:
            dot += fold(total[s, at, :] * read(k, part).astype(jnp.float32))
        dot = dot * inverse + square_ref[...] * inverse * inverse
    else:
        at = message_shape(*shape)[1] - LANES
        lanes = sum(
            read(k, (slice(None), slice(at, at + LANES))).astype(jnp.float32) for k in range(16)
        )
        along = jnp.sum(lanes) / entries
        out_ref[...] = jnp.full(out_ref.shape, along, jnp.float32)
        inverse = 1.0 / scale_ref[0:1, 0:1]
        for s in range(sectors):
            projected = correction_ref[s] - along * (wave_ref[s].astype(jnp.float32) * inverse)
            dot += fold(projected * projected)
    dot_ref[...] = dot
    lanes = down(dot)
    for k, owner in enumerate(sent_devices(me, 1 - core)):
        at = pl.multiple_of(owner * rows, rows)
        ref = near_ref.at[k] if k < near_ref.shape[0] else far_ref.at[k - near_ref.shape[0]]
        for s, row, part in message_parts(*shape):
            ref[:, part] = total[s, pl.ds(at + row, HALF), :].astype(jnp.bfloat16)
        write_lanes(ref, ref.shape[1] - LANES, lanes)


def apply_blocks(me, ints, fields, own, left, right, shape, first, entries):
    slots, order, width = left.shape
    sectors = shape[0]
    message = message_shape(*shape)
    return pl.pallas_call(
        functools.partial(blocks_kernel, first, shape, entries),
        in_specs=[SMEM, SMEM] + [VMEM] * (len(fields) + len(own)) + [HBM] * 2,
        out_specs=[VMEM] * 5,
        scratch_shapes=[
            pltpu.VMEM(left.shape, left.dtype),
            pltpu.VMEM(right.shape, right.dtype),
            pltpu.VMEM((sectors, order, width), jnp.bfloat16),
            pltpu.SemaphoreType.DMA((slots,)),
            pltpu.SemaphoreType.DMA((slots,)),
        ],
        out_shape=[
            jax.ShapeDtypeStruct((sectors, order, width), jnp.float32),
            jax.ShapeDtypeStruct((2, *message), jnp.bfloat16),
            jax.ShapeDtypeStruct((2 * ROUNDS - 2, *message), jnp.bfloat16),
            jax.ShapeDtypeStruct((8, 128), jnp.float32),
            jax.ShapeDtypeStruct((8, 128), jnp.float32),
        ],
        compiler_params=PARAMS,
        cost_estimate=pl.CostEstimate(
            flops=4 * slots * order * order * width,
            bytes_accessed=4 * slots * order * order,
            transcendentals=0,
        ),
    )(me, ints, *fields, *own, left, right)


def chain_kernel(shape, k, index, me_ref, total_ref, dot_ref, other_ref, *refs):
    *arrived_refs, out_ref = refs
    _, rows, _ = shape
    me = me_ref[0]
    start = pl.multiple_of(sent_devices(me, me % 2)[k] * rows, rows)
    for s, row, part in message_parts(*shape):
        value = total_ref[s, pl.ds(start + row, HALF), :]
        value += other_ref[index, :, part].astype(jnp.float32)
        for ref in arrived_refs:
            value += ref[:, part].astype(jnp.float32)
        out_ref[:, part] = value.astype(jnp.bfloat16)
    at = out_ref.shape[1] - LANES
    lanes = down(dot_ref[...]) + read_lanes(other_ref.at[index], at)
    for ref in arrived_refs:
        lanes += read_lanes(ref, at)
    write_lanes(out_ref, at, lanes)


def chain(shape, k, index, me, total, dot, other, *arrived):
    return pl.pallas_call(
        functools.partial(chain_kernel, shape, k, index),
        in_specs=[SMEM] + [VMEM] * (3 + len(arrived)),
        out_specs=VMEM,
        out_shape=jax.ShapeDtypeStruct(message_shape(*shape), jnp.bfloat16),
        compiler_params=PARAMS,
    )(me, total, dot, other, *arrived)


def own_terms(shape, sector, ours, theirs):
    values = []
    for s, _, part in message_parts(*shape):
        if s == sector:
            values.append(ours[:, part].astype(jnp.float32) + theirs[:, part].astype(jnp.float32))
    return jnp.concatenate(values, axis=0)


def own_scalar(ours, theirs):
    at = ours.shape[1] - LANES
    return jnp.sum(read_lanes(ours, at) + read_lanes(theirs, at))


def step_kernel(entries, scale_ref, wave_ref, diag_ref, ours_ref, theirs_ref, *refs):
    first_ref, terms_ref, correction_ref, message_ref = refs
    shape = wave_ref.shape
    ritz = own_scalar(ours_ref, theirs_ref) / entries
    inverse = 1.0 / scale_ref[0:1, 0:1]
    dots = jnp.zeros((8, 128), jnp.float32)
    for s in range(shape[0]):
        start = wave_ref[s].astype(jnp.float32) * inverse
        diag = diag_ref[s].astype(jnp.float32)
        terms = own_terms(shape, s, ours_ref, theirs_ref)
        first = terms + diag * start
        correction = (first - ritz * start) / jnp.maximum(jnp.abs(diag - ritz), 1.0)
        first_ref[s] = first
        terms_ref[s] = terms
        correction_ref[s] = correction
        dots += fold(start * correction)
        for t, row, part in message_parts(*shape):
            if t == s:
                message_ref[:, part] = correction[row : row + HALF].astype(jnp.bfloat16)
    write_lanes(message_ref, message_ref.shape[1] - LANES, down(dots))


def davidson_step(scale, wave, diag, sums, entries):
    full = jax.ShapeDtypeStruct(wave.shape, jnp.float32)
    return pl.pallas_call(
        functools.partial(step_kernel, entries),
        in_specs=[VMEM] * 5,
        out_specs=[VMEM] * 4,
        out_shape=[full, full, full, jax.ShapeDtypeStruct(message_shape(*wave.shape), jnp.bfloat16)],
        compiler_params=PARAMS,
    )(scale, wave, diag, *sums)


def finish_kernel(entries, along_ref, scale_ref, wave_ref, diag_ref, *refs):
    terms_ref, correction_ref, ours_ref, theirs_ref, vector_ref, image_ref = refs
    shape = wave_ref.shape
    along = along_ref[0:1, 0:1]
    norm = jnp.sqrt(jnp.full((1, 1), own_scalar(ours_ref, theirs_ref) / entries, jnp.float32))
    inverse = 1.0 / norm
    start_scale = 1.0 / scale_ref[0:1, 0:1]
    for s in range(shape[0]):
        start = wave_ref[s].astype(jnp.float32) * start_scale
        second = (correction_ref[s] - along * start) * inverse
        vector_ref[s] = second
        image = (own_terms(shape, s, ours_ref, theirs_ref) - along * terms_ref[s]) * inverse
        image_ref[s] = image + diag_ref[s].astype(jnp.float32) * second


def finish(along, scale, wave, diag, terms, correction, sums, entries):
    full = jax.ShapeDtypeStruct(wave.shape, jnp.float32)
    return pl.pallas_call(
        functools.partial(finish_kernel, entries),
        in_specs=[VMEM] * 8,
        out_specs=[VMEM] * 2,
        out_shape=[full, full],
        compiler_params=PARAMS,
    )(along, scale, wave, diag, terms, correction, *sums)


def flip(value):
    return lax.ppermute(value, "term", [(i, i ^ 1) for i in range(16)])


def hop(value, cores=(0, 1)):
    order = [0, 2, 4, 6, 7, 5, 3, 1]
    pairs = []
    for place in range(8):
        for core in (0, 1):
            there = order[(place + 1 - 2 * core) % 8] if core in cores else order[place]
            pairs.append((order[place] * 2 + core, there * 2 + core))
    return lax.ppermute(value, "term", pairs)


def gather(own):
    one, two = own, flip(own)
    pieces = [one, two]
    flipped = ()
    for _ in (1, 2, 3):
        one, two = hop(one), hop(two)
        pieces += [one, two]
        if flipped:
            one, *flipped = lax.optimization_barrier((one, *flipped))
        flipped = (flip(one), flip(two))
        pieces += flipped
    one, two = hop(one, (1,)), hop(two, (1,))
    return pieces + [one, two, flip(one), flip(two)], two


def scatter(shape, me, total, near, far, dot):
    near = flip(near)
    near, far = lax.optimization_barrier((near, far))
    far = flip(far)
    one = hop(chain(shape, 0, 0, me, total, dot, near))
    two = hop(chain(shape, 1, 1, me, total, dot, near))
    for k in (2, 4):
        one = hop(chain(shape, k, k - 2, me, total, dot, far, one))
        two = hop(chain(shape, k + 1, k - 1, me, total, dot, far, two))
    one = hop(chain(shape, 6, 4, me, total, dot, far, one), (1,))
    two = hop(chain(shape, 7, 5, me, total, dot, far, two), (1,))
    return one, flip(two)


def on_ring(
    wavefunction, diagonal, left_blocks, right_blocks, block_source, block_target, live_count
):
    shape = wavefunction.shape
    sectors, rows, width = shape
    entries = float(sectors * rows * lax.axis_size("term") * width)
    me = lax.axis_index("term").astype(jnp.int32).reshape(1)
    ints = jnp.concatenate([block_source, block_target, live_count])
    blocks = (left_blocks, right_blocks, shape)

    fields, last = gather(wavefunction)
    fields[0], square = prepare(wavefunction, diagonal, last)
    total, near, far, dot, scale = apply_blocks(me, ints, fields, (square,), *blocks, True, entries)
    first_image, terms, correction, message = davidson_step(
        scale, wavefunction, diagonal, scatter(shape, me, total, near, far, dot), entries
    )
    fields, _ = gather(message)
    own = (scale, wavefunction, correction)
    total, near, far, dot, along = apply_blocks(me, ints, fields, own, *blocks, False, entries)
    second_vector, second_image = finish(
        along, scale, wavefunction, diagonal, terms, correction,
        scatter(shape, me, total, near, far, dot), entries,
    )
    return (first_image, second_vector, second_image)


def block_loop(field_rounded, left_ops, right_ops, sources, targets, last_slot, partial_sum):

    def add_block(slot_index, running):
        left_op = lax.dynamic_index_in_dim(left_ops, slot_index, 0, keepdims=False)
        right_op = lax.dynamic_index_in_dim(right_ops, slot_index, 0, keepdims=False)
        source = lax.dynamic_index_in_dim(sources, slot_index, 0, keepdims=False)
        target = lax.dynamic_index_in_dim(targets, slot_index, 0, keepdims=False)
        piece = lax.dynamic_index_in_dim(field_rounded, source, 0, keepdims=False)
        product = jnp.dot(left_op, piece, preferred_element_type=jnp.float32).astype(jnp.bfloat16)
        term_value = jnp.dot(product, right_op.T, preferred_element_type=jnp.float32)
        before = lax.dynamic_index_in_dim(running, target, 0, keepdims=False)
        return lax.dynamic_update_index_in_dim(running, before + term_value, target, 0)

    return lax.fori_loop(0, last_slot, add_block, partial_sum)


def on_any(
    wavefunction, diagonal, left_blocks, right_blocks, block_source, block_target, live_count
):
    devices = lax.axis_size("term")
    position = lax.axis_index("term")
    row_count = wavefunction.shape[1]
    sector_count = wavefunction.shape[0]
    width = wavefunction.shape[2]
    entries = float(sector_count * row_count * devices * width)
    own_count = live_count[0]
    diag_own = diagonal.astype(jnp.float32)
    whole_wave = lax.all_gather(wavefunction, "term", axis=1, tiled=True).astype(jnp.float32)
    scale = jnp.sqrt(jnp.sum(whole_wave * whole_wave) / entries)
    start_whole = whole_wave / scale
    empty_sum = jnp.zeros(start_whole.shape, jnp.float32)
    first_terms = block_loop(
        start_whole.astype(jnp.bfloat16),
        left_blocks,
        right_blocks,
        block_source,
        block_target,
        own_count,
        empty_sum,
    )
    row_start = position * row_count
    whole_diag = lax.all_gather(diagonal, "term", axis=1, tiled=True).astype(jnp.float32)
    first_whole = lax.psum(first_terms, "term") + whole_diag * start_whole
    ritz_value = jnp.sum(start_whole * first_whole) / entries
    correction = (first_whole - ritz_value * start_whole) / jnp.maximum(
        jnp.abs(whole_diag - ritz_value), 1.0
    )
    correlation = jnp.sum(start_whole * correction) / entries
    projected = correction - correlation * start_whole
    second_whole = projected / jnp.sqrt(jnp.sum(projected * projected) / entries)
    first_image = lax.dynamic_slice_in_dim(first_whole, row_start, row_count, 1)
    second_vector = lax.dynamic_slice_in_dim(second_whole, row_start, row_count, 1)
    second_rounded = second_whole.astype(jnp.bfloat16)
    second_terms = block_loop(
        second_rounded, left_blocks, right_blocks, block_source, block_target, own_count, empty_sum
    )
    second_image = (
        lax.psum_scatter(second_terms, "term", scatter_dimension=1, tiled=True)
        + diag_own * second_vector
    )
    return (first_image, second_vector, second_image)


def solution(mesh):
    placed = (
        P("grp", "term", None),
        P("grp", "term", None),
        P(("grp", "term"), None, None),
        P(("grp", "term"), None, None),
        P(("grp", "term")),
        P(("grp", "term")),
        P(("grp", "term")),
    )
    on_device = on_ring if mesh.shape["term"] == 16 else on_any
    return jax.shard_map(
        on_device,
        mesh=mesh,
        in_specs=placed,
        out_specs=(P("grp", "term", None), P("grp", "term", None), P("grp", "term", None)),
        check_vma=False,
    )
```

```python
import functools

import jax
import jax.numpy as jnp
from jax import lax
from jax.experimental import pallas as pl
from jax.experimental.pallas import tpu as pltpu
from jax.sharding import PartitionSpec as P

VMEM = pl.BlockSpec(memory_space=pltpu.VMEM)
SMEM = pl.BlockSpec(memory_space=pltpu.SMEM)
HBM = pl.BlockSpec(memory_space=pltpu.HBM)
PARAMS = pltpu.CompilerParams(vmem_limit_bytes=48 * 1024 * 1024)
HALF = 16
LANES = 128


def fold(value):
    rows, width = value.shape
    summed = jnp.sum(value.reshape(rows // 8, 8, width), axis=0)
    return sum(summed[:, k * 128 : (k + 1) * 128] for k in range(width // 128))


def down(value):
    return jnp.sum(value, axis=0, keepdims=True)


def halves(rows, width, start=0):
    for h in range(rows // HALF):
        yield h * HALF, slice(start + h * width, start + (h + 1) * width)


def write_lanes(ref, at, lanes):
    whole = jnp.broadcast_to(lanes, (HALF, LANES))
    high = whole.astype(jnp.bfloat16).astype(jnp.float32)
    rest = whole - high
    middle = rest.astype(jnp.bfloat16).astype(jnp.float32)
    low = rest - middle
    row = lax.broadcasted_iota(jnp.int32, whole.shape, 0)
    value = jnp.where(row == 0, high, jnp.where(row == 1, middle, jnp.where(row == 2, low, 0.0)))
    ref[:, at : at + LANES] = value.astype(jnp.bfloat16)


def read_lanes(ref, at):
    return down(ref[:, at : at + LANES].astype(jnp.float32))


def chip_at(place):
    place = lax.rem(place + 8, 8)
    return jnp.where(place < 4, 2 * place, 15 - 2 * place)


def ring_place(me):
    chip, core = me // 2, me % 2
    place = jnp.where(chip % 2 == 0, chip // 2, (15 - chip) // 2)
    return place, core


def ahead(me, distance, half, core=None):
    place, own = ring_place(me)
    core = own if core is None else core
    return chip_at(place + (1 - 2 * core) * distance) * 2 + half


ROUNDS = 3


def sent_devices(me, core):
    devices = []
    for k in range(ROUNDS):
        for half in (core, 1 - core):
            devices.append(ahead(me, ROUNDS - k, half, core))
    return devices + [ahead(me, 4, core, core), ahead(me, 0, core, core)]


def gathered_devices(me):
    core = me % 2
    devices = [ahead(me, 0, core), ahead(me, 0, 1 - core)]
    for k in range(1, ROUNDS + 1):
        devices += [ahead(me, -k, core), ahead(me, -k, 1 - core)]
        devices += [ahead(me, k, 1 - core), ahead(me, k, core)]
    return devices + [ahead(me, 4, core), ahead(me, 4, 1 - core)]


def message_parts(sectors, rows, width):
    for s in range(sectors):
        for row, part in halves(rows, width, s * (rows // HALF) * width):
            yield s, row, part


def message_shape(sectors, rows, width):
    return (HALF, rows // HALF * sectors * width + LANES)


def prepare_kernel(wave_ref, diag_ref, _, own_ref, square_ref):
    own_ref[...] = wave_ref[...]
    square = jnp.zeros((8, 128), jnp.float32)
    for s in range(wave_ref.shape[0]):
        wave = wave_ref[s].astype(jnp.float32)
        square += fold(diag_ref[s].astype(jnp.float32) * wave * wave)
    square_ref[...] = square


def prepare(wave, diag, after):
    return pl.pallas_call(
        prepare_kernel,
        in_specs=[VMEM, VMEM, HBM],
        out_specs=[VMEM, VMEM],
        out_shape=[
            jax.ShapeDtypeStruct(wave.shape, wave.dtype),
            jax.ShapeDtypeStruct((8, 128), jnp.float32),
        ],
        compiler_params=PARAMS,
    )(wave, diag, after)


def blocks_kernel(first, shape, entries, me_ref, ints_ref, *refs):
    sectors, rows, width = shape
    field_refs, refs = refs[:16], refs[16:]
    if first:
        square_ref, *refs = refs
    else:
        scale_ref, wave_ref, correction_ref, *refs = refs
    left_hbm, right_hbm, *refs = refs
    total, near_ref, far_ref, dot_ref, out_ref, left, right, field, left_sem, right_sem = refs
    slots = left.shape[0]

    def copies(slot):
        return (
            pltpu.make_async_copy(left_hbm.at[slot], left.at[slot], left_sem.at[slot]),
            pltpu.make_async_copy(right_hbm.at[slot], right.at[slot], right_sem.at[slot]),
        )

    for slot in range(slots):
        for copy in copies(slot):
            copy.start()

    me = me_ref[0]
    core = me % 2

    pieces = []
    for k, owner in enumerate(gathered_devices(me)):
        at = pl.multiple_of(owner * rows, rows)
        if first:
            for s in range(sectors):
                pieces.append((k, (s,), s, pl.ds(at, rows)))
        else:
            for s, row, part in message_parts(sectors, rows, width):
                pieces.append((k, (slice(None), part), s, pl.ds(at + row, HALF)))

    total[...] = jnp.zeros_like(total)
    if first:
        dot = jnp.zeros((8, 128), jnp.float32)
        for k, part, _, _ in pieces:
            value = field_refs[k][part].astype(jnp.float32)
            dot += fold(value * value)
        scale = jnp.sqrt(jnp.sum(dot) / entries)
        inverse = 1.0 / scale
        out_ref[...] = jnp.full(out_ref.shape, scale, jnp.float32)
        for k, part, s, at in pieces:
            field[s, at, :] = (field_refs[k][part].astype(jnp.float32) * inverse).astype(jnp.bfloat16)
    else:
        for k, part, s, at in pieces:
            field[s, at, :] = field_refs[k][part]

    used = ints_ref[2 * slots]

    def add_pair(step, carry):
        one, two = 2 * step, 2 * step + 1
        for slot in (one, two):
            for copy in copies(slot):
                copy.wait()

        @pl.when(one < used)
        def _():
            products = [
                jnp.dot(
                    left[slot], field[ints_ref[slot]], preferred_element_type=jnp.float32
                ).astype(jnp.bfloat16)
                for slot in (one, two)
            ]
            products[1] = jnp.where(two < used, products[1], jnp.zeros_like(products[1]))
            for slot, product in zip((one, two), products):
                total[ints_ref[slots + slot]] += lax.dot_general(
                    product,
                    right[slot],
                    (((1,), (1,)), ((), ())),
                    preferred_element_type=jnp.float32,
                )

        return carry

    lax.fori_loop(0, slots // 2, add_pair, 0)

    dot = jnp.zeros((8, 128), jnp.float32)
    if first:
        for k, part, s, at in pieces:
            dot += fold(total[s, at, :] * field_refs[k][part].astype(jnp.float32))
        dot = dot * inverse + square_ref[...] * inverse * inverse
    else:
        at = message_shape(*shape)[1] - LANES
        lanes = sum(
            ref[:, at : at + LANES].astype(jnp.float32) for ref in field_refs
        )
        along = jnp.sum(lanes) / entries
        out_ref[...] = jnp.full(out_ref.shape, along, jnp.float32)
        inverse = 1.0 / scale_ref[0:1, 0:1]
        for s in range(sectors):
            projected = correction_ref[s] - along * (wave_ref[s].astype(jnp.float32) * inverse)
            dot += fold(projected * projected)
    dot_ref[...] = dot
    lanes = down(dot)
    for k, owner in enumerate(sent_devices(me, 1 - core)):
        at = pl.multiple_of(owner * rows, rows)
        ref = near_ref.at[k] if k < near_ref.shape[0] else far_ref.at[k - near_ref.shape[0]]
        for s, row, part in message_parts(*shape):
            ref[:, part] = total[s, pl.ds(at + row, HALF), :].astype(jnp.bfloat16)
        write_lanes(ref, ref.shape[1] - LANES, lanes)


def apply_blocks(me, ints, fields, own, left, right, shape, first, entries):
    slots, order, width = left.shape
    sectors = shape[0]
    message = message_shape(*shape)
    return pl.pallas_call(
        functools.partial(blocks_kernel, first, shape, entries),
        in_specs=[SMEM, SMEM] + [VMEM] * (len(fields) + len(own)) + [HBM] * 2,
        out_specs=[VMEM] * 5,
        scratch_shapes=[
            pltpu.VMEM(left.shape, left.dtype),
            pltpu.VMEM(right.shape, right.dtype),
            pltpu.VMEM((sectors, order, width), jnp.bfloat16),
            pltpu.SemaphoreType.DMA((slots,)),
            pltpu.SemaphoreType.DMA((slots,)),
        ],
        out_shape=[
            jax.ShapeDtypeStruct((sectors, order, width), jnp.float32),
            jax.ShapeDtypeStruct((2, *message), jnp.bfloat16),
            jax.ShapeDtypeStruct((2 * ROUNDS, *message), jnp.bfloat16),
            jax.ShapeDtypeStruct((8, 128), jnp.float32),
            jax.ShapeDtypeStruct((8, 128), jnp.float32),
        ],
        compiler_params=PARAMS,
        cost_estimate=pl.CostEstimate(
            flops=4 * slots * order * order * width,
            bytes_accessed=4 * slots * order * order,
            transcendentals=0,
        ),
    )(me, ints, *fields, *own, left, right)


def chain_kernel(shape, k, index, me_ref, total_ref, dot_ref, other_ref, *refs):
    *arrived_refs, out_ref = refs
    _, rows, _ = shape
    me = me_ref[0]
    start = pl.multiple_of(sent_devices(me, me % 2)[k] * rows, rows)
    for s, row, part in message_parts(*shape):
        value = total_ref[s, pl.ds(start + row, HALF), :]
        value += other_ref[index, :, part].astype(jnp.float32)
        for ref in arrived_refs:
            value += ref[:, part].astype(jnp.float32)
        out_ref[:, part] = value.astype(jnp.bfloat16)
    at = out_ref.shape[1] - LANES
    lanes = down(dot_ref[...]) + read_lanes(other_ref.at[index], at)
    for ref in arrived_refs:
        lanes += read_lanes(ref, at)
    write_lanes(out_ref, at, lanes)


def chain(shape, k, index, me, total, dot, other, *arrived):
    return pl.pallas_call(
        functools.partial(chain_kernel, shape, k, index),
        in_specs=[SMEM] + [VMEM] * (3 + len(arrived)),
        out_specs=VMEM,
        out_shape=jax.ShapeDtypeStruct(message_shape(*shape), jnp.bfloat16),
        compiler_params=PARAMS,
    )(me, total, dot, other, *arrived)


def own_terms(shape, sector, me_ref, total_ref, other_ref, _, *arrived_refs):
    start = pl.multiple_of(me_ref[0] * shape[1], shape[1])
    values = []
    for s, row, part in message_parts(*shape):
        if s == sector:
            value = total_ref[s, pl.ds(start + row, HALF), :]
            value += other_ref[other_ref.shape[0] - 1, :, part].astype(jnp.float32)
            for ref in arrived_refs:
                value += ref[:, part].astype(jnp.float32)
            values.append(value)
    return jnp.concatenate(values, axis=0)


def own_scalar(me_ref, total_ref, other_ref, dot_ref, *arrived_refs):
    at = other_ref.shape[2] - LANES
    lanes = down(dot_ref[...]) + read_lanes(other_ref.at[other_ref.shape[0] - 1], at)
    return jnp.sum(lanes + sum(read_lanes(ref, at) for ref in arrived_refs))


def step_kernel(entries, scale_ref, wave_ref, diag_ref, *refs):
    *sums, first_ref, terms_ref, correction_ref, message_ref = refs
    shape = wave_ref.shape
    ritz = own_scalar(*sums) / entries
    inverse = 1.0 / scale_ref[0:1, 0:1]
    dots = jnp.zeros((8, 128), jnp.float32)
    for s in range(shape[0]):
        start = wave_ref[s].astype(jnp.float32) * inverse
        diag = diag_ref[s].astype(jnp.float32)
        terms = own_terms(shape, s, *sums)
        first = terms + diag * start
        correction = (first - ritz * start) / jnp.maximum(jnp.abs(diag - ritz), 1.0)
        first_ref[s] = first
        terms_ref[s] = terms
        correction_ref[s] = correction
        dots += fold(start * correction)
        for t, row, part in message_parts(*shape):
            if t == s:
                message_ref[:, part] = correction[row : row + HALF].astype(jnp.bfloat16)
    write_lanes(message_ref, message_ref.shape[1] - LANES, down(dots))


def davidson_step(scale, wave, diag, sums, entries):
    full = jax.ShapeDtypeStruct(wave.shape, jnp.float32)
    return pl.pallas_call(
        functools.partial(step_kernel, entries),
        in_specs=[VMEM] * 3 + [SMEM] + [VMEM] * (len(sums) - 1),
        out_specs=[VMEM] * 4,
        out_shape=[full, full, full, jax.ShapeDtypeStruct(message_shape(*wave.shape), jnp.bfloat16)],
        compiler_params=PARAMS,
    )(scale, wave, diag, *sums)


def finish_kernel(entries, along_ref, scale_ref, wave_ref, diag_ref, *refs):
    terms_ref, correction_ref, *sums, vector_ref, image_ref = refs
    shape = wave_ref.shape
    along = along_ref[0:1, 0:1]
    norm = jnp.sqrt(jnp.full((1, 1), own_scalar(*sums) / entries, jnp.float32))
    inverse = 1.0 / norm
    start_scale = 1.0 / scale_ref[0:1, 0:1]
    for s in range(shape[0]):
        start = wave_ref[s].astype(jnp.float32) * start_scale
        second = (correction_ref[s] - along * start) * inverse
        vector_ref[s] = second
        image = (own_terms(shape, s, *sums) - along * terms_ref[s]) * inverse
        image_ref[s] = image + diag_ref[s].astype(jnp.float32) * second


def finish(along, scale, wave, diag, terms, correction, sums, entries):
    full = jax.ShapeDtypeStruct(wave.shape, jnp.float32)
    return pl.pallas_call(
        functools.partial(finish_kernel, entries),
        in_specs=[VMEM] * 6 + [SMEM] + [VMEM] * (len(sums) - 1),
        out_specs=[VMEM] * 2,
        out_shape=[full, full],
        compiler_params=PARAMS,
    )(along, scale, wave, diag, terms, correction, *sums)


def flip(value):
    return lax.ppermute(value, "term", [(i, i ^ 1) for i in range(16)])


def hop(value, up=1, down=-1):
    order = [0, 2, 4, 6, 7, 5, 3, 1]
    pairs = []
    for place in range(8):
        for core, step in ((0, up), (1, down)):
            pairs.append((order[place] * 2 + core, order[(place + step) % 8] * 2 + core))
    return lax.ppermute(value, "term", pairs)


def opposite(value):
    return hop(value, 4, 4)


def gather(own):
    one, two = own, flip(own)
    across, two = lax.optimization_barrier((own, two))
    pieces = [one, two]
    across = opposite(across)
    for _ in range(ROUNDS):
        one, two = hop(one), hop(two)
        pieces += [one, two, flip(one), flip(two)]
    return pieces + [across, flip(across)], two


def scatter(shape, me, total, near, far, dot):
    near = flip(near)
    near, far = lax.optimization_barrier((near, far))
    far = flip(far)
    one = hop(chain(shape, 0, 0, me, total, dot, near))
    two = hop(chain(shape, 1, 1, me, total, dot, near))
    across = opposite(chain(shape, 6, 4, me, total, dot, far))
    for k in (2, 4):
        one = hop(chain(shape, k, k - 2, me, total, dot, far, one))
        two = hop(chain(shape, k + 1, k - 1, me, total, dot, far, two))
    return me, total, far, dot, one, flip(two), across


def on_ring(
    wavefunction, diagonal, left_blocks, right_blocks, block_source, block_target, live_count
):
    shape = wavefunction.shape
    sectors, rows, width = shape
    entries = float(sectors * rows * lax.axis_size("term") * width)
    me = lax.axis_index("term").astype(jnp.int32).reshape(1)
    ints = jnp.concatenate([block_source, block_target, live_count])
    blocks = (left_blocks, right_blocks, shape)

    fields, last = gather(wavefunction)
    fields[0], square = prepare(wavefunction, diagonal, last)
    total, near, far, dot, scale = apply_blocks(me, ints, fields, (square,), *blocks, True, entries)
    first_image, terms, correction, message = davidson_step(
        scale, wavefunction, diagonal, scatter(shape, me, total, near, far, dot), entries
    )
    fields, _ = gather(message)
    own = (scale, wavefunction, correction)
    total, near, far, dot, along = apply_blocks(me, ints, fields, own, *blocks, False, entries)
    second_vector, second_image = finish(
        along, scale, wavefunction, diagonal, terms, correction,
        scatter(shape, me, total, near, far, dot), entries,
    )
    return (first_image, second_vector, second_image)


def block_loop(field_rounded, left_ops, right_ops, sources, targets, last_slot, partial_sum):

    def add_block(slot_index, running):
        left_op = lax.dynamic_index_in_dim(left_ops, slot_index, 0, keepdims=False)
        right_op = lax.dynamic_index_in_dim(right_ops, slot_index, 0, keepdims=False)
        source = lax.dynamic_index_in_dim(sources, slot_index, 0, keepdims=False)
        target = lax.dynamic_index_in_dim(targets, slot_index, 0, keepdims=False)
        piece = lax.dynamic_index_in_dim(field_rounded, source, 0, keepdims=False)
        product = jnp.dot(left_op, piece, preferred_element_type=jnp.float32).astype(jnp.bfloat16)
        term_value = jnp.dot(product, right_op.T, preferred_element_type=jnp.float32)
        before = lax.dynamic_index_in_dim(running, target, 0, keepdims=False)
        return lax.dynamic_update_index_in_dim(running, before + term_value, target, 0)

    return lax.fori_loop(0, last_slot, add_block, partial_sum)


def on_any(
    wavefunction, diagonal, left_blocks, right_blocks, block_source, block_target, live_count
):
    devices = lax.axis_size("term")
    position = lax.axis_index("term")
    row_count = wavefunction.shape[1]
    sector_count = wavefunction.shape[0]
    width = wavefunction.shape[2]
    entries = float(sector_count * row_count * devices * width)
    own_count = live_count[0]
    diag_own = diagonal.astype(jnp.float32)
    whole_wave = lax.all_gather(wavefunction, "term", axis=1, tiled=True).astype(jnp.float32)
    scale = jnp.sqrt(jnp.sum(whole_wave * whole_wave) / entries)
    start_whole = whole_wave / scale
    empty_sum = jnp.zeros(start_whole.shape, jnp.float32)
    first_terms = block_loop(
        start_whole.astype(jnp.bfloat16),
        left_blocks,
        right_blocks,
        block_source,
        block_target,
        own_count,
        empty_sum,
    )
    row_start = position * row_count
    whole_diag = lax.all_gather(diagonal, "term", axis=1, tiled=True).astype(jnp.float32)
    first_whole = lax.psum(first_terms, "term") + whole_diag * start_whole
    ritz_value = jnp.sum(start_whole * first_whole) / entries
    correction = (first_whole - ritz_value * start_whole) / jnp.maximum(
        jnp.abs(whole_diag - ritz_value), 1.0
    )
    correlation = jnp.sum(start_whole * correction) / entries
    projected = correction - correlation * start_whole
    second_whole = projected / jnp.sqrt(jnp.sum(projected * projected) / entries)
    first_image = lax.dynamic_slice_in_dim(first_whole, row_start, row_count, 1)
    second_vector = lax.dynamic_slice_in_dim(second_whole, row_start, row_count, 1)
    second_rounded = second_whole.astype(jnp.bfloat16)
    second_terms = block_loop(
        second_rounded, left_blocks, right_blocks, block_source, block_target, own_count, empty_sum
    )
    second_image = (
        lax.psum_scatter(second_terms, "term", scatter_dimension=1, tiled=True)
        + diag_own * second_vector
    )
    return (first_image, second_vector, second_image)


def solution(mesh):
    placed = (
        P("grp", "term", None),
        P("grp", "term", None),
        P(("grp", "term"), None, None),
        P(("grp", "term"), None, None),
        P(("grp", "term")),
        P(("grp", "term")),
        P(("grp", "term")),
    )
    on_device = on_ring if mesh.shape["term"] == 16 else on_any
    return jax.shard_map(
        on_device,
        mesh=mesh,
        in_specs=placed,
        out_specs=(P("grp", "term", None), P("grp", "term", None), P("grp", "term", None)),
        check_vma=False,
    )
```

```python
import functools

import jax
import jax.numpy as jnp
from jax import lax
from jax.experimental import pallas as pl
from jax.experimental.pallas import tpu as pltpu
from jax.sharding import PartitionSpec as P

VMEM = pl.BlockSpec(memory_space=pltpu.VMEM)
SMEM = pl.BlockSpec(memory_space=pltpu.SMEM)
HBM = pl.BlockSpec(memory_space=pltpu.HBM)
PARAMS = pltpu.CompilerParams(vmem_limit_bytes=48 * 1024 * 1024)
HALF = 16
LANES = 128


def fold(value):
    rows, width = value.shape
    summed = jnp.sum(value.reshape(rows // 8, 8, width), axis=0)
    return sum(summed[:, k * 128 : (k + 1) * 128] for k in range(width // 128))


def down(value):
    return jnp.sum(value, axis=0, keepdims=True)


def halves(rows, width, start=0):
    for h in range(rows // HALF):
        yield h * HALF, slice(start + h * width, start + (h + 1) * width)


def write_lanes(ref, at, lanes):
    whole = jnp.broadcast_to(lanes, (HALF, LANES))
    high = whole.astype(jnp.bfloat16).astype(jnp.float32)
    rest = whole - high
    middle = rest.astype(jnp.bfloat16).astype(jnp.float32)
    low = rest - middle
    row = lax.broadcasted_iota(jnp.int32, whole.shape, 0)
    value = jnp.where(row == 0, high, jnp.where(row == 1, middle, jnp.where(row == 2, low, 0.0)))
    ref[:, at : at + LANES] = value.astype(jnp.bfloat16)


def read_lanes(ref, at):
    return down(ref[:, at : at + LANES].astype(jnp.float32))


def chip_at(place):
    place = lax.rem(place + 8, 8)
    return jnp.where(place < 4, 2 * place, 15 - 2 * place)


def ring_place(me):
    chip, core = me // 2, me % 2
    place = jnp.where(chip % 2 == 0, chip // 2, (15 - chip) // 2)
    return place, core


def ahead(me, distance, half, core=None):
    place, own = ring_place(me)
    core = own if core is None else core
    return chip_at(place + (1 - 2 * core) * distance) * 2 + half


ROUNDS = 3


def sent_devices(me, core):
    devices = []
    for k in range(ROUNDS):
        for half in (core, 1 - core):
            devices.append(ahead(me, ROUNDS - k, half, core))
    return devices + [ahead(me, 4, core, core), ahead(me, 0, core, core)]


def gathered_devices(me):
    core = me % 2
    devices = [ahead(me, 0, core), ahead(me, 0, 1 - core)]
    for k in range(1, ROUNDS + 1):
        devices += [ahead(me, -k, core), ahead(me, -k, 1 - core)]
        devices += [ahead(me, k, 1 - core), ahead(me, k, core)]
    return devices + [ahead(me, 4, core), ahead(me, 4, 1 - core)]


def message_parts(sectors, rows, width):
    for s in range(sectors):
        for row, part in halves(rows, width, s * (rows // HALF) * width):
            yield s, row, part


def message_shape(sectors, rows, width):
    return (HALF, rows // HALF * sectors * width + LANES)


def copy_kernel(in_ref, out_ref):
    out_ref[...] = in_ref[...]


def copied(value):
    return pl.pallas_call(
        copy_kernel,
        in_specs=[VMEM],
        out_specs=VMEM,
        out_shape=jax.ShapeDtypeStruct(value.shape, value.dtype),
        compiler_params=PARAMS,
    )(value)


def square_kernel(wave_ref, diag_ref, square_ref):
    square = jnp.zeros((8, 128), jnp.float32)
    for s in range(wave_ref.shape[0]):
        wave = wave_ref[s].astype(jnp.float32)
        square += fold(diag_ref[s].astype(jnp.float32) * wave * wave)
    square_ref[...] = square


def weighted_square(wave, diag):
    return pl.pallas_call(
        square_kernel,
        in_specs=[VMEM, VMEM],
        out_specs=VMEM,
        out_shape=jax.ShapeDtypeStruct((8, 128), jnp.float32),
        compiler_params=PARAMS,
    )(wave, diag)


def blocks_kernel(first, shape, entries, me_ref, ints_ref, *refs):
    sectors, rows, width = shape
    field_refs, refs = refs[:16], refs[16:]
    if first:
        square_ref, *refs = refs
    else:
        scale_ref, wave_ref, correction_ref, *refs = refs
    left_hbm, right_hbm, *refs = refs
    total, near_ref, far_ref, dot_ref, out_ref, left, right, field, left_sem, right_sem = refs
    slots = left.shape[0]

    def copies(slot):
        return (
            pltpu.make_async_copy(left_hbm.at[slot], left.at[slot], left_sem.at[slot]),
            pltpu.make_async_copy(right_hbm.at[slot], right.at[slot], right_sem.at[slot]),
        )

    for slot in range(slots):
        for copy in copies(slot):
            copy.start()

    me = me_ref[0]
    core = me % 2

    pieces = []
    for k, owner in enumerate(gathered_devices(me)):
        at = pl.multiple_of(owner * rows, rows)
        if first:
            for s in range(sectors):
                pieces.append((k, (s,), s, pl.ds(at, rows)))
        else:
            for s, row, part in message_parts(sectors, rows, width):
                pieces.append((k, (slice(None), part), s, pl.ds(at + row, HALF)))

    total[...] = jnp.zeros_like(total)
    if first:
        dot = jnp.zeros((8, 128), jnp.float32)
        for k, part, _, _ in pieces:
            value = field_refs[k][part].astype(jnp.float32)
            dot += fold(value * value)
        scale = jnp.sqrt(jnp.sum(dot) / entries)
        inverse = 1.0 / scale
        out_ref[...] = jnp.full(out_ref.shape, scale, jnp.float32)
        for k, part, s, at in pieces:
            field[s, at, :] = (field_refs[k][part].astype(jnp.float32) * inverse).astype(jnp.bfloat16)
    else:
        for k, part, s, at in pieces:
            field[s, at, :] = field_refs[k][part]

    used = ints_ref[2 * slots]

    def add_pair(step, carry):
        one, two = 2 * step, 2 * step + 1
        for slot in (one, two):
            for copy in copies(slot):
                copy.wait()

        @pl.when(one < used)
        def _():
            products = [
                jnp.dot(
                    left[slot], field[ints_ref[slot]], preferred_element_type=jnp.float32
                ).astype(jnp.bfloat16)
                for slot in (one, two)
            ]
            products[1] = jnp.where(two < used, products[1], jnp.zeros_like(products[1]))
            for slot, product in zip((one, two), products):
                total[ints_ref[slots + slot]] += lax.dot_general(
                    product,
                    right[slot],
                    (((1,), (1,)), ((), ())),
                    preferred_element_type=jnp.float32,
                )

        return carry

    lax.fori_loop(0, slots // 2, add_pair, 0)

    dot = jnp.zeros((8, 128), jnp.float32)
    if first:
        for k, part, s, at in pieces:
            dot += fold(total[s, at, :] * field_refs[k][part].astype(jnp.float32))
        dot = dot * inverse + square_ref[...] * inverse * inverse
    else:
        at = message_shape(*shape)[1] - LANES
        lanes = sum(
            ref[:, at : at + LANES].astype(jnp.float32) for ref in field_refs
        )
        along = jnp.sum(lanes) / entries
        out_ref[...] = jnp.full(out_ref.shape, along, jnp.float32)
        inverse = 1.0 / scale_ref[0:1, 0:1]
        for s in range(sectors):
            projected = correction_ref[s] - along * (wave_ref[s].astype(jnp.float32) * inverse)
            dot += fold(projected * projected)
    dot_ref[...] = dot
    lanes = down(dot)
    for k, owner in enumerate(sent_devices(me, 1 - core)):
        at = pl.multiple_of(owner * rows, rows)
        ref = near_ref.at[k] if k < near_ref.shape[0] else far_ref.at[k - near_ref.shape[0]]
        for s, row, part in message_parts(*shape):
            ref[:, part] = total[s, pl.ds(at + row, HALF), :].astype(jnp.bfloat16)
        write_lanes(ref, ref.shape[1] - LANES, lanes)


def apply_blocks(me, ints, fields, own, left, right, shape, first, entries):
    slots, order, width = left.shape
    sectors = shape[0]
    message = message_shape(*shape)
    return pl.pallas_call(
        functools.partial(blocks_kernel, first, shape, entries),
        in_specs=[SMEM, SMEM] + [VMEM] * (len(fields) + len(own)) + [HBM] * 2,
        out_specs=[VMEM] * 5,
        scratch_shapes=[
            pltpu.VMEM(left.shape, left.dtype),
            pltpu.VMEM(right.shape, right.dtype),
            pltpu.VMEM((sectors, order, width), jnp.bfloat16),
            pltpu.SemaphoreType.DMA((slots,)),
            pltpu.SemaphoreType.DMA((slots,)),
        ],
        out_shape=[
            jax.ShapeDtypeStruct((sectors, order, width), jnp.float32),
            jax.ShapeDtypeStruct((2, *message), jnp.bfloat16),
            jax.ShapeDtypeStruct((2 * ROUNDS, *message), jnp.bfloat16),
            jax.ShapeDtypeStruct((8, 128), jnp.float32),
            jax.ShapeDtypeStruct((8, 128), jnp.float32),
        ],
        compiler_params=PARAMS,
        cost_estimate=pl.CostEstimate(
            flops=4 * slots * order * order * width,
            bytes_accessed=4 * slots * order * order,
            transcendentals=0,
        ),
    )(me, ints, *fields, *own, left, right)


def chain_kernel(shape, k, index, me_ref, total_ref, dot_ref, other_ref, *refs):
    *arrived_refs, out_ref = refs
    _, rows, _ = shape
    me = me_ref[0]
    start = pl.multiple_of(sent_devices(me, me % 2)[k] * rows, rows)
    for s, row, part in message_parts(*shape):
        value = total_ref[s, pl.ds(start + row, HALF), :]
        value += other_ref[index, :, part].astype(jnp.float32)
        for ref in arrived_refs:
            value += ref[:, part].astype(jnp.float32)
        out_ref[:, part] = value.astype(jnp.bfloat16)
    at = out_ref.shape[1] - LANES
    lanes = down(dot_ref[...]) + read_lanes(other_ref.at[index], at)
    for ref in arrived_refs:
        lanes += read_lanes(ref, at)
    write_lanes(out_ref, at, lanes)


def chain(shape, k, index, me, total, dot, other, *arrived):
    return pl.pallas_call(
        functools.partial(chain_kernel, shape, k, index),
        in_specs=[SMEM] + [VMEM] * (3 + len(arrived)),
        out_specs=VMEM,
        out_shape=jax.ShapeDtypeStruct(message_shape(*shape), jnp.bfloat16),
        compiler_params=PARAMS,
    )(me, total, dot, other, *arrived)


def own_terms(shape, sector, me_ref, total_ref, other_ref, _, *arrived_refs):
    start = pl.multiple_of(me_ref[0] * shape[1], shape[1])
    values = []
    for s, row, part in message_parts(*shape):
        if s == sector:
            value = total_ref[s, pl.ds(start + row, HALF), :]
            value += other_ref[other_ref.shape[0] - 1, :, part].astype(jnp.float32)
            for ref in arrived_refs:
                value += ref[:, part].astype(jnp.float32)
            values.append(value)
    return jnp.concatenate(values, axis=0)


def own_scalar(me_ref, total_ref, other_ref, dot_ref, *arrived_refs):
    at = other_ref.shape[2] - LANES
    lanes = down(dot_ref[...]) + read_lanes(other_ref.at[other_ref.shape[0] - 1], at)
    return jnp.sum(lanes + sum(read_lanes(ref, at) for ref in arrived_refs))


def step_kernel(entries, scale_ref, wave_ref, diag_ref, *refs):
    *sums, first_ref, terms_ref, correction_ref, message_ref = refs
    shape = wave_ref.shape
    ritz = own_scalar(*sums) / entries
    inverse = 1.0 / scale_ref[0:1, 0:1]
    dots = jnp.zeros((8, 128), jnp.float32)
    for s in range(shape[0]):
        start = wave_ref[s].astype(jnp.float32) * inverse
        diag = diag_ref[s].astype(jnp.float32)
        terms = own_terms(shape, s, *sums)
        first = terms + diag * start
        correction = (first - ritz * start) / jnp.maximum(jnp.abs(diag - ritz), 1.0)
        first_ref[s] = first
        terms_ref[s] = terms
        correction_ref[s] = correction
        dots += fold(start * correction)
        for t, row, part in message_parts(*shape):
            if t == s:
                message_ref[:, part] = correction[row : row + HALF].astype(jnp.bfloat16)
    write_lanes(message_ref, message_ref.shape[1] - LANES, down(dots))


def davidson_step(scale, wave, diag, sums, entries):
    full = jax.ShapeDtypeStruct(wave.shape, jnp.float32)
    return pl.pallas_call(
        functools.partial(step_kernel, entries),
        in_specs=[VMEM] * 3 + [SMEM] + [VMEM] * (len(sums) - 1),
        out_specs=[VMEM] * 4,
        out_shape=[full, full, full, jax.ShapeDtypeStruct(message_shape(*wave.shape), jnp.bfloat16)],
        compiler_params=PARAMS,
    )(scale, wave, diag, *sums)


def finish_kernel(entries, along_ref, scale_ref, wave_ref, diag_ref, *refs):
    terms_ref, correction_ref, *sums, vector_ref, image_ref = refs
    shape = wave_ref.shape
    along = along_ref[0:1, 0:1]
    norm = jnp.sqrt(jnp.full((1, 1), own_scalar(*sums) / entries, jnp.float32))
    inverse = 1.0 / norm
    start_scale = 1.0 / scale_ref[0:1, 0:1]
    for s in range(shape[0]):
        start = wave_ref[s].astype(jnp.float32) * start_scale
        second = (correction_ref[s] - along * start) * inverse
        vector_ref[s] = second
        image = (own_terms(shape, s, *sums) - along * terms_ref[s]) * inverse
        image_ref[s] = image + diag_ref[s].astype(jnp.float32) * second


def finish(along, scale, wave, diag, terms, correction, sums, entries):
    full = jax.ShapeDtypeStruct(wave.shape, jnp.float32)
    return pl.pallas_call(
        functools.partial(finish_kernel, entries),
        in_specs=[VMEM] * 6 + [SMEM] + [VMEM] * (len(sums) - 1),
        out_specs=[VMEM] * 2,
        out_shape=[full, full],
        compiler_params=PARAMS,
    )(along, scale, wave, diag, terms, correction, *sums)


def flip(value):
    return lax.ppermute(value, "term", [(i, i ^ 1) for i in range(16)])


def hop(value, up=1, down=-1):
    order = [0, 2, 4, 6, 7, 5, 3, 1]
    pairs = []
    for place in range(8):
        for core, step in ((0, up), (1, down)):
            pairs.append((order[place] * 2 + core, order[(place + step) % 8] * 2 + core))
    return lax.ppermute(value, "term", pairs)


def opposite(value):
    return hop(value, 4, 4)


def gather(own, beside=()):
    one, two = own, flip(own)
    across, two = lax.optimization_barrier((own, two))
    pieces = [one, two]
    across = opposite(across)
    results = []
    for k in range(ROUNDS):
        one, two = hop(one), hop(two)
        if k < len(beside):
            results.append(beside[k](*results))
        if k < ROUNDS - 1:
            ready = results[-1:] if beside else []
            if k == 1:
                two, across, ready = lax.optimization_barrier((two, across, ready))
            else:
                two, ready = lax.optimization_barrier((two, ready))
            if ready:
                results[-1] = ready[0]
        pieces += [one, two, flip(one), flip(two)]
    return pieces + [across, flip(across)], results


def scatter(shape, me, total, near, far, dot):
    near = flip(near)
    near, far = lax.optimization_barrier((near, far))
    far = flip(far)
    one = hop(chain(shape, 0, 0, me, total, dot, near))
    two = hop(chain(shape, 1, 1, me, total, dot, near))
    across = opposite(chain(shape, 6, 4, me, total, dot, far))
    for k in (2, 4):
        one = hop(chain(shape, k, k - 2, me, total, dot, far, one))
        if k == 4:
            two, across = lax.optimization_barrier((two, across))
        two = hop(chain(shape, k + 1, k - 1, me, total, dot, far, two))
    return me, total, far, dot, one, flip(two), across


def on_ring(
    wavefunction, diagonal, left_blocks, right_blocks, block_source, block_target, live_count
):
    shape = wavefunction.shape
    sectors, rows, width = shape
    entries = float(sectors * rows * lax.axis_size("term") * width)
    me = lax.axis_index("term").astype(jnp.int32).reshape(1)
    blocks = (left_blocks, right_blocks, shape)

    beside = (
        lambda: jnp.concatenate([block_source, block_target, live_count]),
        lambda _: copied(wavefunction),
        lambda _, own: weighted_square(own, diagonal),
    )
    (_, *fields), (ints, own, square) = gather(wavefunction, beside)
    fields = [own, *fields]
    total, near, far, dot, scale = apply_blocks(me, ints, fields, (square,), *blocks, True, entries)
    first_image, terms, correction, message = davidson_step(
        scale, wavefunction, diagonal, scatter(shape, me, total, near, far, dot), entries
    )
    fields, _ = gather(message)
    own = (scale, wavefunction, correction)
    total, near, far, dot, along = apply_blocks(me, ints, fields, own, *blocks, False, entries)
    second_vector, second_image = finish(
        along, scale, wavefunction, diagonal, terms, correction,
        scatter(shape, me, total, near, far, dot), entries,
    )
    return (first_image, second_vector, second_image)


def block_loop(field_rounded, left_ops, right_ops, sources, targets, last_slot, partial_sum):

    def add_block(slot_index, running):
        left_op = lax.dynamic_index_in_dim(left_ops, slot_index, 0, keepdims=False)
        right_op = lax.dynamic_index_in_dim(right_ops, slot_index, 0, keepdims=False)
        source = lax.dynamic_index_in_dim(sources, slot_index, 0, keepdims=False)
        target = lax.dynamic_index_in_dim(targets, slot_index, 0, keepdims=False)
        piece = lax.dynamic_index_in_dim(field_rounded, source, 0, keepdims=False)
        product = jnp.dot(left_op, piece, preferred_element_type=jnp.float32).astype(jnp.bfloat16)
        term_value = jnp.dot(product, right_op.T, preferred_element_type=jnp.float32)
        before = lax.dynamic_index_in_dim(running, target, 0, keepdims=False)
        return lax.dynamic_update_index_in_dim(running, before + term_value, target, 0)

    return lax.fori_loop(0, last_slot, add_block, partial_sum)


def on_any(
    wavefunction, diagonal, left_blocks, right_blocks, block_source, block_target, live_count
):
    devices = lax.axis_size("term")
    position = lax.axis_index("term")
    row_count = wavefunction.shape[1]
    sector_count = wavefunction.shape[0]
    width = wavefunction.shape[2]
    entries = float(sector_count * row_count * devices * width)
    own_count = live_count[0]
    diag_own = diagonal.astype(jnp.float32)
    whole_wave = lax.all_gather(wavefunction, "term", axis=1, tiled=True).astype(jnp.float32)
    scale = jnp.sqrt(jnp.sum(whole_wave * whole_wave) / entries)
    start_whole = whole_wave / scale
    empty_sum = jnp.zeros(start_whole.shape, jnp.float32)
    first_terms = block_loop(
        start_whole.astype(jnp.bfloat16),
        left_blocks,
        right_blocks,
        block_source,
        block_target,
        own_count,
        empty_sum,
    )
    row_start = position * row_count
    whole_diag = lax.all_gather(diagonal, "term", axis=1, tiled=True).astype(jnp.float32)
    first_whole = lax.psum(first_terms, "term") + whole_diag * start_whole
    ritz_value = jnp.sum(start_whole * first_whole) / entries
    correction = (first_whole - ritz_value * start_whole) / jnp.maximum(
        jnp.abs(whole_diag - ritz_value), 1.0
    )
    correlation = jnp.sum(start_whole * correction) / entries
    projected = correction - correlation * start_whole
    second_whole = projected / jnp.sqrt(jnp.sum(projected * projected) / entries)
    first_image = lax.dynamic_slice_in_dim(first_whole, row_start, row_count, 1)
    second_vector = lax.dynamic_slice_in_dim(second_whole, row_start, row_count, 1)
    second_rounded = second_whole.astype(jnp.bfloat16)
    second_terms = block_loop(
        second_rounded, left_blocks, right_blocks, block_source, block_target, own_count, empty_sum
    )
    second_image = (
        lax.psum_scatter(second_terms, "term", scatter_dimension=1, tiled=True)
        + diag_own * second_vector
    )
    return (first_image, second_vector, second_image)


def solution(mesh):
    placed = (
        P("grp", "term", None),
        P("grp", "term", None),
        P(("grp", "term"), None, None),
        P(("grp", "term"), None, None),
        P(("grp", "term")),
        P(("grp", "term")),
        P(("grp", "term")),
    )
    on_device = on_ring if mesh.shape["term"] == 16 else on_any
    return jax.shard_map(
        on_device,
        mesh=mesh,
        in_specs=placed,
        out_specs=(P("grp", "term", None), P("grp", "term", None), P("grp", "term", None)),
        check_vma=False,
    )
```

```python
import functools

import jax
import jax.numpy as jnp
from jax import lax
from jax.experimental import pallas as pl
from jax.experimental.pallas import tpu as pltpu
from jax.sharding import PartitionSpec as P

VMEM = pl.BlockSpec(memory_space=pltpu.VMEM)
SMEM = pl.BlockSpec(memory_space=pltpu.SMEM)
HBM = pl.BlockSpec(memory_space=pltpu.HBM)
PARAMS = pltpu.CompilerParams(vmem_limit_bytes=48 * 1024 * 1024)
HALF = 16
LANES = 128


def fold(value):
    rows, width = value.shape
    summed = jnp.sum(value.reshape(rows // 8, 8, width), axis=0)
    return sum(summed[:, k * 128 : (k + 1) * 128] for k in range(width // 128))


def down(value):
    return jnp.sum(value, axis=0, keepdims=True)


def halves(rows, width, start=0):
    for h in range(rows // HALF):
        yield h * HALF, slice(start + h * width, start + (h + 1) * width)


def write_lanes(ref, at, lanes):
    whole = jnp.broadcast_to(lanes, (HALF, LANES))
    high = whole.astype(jnp.bfloat16).astype(jnp.float32)
    rest = whole - high
    middle = rest.astype(jnp.bfloat16).astype(jnp.float32)
    low = rest - middle
    row = lax.broadcasted_iota(jnp.int32, whole.shape, 0)
    value = jnp.where(row == 0, high, jnp.where(row == 1, middle, jnp.where(row == 2, low, 0.0)))
    ref[:, at : at + LANES] = value.astype(jnp.bfloat16)


def read_lanes(ref, at):
    return down(ref[:, at : at + LANES].astype(jnp.float32))


def chip_at(place):
    place = lax.rem(place + 8, 8)
    return jnp.where(place < 4, 2 * place, 15 - 2 * place)


def ring_place(me):
    chip, core = me // 2, me % 2
    place = jnp.where(chip % 2 == 0, chip // 2, (15 - chip) // 2)
    return place, core


def ahead(me, distance, half, core=None):
    place, own = ring_place(me)
    core = own if core is None else core
    return chip_at(place + (1 - 2 * core) * distance) * 2 + half


ROUNDS = 3


def sent_devices(me, core):
    devices = []
    for k in range(ROUNDS):
        for half in (core, 1 - core):
            devices.append(ahead(me, ROUNDS - k, half, core))
    return devices + [ahead(me, 4, core, core), ahead(me, 0, core, core)]


def gathered_devices(me):
    core = me % 2
    devices = []
    for sign, mine in ((-1, core), (1, 1 - core)):
        devices += [ahead(me, 0, mine), ahead(me, sign, mine)]
        for d in (1, 2, 3):
            devices += [ahead(me, sign * (d + 1), mine), ahead(me, sign * d, 1 - mine)]
    return devices


def message_parts(sectors, rows, width):
    for s in range(sectors):
        for row, part in halves(rows, width, s * (rows // HALF) * width):
            yield s, row, part


def message_shape(sectors, rows, width):
    return (HALF, rows // HALF * sectors * width + LANES)


def message_kernel(wave_ref, all_ref, *out_refs):
    sectors, rows, width = wave_ref.shape
    for s in range(sectors):
        for row, part in halves(rows, width):
            value = wave_ref[s, row : row + HALF, :]
            all_ref[s, :, part] = value
            out_refs[s][0, :, part] = value


def as_messages(wave):
    sectors, rows, width = wave.shape
    shape = (HALF, rows // HALF * width)
    return pl.pallas_call(
        message_kernel,
        in_specs=[VMEM],
        out_specs=[VMEM] * (1 + sectors),
        out_shape=[jax.ShapeDtypeStruct((sectors, *shape), wave.dtype)]
        + [jax.ShapeDtypeStruct((1, *shape), wave.dtype)] * sectors,
        compiler_params=PARAMS,
    )(wave)


def pair_kernel(s, one_ref, two_ref, out_ref):
    out_ref[0] = one_ref[0]
    out_ref[1] = two_ref[s, :, : one_ref.shape[2]]


def pair(s, one, two):
    return pl.pallas_call(
        functools.partial(pair_kernel, s),
        in_specs=[VMEM, VMEM],
        out_specs=VMEM,
        out_shape=jax.ShapeDtypeStruct((2, *one.shape[1:]), one.dtype),
        compiler_params=PARAMS,
    )(one, two)


def pack_kernel(*refs):
    *in_refs, out_ref = refs
    at = 0
    for ref in in_refs:
        for k in range(ref.shape[0]):
            out_ref[at, :, : ref.shape[2]] = ref[k]
            at += 1


def pack(*messages):
    lanes = max(m.shape[2] for m in messages)
    count = sum(m.shape[0] for m in messages)
    return pl.pallas_call(
        pack_kernel,
        in_specs=[VMEM] * len(messages),
        out_specs=VMEM,
        out_shape=jax.ShapeDtypeStruct((count, HALF, lanes), messages[0].dtype),
        compiler_params=PARAMS,
    )(*messages)


def square_kernel(diag_ref, wave_ref, square_ref):
    square = jnp.zeros((8, 128), jnp.float32)
    for s in range(wave_ref.shape[0]):
        for row, part in halves(diag_ref.shape[1], diag_ref.shape[2]):
            wave = wave_ref[s, :, part].astype(jnp.float32)
            square += fold(diag_ref[s, row : row + HALF, :].astype(jnp.float32) * wave * wave)
    square_ref[...] = square


def weighted_square(diag, wave):
    return pl.pallas_call(
        square_kernel,
        in_specs=[VMEM, VMEM],
        out_specs=VMEM,
        out_shape=jax.ShapeDtypeStruct((8, 128), jnp.float32),
        compiler_params=PARAMS,
    )(diag, wave)


def blocks_kernel(first, shape, entries, me_ref, ints_ref, *refs):
    sectors, rows, width = shape
    views = []
    (partner_ref, theirs_ref), refs = refs[:2], refs[2:]
    for s in range(sectors):
        mine, refs = refs[:5], refs[5:]
        views.append(
            [ref.at[k] for ref in mine for k in range(ref.shape[0])]
            + [partner_ref.at[s]]
            + [theirs_ref.at[s * 7 + k] for k in range(7)]
        )
    if first:
        square_ref, *refs = refs
    else:
        scale_ref, wave_ref, correction_ref, *refs = refs
    left_hbm, right_hbm, *refs = refs
    total, near_ref, far_ref, dot_ref, out_ref, left, right, field, left_sem, right_sem = refs
    slots = left.shape[0]

    def copies(slot):
        return (
            pltpu.make_async_copy(left_hbm.at[slot], left.at[slot], left_sem.at[slot]),
            pltpu.make_async_copy(right_hbm.at[slot], right.at[slot], right_sem.at[slot]),
        )

    for slot in range(slots):
        for copy in copies(slot):
            copy.start()

    me = me_ref[0]
    core = me % 2

    pieces = []
    for k, owner in enumerate(gathered_devices(me)):
        at = pl.multiple_of(owner * rows, rows)
        for s in range(sectors):
            for row, part in halves(rows, width):
                pieces.append((views[s][k], part, s, pl.ds(at + row, HALF)))

    total[...] = jnp.zeros_like(total)
    if first:
        dot = jnp.zeros((8, 128), jnp.float32)
        for ref, part, _, _ in pieces:
            value = ref[:, part].astype(jnp.float32)
            dot += fold(value * value)
        scale = jnp.sqrt(jnp.sum(dot) / entries)
        inverse = 1.0 / scale
        out_ref[...] = jnp.full(out_ref.shape, scale, jnp.float32)
        for ref, part, s, at in pieces:
            field[s, at, :] = (ref[:, part].astype(jnp.float32) * inverse).astype(jnp.bfloat16)
    else:
        for ref, part, s, at in pieces:
            field[s, at, :] = ref[:, part]

    used = ints_ref[2 * slots]

    def add_pair(step, carry):
        one, two = 2 * step, 2 * step + 1
        for slot in (one, two):
            for copy in copies(slot):
                copy.wait()

        @pl.when(one < used)
        def _():
            products = [
                jnp.dot(
                    left[slot], field[ints_ref[slot]], preferred_element_type=jnp.float32
                ).astype(jnp.bfloat16)
                for slot in (one, two)
            ]
            products[1] = jnp.where(two < used, products[1], jnp.zeros_like(products[1]))
            for slot, product in zip((one, two), products):
                total[ints_ref[slots + slot]] += lax.dot_general(
                    product,
                    right[slot],
                    (((1,), (1,)), ((), ())),
                    preferred_element_type=jnp.float32,
                )

        return carry

    lax.fori_loop(0, slots // 2, add_pair, 0)

    dot = jnp.zeros((8, 128), jnp.float32)
    if first:
        for ref, part, s, at in pieces:
            dot += fold(total[s, at, :] * ref[:, part].astype(jnp.float32))
        dot = dot * inverse + square_ref[...] * inverse * inverse
    else:
        lanes = sum(read_lanes(view, rows // HALF * width) for view in views[sectors - 1])
        along = jnp.sum(lanes) / entries
        out_ref[...] = jnp.full(out_ref.shape, along, jnp.float32)
        inverse = 1.0 / scale_ref[0:1, 0:1]
        for s in range(sectors):
            projected = correction_ref[s] - along * (wave_ref[s].astype(jnp.float32) * inverse)
            dot += fold(projected * projected)
    dot_ref[...] = dot
    lanes = down(dot)
    for k, owner in enumerate(sent_devices(me, 1 - core)):
        at = pl.multiple_of(owner * rows, rows)
        ref = near_ref.at[k] if k < near_ref.shape[0] else far_ref.at[k - near_ref.shape[0]]
        for s, row, part in message_parts(*shape):
            ref[:, part] = total[s, pl.ds(at + row, HALF), :].astype(jnp.bfloat16)
        write_lanes(ref, ref.shape[1] - LANES, lanes)


def apply_blocks(me, ints, fields, own, left, right, shape, first, entries):
    slots, order, width = left.shape
    sectors = shape[0]
    message = message_shape(*shape)
    return pl.pallas_call(
        functools.partial(blocks_kernel, first, shape, entries),
        in_specs=[SMEM, SMEM] + [VMEM] * (len(fields) + len(own)) + [HBM] * 2,
        out_specs=[VMEM] * 5,
        scratch_shapes=[
            pltpu.VMEM(left.shape, left.dtype),
            pltpu.VMEM(right.shape, right.dtype),
            pltpu.VMEM((sectors, order, width), jnp.bfloat16),
            pltpu.SemaphoreType.DMA((slots,)),
            pltpu.SemaphoreType.DMA((slots,)),
        ],
        out_shape=[
            jax.ShapeDtypeStruct((sectors, order, width), jnp.float32),
            jax.ShapeDtypeStruct((2, *message), jnp.bfloat16),
            jax.ShapeDtypeStruct((2 * ROUNDS, *message), jnp.bfloat16),
            jax.ShapeDtypeStruct((8, 128), jnp.float32),
            jax.ShapeDtypeStruct((8, 128), jnp.float32),
        ],
        compiler_params=PARAMS,
        cost_estimate=pl.CostEstimate(
            flops=4 * slots * order * order * width,
            bytes_accessed=4 * slots * order * order,
            transcendentals=0,
        ),
    )(me, ints, *fields, *own, left, right)


def chain_kernel(shape, k, index, me_ref, total_ref, dot_ref, other_ref, *refs):
    *arrived_refs, out_ref = refs
    _, rows, _ = shape
    me = me_ref[0]
    start = pl.multiple_of(sent_devices(me, me % 2)[k] * rows, rows)
    for s, row, part in message_parts(*shape):
        value = total_ref[s, pl.ds(start + row, HALF), :]
        value += other_ref[index, :, part].astype(jnp.float32)
        for ref in arrived_refs:
            value += ref[:, part].astype(jnp.float32)
        out_ref[:, part] = value.astype(jnp.bfloat16)
    at = out_ref.shape[1] - LANES
    lanes = down(dot_ref[...]) + read_lanes(other_ref.at[index], at)
    for ref in arrived_refs:
        lanes += read_lanes(ref, at)
    write_lanes(out_ref, at, lanes)


def chain(shape, k, index, me, total, dot, other, *arrived):
    return pl.pallas_call(
        functools.partial(chain_kernel, shape, k, index),
        in_specs=[SMEM] + [VMEM] * (3 + len(arrived)),
        out_specs=VMEM,
        out_shape=jax.ShapeDtypeStruct(message_shape(*shape), jnp.bfloat16),
        compiler_params=PARAMS,
    )(me, total, dot, other, *arrived)


def own_terms(shape, sector, me_ref, total_ref, other_ref, _, *arrived_refs):
    start = pl.multiple_of(me_ref[0] * shape[1], shape[1])
    values = []
    for s, row, part in message_parts(*shape):
        if s == sector:
            value = total_ref[s, pl.ds(start + row, HALF), :]
            value += other_ref[other_ref.shape[0] - 1, :, part].astype(jnp.float32)
            for ref in arrived_refs:
                value += ref[:, part].astype(jnp.float32)
            values.append(value)
    return jnp.concatenate(values, axis=0)


def own_scalar(me_ref, total_ref, other_ref, dot_ref, *arrived_refs):
    at = other_ref.shape[2] - LANES
    lanes = down(dot_ref[...]) + read_lanes(other_ref.at[other_ref.shape[0] - 1], at)
    return jnp.sum(lanes + sum(read_lanes(ref, at) for ref in arrived_refs))


def step_kernel(entries, scale_ref, wave_ref, diag_ref, *refs):
    shape = wave_ref.shape
    sectors, rows, width = shape
    *sums, first_ref, terms_ref, correction_ref, all_ref = refs[:-sectors]
    message_refs = refs[-sectors:]
    ritz = own_scalar(*sums) / entries
    inverse = 1.0 / scale_ref[0:1, 0:1]
    dots = jnp.zeros((8, 128), jnp.float32)
    for s in range(shape[0]):
        start = wave_ref[s].astype(jnp.float32) * inverse
        diag = diag_ref[s].astype(jnp.float32)
        terms = own_terms(shape, s, *sums)
        first = terms + diag * start
        correction = (first - ritz * start) / jnp.maximum(jnp.abs(diag - ritz), 1.0)
        first_ref[s] = first
        terms_ref[s] = terms
        correction_ref[s] = correction
        dots += fold(start * correction)
        for row, part in halves(rows, width):
            value = correction[row : row + HALF].astype(jnp.bfloat16)
            all_ref[s, :, part] = value
            message_refs[s][0, :, part] = value
    for ref in (all_ref.at[sectors - 1], message_refs[-1].at[0]):
        write_lanes(ref, rows // HALF * width, down(dots))


def davidson_step(scale, wave, diag, sums, entries):
    full = jax.ShapeDtypeStruct(wave.shape, jnp.float32)
    sectors, rows, width = wave.shape
    data = rows // HALF * width
    shapes = [(sectors, HALF, data + LANES)] + [(1, HALF, data)] * (sectors - 1)
    shapes.append((1, HALF, data + LANES))
    return pl.pallas_call(
        functools.partial(step_kernel, entries),
        in_specs=[VMEM] * 3 + [SMEM] + [VMEM] * (len(sums) - 1),
        out_specs=[VMEM] * (4 + sectors),
        out_shape=[full] * 3 + [jax.ShapeDtypeStruct(s, jnp.bfloat16) for s in shapes],
        compiler_params=PARAMS,
    )(scale, wave, diag, *sums)


def finish_kernel(entries, along_ref, scale_ref, wave_ref, diag_ref, *refs):
    terms_ref, correction_ref, *sums, vector_ref, image_ref = refs
    shape = wave_ref.shape
    along = along_ref[0:1, 0:1]
    norm = jnp.sqrt(jnp.full((1, 1), own_scalar(*sums) / entries, jnp.float32))
    inverse = 1.0 / norm
    start_scale = 1.0 / scale_ref[0:1, 0:1]
    for s in range(shape[0]):
        start = wave_ref[s].astype(jnp.float32) * start_scale
        second = (correction_ref[s] - along * start) * inverse
        vector_ref[s] = second
        image = (own_terms(shape, s, *sums) - along * terms_ref[s]) * inverse
        image_ref[s] = image + diag_ref[s].astype(jnp.float32) * second


def finish(along, scale, wave, diag, terms, correction, sums, entries):
    full = jax.ShapeDtypeStruct(wave.shape, jnp.float32)
    return pl.pallas_call(
        functools.partial(finish_kernel, entries),
        in_specs=[VMEM] * 6 + [SMEM] + [VMEM] * (len(sums) - 1),
        out_specs=[VMEM] * 2,
        out_shape=[full, full],
        compiler_params=PARAMS,
    )(along, scale, wave, diag, terms, correction, *sums)


def flip(value):
    return lax.ppermute(value, "term", [(i, i ^ 1) for i in range(16)])


def hop(value, up=1, down=-1):
    order = [0, 2, 4, 6, 7, 5, 3, 1]
    pairs = []
    for place in range(8):
        for core, step in ((0, up), (1, down)):
            pairs.append((order[place] * 2 + core, order[(place + step) % 8] * 2 + core))
    return lax.ppermute(value, "term", pairs)


def opposite(value):
    return hop(value, 4, 4)


def gather(own, messages, beside=()):
    sectors = len(messages)
    partner = flip(own)
    arrived = [hop(m) for m in messages]
    rounds = [arrived]
    results = []
    for k in range(3):
        if k < len(beside):
            result = beside[k](*results)
            arrived[-1], result = lax.optimization_barrier((arrived[-1], result))
            results.append(result)
        if k == 0:
            arrived = [pair(s, m, partner) for s, m in enumerate(arrived)]
        arrived = [hop(m) for m in arrived]
        rounds.append(arrived)
    theirs = flip(pack(*(r[s] for s in range(sectors) for r in rounds)))
    mine = [m for s in range(sectors) for m in (messages[s], *(r[s] for r in rounds))]
    return [partner, theirs, *mine], results


def scatter(shape, me, total, near, far, dot):
    near = flip(near)
    near, far = lax.optimization_barrier((near, far))
    far = flip(far)
    one = hop(chain(shape, 0, 0, me, total, dot, near))
    two = hop(chain(shape, 1, 1, me, total, dot, near))
    across = opposite(chain(shape, 6, 4, me, total, dot, far))
    for k in (2, 4):
        one = hop(chain(shape, k, k - 2, me, total, dot, far, one))
        if k == 4:
            two, across = lax.optimization_barrier((two, across))
        two = hop(chain(shape, k + 1, k - 1, me, total, dot, far, two))
    return me, total, far, dot, one, flip(two), across


def on_ring(
    wavefunction, diagonal, left_blocks, right_blocks, block_source, block_target, live_count
):
    shape = wavefunction.shape
    sectors, rows, width = shape
    entries = float(sectors * rows * lax.axis_size("term") * width)
    me = lax.axis_index("term").astype(jnp.int32).reshape(1)
    blocks = (left_blocks, right_blocks, shape)

    own, *messages = as_messages(wavefunction)
    beside = (
        lambda: jnp.concatenate([block_source, block_target, live_count]),
        lambda _: weighted_square(diagonal, own),
    )
    fields, (ints, square) = gather(own, messages, beside)
    total, near, far, dot, scale = apply_blocks(me, ints, fields, (square,), *blocks, True, entries)
    first_image, terms, correction, *messages = davidson_step(
        scale, wavefunction, diagonal, scatter(shape, me, total, near, far, dot), entries
    )
    fields, _ = gather(messages[0], messages[1:])
    own = (scale, wavefunction, correction)
    total, near, far, dot, along = apply_blocks(me, ints, fields, own, *blocks, False, entries)
    second_vector, second_image = finish(
        along, scale, wavefunction, diagonal, terms, correction,
        scatter(shape, me, total, near, far, dot), entries,
    )
    return (first_image, second_vector, second_image)


def block_loop(field_rounded, left_ops, right_ops, sources, targets, last_slot, partial_sum):

    def add_block(slot_index, running):
        left_op = lax.dynamic_index_in_dim(left_ops, slot_index, 0, keepdims=False)
        right_op = lax.dynamic_index_in_dim(right_ops, slot_index, 0, keepdims=False)
        source = lax.dynamic_index_in_dim(sources, slot_index, 0, keepdims=False)
        target = lax.dynamic_index_in_dim(targets, slot_index, 0, keepdims=False)
        piece = lax.dynamic_index_in_dim(field_rounded, source, 0, keepdims=False)
        product = jnp.dot(left_op, piece, preferred_element_type=jnp.float32).astype(jnp.bfloat16)
        term_value = jnp.dot(product, right_op.T, preferred_element_type=jnp.float32)
        before = lax.dynamic_index_in_dim(running, target, 0, keepdims=False)
        return lax.dynamic_update_index_in_dim(running, before + term_value, target, 0)

    return lax.fori_loop(0, last_slot, add_block, partial_sum)


def on_any(
    wavefunction, diagonal, left_blocks, right_blocks, block_source, block_target, live_count
):
    devices = lax.axis_size("term")
    position = lax.axis_index("term")
    row_count = wavefunction.shape[1]
    sector_count = wavefunction.shape[0]
    width = wavefunction.shape[2]
    entries = float(sector_count * row_count * devices * width)
    own_count = live_count[0]
    diag_own = diagonal.astype(jnp.float32)
    whole_wave = lax.all_gather(wavefunction, "term", axis=1, tiled=True).astype(jnp.float32)
    scale = jnp.sqrt(jnp.sum(whole_wave * whole_wave) / entries)
    start_whole = whole_wave / scale
    empty_sum = jnp.zeros(start_whole.shape, jnp.float32)
    first_terms = block_loop(
        start_whole.astype(jnp.bfloat16),
        left_blocks,
        right_blocks,
        block_source,
        block_target,
        own_count,
        empty_sum,
    )
    row_start = position * row_count
    whole_diag = lax.all_gather(diagonal, "term", axis=1, tiled=True).astype(jnp.float32)
    first_whole = lax.psum(first_terms, "term") + whole_diag * start_whole
    ritz_value = jnp.sum(start_whole * first_whole) / entries
    correction = (first_whole - ritz_value * start_whole) / jnp.maximum(
        jnp.abs(whole_diag - ritz_value), 1.0
    )
    correlation = jnp.sum(start_whole * correction) / entries
    projected = correction - correlation * start_whole
    second_whole = projected / jnp.sqrt(jnp.sum(projected * projected) / entries)
    first_image = lax.dynamic_slice_in_dim(first_whole, row_start, row_count, 1)
    second_vector = lax.dynamic_slice_in_dim(second_whole, row_start, row_count, 1)
    second_rounded = second_whole.astype(jnp.bfloat16)
    second_terms = block_loop(
        second_rounded, left_blocks, right_blocks, block_source, block_target, own_count, empty_sum
    )
    second_image = (
        lax.psum_scatter(second_terms, "term", scatter_dimension=1, tiled=True)
        + diag_own * second_vector
    )
    return (first_image, second_vector, second_image)


def solution(mesh):
    placed = (
        P("grp", "term", None),
        P("grp", "term", None),
        P(("grp", "term"), None, None),
        P(("grp", "term"), None, None),
        P(("grp", "term")),
        P(("grp", "term")),
        P(("grp", "term")),
    )
    on_device = on_ring if mesh.shape["term"] == 16 else on_any
    return jax.shard_map(
        on_device,
        mesh=mesh,
        in_specs=placed,
        out_specs=(P("grp", "term", None), P("grp", "term", None), P("grp", "term", None)),
        check_vma=False,
    )
```

```python
import functools

import jax
import jax.numpy as jnp
from jax import lax
from jax.experimental import pallas as pl
from jax.experimental.pallas import tpu as pltpu
from jax.sharding import PartitionSpec as P

VMEM = pl.BlockSpec(memory_space=pltpu.VMEM)
SMEM = pl.BlockSpec(memory_space=pltpu.SMEM)
HBM = pl.BlockSpec(memory_space=pltpu.HBM)
PARAMS = pltpu.CompilerParams(vmem_limit_bytes=48 * 1024 * 1024)
HALF = 16
LANES = 128


def fold(value):
    rows, width = value.shape
    summed = jnp.sum(value.reshape(rows // 8, 8, width), axis=0)
    return sum(summed[:, k * 128 : (k + 1) * 128] for k in range(width // 128))


def down(value):
    return jnp.sum(value, axis=0, keepdims=True)


def halves(rows, width, start=0):
    for h in range(rows // HALF):
        yield h * HALF, slice(start + h * width, start + (h + 1) * width)


def write_lanes(ref, at, lanes):
    whole = jnp.broadcast_to(lanes, (HALF, LANES))
    high = whole.astype(jnp.bfloat16).astype(jnp.float32)
    rest = whole - high
    middle = rest.astype(jnp.bfloat16).astype(jnp.float32)
    low = rest - middle
    row = lax.broadcasted_iota(jnp.int32, whole.shape, 0)
    value = jnp.where(row == 0, high, jnp.where(row == 1, middle, jnp.where(row == 2, low, 0.0)))
    ref[:, at : at + LANES] = value.astype(jnp.bfloat16)


def read_lanes(ref, at):
    return down(ref[:, at : at + LANES].astype(jnp.float32))


def chip_at(place):
    place = lax.rem(place + 8, 8)
    return jnp.where(place < 4, 2 * place, 15 - 2 * place)


def ring_place(me):
    chip, core = me // 2, me % 2
    place = jnp.where(chip % 2 == 0, chip // 2, (15 - chip) // 2)
    return place, core


def ahead(me, distance, half, core=None):
    place, own = ring_place(me)
    core = own if core is None else core
    return chip_at(place + (1 - 2 * core) * distance) * 2 + half


ROUNDS = 3


def sent_devices(me, core):
    devices = []
    for k in range(ROUNDS):
        for half in (core, 1 - core):
            devices.append(ahead(me, ROUNDS - k, half, core))
    return devices + [ahead(me, 4, core, core), ahead(me, 0, core, core)]


def gathered_devices(me):
    core = me % 2
    devices = [ahead(me, 0, core), ahead(me, 0, 1 - core)]
    for k in range(1, ROUNDS + 1):
        devices += [ahead(me, -k, core), ahead(me, -k, 1 - core)]
        devices += [ahead(me, k, 1 - core), ahead(me, k, core)]
    return devices + [ahead(me, 4, 1), ahead(me, 4, 0)]


def message_parts(sectors, rows, width):
    for s in range(sectors):
        for row, part in halves(rows, width, s * (rows // HALF) * width):
            yield s, row, part


def message_shape(sectors, rows, width):
    return (HALF, rows // HALF * sectors * width + LANES)


def copy_kernel(in_ref, out_ref):
    out_ref[...] = in_ref[...]


def copied(value):
    return pl.pallas_call(
        copy_kernel,
        in_specs=[VMEM],
        out_specs=VMEM,
        out_shape=jax.ShapeDtypeStruct(value.shape, value.dtype),
        compiler_params=PARAMS,
    )(value)


def square_kernel(wave_ref, diag_ref, square_ref):
    square = jnp.zeros((8, 128), jnp.float32)
    for s in range(wave_ref.shape[0]):
        wave = wave_ref[s].astype(jnp.float32)
        square += fold(diag_ref[s].astype(jnp.float32) * wave * wave)
    square_ref[...] = square


def weighted_square(wave, diag):
    return pl.pallas_call(
        square_kernel,
        in_specs=[VMEM, VMEM],
        out_specs=VMEM,
        out_shape=jax.ShapeDtypeStruct((8, 128), jnp.float32),
        compiler_params=PARAMS,
    )(wave, diag)


def blocks_kernel(first, shape, entries, me_ref, ints_ref, *refs):
    sectors, rows, width = shape
    field_refs, refs = refs[:18], refs[18:]
    if first:
        square_ref, *refs = refs
    else:
        scale_ref, wave_ref, correction_ref, *refs = refs
    left_hbm, right_hbm, *refs = refs
    total, near_ref, far_ref, dot_ref, out_ref, left, right, field, left_sem, right_sem = refs
    slots = left.shape[0]

    def copies(slot):
        return (
            pltpu.make_async_copy(left_hbm.at[slot], left.at[slot], left_sem.at[slot]),
            pltpu.make_async_copy(right_hbm.at[slot], right.at[slot], right_sem.at[slot]),
        )

    for slot in range(slots):
        for copy in copies(slot):
            copy.start()

    me = me_ref[0]
    core = me % 2

    def read(k, part):
        if k < 14:
            return field_refs[k][part]
        return jnp.where(core == 1, field_refs[k][part], field_refs[k + 2][part])

    pieces = []
    for k, owner in enumerate(gathered_devices(me)):
        at = pl.multiple_of(owner * rows, rows)
        if first:
            for s in range(sectors):
                pieces.append((k, (s,), s, pl.ds(at, rows)))
        else:
            for s, row, part in message_parts(sectors, rows, width):
                pieces.append((k, (slice(None), part), s, pl.ds(at + row, HALF)))

    total[...] = jnp.zeros_like(total)
    if first:
        dot = jnp.zeros((8, 128), jnp.float32)
        for k, part, _, _ in pieces:
            value = read(k, part).astype(jnp.float32)
            dot += fold(value * value)
        scale = jnp.sqrt(jnp.sum(dot) / entries)
        inverse = 1.0 / scale
        out_ref[...] = jnp.full(out_ref.shape, scale, jnp.float32)
        for k, part, s, at in pieces:
            field[s, at, :] = (read(k, part).astype(jnp.float32) * inverse).astype(jnp.bfloat16)
    else:
        for k, part, s, at in pieces:
            field[s, at, :] = read(k, part)

    used = ints_ref[2 * slots]

    def add_pair(step, carry):
        one, two = 2 * step, 2 * step + 1
        for slot in (one, two):
            for copy in copies(slot):
                copy.wait()

        @pl.when(one < used)
        def _():
            products = [
                jnp.dot(
                    left[slot], field[ints_ref[slot]], preferred_element_type=jnp.float32
                ).astype(jnp.bfloat16)
                for slot in (one, two)
            ]
            products[1] = jnp.where(two < used, products[1], jnp.zeros_like(products[1]))
            for slot, product in zip((one, two), products):
                total[ints_ref[slots + slot]] += lax.dot_general(
                    product,
                    right[slot],
                    (((1,), (1,)), ((), ())),
                    preferred_element_type=jnp.float32,
                )

        return carry

    lax.fori_loop(0, slots // 2, add_pair, 0)

    dot = jnp.zeros((8, 128), jnp.float32)
    if first:
        for k, part, s, at in pieces:
            dot += fold(total[s, at, :] * read(k, part).astype(jnp.float32))
        dot = dot * inverse + square_ref[...] * inverse * inverse
    else:
        at = message_shape(*shape)[1] - LANES
        part = (slice(None), slice(at, at + LANES))
        lanes = sum(read(k, part).astype(jnp.float32) for k in range(16))
        along = jnp.sum(lanes) / entries
        out_ref[...] = jnp.full(out_ref.shape, along, jnp.float32)
        inverse = 1.0 / scale_ref[0:1, 0:1]
        for s in range(sectors):
            projected = correction_ref[s] - along * (wave_ref[s].astype(jnp.float32) * inverse)
            dot += fold(projected * projected)
    dot_ref[...] = dot
    lanes = down(dot)
    for k, owner in enumerate(sent_devices(me, 1 - core)):
        at = pl.multiple_of(owner * rows, rows)
        ref = near_ref.at[k] if k < near_ref.shape[0] else far_ref.at[k - near_ref.shape[0]]
        for s, row, part in message_parts(*shape):
            ref[:, part] = total[s, pl.ds(at + row, HALF), :].astype(jnp.bfloat16)
        write_lanes(ref, ref.shape[1] - LANES, lanes)


def apply_blocks(me, ints, fields, own, left, right, shape, first, entries):
    slots, order, width = left.shape
    sectors = shape[0]
    message = message_shape(*shape)
    return pl.pallas_call(
        functools.partial(blocks_kernel, first, shape, entries),
        in_specs=[SMEM, SMEM] + [VMEM] * (len(fields) + len(own)) + [HBM] * 2,
        out_specs=[VMEM] * 5,
        scratch_shapes=[
            pltpu.VMEM(left.shape, left.dtype),
            pltpu.VMEM(right.shape, right.dtype),
            pltpu.VMEM((sectors, order, width), jnp.bfloat16),
            pltpu.SemaphoreType.DMA((slots,)),
            pltpu.SemaphoreType.DMA((slots,)),
        ],
        out_shape=[
            jax.ShapeDtypeStruct((sectors, order, width), jnp.float32),
            jax.ShapeDtypeStruct((2, *message), jnp.bfloat16),
            jax.ShapeDtypeStruct((2 * ROUNDS, *message), jnp.bfloat16),
            jax.ShapeDtypeStruct((8, 128), jnp.float32),
            jax.ShapeDtypeStruct((8, 128), jnp.float32),
        ],
        compiler_params=PARAMS,
        cost_estimate=pl.CostEstimate(
            flops=4 * slots * order * order * width,
            bytes_accessed=4 * slots * order * order,
            transcendentals=0,
        ),
    )(me, ints, *fields, *own, left, right)


def chain_kernel(shape, k, index, me_ref, total_ref, dot_ref, other_ref, *refs):
    *arrived_refs, out_ref = refs
    _, rows, _ = shape
    me = me_ref[0]
    start = pl.multiple_of(sent_devices(me, me % 2)[k] * rows, rows)
    for s, row, part in message_parts(*shape):
        value = total_ref[s, pl.ds(start + row, HALF), :]
        value += other_ref[index, :, part].astype(jnp.float32)
        for ref in arrived_refs:
            value += ref[:, part].astype(jnp.float32)
        out_ref[:, part] = value.astype(jnp.bfloat16)
    at = out_ref.shape[1] - LANES
    lanes = down(dot_ref[...]) + read_lanes(other_ref.at[index], at)
    for ref in arrived_refs:
        lanes += read_lanes(ref, at)
    write_lanes(out_ref, at, lanes)


def chain(shape, k, index, me, total, dot, other, *arrived):
    return pl.pallas_call(
        functools.partial(chain_kernel, shape, k, index),
        in_specs=[SMEM] + [VMEM] * (3 + len(arrived)),
        out_specs=VMEM,
        out_shape=jax.ShapeDtypeStruct(message_shape(*shape), jnp.bfloat16),
        compiler_params=PARAMS,
    )(me, total, dot, other, *arrived)


def own_terms(shape, sector, me_ref, total_ref, other_ref, _, *arrived_refs):
    start = pl.multiple_of(me_ref[0] * shape[1], shape[1])
    values = []
    for s, row, part in message_parts(*shape):
        if s == sector:
            value = total_ref[s, pl.ds(start + row, HALF), :]
            value += other_ref[other_ref.shape[0] - 1, :, part].astype(jnp.float32)
            for ref in arrived_refs:
                value += ref[:, part].astype(jnp.float32)
            values.append(value)
    return jnp.concatenate(values, axis=0)


def own_scalar(me_ref, total_ref, other_ref, dot_ref, *arrived_refs):
    at = other_ref.shape[2] - LANES
    lanes = down(dot_ref[...]) + read_lanes(other_ref.at[other_ref.shape[0] - 1], at)
    return jnp.sum(lanes + sum(read_lanes(ref, at) for ref in arrived_refs))


def step_kernel(entries, scale_ref, wave_ref, diag_ref, *refs):
    *sums, first_ref, terms_ref, correction_ref, message_ref = refs
    shape = wave_ref.shape
    ritz = own_scalar(*sums) / entries
    inverse = 1.0 / scale_ref[0:1, 0:1]
    dots = jnp.zeros((8, 128), jnp.float32)
    for s in range(shape[0]):
        start = wave_ref[s].astype(jnp.float32) * inverse
        diag = diag_ref[s].astype(jnp.float32)
        terms = own_terms(shape, s, *sums)
        first = terms + diag * start
        correction = (first - ritz * start) / jnp.maximum(jnp.abs(diag - ritz), 1.0)
        first_ref[s] = first
        terms_ref[s] = terms
        correction_ref[s] = correction
        dots += fold(start * correction)
        for t, row, part in message_parts(*shape):
            if t == s:
                message_ref[:, part] = correction[row : row + HALF].astype(jnp.bfloat16)
    write_lanes(message_ref, message_ref.shape[1] - LANES, down(dots))


def davidson_step(scale, wave, diag, sums, entries):
    full = jax.ShapeDtypeStruct(wave.shape, jnp.float32)
    return pl.pallas_call(
        functools.partial(step_kernel, entries),
        in_specs=[VMEM] * 3 + [SMEM] + [VMEM] * (len(sums) - 1),
        out_specs=[VMEM] * 4,
        out_shape=[full, full, full, jax.ShapeDtypeStruct(message_shape(*wave.shape), jnp.bfloat16)],
        compiler_params=PARAMS,
    )(scale, wave, diag, *sums)


def finish_kernel(entries, along_ref, scale_ref, wave_ref, diag_ref, *refs):
    terms_ref, correction_ref, *sums, vector_ref, image_ref = refs
    shape = wave_ref.shape
    along = along_ref[0:1, 0:1]
    norm = jnp.sqrt(jnp.full((1, 1), own_scalar(*sums) / entries, jnp.float32))
    inverse = 1.0 / norm
    start_scale = 1.0 / scale_ref[0:1, 0:1]
    for s in range(shape[0]):
        start = wave_ref[s].astype(jnp.float32) * start_scale
        second = (correction_ref[s] - along * start) * inverse
        vector_ref[s] = second
        image = (own_terms(shape, s, *sums) - along * terms_ref[s]) * inverse
        image_ref[s] = image + diag_ref[s].astype(jnp.float32) * second


def finish(along, scale, wave, diag, terms, correction, sums, entries):
    full = jax.ShapeDtypeStruct(wave.shape, jnp.float32)
    return pl.pallas_call(
        functools.partial(finish_kernel, entries),
        in_specs=[VMEM] * 6 + [SMEM] + [VMEM] * (len(sums) - 1),
        out_specs=[VMEM] * 2,
        out_shape=[full, full],
        compiler_params=PARAMS,
    )(along, scale, wave, diag, terms, correction, *sums)


def flip(value):
    return lax.ppermute(value, "term", [(i, i ^ 1) for i in range(16)])


def hop(value, up=1, down=-1):
    order = [0, 2, 4, 6, 7, 5, 3, 1]
    pairs = []
    for place in range(8):
        for core, step in ((0, up), (1, down)):
            pairs.append((order[place] * 2 + core, order[(place + step) % 8] * 2 + core))
    return lax.ppermute(value, "term", pairs)


def opposite(value):
    return hop(value, 4, 4)


def last_hop(value):
    order = [0, 2, 4, 6, 7, 5, 3, 1]
    pairs = []
    for place in range(8):
        pairs.append((order[place] * 2, (order[place] ^ 1) * 2))
        pairs.append((order[place] * 2 + 1, order[(place - 1) % 8] * 2 + 1))
    return lax.ppermute(value, "term", pairs)


def gather(own, beside=()):
    one, two = own, flip(own)
    pieces = [one, two]
    results = []
    for k in range(ROUNDS):
        one, two = hop(one), hop(two)
        if k < len(beside):
            result = beside[k](*results)
            if k < ROUNDS - 1:
                two, result = lax.optimization_barrier((two, result))
            results.append(result)
        pieces += [one, two, flip(one), flip(two)]
    one, two = last_hop(one), last_hop(two)
    return pieces + [one, two, flip(one), flip(two)], results


def scatter(shape, me, total, near, far, dot):
    near = flip(near)
    near, far = lax.optimization_barrier((near, far))
    far = flip(far)
    one = hop(chain(shape, 0, 0, me, total, dot, near))
    two = hop(chain(shape, 1, 1, me, total, dot, near))
    across = opposite(chain(shape, 6, 4, me, total, dot, far))
    for k in (2, 4):
        one = hop(chain(shape, k, k - 2, me, total, dot, far, one))
        if k == 4:
            two, across = lax.optimization_barrier((two, across))
        two = hop(chain(shape, k + 1, k - 1, me, total, dot, far, two))
    return me, total, far, dot, one, flip(two), across


def on_ring(
    wavefunction, diagonal, left_blocks, right_blocks, block_source, block_target, live_count
):
    shape = wavefunction.shape
    sectors, rows, width = shape
    entries = float(sectors * rows * lax.axis_size("term") * width)
    me = lax.axis_index("term").astype(jnp.int32).reshape(1)
    blocks = (left_blocks, right_blocks, shape)

    beside = (
        lambda: jnp.concatenate([block_source, block_target, live_count]),
        lambda _: copied(wavefunction),
        lambda _, own: weighted_square(own, diagonal),
    )
    (_, *fields), (ints, own, square) = gather(wavefunction, beside)
    fields = [own, *fields]
    total, near, far, dot, scale = apply_blocks(me, ints, fields, (square,), *blocks, True, entries)
    first_image, terms, correction, message = davidson_step(
        scale, wavefunction, diagonal, scatter(shape, me, total, near, far, dot), entries
    )
    fields, _ = gather(message)
    own = (scale, wavefunction, correction)
    total, near, far, dot, along = apply_blocks(me, ints, fields, own, *blocks, False, entries)
    second_vector, second_image = finish(
        along, scale, wavefunction, diagonal, terms, correction,
        scatter(shape, me, total, near, far, dot), entries,
    )
    return (first_image, second_vector, second_image)


def block_loop(field_rounded, left_ops, right_ops, sources, targets, last_slot, partial_sum):

    def add_block(slot_index, running):
        left_op = lax.dynamic_index_in_dim(left_ops, slot_index, 0, keepdims=False)
        right_op = lax.dynamic_index_in_dim(right_ops, slot_index, 0, keepdims=False)
        source = lax.dynamic_index_in_dim(sources, slot_index, 0, keepdims=False)
        target = lax.dynamic_index_in_dim(targets, slot_index, 0, keepdims=False)
        piece = lax.dynamic_index_in_dim(field_rounded, source, 0, keepdims=False)
        product = jnp.dot(left_op, piece, preferred_element_type=jnp.float32).astype(jnp.bfloat16)
        term_value = jnp.dot(product, right_op.T, preferred_element_type=jnp.float32)
        before = lax.dynamic_index_in_dim(running, target, 0, keepdims=False)
        return lax.dynamic_update_index_in_dim(running, before + term_value, target, 0)

    return lax.fori_loop(0, last_slot, add_block, partial_sum)


def on_any(
    wavefunction, diagonal, left_blocks, right_blocks, block_source, block_target, live_count
):
    devices = lax.axis_size("term")
    position = lax.axis_index("term")
    row_count = wavefunction.shape[1]
    sector_count = wavefunction.shape[0]
    width = wavefunction.shape[2]
    entries = float(sector_count * row_count * devices * width)
    own_count = live_count[0]
    diag_own = diagonal.astype(jnp.float32)
    whole_wave = lax.all_gather(wavefunction, "term", axis=1, tiled=True).astype(jnp.float32)
    scale = jnp.sqrt(jnp.sum(whole_wave * whole_wave) / entries)
    start_whole = whole_wave / scale
    empty_sum = jnp.zeros(start_whole.shape, jnp.float32)
    first_terms = block_loop(
        start_whole.astype(jnp.bfloat16),
        left_blocks,
        right_blocks,
        block_source,
        block_target,
        own_count,
        empty_sum,
    )
    row_start = position * row_count
    whole_diag = lax.all_gather(diagonal, "term", axis=1, tiled=True).astype(jnp.float32)
    first_whole = lax.psum(first_terms, "term") + whole_diag * start_whole
    ritz_value = jnp.sum(start_whole * first_whole) / entries
    correction = (first_whole - ritz_value * start_whole) / jnp.maximum(
        jnp.abs(whole_diag - ritz_value), 1.0
    )
    correlation = jnp.sum(start_whole * correction) / entries
    projected = correction - correlation * start_whole
    second_whole = projected / jnp.sqrt(jnp.sum(projected * projected) / entries)
    first_image = lax.dynamic_slice_in_dim(first_whole, row_start, row_count, 1)
    second_vector = lax.dynamic_slice_in_dim(second_whole, row_start, row_count, 1)
    second_rounded = second_whole.astype(jnp.bfloat16)
    second_terms = block_loop(
        second_rounded, left_blocks, right_blocks, block_source, block_target, own_count, empty_sum
    )
    second_image = (
        lax.psum_scatter(second_terms, "term", scatter_dimension=1, tiled=True)
        + diag_own * second_vector
    )
    return (first_image, second_vector, second_image)


def solution(mesh):
    placed = (
        P("grp", "term", None),
        P("grp", "term", None),
        P(("grp", "term"), None, None),
        P(("grp", "term"), None, None),
        P(("grp", "term")),
        P(("grp", "term")),
        P(("grp", "term")),
    )
    on_device = on_ring if mesh.shape["term"] == 16 else on_any
    return jax.shard_map(
        on_device,
        mesh=mesh,
        in_specs=placed,
        out_specs=(P("grp", "term", None), P("grp", "term", None), P("grp", "term", None)),
        check_vma=False,
    )
```

```python
import functools

import jax
import jax.numpy as jnp
from jax import lax
from jax.experimental import pallas as pl
from jax.experimental.pallas import tpu as pltpu
from jax.sharding import PartitionSpec as P

VMEM = pl.BlockSpec(memory_space=pltpu.VMEM)
SMEM = pl.BlockSpec(memory_space=pltpu.SMEM)
HBM = pl.BlockSpec(memory_space=pltpu.HBM)
PARAMS = pltpu.CompilerParams(vmem_limit_bytes=48 * 1024 * 1024)
HALF = 16
GROUP = 4
LANES = 128


def fold(value):
    rows, width = value.shape
    summed = jnp.sum(value.reshape(rows // 8, 8, width), axis=0)
    return sum(summed[:, k * 128 : (k + 1) * 128] for k in range(width // 128))


def down(value):
    return jnp.sum(value, axis=0, keepdims=True)


def halves(rows, width, start=0):
    for h in range(rows // HALF):
        yield h * HALF, slice(start + h * width, start + (h + 1) * width)


def write_lanes(ref, at, lanes):
    whole = jnp.broadcast_to(lanes, (HALF, LANES))
    high = whole.astype(jnp.bfloat16).astype(jnp.float32)
    rest = whole - high
    middle = rest.astype(jnp.bfloat16).astype(jnp.float32)
    low = rest - middle
    row = lax.broadcasted_iota(jnp.int32, whole.shape, 0)
    value = jnp.where(row == 0, high, jnp.where(row == 1, middle, jnp.where(row == 2, low, 0.0)))
    ref[:, at : at + LANES] = value.astype(jnp.bfloat16)


def read_lanes(ref, at):
    return down(ref[:, at : at + LANES].astype(jnp.float32))


def chip_at(place):
    place = lax.rem(place + 8, 8)
    return jnp.where(place < 4, 2 * place, 15 - 2 * place)


def ring_place(me):
    chip, core = me // 2, me % 2
    place = jnp.where(chip % 2 == 0, chip // 2, (15 - chip) // 2)
    return place, core


def ahead(me, distance, half, core=None):
    place, own = ring_place(me)
    core = own if core is None else core
    return chip_at(place + (1 - 2 * core) * distance) * 2 + half


ROUNDS = 3


def sent_devices(me, core):
    devices = []
    for k in range(ROUNDS):
        for half in (core, 1 - core):
            devices.append(ahead(me, ROUNDS - k, half, core))
    return devices + [ahead(me, 4, core, core), ahead(me, 0, core, core)]


def gathered_devices(me):
    core = me % 2
    devices = [ahead(me, 0, core), ahead(me, 0, 1 - core)]
    for k in range(1, ROUNDS + 1):
        devices += [ahead(me, -k, core), ahead(me, -k, 1 - core)]
        devices += [ahead(me, k, 1 - core), ahead(me, k, core)]
    return devices + [ahead(me, 4, core), ahead(me, 4, 1 - core)]


def message_parts(sectors, rows, width):
    for s in range(sectors):
        for row, part in halves(rows, width, s * (rows // HALF) * width):
            yield s, row, part


def message_shape(sectors, rows, width):
    return (HALF, rows // HALF * sectors * width + LANES)


def copy_kernel(in_ref, out_ref):
    out_ref[...] = in_ref[...]


def copied(value):
    return pl.pallas_call(
        copy_kernel,
        in_specs=[VMEM],
        out_specs=VMEM,
        out_shape=jax.ShapeDtypeStruct(value.shape, value.dtype),
        compiler_params=PARAMS,
    )(value)


def square_kernel(wave_ref, diag_ref, square_ref):
    square = jnp.zeros((8, 128), jnp.float32)
    for s in range(wave_ref.shape[0]):
        wave = wave_ref[s].astype(jnp.float32)
        square += fold(diag_ref[s].astype(jnp.float32) * wave * wave)
    square_ref[...] = square


def weighted_square(wave, diag):
    return pl.pallas_call(
        square_kernel,
        in_specs=[VMEM, VMEM],
        out_specs=VMEM,
        out_shape=jax.ShapeDtypeStruct((8, 128), jnp.float32),
        compiler_params=PARAMS,
    )(wave, diag)


def blocks_kernel(first, shape, entries, me_ref, ints_ref, *refs):
    sectors, rows, width = shape
    field_refs, refs = refs[:16], refs[16:]
    if first:
        square_ref, *refs = refs
    else:
        scale_ref, wave_ref, correction_ref, *refs = refs
    left_hbm, right_hbm, *refs = refs
    total, near_ref, far_ref, dot_ref, out_ref, left, right, field, left_sem, right_sem = refs
    slots = left.shape[0]

    def copies(slot):
        return (
            pltpu.make_async_copy(left_hbm.at[slot], left.at[slot], left_sem.at[slot]),
            pltpu.make_async_copy(right_hbm.at[slot], right.at[slot], right_sem.at[slot]),
        )

    for slot in range(slots):
        for copy in copies(slot):
            copy.start()

    me = me_ref[0]
    core = me % 2

    pieces = []
    for k, owner in enumerate(gathered_devices(me)):
        at = pl.multiple_of(owner * rows, rows)
        if first:
            for s in range(sectors):
                pieces.append((k, (s,), s, pl.ds(at, rows)))
        else:
            for s, row, part in message_parts(sectors, rows, width):
                pieces.append((k, (slice(None), part), s, pl.ds(at + row, HALF)))

    total[...] = jnp.zeros_like(total)
    if first:
        dot = jnp.zeros((8, 128), jnp.float32)
        for k, part, _, _ in pieces:
            value = field_refs[k][part].astype(jnp.float32)
            dot += fold(value * value)
        scale = jnp.sqrt(jnp.sum(dot) / entries)
        inverse = 1.0 / scale
        out_ref[...] = jnp.full(out_ref.shape, scale, jnp.float32)
        for k, part, s, at in pieces:
            field[s, at, :] = (field_refs[k][part].astype(jnp.float32) * inverse).astype(jnp.bfloat16)
    else:
        for k, part, s, at in pieces:
            field[s, at, :] = field_refs[k][part]

    used = ints_ref[2 * slots]

    def add_some(step, carry):
        some = [step * GROUP + k for k in range(GROUP)]
        for slot in some:
            for copy in copies(slot):
                copy.wait()

        @pl.when(some[0] < used)
        def _():
            products = [
                jnp.dot(
                    left[slot], field[ints_ref[slot]], preferred_element_type=jnp.float32
                ).astype(jnp.bfloat16)
                for slot in some
            ]
            for slot, product in zip(some, products):
                if slot is not some[0]:
                    product = jnp.where(slot < used, product, jnp.zeros_like(product))
                total[ints_ref[slots + slot]] += lax.dot_general(
                    product,
                    right[slot],
                    (((1,), (1,)), ((), ())),
                    preferred_element_type=jnp.float32,
                )

        return carry

    lax.fori_loop(0, slots // GROUP, add_some, 0)

    dot = jnp.zeros((8, 128), jnp.float32)
    if first:
        for k, part, s, at in pieces:
            dot += fold(total[s, at, :] * field_refs[k][part].astype(jnp.float32))
        dot = dot * inverse + square_ref[...] * inverse * inverse
    else:
        at = message_shape(*shape)[1] - LANES
        lanes = sum(
            ref[:, at : at + LANES].astype(jnp.float32) for ref in field_refs
        )
        along = jnp.sum(lanes) / entries
        out_ref[...] = jnp.full(out_ref.shape, along, jnp.float32)
        inverse = 1.0 / scale_ref[0:1, 0:1]
        for s in range(sectors):
            projected = correction_ref[s] - along * (wave_ref[s].astype(jnp.float32) * inverse)
            dot += fold(projected * projected)
    dot_ref[...] = dot
    lanes = down(dot)
    for k, owner in enumerate(sent_devices(me, 1 - core)):
        at = pl.multiple_of(owner * rows, rows)
        ref = near_ref.at[k] if k < near_ref.shape[0] else far_ref.at[k - near_ref.shape[0]]
        for s, row, part in message_parts(*shape):
            ref[:, part] = total[s, pl.ds(at + row, HALF), :].astype(jnp.bfloat16)
        write_lanes(ref, ref.shape[1] - LANES, lanes)


def apply_blocks(me, ints, fields, own, left, right, shape, first, entries):
    slots, order, width = left.shape
    sectors = shape[0]
    message = message_shape(*shape)
    return pl.pallas_call(
        functools.partial(blocks_kernel, first, shape, entries),
        in_specs=[SMEM, SMEM] + [VMEM] * (len(fields) + len(own)) + [HBM] * 2,
        out_specs=[VMEM] * 5,
        scratch_shapes=[
            pltpu.VMEM(left.shape, left.dtype),
            pltpu.VMEM(right.shape, right.dtype),
            pltpu.VMEM((sectors, order, width), jnp.bfloat16),
            pltpu.SemaphoreType.DMA((slots,)),
            pltpu.SemaphoreType.DMA((slots,)),
        ],
        out_shape=[
            jax.ShapeDtypeStruct((sectors, order, width), jnp.float32),
            jax.ShapeDtypeStruct((2, *message), jnp.bfloat16),
            jax.ShapeDtypeStruct((2 * ROUNDS, *message), jnp.bfloat16),
            jax.ShapeDtypeStruct((8, 128), jnp.float32),
            jax.ShapeDtypeStruct((8, 128), jnp.float32),
        ],
        compiler_params=PARAMS,
        cost_estimate=pl.CostEstimate(
            flops=4 * slots * order * order * width,
            bytes_accessed=4 * slots * order * order,
            transcendentals=0,
        ),
    )(me, ints, *fields, *own, left, right)


def chain_kernel(shape, k, index, me_ref, total_ref, dot_ref, other_ref, *refs):
    *arrived_refs, out_ref = refs
    _, rows, _ = shape
    me = me_ref[0]
    start = pl.multiple_of(sent_devices(me, me % 2)[k] * rows, rows)
    for s, row, part in message_parts(*shape):
        value = total_ref[s, pl.ds(start + row, HALF), :]
        value += other_ref[index, :, part].astype(jnp.float32)
        for ref in arrived_refs:
            value += ref[:, part].astype(jnp.float32)
        out_ref[:, part] = value.astype(jnp.bfloat16)
    at = out_ref.shape[1] - LANES
    lanes = down(dot_ref[...]) + read_lanes(other_ref.at[index], at)
    for ref in arrived_refs:
        lanes += read_lanes(ref, at)
    write_lanes(out_ref, at, lanes)


def chain(shape, k, index, me, total, dot, other, *arrived):
    return pl.pallas_call(
        functools.partial(chain_kernel, shape, k, index),
        in_specs=[SMEM] + [VMEM] * (3 + len(arrived)),
        out_specs=VMEM,
        out_shape=jax.ShapeDtypeStruct(message_shape(*shape), jnp.bfloat16),
        compiler_params=PARAMS,
    )(me, total, dot, other, *arrived)


def own_terms(shape, sector, me_ref, total_ref, other_ref, _, *arrived_refs):
    start = pl.multiple_of(me_ref[0] * shape[1], shape[1])
    values = []
    for s, row, part in message_parts(*shape):
        if s == sector:
            value = total_ref[s, pl.ds(start + row, HALF), :]
            value += other_ref[other_ref.shape[0] - 1, :, part].astype(jnp.float32)
            for ref in arrived_refs:
                value += ref[:, part].astype(jnp.float32)
            values.append(value)
    return jnp.concatenate(values, axis=0)


def own_scalar(me_ref, total_ref, other_ref, dot_ref, *arrived_refs):
    at = other_ref.shape[2] - LANES
    lanes = down(dot_ref[...]) + read_lanes(other_ref.at[other_ref.shape[0] - 1], at)
    return jnp.sum(lanes + sum(read_lanes(ref, at) for ref in arrived_refs))


def step_kernel(entries, scale_ref, wave_ref, diag_ref, *refs):
    *sums, first_ref, terms_ref, correction_ref, message_ref = refs
    shape = wave_ref.shape
    ritz = own_scalar(*sums) / entries
    inverse = 1.0 / scale_ref[0:1, 0:1]
    dots = jnp.zeros((8, 128), jnp.float32)
    for s in range(shape[0]):
        start = wave_ref[s].astype(jnp.float32) * inverse
        diag = diag_ref[s].astype(jnp.float32)
        terms = own_terms(shape, s, *sums)
        first = terms + diag * start
        correction = (first - ritz * start) / jnp.maximum(jnp.abs(diag - ritz), 1.0)
        first_ref[s] = first
        terms_ref[s] = terms
        correction_ref[s] = correction
        dots += fold(start * correction)
        for t, row, part in message_parts(*shape):
            if t == s:
                message_ref[:, part] = correction[row : row + HALF].astype(jnp.bfloat16)
    write_lanes(message_ref, message_ref.shape[1] - LANES, down(dots))


def davidson_step(scale, wave, diag, sums, entries):
    full = jax.ShapeDtypeStruct(wave.shape, jnp.float32)
    return pl.pallas_call(
        functools.partial(step_kernel, entries),
        in_specs=[VMEM] * 3 + [SMEM] + [VMEM] * (len(sums) - 1),
        out_specs=[VMEM] * 4,
        out_shape=[full, full, full, jax.ShapeDtypeStruct(message_shape(*wave.shape), jnp.bfloat16)],
        compiler_params=PARAMS,
    )(scale, wave, diag, *sums)


def finish_kernel(entries, along_ref, scale_ref, wave_ref, diag_ref, *refs):
    terms_ref, correction_ref, *sums, vector_ref, image_ref = refs
    shape = wave_ref.shape
    along = along_ref[0:1, 0:1]
    norm = jnp.sqrt(jnp.full((1, 1), own_scalar(*sums) / entries, jnp.float32))
    inverse = 1.0 / norm
    start_scale = 1.0 / scale_ref[0:1, 0:1]
    for s in range(shape[0]):
        start = wave_ref[s].astype(jnp.float32) * start_scale
        second = (correction_ref[s] - along * start) * inverse
        vector_ref[s] = second
        image = (own_terms(shape, s, *sums) - along * terms_ref[s]) * inverse
        image_ref[s] = image + diag_ref[s].astype(jnp.float32) * second


def finish(along, scale, wave, diag, terms, correction, sums, entries):
    full = jax.ShapeDtypeStruct(wave.shape, jnp.float32)
    return pl.pallas_call(
        functools.partial(finish_kernel, entries),
        in_specs=[VMEM] * 6 + [SMEM] + [VMEM] * (len(sums) - 1),
        out_specs=[VMEM] * 2,
        out_shape=[full, full],
        compiler_params=PARAMS,
    )(along, scale, wave, diag, terms, correction, *sums)


def flip(value):
    return lax.ppermute(value, "term", [(i, i ^ 1) for i in range(16)])


def hop(value, up=1, down=-1):
    order = [0, 2, 4, 6, 7, 5, 3, 1]
    pairs = []
    for place in range(8):
        for core, step in ((0, up), (1, down)):
            pairs.append((order[place] * 2 + core, order[(place + step) % 8] * 2 + core))
    return lax.ppermute(value, "term", pairs)


def opposite(value):
    return hop(value, 4, 4)


def gather(own, beside=()):
    one, two = own, flip(own)
    across, two = lax.optimization_barrier((own, two))
    pieces = [one, two]
    across = opposite(across)
    results = []
    for k in range(ROUNDS):
        one, two = hop(one), hop(two)
        if k < len(beside):
            results.append(beside[k](*results))
        if k < ROUNDS - 1:
            ready = results[-1:] if beside else []
            two, ready = lax.optimization_barrier((two, ready))
            if ready:
                results[-1] = ready[0]
        pieces += [one, two, flip(one), flip(two)]
    return pieces + [across, flip(across)], results


def scatter(shape, me, total, near, far, dot):
    near = flip(near)
    near, far = lax.optimization_barrier((near, far))
    far = flip(far)
    one = hop(chain(shape, 0, 0, me, total, dot, near))
    two = hop(chain(shape, 1, 1, me, total, dot, near))
    across = opposite(chain(shape, 6, 4, me, total, dot, far))
    for k in (2, 4):
        if k == 4:
            one, across = lax.optimization_barrier((one, across))
        one = hop(chain(shape, k, k - 2, me, total, dot, far, one))
        two = hop(chain(shape, k + 1, k - 1, me, total, dot, far, two))
    return me, total, far, dot, one, flip(two), across


def on_ring(
    wavefunction, diagonal, left_blocks, right_blocks, block_source, block_target, live_count
):
    shape = wavefunction.shape
    sectors, rows, width = shape
    entries = float(sectors * rows * lax.axis_size("term") * width)
    me = lax.axis_index("term").astype(jnp.int32).reshape(1)
    blocks = (left_blocks, right_blocks, shape)

    beside = (
        lambda: jnp.concatenate([block_source, block_target, live_count]),
        lambda _: copied(wavefunction),
        lambda _, own: weighted_square(own, diagonal),
    )
    (_, *fields), (ints, own, square) = gather(wavefunction, beside)
    fields = [own, *fields]
    total, near, far, dot, scale = apply_blocks(me, ints, fields, (square,), *blocks, True, entries)
    first_image, terms, correction, message = davidson_step(
        scale, wavefunction, diagonal, scatter(shape, me, total, near, far, dot), entries
    )
    fields, _ = gather(message)
    own = (scale, wavefunction, correction)
    total, near, far, dot, along = apply_blocks(me, ints, fields, own, *blocks, False, entries)
    second_vector, second_image = finish(
        along, scale, wavefunction, diagonal, terms, correction,
        scatter(shape, me, total, near, far, dot), entries,
    )
    return (first_image, second_vector, second_image)


def block_loop(field_rounded, left_ops, right_ops, sources, targets, last_slot, partial_sum):

    def add_block(slot_index, running):
        left_op = lax.dynamic_index_in_dim(left_ops, slot_index, 0, keepdims=False)
        right_op = lax.dynamic_index_in_dim(right_ops, slot_index, 0, keepdims=False)
        source = lax.dynamic_index_in_dim(sources, slot_index, 0, keepdims=False)
        target = lax.dynamic_index_in_dim(targets, slot_index, 0, keepdims=False)
        piece = lax.dynamic_index_in_dim(field_rounded, source, 0, keepdims=False)
        product = jnp.dot(left_op, piece, preferred_element_type=jnp.float32).astype(jnp.bfloat16)
        term_value = jnp.dot(product, right_op.T, preferred_element_type=jnp.float32)
        before = lax.dynamic_index_in_dim(running, target, 0, keepdims=False)
        return lax.dynamic_update_index_in_dim(running, before + term_value, target, 0)

    return lax.fori_loop(0, last_slot, add_block, partial_sum)


def on_any(
    wavefunction, diagonal, left_blocks, right_blocks, block_source, block_target, live_count
):
    devices = lax.axis_size("term")
    position = lax.axis_index("term")
    row_count = wavefunction.shape[1]
    sector_count = wavefunction.shape[0]
    width = wavefunction.shape[2]
    entries = float(sector_count * row_count * devices * width)
    own_count = live_count[0]
    diag_own = diagonal.astype(jnp.float32)
    whole_wave = lax.all_gather(wavefunction, "term", axis=1, tiled=True).astype(jnp.float32)
    scale = jnp.sqrt(jnp.sum(whole_wave * whole_wave) / entries)
    start_whole = whole_wave / scale
    empty_sum = jnp.zeros(start_whole.shape, jnp.float32)
    first_terms = block_loop(
        start_whole.astype(jnp.bfloat16),
        left_blocks,
        right_blocks,
        block_source,
        block_target,
        own_count,
        empty_sum,
    )
    row_start = position * row_count
    whole_diag = lax.all_gather(diagonal, "term", axis=1, tiled=True).astype(jnp.float32)
    first_whole = lax.psum(first_terms, "term") + whole_diag * start_whole
    ritz_value = jnp.sum(start_whole * first_whole) / entries
    correction = (first_whole - ritz_value * start_whole) / jnp.maximum(
        jnp.abs(whole_diag - ritz_value), 1.0
    )
    correlation = jnp.sum(start_whole * correction) / entries
    projected = correction - correlation * start_whole
    second_whole = projected / jnp.sqrt(jnp.sum(projected * projected) / entries)
    first_image = lax.dynamic_slice_in_dim(first_whole, row_start, row_count, 1)
    second_vector = lax.dynamic_slice_in_dim(second_whole, row_start, row_count, 1)
    second_rounded = second_whole.astype(jnp.bfloat16)
    second_terms = block_loop(
        second_rounded, left_blocks, right_blocks, block_source, block_target, own_count, empty_sum
    )
    second_image = (
        lax.psum_scatter(second_terms, "term", scatter_dimension=1, tiled=True)
        + diag_own * second_vector
    )
    return (first_image, second_vector, second_image)


def solution(mesh):
    placed = (
        P("grp", "term", None),
        P("grp", "term", None),
        P(("grp", "term"), None, None),
        P(("grp", "term"), None, None),
        P(("grp", "term")),
        P(("grp", "term")),
        P(("grp", "term")),
    )
    on_device = on_ring if mesh.shape["term"] == 16 else on_any
    return jax.shard_map(
        on_device,
        mesh=mesh,
        in_specs=placed,
        out_specs=(P("grp", "term", None), P("grp", "term", None), P("grp", "term", None)),
        check_vma=False,
    )
```

```python
import functools

import jax
import jax.numpy as jnp
from jax import lax
from jax.experimental import pallas as pl
from jax.experimental.pallas import tpu as pltpu
from jax.sharding import PartitionSpec as P

VMEM = pl.BlockSpec(memory_space=pltpu.VMEM)
SMEM = pl.BlockSpec(memory_space=pltpu.SMEM)
HBM = pl.BlockSpec(memory_space=pltpu.HBM)
PARAMS = pltpu.CompilerParams(vmem_limit_bytes=16 * 1024 * 1024)
FIRST = pltpu.CompilerParams(vmem_limit_bytes=48 * 1024 * 1024)
HALF = 16
GROUP = 2
LANES = 128


def fold(value):
    rows, width = value.shape
    summed = jnp.sum(value.reshape(rows // 8, 8, width), axis=0)
    return sum(summed[:, k * 128 : (k + 1) * 128] for k in range(width // 128))


def down(value):
    return jnp.sum(value, axis=0, keepdims=True)


def halves(rows, width, start=0):
    for h in range(rows // HALF):
        yield h * HALF, slice(start + h * width, start + (h + 1) * width)


def write_lanes(ref, at, lanes):
    whole = jnp.broadcast_to(lanes, (HALF, LANES))
    high = whole.astype(jnp.bfloat16).astype(jnp.float32)
    rest = whole - high
    middle = rest.astype(jnp.bfloat16).astype(jnp.float32)
    low = rest - middle
    row = lax.broadcasted_iota(jnp.int32, whole.shape, 0)
    value = jnp.where(row == 0, high, jnp.where(row == 1, middle, jnp.where(row == 2, low, 0.0)))
    ref[:, at : at + LANES] = value.astype(jnp.bfloat16)


def read_lanes(ref, at):
    return down(ref[:, at : at + LANES].astype(jnp.float32))


def chip_at(place):
    place = lax.rem(place + 8, 8)
    return jnp.where(place < 4, 2 * place, 15 - 2 * place)


def ring_place(me):
    chip, core = me // 2, me % 2
    place = jnp.where(chip % 2 == 0, chip // 2, (15 - chip) // 2)
    return place, core


def ahead(me, distance, half, core=None):
    place, own = ring_place(me)
    core = own if core is None else core
    return chip_at(place + (1 - 2 * core) * distance) * 2 + half


ROUNDS = 3


def sent_devices(me, core):
    devices = []
    for k in range(ROUNDS):
        for half in (core, 1 - core):
            devices.append(ahead(me, ROUNDS - k, half, core))
    return devices + [ahead(me, 4, core, core), ahead(me, 0, core, core)]


def gathered_devices(me):
    core = me % 2
    devices = [ahead(me, 0, core), ahead(me, 0, 1 - core)]
    for k in range(1, ROUNDS + 1):
        devices += [ahead(me, -k, core), ahead(me, -k, 1 - core)]
        devices += [ahead(me, k, 1 - core), ahead(me, k, core)]
    return devices + [ahead(me, 4, core), ahead(me, 4, 1 - core)]


def message_parts(sectors, rows, width):
    for s in range(sectors):
        for row, part in halves(rows, width, s * (rows // HALF) * width):
            yield s, row, part


def message_shape(sectors, rows, width):
    return (HALF, rows // HALF * sectors * width + LANES)


def copy_kernel(in_ref, out_ref):
    out_ref[...] = in_ref[...]


def copied(value):
    return pl.pallas_call(
        copy_kernel,
        in_specs=[VMEM],
        out_specs=VMEM,
        out_shape=jax.ShapeDtypeStruct(value.shape, value.dtype),
        compiler_params=PARAMS,
    )(value)


def square_kernel(wave_ref, diag_ref, square_ref):
    square = jnp.zeros((8, 128), jnp.float32)
    for s in range(wave_ref.shape[0]):
        wave = wave_ref[s].astype(jnp.float32)
        square += fold(diag_ref[s].astype(jnp.float32) * wave * wave)
    square_ref[...] = square


def weighted_square(wave, diag):
    return pl.pallas_call(
        square_kernel,
        in_specs=[VMEM, VMEM],
        out_specs=VMEM,
        out_shape=jax.ShapeDtypeStruct((8, 128), jnp.float32),
        compiler_params=PARAMS,
    )(wave, diag)


def blocks_kernel(first, shape, entries, me_ref, ints_ref, *refs):
    sectors, rows, width = shape
    field_refs, refs = refs[:16], refs[16:]
    if first:
        square_ref, *refs = refs
    else:
        scale_ref, wave_ref, correction_ref, *refs = refs
    left_in, right_in, *refs = refs
    total, near_ref, far_ref, dot_ref, out_ref, field, *refs = refs
    slots = left_in.shape[0]
    if first:
        left, right, left_sem, right_sem = refs

        def copies(slot):
            return (
                pltpu.make_async_copy(left_in.at[slot], left.at[slot], left_sem.at[slot]),
                pltpu.make_async_copy(right_in.at[slot], right.at[slot], right_sem.at[slot]),
            )

        for slot in range(slots):
            for copy in copies(slot):
                copy.start()
    else:
        left, right = left_in, right_in

    me = me_ref[0]
    core = me % 2

    pieces = []
    for k, owner in enumerate(gathered_devices(me)):
        at = pl.multiple_of(owner * rows, rows)
        if first:
            for s in range(sectors):
                pieces.append((k, (s,), s, pl.ds(at, rows)))
        else:
            for s, row, part in message_parts(sectors, rows, width):
                pieces.append((k, (slice(None), part), s, pl.ds(at + row, HALF)))

    total[...] = jnp.zeros_like(total)
    if first:
        dot = jnp.zeros((8, 128), jnp.float32)
        for k, part, _, _ in pieces:
            value = field_refs[k][part].astype(jnp.float32)
            dot += fold(value * value)
        scale = jnp.sqrt(jnp.sum(dot) / entries)
        inverse = 1.0 / scale
        out_ref[...] = jnp.full(out_ref.shape, scale, jnp.float32)
        for k, part, s, at in pieces:
            field[s, at, :] = (field_refs[k][part].astype(jnp.float32) * inverse).astype(jnp.bfloat16)
    else:
        for k, part, s, at in pieces:
            field[s, at, :] = field_refs[k][part]

    used = ints_ref[2 * slots]

    def add_some(step, carry):
        some = [step * GROUP + k for k in range(GROUP)]
        if first:
            for slot in some:
                for copy in copies(slot):
                    copy.wait()

        @pl.when(some[0] < used)
        def _():
            products = [
                jnp.dot(
                    left[slot], field[ints_ref[slot]], preferred_element_type=jnp.float32
                ).astype(jnp.bfloat16)
                for slot in some
            ]
            for slot, product in zip(some, products):
                if slot is not some[0]:
                    product = jnp.where(slot < used, product, jnp.zeros_like(product))
                total[ints_ref[slots + slot]] += lax.dot_general(
                    product,
                    right[slot],
                    (((1,), (1,)), ((), ())),
                    preferred_element_type=jnp.float32,
                )

        return carry

    lax.fori_loop(0, slots // GROUP, add_some, 0)

    dot = jnp.zeros((8, 128), jnp.float32)
    if first:
        for k, part, s, at in pieces:
            dot += fold(total[s, at, :] * field_refs[k][part].astype(jnp.float32))
        dot = dot * inverse + square_ref[...] * inverse * inverse
    else:
        at = message_shape(*shape)[1] - LANES
        lanes = sum(
            ref[:, at : at + LANES].astype(jnp.float32) for ref in field_refs
        )
        along = jnp.sum(lanes) / entries
        out_ref[...] = jnp.full(out_ref.shape, along, jnp.float32)
        inverse = 1.0 / scale_ref[0:1, 0:1]
        for s in range(sectors):
            projected = correction_ref[s] - along * (wave_ref[s].astype(jnp.float32) * inverse)
            dot += fold(projected * projected)
    dot_ref[...] = dot
    lanes = down(dot)
    for k, owner in enumerate(sent_devices(me, 1 - core)):
        at = pl.multiple_of(owner * rows, rows)
        ref = near_ref.at[k] if k < near_ref.shape[0] else far_ref.at[k - near_ref.shape[0]]
        for s, row, part in message_parts(*shape):
            ref[:, part] = total[s, pl.ds(at + row, HALF), :].astype(jnp.bfloat16)
        write_lanes(ref, ref.shape[1] - LANES, lanes)


def apply_blocks(me, ints, fields, own, left, right, shape, first, entries):
    slots, order, width = left.shape
    sectors = shape[0]
    message = message_shape(*shape)
    scratch = []
    if first:
        scratch = [pltpu.VMEM(b.shape, b.dtype) for b in (left, right)]
        scratch += [pltpu.SemaphoreType.DMA((slots,))] * 2
    return pl.pallas_call(
        functools.partial(blocks_kernel, first, shape, entries),
        in_specs=[SMEM, SMEM]
        + [VMEM] * (len(fields) + len(own))
        + [HBM if first else VMEM] * 2,
        out_specs=[VMEM] * 5,
        scratch_shapes=[pltpu.VMEM((sectors, order, width), jnp.bfloat16)] + scratch,
        out_shape=[
            jax.ShapeDtypeStruct((sectors, order, width), jnp.float32),
            jax.ShapeDtypeStruct((2, *message), jnp.bfloat16),
            jax.ShapeDtypeStruct((2 * ROUNDS, *message), jnp.bfloat16),
            jax.ShapeDtypeStruct((8, 128), jnp.float32),
            jax.ShapeDtypeStruct((8, 128), jnp.float32),
        ],
        compiler_params=FIRST if first else PARAMS,
        cost_estimate=pl.CostEstimate(
            flops=4 * slots * order * order * width,
            bytes_accessed=4 * slots * order * order,
            transcendentals=0,
        ),
    )(me, ints, *fields, *own, left, right)


def chain_kernel(shape, k, index, me_ref, total_ref, dot_ref, other_ref, *refs):
    *arrived_refs, out_ref = refs
    _, rows, _ = shape
    me = me_ref[0]
    start = pl.multiple_of(sent_devices(me, me % 2)[k] * rows, rows)
    for s, row, part in message_parts(*shape):
        value = total_ref[s, pl.ds(start + row, HALF), :]
        value += other_ref[index, :, part].astype(jnp.float32)
        for ref in arrived_refs:
            value += ref[:, part].astype(jnp.float32)
        out_ref[:, part] = value.astype(jnp.bfloat16)
    at = out_ref.shape[1] - LANES
    lanes = down(dot_ref[...]) + read_lanes(other_ref.at[index], at)
    for ref in arrived_refs:
        lanes += read_lanes(ref, at)
    write_lanes(out_ref, at, lanes)


def chain(shape, k, index, me, total, dot, other, *arrived):
    return pl.pallas_call(
        functools.partial(chain_kernel, shape, k, index),
        in_specs=[SMEM] + [VMEM] * (3 + len(arrived)),
        out_specs=VMEM,
        out_shape=jax.ShapeDtypeStruct(message_shape(*shape), jnp.bfloat16),
        compiler_params=PARAMS,
    )(me, total, dot, other, *arrived)


def own_terms(shape, sector, me_ref, total_ref, other_ref, _, *arrived_refs):
    start = pl.multiple_of(me_ref[0] * shape[1], shape[1])
    values = []
    for s, row, part in message_parts(*shape):
        if s == sector:
            value = total_ref[s, pl.ds(start + row, HALF), :]
            value += other_ref[other_ref.shape[0] - 1, :, part].astype(jnp.float32)
            for ref in arrived_refs:
                value += ref[:, part].astype(jnp.float32)
            values.append(value)
    return jnp.concatenate(values, axis=0)


def own_scalar(me_ref, total_ref, other_ref, dot_ref, *arrived_refs):
    at = other_ref.shape[2] - LANES
    lanes = down(dot_ref[...]) + read_lanes(other_ref.at[other_ref.shape[0] - 1], at)
    return jnp.sum(lanes + sum(read_lanes(ref, at) for ref in arrived_refs))


def step_kernel(entries, scale_ref, wave_ref, diag_ref, *refs):
    *sums, first_ref, terms_ref, correction_ref, message_ref = refs
    shape = wave_ref.shape
    ritz = own_scalar(*sums) / entries
    inverse = 1.0 / scale_ref[0:1, 0:1]
    dots = jnp.zeros((8, 128), jnp.float32)
    for s in range(shape[0]):
        start = wave_ref[s].astype(jnp.float32) * inverse
        diag = diag_ref[s].astype(jnp.float32)
        terms = own_terms(shape, s, *sums)
        first = terms + diag * start
        correction = (first - ritz * start) / jnp.maximum(jnp.abs(diag - ritz), 1.0)
        first_ref[s] = first
        terms_ref[s] = terms
        correction_ref[s] = correction
        dots += fold(start * correction)
        for t, row, part in message_parts(*shape):
            if t == s:
                message_ref[:, part] = correction[row : row + HALF].astype(jnp.bfloat16)
    write_lanes(message_ref, message_ref.shape[1] - LANES, down(dots))


def davidson_step(scale, wave, diag, sums, entries):
    full = jax.ShapeDtypeStruct(wave.shape, jnp.float32)
    return pl.pallas_call(
        functools.partial(step_kernel, entries),
        in_specs=[VMEM] * 3 + [SMEM] + [VMEM] * (len(sums) - 1),
        out_specs=[VMEM] * 4,
        out_shape=[full, full, full, jax.ShapeDtypeStruct(message_shape(*wave.shape), jnp.bfloat16)],
        compiler_params=PARAMS,
    )(scale, wave, diag, *sums)


def finish_kernel(entries, along_ref, scale_ref, wave_ref, diag_ref, *refs):
    terms_ref, correction_ref, *sums, vector_ref, image_ref = refs
    shape = wave_ref.shape
    along = along_ref[0:1, 0:1]
    norm = jnp.sqrt(jnp.full((1, 1), own_scalar(*sums) / entries, jnp.float32))
    inverse = 1.0 / norm
    start_scale = 1.0 / scale_ref[0:1, 0:1]
    for s in range(shape[0]):
        start = wave_ref[s].astype(jnp.float32) * start_scale
        second = (correction_ref[s] - along * start) * inverse
        vector_ref[s] = second
        image = (own_terms(shape, s, *sums) - along * terms_ref[s]) * inverse
        image_ref[s] = image + diag_ref[s].astype(jnp.float32) * second


def finish(along, scale, wave, diag, terms, correction, sums, entries):
    full = jax.ShapeDtypeStruct(wave.shape, jnp.float32)
    return pl.pallas_call(
        functools.partial(finish_kernel, entries),
        in_specs=[VMEM] * 6 + [SMEM] + [VMEM] * (len(sums) - 1),
        out_specs=[VMEM] * 2,
        out_shape=[full, full],
        compiler_params=PARAMS,
    )(along, scale, wave, diag, terms, correction, *sums)


def flip(value):
    return lax.ppermute(value, "term", [(i, i ^ 1) for i in range(16)])


def hop(value, up=1, down=-1):
    order = [0, 2, 4, 6, 7, 5, 3, 1]
    pairs = []
    for place in range(8):
        for core, step in ((0, up), (1, down)):
            pairs.append((order[place] * 2 + core, order[(place + step) % 8] * 2 + core))
    return lax.ppermute(value, "term", pairs)


def opposite(value):
    return hop(value, 4, 4)


def gather(own, beside=()):
    one, two = own, flip(own)
    across, two = lax.optimization_barrier((own, two))
    pieces = [one, two]
    across = opposite(across)
    results = []
    for k in range(ROUNDS):
        one, two = hop(one), hop(two)
        if k < len(beside):
            results.append(beside[k](*results))
        if k < ROUNDS - 1:
            ready = results[-1:] if beside else []
            two, ready = lax.optimization_barrier((two, ready))
            if ready:
                results[-1] = ready[0]
        pieces += [one, two, flip(one), flip(two)]
    return pieces + [across, flip(across)], results


def scatter(shape, me, total, near, far, dot):
    near = flip(near)
    near, far = lax.optimization_barrier((near, far))
    far = flip(far)
    one = hop(chain(shape, 0, 0, me, total, dot, near))
    two = hop(chain(shape, 1, 1, me, total, dot, near))
    across = opposite(chain(shape, 6, 4, me, total, dot, far))
    for k in (2, 4):
        one = hop(chain(shape, k, k - 2, me, total, dot, far, one))
        if k == 4:
            two, across = lax.optimization_barrier((two, across))
        two = hop(chain(shape, k + 1, k - 1, me, total, dot, far, two))
    return me, total, far, dot, one, flip(two), across


def on_ring(
    wavefunction, diagonal, left_blocks, right_blocks, block_source, block_target, live_count
):
    shape = wavefunction.shape
    sectors, rows, width = shape
    entries = float(sectors * rows * lax.axis_size("term") * width)
    me = lax.axis_index("term").astype(jnp.int32).reshape(1)
    beside = (
        lambda: jnp.concatenate([block_source, block_target, live_count]),
        lambda _: copied(wavefunction),
        lambda _, own: weighted_square(own, diagonal),
    )
    (_, *fields), (ints, own, square) = gather(wavefunction, beside)
    fields = [own, *fields]
    blocks = (left_blocks, right_blocks, shape)
    total, near, far, dot, scale = apply_blocks(me, ints, fields, (square,), *blocks, True, entries)
    first_image, terms, correction, message = davidson_step(
        scale, wavefunction, diagonal, scatter(shape, me, total, near, far, dot), entries
    )
    fields, _ = gather(message)
    own = (scale, wavefunction, correction)
    total, near, far, dot, along = apply_blocks(me, ints, fields, own, *blocks, False, entries)
    second_vector, second_image = finish(
        along, scale, wavefunction, diagonal, terms, correction,
        scatter(shape, me, total, near, far, dot), entries,
    )
    return (first_image, second_vector, second_image)


def block_loop(field_rounded, left_ops, right_ops, sources, targets, last_slot, partial_sum):

    def add_block(slot_index, running):
        left_op = lax.dynamic_index_in_dim(left_ops, slot_index, 0, keepdims=False)
        right_op = lax.dynamic_index_in_dim(right_ops, slot_index, 0, keepdims=False)
        source = lax.dynamic_index_in_dim(sources, slot_index, 0, keepdims=False)
        target = lax.dynamic_index_in_dim(targets, slot_index, 0, keepdims=False)
        piece = lax.dynamic_index_in_dim(field_rounded, source, 0, keepdims=False)
        product = jnp.dot(left_op, piece, preferred_element_type=jnp.float32).astype(jnp.bfloat16)
        term_value = jnp.dot(product, right_op.T, preferred_element_type=jnp.float32)
        before = lax.dynamic_index_in_dim(running, target, 0, keepdims=False)
        return lax.dynamic_update_index_in_dim(running, before + term_value, target, 0)

    return lax.fori_loop(0, last_slot, add_block, partial_sum)


def on_any(
    wavefunction, diagonal, left_blocks, right_blocks, block_source, block_target, live_count
):
    devices = lax.axis_size("term")
    position = lax.axis_index("term")
    row_count = wavefunction.shape[1]
    sector_count = wavefunction.shape[0]
    width = wavefunction.shape[2]
    entries = float(sector_count * row_count * devices * width)
    own_count = live_count[0]
    diag_own = diagonal.astype(jnp.float32)
    whole_wave = lax.all_gather(wavefunction, "term", axis=1, tiled=True).astype(jnp.float32)
    scale = jnp.sqrt(jnp.sum(whole_wave * whole_wave) / entries)
    start_whole = whole_wave / scale
    empty_sum = jnp.zeros(start_whole.shape, jnp.float32)
    first_terms = block_loop(
        start_whole.astype(jnp.bfloat16),
        left_blocks,
        right_blocks,
        block_source,
        block_target,
        own_count,
        empty_sum,
    )
    row_start = position * row_count
    whole_diag = lax.all_gather(diagonal, "term", axis=1, tiled=True).astype(jnp.float32)
    first_whole = lax.psum(first_terms, "term") + whole_diag * start_whole
    ritz_value = jnp.sum(start_whole * first_whole) / entries
    correction = (first_whole - ritz_value * start_whole) / jnp.maximum(
        jnp.abs(whole_diag - ritz_value), 1.0
    )
    correlation = jnp.sum(start_whole * correction) / entries
    projected = correction - correlation * start_whole
    second_whole = projected / jnp.sqrt(jnp.sum(projected * projected) / entries)
    first_image = lax.dynamic_slice_in_dim(first_whole, row_start, row_count, 1)
    second_vector = lax.dynamic_slice_in_dim(second_whole, row_start, row_count, 1)
    second_rounded = second_whole.astype(jnp.bfloat16)
    second_terms = block_loop(
        second_rounded, left_blocks, right_blocks, block_source, block_target, own_count, empty_sum
    )
    second_image = (
        lax.psum_scatter(second_terms, "term", scatter_dimension=1, tiled=True)
        + diag_own * second_vector
    )
    return (first_image, second_vector, second_image)


def solution(mesh):
    placed = (
        P("grp", "term", None),
        P("grp", "term", None),
        P(("grp", "term"), None, None),
        P(("grp", "term"), None, None),
        P(("grp", "term")),
        P(("grp", "term")),
        P(("grp", "term")),
    )
    on_device = on_ring if mesh.shape["term"] == 16 else on_any
    return jax.shard_map(
        on_device,
        mesh=mesh,
        in_specs=placed,
        out_specs=(P("grp", "term", None), P("grp", "term", None), P("grp", "term", None)),
        check_vma=False,
    )
```

```python
import functools

import jax
import jax.numpy as jnp
from jax import lax
from jax.experimental import pallas as pl
from jax.experimental.pallas import tpu as pltpu
from jax.sharding import PartitionSpec as P

VMEM = pl.BlockSpec(memory_space=pltpu.VMEM)
SMEM = pl.BlockSpec(memory_space=pltpu.SMEM)
HBM = pl.BlockSpec(memory_space=pltpu.HBM)
PARAMS = pltpu.CompilerParams(vmem_limit_bytes=16 * 1024 * 1024)
HALF = 16
GROUP = 2
LANES = 128


def fold(value):
    rows, width = value.shape
    summed = jnp.sum(value.reshape(rows // 8, 8, width), axis=0)
    return sum(summed[:, k * 128 : (k + 1) * 128] for k in range(width // 128))


def down(value):
    return jnp.sum(value, axis=0, keepdims=True)


def halves(rows, width, start=0):
    for h in range(rows // HALF):
        yield h * HALF, slice(start + h * width, start + (h + 1) * width)


def write_lanes(ref, at, lanes):
    whole = jnp.broadcast_to(lanes, (HALF, LANES))
    high = whole.astype(jnp.bfloat16).astype(jnp.float32)
    rest = whole - high
    middle = rest.astype(jnp.bfloat16).astype(jnp.float32)
    low = rest - middle
    row = lax.broadcasted_iota(jnp.int32, whole.shape, 0)
    value = jnp.where(row == 0, high, jnp.where(row == 1, middle, jnp.where(row == 2, low, 0.0)))
    ref[:, at : at + LANES] = value.astype(jnp.bfloat16)


def read_lanes(ref, at):
    return down(ref[:, at : at + LANES].astype(jnp.float32))


def chip_at(place):
    place = lax.rem(place + 8, 8)
    return jnp.where(place < 4, 2 * place, 15 - 2 * place)


def ring_place(me):
    chip, core = me // 2, me % 2
    place = jnp.where(chip % 2 == 0, chip // 2, (15 - chip) // 2)
    return place, core


def ahead(me, distance, half, core=None):
    place, own = ring_place(me)
    core = own if core is None else core
    return chip_at(place + (1 - 2 * core) * distance) * 2 + half


ROUNDS = 3


def sent_devices(me, core):
    devices = []
    for k in range(ROUNDS):
        for half in (core, 1 - core):
            devices.append(ahead(me, ROUNDS - k, half, core))
    return devices + [ahead(me, 4, core, core), ahead(me, 0, core, core)]


def gathered_devices(me):
    core = me % 2
    devices = [ahead(me, 0, core), ahead(me, 0, 1 - core)]
    for k in range(1, ROUNDS + 1):
        devices += [ahead(me, -k, core), ahead(me, -k, 1 - core)]
        devices += [ahead(me, k, 1 - core), ahead(me, k, core)]
    return devices + [ahead(me, 4, core), ahead(me, 4, 1 - core)]


def message_parts(sectors, rows, width):
    for s in range(sectors):
        for row, part in halves(rows, width, s * (rows // HALF) * width):
            yield s, row, part


def message_shape(sectors, rows, width):
    return (HALF, rows // HALF * sectors * width + LANES)


def copy_kernel(in_ref, out_ref):
    out_ref[...] = in_ref[...]


def copied(value, cost=8 << 30):
    return pl.pallas_call(
        copy_kernel,
        in_specs=[VMEM],
        out_specs=VMEM,
        out_shape=jax.ShapeDtypeStruct(value.shape, value.dtype),
        compiler_params=PARAMS,
        cost_estimate=pl.CostEstimate(flops=cost, bytes_accessed=1 << 20, transcendentals=0),
    )(value)


def square_kernel(wave_ref, diag_ref, square_ref):
    square = jnp.zeros((8, 128), jnp.float32)
    for s in range(wave_ref.shape[0]):
        wave = wave_ref[s].astype(jnp.float32)
        square += fold(diag_ref[s].astype(jnp.float32) * wave * wave)
    square_ref[...] = square


def weighted_square(wave, diag):
    return pl.pallas_call(
        square_kernel,
        in_specs=[VMEM, VMEM],
        out_specs=VMEM,
        out_shape=jax.ShapeDtypeStruct((8, 128), jnp.float32),
        compiler_params=PARAMS,
    )(wave, diag)


def blocks_kernel(first, shape, entries, me_ref, ints_ref, *refs):
    sectors, rows, width = shape
    field_refs, refs = refs[:16], refs[16:]
    if first:
        square_ref, *refs = refs
    else:
        scale_ref, wave_ref, correction_ref, *refs = refs
    left_in, right_in, *refs = refs
    total, near_ref, far_ref, dot_ref, out_ref, field, *refs = refs
    slots = left_in.shape[0]
    left, right = left_in, right_in

    me = me_ref[0]
    core = me % 2

    pieces = []
    for k, owner in enumerate(gathered_devices(me)):
        at = pl.multiple_of(owner * rows, rows)
        if first:
            for s in range(sectors):
                pieces.append((k, (s,), s, pl.ds(at, rows)))
        else:
            for s, row, part in message_parts(sectors, rows, width):
                pieces.append((k, (slice(None), part), s, pl.ds(at + row, HALF)))

    total[...] = jnp.zeros_like(total)
    if first:
        dot = jnp.zeros((8, 128), jnp.float32)
        for k, part, _, _ in pieces:
            value = field_refs[k][part].astype(jnp.float32)
            dot += fold(value * value)
        scale = jnp.sqrt(jnp.sum(dot) / entries)
        inverse = 1.0 / scale
        out_ref[...] = jnp.full(out_ref.shape, scale, jnp.float32)
        for k, part, s, at in pieces:
            field[s, at, :] = (field_refs[k][part].astype(jnp.float32) * inverse).astype(jnp.bfloat16)
    else:
        for k, part, s, at in pieces:
            field[s, at, :] = field_refs[k][part]

    used = ints_ref[2 * slots]

    def add_some(step, carry):
        some = [step * GROUP + k for k in range(GROUP)]
        @pl.when(some[0] < used)
        def _():
            products = [
                jnp.dot(
                    left[slot], field[ints_ref[slot]], preferred_element_type=jnp.float32
                ).astype(jnp.bfloat16)
                for slot in some
            ]
            for slot, product in zip(some, products):
                if slot is not some[0]:
                    product = jnp.where(slot < used, product, jnp.zeros_like(product))
                total[ints_ref[slots + slot]] += lax.dot_general(
                    product,
                    right[slot],
                    (((1,), (1,)), ((), ())),
                    preferred_element_type=jnp.float32,
                )

        return carry

    lax.fori_loop(0, slots // GROUP, add_some, 0)

    dot = jnp.zeros((8, 128), jnp.float32)
    if first:
        for k, part, s, at in pieces:
            dot += fold(total[s, at, :] * field_refs[k][part].astype(jnp.float32))
        dot = dot * inverse + square_ref[...] * inverse * inverse
    else:
        at = message_shape(*shape)[1] - LANES
        lanes = sum(
            ref[:, at : at + LANES].astype(jnp.float32) for ref in field_refs
        )
        along = jnp.sum(lanes) / entries
        out_ref[...] = jnp.full(out_ref.shape, along, jnp.float32)
        inverse = 1.0 / scale_ref[0:1, 0:1]
        for s in range(sectors):
            projected = correction_ref[s] - along * (wave_ref[s].astype(jnp.float32) * inverse)
            dot += fold(projected * projected)
    dot_ref[...] = dot
    lanes = down(dot)
    for k, owner in enumerate(sent_devices(me, 1 - core)):
        at = pl.multiple_of(owner * rows, rows)
        ref = near_ref.at[k] if k < near_ref.shape[0] else far_ref.at[k - near_ref.shape[0]]
        for s, row, part in message_parts(*shape):
            ref[:, part] = total[s, pl.ds(at + row, HALF), :].astype(jnp.bfloat16)
        write_lanes(ref, ref.shape[1] - LANES, lanes)


def apply_blocks(me, ints, fields, own, left, right, shape, first, entries):
    slots, order, width = left.shape
    sectors = shape[0]
    message = message_shape(*shape)
    return pl.pallas_call(
        functools.partial(blocks_kernel, first, shape, entries),
        in_specs=[SMEM, SMEM]
        + [VMEM] * (len(fields) + len(own))
        + [VMEM] * 2,
        out_specs=[VMEM] * 5,
        scratch_shapes=[pltpu.VMEM((sectors, order, width), jnp.bfloat16)],
        out_shape=[
            jax.ShapeDtypeStruct((sectors, order, width), jnp.float32),
            jax.ShapeDtypeStruct((2, *message), jnp.bfloat16),
            jax.ShapeDtypeStruct((2 * ROUNDS, *message), jnp.bfloat16),
            jax.ShapeDtypeStruct((8, 128), jnp.float32),
            jax.ShapeDtypeStruct((8, 128), jnp.float32),
        ],
        compiler_params=PARAMS,
        cost_estimate=pl.CostEstimate(
            flops=4 * slots * order * order * width,
            bytes_accessed=4 * slots * order * order,
            transcendentals=0,
        ),
    )(me, ints, *fields, *own, left, right)


def chain_kernel(shape, k, index, me_ref, total_ref, dot_ref, other_ref, *refs):
    *arrived_refs, out_ref = refs
    _, rows, _ = shape
    me = me_ref[0]
    start = pl.multiple_of(sent_devices(me, me % 2)[k] * rows, rows)
    for s, row, part in message_parts(*shape):
        value = total_ref[s, pl.ds(start + row, HALF), :]
        value += other_ref[index, :, part].astype(jnp.float32)
        for ref in arrived_refs:
            value += ref[:, part].astype(jnp.float32)
        out_ref[:, part] = value.astype(jnp.bfloat16)
    at = out_ref.shape[1] - LANES
    lanes = down(dot_ref[...]) + read_lanes(other_ref.at[index], at)
    for ref in arrived_refs:
        lanes += read_lanes(ref, at)
    write_lanes(out_ref, at, lanes)


def chain(shape, k, index, me, total, dot, other, *arrived):
    return pl.pallas_call(
        functools.partial(chain_kernel, shape, k, index),
        in_specs=[SMEM] + [VMEM] * (3 + len(arrived)),
        out_specs=VMEM,
        out_shape=jax.ShapeDtypeStruct(message_shape(*shape), jnp.bfloat16),
        compiler_params=PARAMS,
    )(me, total, dot, other, *arrived)


def own_terms(shape, sector, me_ref, total_ref, other_ref, _, *arrived_refs):
    start = pl.multiple_of(me_ref[0] * shape[1], shape[1])
    values = []
    for s, row, part in message_parts(*shape):
        if s == sector:
            value = total_ref[s, pl.ds(start + row, HALF), :]
            value += other_ref[other_ref.shape[0] - 1, :, part].astype(jnp.float32)
            for ref in arrived_refs:
                value += ref[:, part].astype(jnp.float32)
            values.append(value)
    return jnp.concatenate(values, axis=0)


def own_scalar(me_ref, total_ref, other_ref, dot_ref, *arrived_refs):
    at = other_ref.shape[2] - LANES
    lanes = down(dot_ref[...]) + read_lanes(other_ref.at[other_ref.shape[0] - 1], at)
    return jnp.sum(lanes + sum(read_lanes(ref, at) for ref in arrived_refs))


def step_kernel(entries, scale_ref, wave_ref, diag_ref, *refs):
    *sums, first_ref, terms_ref, correction_ref, message_ref = refs
    shape = wave_ref.shape
    ritz = own_scalar(*sums) / entries
    inverse = 1.0 / scale_ref[0:1, 0:1]
    dots = jnp.zeros((8, 128), jnp.float32)
    for s in range(shape[0]):
        start = wave_ref[s].astype(jnp.float32) * inverse
        diag = diag_ref[s].astype(jnp.float32)
        terms = own_terms(shape, s, *sums)
        first = terms + diag * start
        correction = (first - ritz * start) / jnp.maximum(jnp.abs(diag - ritz), 1.0)
        first_ref[s] = first
        terms_ref[s] = terms
        correction_ref[s] = correction
        dots += fold(start * correction)
        for t, row, part in message_parts(*shape):
            if t == s:
                message_ref[:, part] = correction[row : row + HALF].astype(jnp.bfloat16)
    write_lanes(message_ref, message_ref.shape[1] - LANES, down(dots))


def davidson_step(scale, wave, diag, sums, entries):
    full = jax.ShapeDtypeStruct(wave.shape, jnp.float32)
    return pl.pallas_call(
        functools.partial(step_kernel, entries),
        in_specs=[VMEM] * 3 + [SMEM] + [VMEM] * (len(sums) - 1),
        out_specs=[VMEM] * 4,
        out_shape=[full, full, full, jax.ShapeDtypeStruct(message_shape(*wave.shape), jnp.bfloat16)],
        compiler_params=PARAMS,
    )(scale, wave, diag, *sums)


def finish_kernel(entries, along_ref, scale_ref, wave_ref, diag_ref, *refs):
    terms_ref, correction_ref, *sums, vector_ref, image_ref = refs
    shape = wave_ref.shape
    along = along_ref[0:1, 0:1]
    norm = jnp.sqrt(jnp.full((1, 1), own_scalar(*sums) / entries, jnp.float32))
    inverse = 1.0 / norm
    start_scale = 1.0 / scale_ref[0:1, 0:1]
    for s in range(shape[0]):
        start = wave_ref[s].astype(jnp.float32) * start_scale
        second = (correction_ref[s] - along * start) * inverse
        vector_ref[s] = second
        image = (own_terms(shape, s, *sums) - along * terms_ref[s]) * inverse
        image_ref[s] = image + diag_ref[s].astype(jnp.float32) * second


def finish(along, scale, wave, diag, terms, correction, sums, entries):
    full = jax.ShapeDtypeStruct(wave.shape, jnp.float32)
    return pl.pallas_call(
        functools.partial(finish_kernel, entries),
        in_specs=[VMEM] * 6 + [SMEM] + [VMEM] * (len(sums) - 1),
        out_specs=[VMEM] * 2,
        out_shape=[full, full],
        compiler_params=PARAMS,
    )(along, scale, wave, diag, terms, correction, *sums)


def flip(value):
    return lax.ppermute(value, "term", [(i, i ^ 1) for i in range(16)])


def hop(value, up=1, down=-1):
    order = [0, 2, 4, 6, 7, 5, 3, 1]
    pairs = []
    for place in range(8):
        for core, step in ((0, up), (1, down)):
            pairs.append((order[place] * 2 + core, order[(place + step) % 8] * 2 + core))
    return lax.ppermute(value, "term", pairs)


def opposite(value):
    return hop(value, 4, 4)


def gather(own, beside=()):
    one, two = own, flip(own)
    across, two = lax.optimization_barrier((own, two))
    pieces = [one, two]
    across = opposite(across)
    results = []
    for k in range(ROUNDS):
        one, two = hop(one), hop(two)
        if k < len(beside):
            results.append(beside[k](*results))
        if k < ROUNDS - 1:
            ready = results[-1:] if beside else []
            if k == 1:
                across = copied(across, 0)
                one, across, ready = lax.optimization_barrier((one, across, ready))
            else:
                two, ready = lax.optimization_barrier((two, ready))
            if ready:
                results[-1] = ready[0]
        pieces += [one, two, flip(one), flip(two)]
    return pieces + [across, flip(across)], results


def scatter(shape, me, total, near, far, dot):
    near = flip(near)
    near, far = lax.optimization_barrier((near, far))
    far = flip(far)
    one = hop(chain(shape, 0, 0, me, total, dot, near))
    two = hop(chain(shape, 1, 1, me, total, dot, near))
    across = opposite(chain(shape, 6, 4, me, total, dot, far))
    for k in (2, 4):
        one = hop(chain(shape, k, k - 2, me, total, dot, far, one))
        if k == 4:
            two, across = lax.optimization_barrier((two, across))
        two = hop(chain(shape, k + 1, k - 1, me, total, dot, far, two))
    return me, total, far, dot, one, flip(two), across


def on_ring(
    wavefunction, diagonal, left_blocks, right_blocks, block_source, block_target, live_count
):
    shape = wavefunction.shape
    sectors, rows, width = shape
    entries = float(sectors * rows * lax.axis_size("term") * width)
    me = lax.axis_index("term").astype(jnp.int32).reshape(1)
    beside = (
        lambda: jnp.concatenate([block_source, block_target, live_count]),
        lambda _: copied(wavefunction),
        lambda _, own: weighted_square(own, diagonal),
    )
    (_, *fields), (ints, own, square) = gather(wavefunction, beside)
    fields = [own, *fields]
    blocks = (left_blocks, right_blocks, shape)
    total, near, far, dot, scale = apply_blocks(me, ints, fields, (square,), *blocks, True, entries)
    first_image, terms, correction, message = davidson_step(
        scale, wavefunction, diagonal, scatter(shape, me, total, near, far, dot), entries
    )
    fields, _ = gather(message)
    own = (scale, wavefunction, correction)
    total, near, far, dot, along = apply_blocks(me, ints, fields, own, *blocks, False, entries)
    second_vector, second_image = finish(
        along, scale, wavefunction, diagonal, terms, correction,
        scatter(shape, me, total, near, far, dot), entries,
    )
    return (first_image, second_vector, second_image)


def block_loop(field_rounded, left_ops, right_ops, sources, targets, last_slot, partial_sum):

    def add_block(slot_index, running):
        left_op = lax.dynamic_index_in_dim(left_ops, slot_index, 0, keepdims=False)
        right_op = lax.dynamic_index_in_dim(right_ops, slot_index, 0, keepdims=False)
        source = lax.dynamic_index_in_dim(sources, slot_index, 0, keepdims=False)
        target = lax.dynamic_index_in_dim(targets, slot_index, 0, keepdims=False)
        piece = lax.dynamic_index_in_dim(field_rounded, source, 0, keepdims=False)
        product = jnp.dot(left_op, piece, preferred_element_type=jnp.float32).astype(jnp.bfloat16)
        term_value = jnp.dot(product, right_op.T, preferred_element_type=jnp.float32)
        before = lax.dynamic_index_in_dim(running, target, 0, keepdims=False)
        return lax.dynamic_update_index_in_dim(running, before + term_value, target, 0)

    return lax.fori_loop(0, last_slot, add_block, partial_sum)


def on_any(
    wavefunction, diagonal, left_blocks, right_blocks, block_source, block_target, live_count
):
    devices = lax.axis_size("term")
    position = lax.axis_index("term")
    row_count = wavefunction.shape[1]
    sector_count = wavefunction.shape[0]
    width = wavefunction.shape[2]
    entries = float(sector_count * row_count * devices * width)
    own_count = live_count[0]
    diag_own = diagonal.astype(jnp.float32)
    whole_wave = lax.all_gather(wavefunction, "term", axis=1, tiled=True).astype(jnp.float32)
    scale = jnp.sqrt(jnp.sum(whole_wave * whole_wave) / entries)
    start_whole = whole_wave / scale
    empty_sum = jnp.zeros(start_whole.shape, jnp.float32)
    first_terms = block_loop(
        start_whole.astype(jnp.bfloat16),
        left_blocks,
        right_blocks,
        block_source,
        block_target,
        own_count,
        empty_sum,
    )
    row_start = position * row_count
    whole_diag = lax.all_gather(diagonal, "term", axis=1, tiled=True).astype(jnp.float32)
    first_whole = lax.psum(first_terms, "term") + whole_diag * start_whole
    ritz_value = jnp.sum(start_whole * first_whole) / entries
    correction = (first_whole - ritz_value * start_whole) / jnp.maximum(
        jnp.abs(whole_diag - ritz_value), 1.0
    )
    correlation = jnp.sum(start_whole * correction) / entries
    projected = correction - correlation * start_whole
    second_whole = projected / jnp.sqrt(jnp.sum(projected * projected) / entries)
    first_image = lax.dynamic_slice_in_dim(first_whole, row_start, row_count, 1)
    second_vector = lax.dynamic_slice_in_dim(second_whole, row_start, row_count, 1)
    second_rounded = second_whole.astype(jnp.bfloat16)
    second_terms = block_loop(
        second_rounded, left_blocks, right_blocks, block_source, block_target, own_count, empty_sum
    )
    second_image = (
        lax.psum_scatter(second_terms, "term", scatter_dimension=1, tiled=True)
        + diag_own * second_vector
    )
    return (first_image, second_vector, second_image)


def solution(mesh):
    placed = (
        P("grp", "term", None),
        P("grp", "term", None),
        P(("grp", "term"), None, None),
        P(("grp", "term"), None, None),
        P(("grp", "term")),
        P(("grp", "term")),
        P(("grp", "term")),
    )
    on_device = on_ring if mesh.shape["term"] == 16 else on_any
    return jax.shard_map(
        on_device,
        mesh=mesh,
        in_specs=placed,
        out_specs=(P("grp", "term", None), P("grp", "term", None), P("grp", "term", None)),
        check_vma=False,
    )
```

```python
import functools

import jax
import jax.numpy as jnp
from jax import lax
from jax.experimental import pallas as pl
from jax.experimental.pallas import tpu as pltpu
from jax.sharding import PartitionSpec as P

VMEM = pl.BlockSpec(memory_space=pltpu.VMEM)
SMEM = pl.BlockSpec(memory_space=pltpu.SMEM)
HBM = pl.BlockSpec(memory_space=pltpu.HBM)
PARAMS = pltpu.CompilerParams(vmem_limit_bytes=16 * 1024 * 1024)
HALF = 16
GROUP = 2
LANES = 128


def fold(value):
    rows, width = value.shape
    summed = jnp.sum(value.reshape(rows // 8, 8, width), axis=0)
    return sum(summed[:, k * 128 : (k + 1) * 128] for k in range(width // 128))


def down(value):
    return jnp.sum(value, axis=0, keepdims=True)


def halves(rows, width, start=0):
    for h in range(rows // HALF):
        yield h * HALF, slice(start + h * width, start + (h + 1) * width)


def write_lanes(ref, at, lanes):
    whole = jnp.broadcast_to(lanes, (HALF, LANES))
    high = whole.astype(jnp.bfloat16).astype(jnp.float32)
    rest = whole - high
    middle = rest.astype(jnp.bfloat16).astype(jnp.float32)
    low = rest - middle
    row = lax.broadcasted_iota(jnp.int32, whole.shape, 0)
    value = jnp.where(row == 0, high, jnp.where(row == 1, middle, jnp.where(row == 2, low, 0.0)))
    ref[:, at : at + LANES] = value.astype(jnp.bfloat16)


def read_lanes(ref, at):
    return down(ref[:, at : at + LANES].astype(jnp.float32))


def chip_at(place):
    place = lax.rem(place + 8, 8)
    return jnp.where(place < 4, 2 * place, 15 - 2 * place)


def ring_place(me):
    chip, core = me // 2, me % 2
    place = jnp.where(chip % 2 == 0, chip // 2, (15 - chip) // 2)
    return place, core


def ahead(me, distance, half, core=None):
    place, own = ring_place(me)
    core = own if core is None else core
    return chip_at(place + (1 - 2 * core) * distance) * 2 + half


ROUNDS = 3


def sent_devices(me, core):
    devices = []
    for k in range(ROUNDS):
        for half in (core, 1 - core):
            devices.append(ahead(me, ROUNDS - k, half, core))
    return devices + [ahead(me, 4, core, core), ahead(me, 0, core, core)]


def gathered_devices(me):
    core = me % 2
    devices = [ahead(me, 0, core), ahead(me, 0, 1 - core)]
    for k in range(1, ROUNDS + 1):
        devices += [ahead(me, -k, core), ahead(me, -k, 1 - core)]
        devices += [ahead(me, k, 1 - core), ahead(me, k, core)]
    return devices + [ahead(me, 4, core), ahead(me, 4, 1 - core)]


def message_parts(sectors, rows, width):
    for s in range(sectors):
        for row, part in halves(rows, width, s * (rows // HALF) * width):
            yield s, row, part


def message_shape(sectors, rows, width):
    return (HALF, rows // HALF * sectors * width + LANES)


def copy_kernel(in_ref, out_ref):
    out_ref[...] = in_ref[...]


def copied(value, cost=64 << 30):
    return pl.pallas_call(
        copy_kernel,
        in_specs=[VMEM],
        out_specs=VMEM,
        out_shape=jax.ShapeDtypeStruct(value.shape, value.dtype),
        compiler_params=PARAMS,
        cost_estimate=pl.CostEstimate(flops=cost, bytes_accessed=1 << 20, transcendentals=0),
    )(value)


def square_kernel(wave_ref, diag_ref, square_ref):
    square = jnp.zeros((8, 128), jnp.float32)
    for s in range(wave_ref.shape[0]):
        wave = wave_ref[s].astype(jnp.float32)
        square += fold(diag_ref[s].astype(jnp.float32) * wave * wave)
    square_ref[...] = square


def weighted_square(wave, diag):
    return pl.pallas_call(
        square_kernel,
        in_specs=[VMEM, VMEM],
        out_specs=VMEM,
        out_shape=jax.ShapeDtypeStruct((8, 128), jnp.float32),
        compiler_params=PARAMS,
    )(wave, diag)


def blocks_kernel(first, shape, entries, me_ref, ints_ref, *refs):
    sectors, rows, width = shape
    field_refs, refs = refs[:16], refs[16:]
    if first:
        square_ref, *refs = refs
    else:
        scale_ref, wave_ref, correction_ref, *refs = refs
    left_in, right_in, *refs = refs
    total, near_ref, far_ref, dot_ref, out_ref, field, *refs = refs
    slots = left_in.shape[0]
    left, right = left_in, right_in

    me = me_ref[0]
    core = me % 2

    pieces = []
    for k, owner in enumerate(gathered_devices(me)):
        at = pl.multiple_of(owner * rows, rows)
        if first:
            for s in range(sectors):
                pieces.append((k, (s,), s, pl.ds(at, rows)))
        else:
            for s, row, part in message_parts(sectors, rows, width):
                pieces.append((k, (slice(None), part), s, pl.ds(at + row, HALF)))

    total[...] = jnp.zeros_like(total)
    if first:
        dot = jnp.zeros((8, 128), jnp.float32)
        for k, part, _, _ in pieces:
            value = field_refs[k][part].astype(jnp.float32)
            dot += fold(value * value)
        scale = jnp.sqrt(jnp.sum(dot) / entries)
        inverse = 1.0 / scale
        out_ref[...] = jnp.full(out_ref.shape, scale, jnp.float32)
        for k, part, s, at in pieces:
            field[s, at, :] = (field_refs[k][part].astype(jnp.float32) * inverse).astype(jnp.bfloat16)
    else:
        for k, part, s, at in pieces:
            field[s, at, :] = field_refs[k][part]

    used = ints_ref[2 * slots]

    def add_some(step, carry):
        some = [step * GROUP + k for k in range(GROUP)]
        @pl.when(some[0] < used)
        def _():
            products = [
                jnp.dot(
                    left[slot], field[ints_ref[slot]], preferred_element_type=jnp.float32
                ).astype(jnp.bfloat16)
                for slot in some
            ]
            for slot, product in zip(some, products):
                if slot is not some[0]:
                    product = jnp.where(slot < used, product, jnp.zeros_like(product))
                total[ints_ref[slots + slot]] += lax.dot_general(
                    product,
                    right[slot],
                    (((1,), (1,)), ((), ())),
                    preferred_element_type=jnp.float32,
                )

        return carry

    lax.fori_loop(0, slots // GROUP, add_some, 0)

    dot = jnp.zeros((8, 128), jnp.float32)
    if first:
        for k, part, s, at in pieces:
            dot += fold(total[s, at, :] * field_refs[k][part].astype(jnp.float32))
        dot = dot * inverse + square_ref[...] * inverse * inverse
    else:
        at = message_shape(*shape)[1] - LANES
        lanes = sum(
            ref[:, at : at + LANES].astype(jnp.float32) for ref in field_refs
        )
        along = jnp.sum(lanes) / entries
        out_ref[...] = jnp.full(out_ref.shape, along, jnp.float32)
        inverse = 1.0 / scale_ref[0:1, 0:1]
        for s in range(sectors):
            projected = correction_ref[s] - along * (wave_ref[s].astype(jnp.float32) * inverse)
            dot += fold(projected * projected)
    dot_ref[...] = dot
    lanes = down(dot)
    for k, owner in enumerate(sent_devices(me, 1 - core)):
        at = pl.multiple_of(owner * rows, rows)
        ref = near_ref.at[k] if k < near_ref.shape[0] else far_ref.at[k - near_ref.shape[0]]
        for s, row, part in message_parts(*shape):
            ref[:, part] = total[s, pl.ds(at + row, HALF), :].astype(jnp.bfloat16)
        write_lanes(ref, ref.shape[1] - LANES, lanes)


def apply_blocks(me, ints, fields, own, left, right, shape, first, entries):
    slots, order, width = left.shape
    sectors = shape[0]
    message = message_shape(*shape)
    return pl.pallas_call(
        functools.partial(blocks_kernel, first, shape, entries),
        in_specs=[SMEM, SMEM]
        + [VMEM] * (len(fields) + len(own))
        + [VMEM] * 2,
        out_specs=[VMEM] * 5,
        scratch_shapes=[pltpu.VMEM((sectors, order, width), jnp.bfloat16)],
        out_shape=[
            jax.ShapeDtypeStruct((sectors, order, width), jnp.float32),
            jax.ShapeDtypeStruct((2, *message), jnp.bfloat16),
            jax.ShapeDtypeStruct((2 * ROUNDS, *message), jnp.bfloat16),
            jax.ShapeDtypeStruct((8, 128), jnp.float32),
            jax.ShapeDtypeStruct((8, 128), jnp.float32),
        ],
        compiler_params=PARAMS,
        cost_estimate=pl.CostEstimate(
            flops=4 * slots * order * order * width,
            bytes_accessed=4 * slots * order * order,
            transcendentals=0,
        ),
    )(me, ints, *fields, *own, left, right)


def chain_kernel(shape, k, index, me_ref, total_ref, dot_ref, other_ref, *refs):
    *arrived_refs, out_ref = refs
    _, rows, _ = shape
    me = me_ref[0]
    start = pl.multiple_of(sent_devices(me, me % 2)[k] * rows, rows)
    for s, row, part in message_parts(*shape):
        value = total_ref[s, pl.ds(start + row, HALF), :]
        value += other_ref[index, :, part].astype(jnp.float32)
        for ref in arrived_refs:
            value += ref[:, part].astype(jnp.float32)
        out_ref[:, part] = value.astype(jnp.bfloat16)
    at = out_ref.shape[1] - LANES
    lanes = down(dot_ref[...]) + read_lanes(other_ref.at[index], at)
    for ref in arrived_refs:
        lanes += read_lanes(ref, at)
    write_lanes(out_ref, at, lanes)


def chain(shape, k, index, me, total, dot, other, *arrived):
    return pl.pallas_call(
        functools.partial(chain_kernel, shape, k, index),
        in_specs=[SMEM] + [VMEM] * (3 + len(arrived)),
        out_specs=VMEM,
        out_shape=jax.ShapeDtypeStruct(message_shape(*shape), jnp.bfloat16),
        compiler_params=PARAMS,
    )(me, total, dot, other, *arrived)


def own_terms(shape, sector, me_ref, total_ref, other_ref, _, *arrived_refs):
    start = pl.multiple_of(me_ref[0] * shape[1], shape[1])
    values = []
    for s, row, part in message_parts(*shape):
        if s == sector:
            value = total_ref[s, pl.ds(start + row, HALF), :]
            value += other_ref[other_ref.shape[0] - 1, :, part].astype(jnp.float32)
            for ref in arrived_refs:
                value += ref[:, part].astype(jnp.float32)
            values.append(value)
    return jnp.concatenate(values, axis=0)


def own_scalar(me_ref, total_ref, other_ref, dot_ref, *arrived_refs):
    at = other_ref.shape[2] - LANES
    lanes = down(dot_ref[...]) + read_lanes(other_ref.at[other_ref.shape[0] - 1], at)
    return jnp.sum(lanes + sum(read_lanes(ref, at) for ref in arrived_refs))


def step_kernel(entries, scale_ref, wave_ref, diag_ref, *refs):
    *sums, first_ref, terms_ref, correction_ref, message_ref = refs
    shape = wave_ref.shape
    ritz = own_scalar(*sums) / entries
    inverse = 1.0 / scale_ref[0:1, 0:1]
    dots = jnp.zeros((8, 128), jnp.float32)
    for s in range(shape[0]):
        start = wave_ref[s].astype(jnp.float32) * inverse
        diag = diag_ref[s].astype(jnp.float32)
        terms = own_terms(shape, s, *sums)
        first = terms + diag * start
        correction = (first - ritz * start) / jnp.maximum(jnp.abs(diag - ritz), 1.0)
        first_ref[s] = first
        terms_ref[s] = terms
        correction_ref[s] = correction
        dots += fold(start * correction)
        for t, row, part in message_parts(*shape):
            if t == s:
                message_ref[:, part] = correction[row : row + HALF].astype(jnp.bfloat16)
    write_lanes(message_ref, message_ref.shape[1] - LANES, down(dots))


def davidson_step(scale, wave, diag, sums, entries):
    full = jax.ShapeDtypeStruct(wave.shape, jnp.float32)
    return pl.pallas_call(
        functools.partial(step_kernel, entries),
        in_specs=[VMEM] * 3 + [SMEM] + [VMEM] * (len(sums) - 1),
        out_specs=[VMEM] * 4,
        out_shape=[full, full, full, jax.ShapeDtypeStruct(message_shape(*wave.shape), jnp.bfloat16)],
        compiler_params=PARAMS,
    )(scale, wave, diag, *sums)


def finish_kernel(entries, along_ref, scale_ref, wave_ref, diag_ref, *refs):
    terms_ref, correction_ref, *sums, vector_ref, image_ref = refs
    shape = wave_ref.shape
    along = along_ref[0:1, 0:1]
    norm = jnp.sqrt(jnp.full((1, 1), own_scalar(*sums) / entries, jnp.float32))
    inverse = 1.0 / norm
    start_scale = 1.0 / scale_ref[0:1, 0:1]
    for s in range(shape[0]):
        start = wave_ref[s].astype(jnp.float32) * start_scale
        second = (correction_ref[s] - along * start) * inverse
        vector_ref[s] = second
        image = (own_terms(shape, s, *sums) - along * terms_ref[s]) * inverse
        image_ref[s] = image + diag_ref[s].astype(jnp.float32) * second


def finish(along, scale, wave, diag, terms, correction, sums, entries):
    full = jax.ShapeDtypeStruct(wave.shape, jnp.float32)
    return pl.pallas_call(
        functools.partial(finish_kernel, entries),
        in_specs=[VMEM] * 6 + [SMEM] + [VMEM] * (len(sums) - 1),
        out_specs=[VMEM] * 2,
        out_shape=[full, full],
        compiler_params=PARAMS,
    )(along, scale, wave, diag, terms, correction, *sums)


def flip(value):
    return lax.ppermute(value, "term", [(i, i ^ 1) for i in range(16)])


def hop(value, up=1, down=-1):
    order = [0, 2, 4, 6, 7, 5, 3, 1]
    pairs = []
    for place in range(8):
        for core, step in ((0, up), (1, down)):
            pairs.append((order[place] * 2 + core, order[(place + step) % 8] * 2 + core))
    return lax.ppermute(value, "term", pairs)


def opposite(value):
    return hop(value, 4, 4)


def gather(own, beside=()):
    one, two = own, flip(own)
    across, two = lax.optimization_barrier((own, two))
    pieces = [one, two]
    across = opposite(across)
    results = []
    for k in range(ROUNDS):
        one, two = hop(one), hop(two)
        if k < len(beside):
            results.append(beside[k](*results))
        if k < ROUNDS - 1:
            ready = results[-1:] if beside else []
            two, ready = lax.optimization_barrier((two, ready))
            if ready:
                results[-1] = ready[0]
        pieces += [one, two, flip(one), flip(two)]
    return pieces + [across, flip(across)], results


def scatter(shape, me, total, near, far, dot):
    near = flip(near)
    near, far = lax.optimization_barrier((near, far))
    far = flip(far)
    one = hop(chain(shape, 0, 0, me, total, dot, near))
    two = hop(chain(shape, 1, 1, me, total, dot, near))
    across = opposite(chain(shape, 6, 4, me, total, dot, far))
    for k in (2, 4):
        one = hop(chain(shape, k, k - 2, me, total, dot, far, one))
        if k == 4:
            two, across = lax.optimization_barrier((two, across))
        two = hop(chain(shape, k + 1, k - 1, me, total, dot, far, two))
    return me, total, far, dot, one, flip(two), across


def on_ring(
    wavefunction, diagonal, left_blocks, right_blocks, block_source, block_target, live_count
):
    shape = wavefunction.shape
    sectors, rows, width = shape
    entries = float(sectors * rows * lax.axis_size("term") * width)
    me = lax.axis_index("term").astype(jnp.int32).reshape(1)
    beside = (
        lambda: jnp.concatenate([block_source, block_target, live_count]),
        lambda _: copied(wavefunction),
        lambda _, own: weighted_square(own, diagonal),
    )
    (_, *fields), (ints, own, square) = gather(wavefunction, beside)
    fields = [own, *fields]
    blocks = (left_blocks, right_blocks, shape)
    total, near, far, dot, scale = apply_blocks(me, ints, fields, (square,), *blocks, True, entries)
    first_image, terms, correction, message = davidson_step(
        scale, wavefunction, diagonal, scatter(shape, me, total, near, far, dot), entries
    )
    fields, _ = gather(message)
    own = (scale, wavefunction, correction)
    total, near, far, dot, along = apply_blocks(me, ints, fields, own, *blocks, False, entries)
    second_vector, second_image = finish(
        along, scale, wavefunction, diagonal, terms, correction,
        scatter(shape, me, total, near, far, dot), entries,
    )
    return (first_image, second_vector, second_image)


def block_loop(field_rounded, left_ops, right_ops, sources, targets, last_slot, partial_sum):

    def add_block(slot_index, running):
        left_op = lax.dynamic_index_in_dim(left_ops, slot_index, 0, keepdims=False)
        right_op = lax.dynamic_index_in_dim(right_ops, slot_index, 0, keepdims=False)
        source = lax.dynamic_index_in_dim(sources, slot_index, 0, keepdims=False)
        target = lax.dynamic_index_in_dim(targets, slot_index, 0, keepdims=False)
        piece = lax.dynamic_index_in_dim(field_rounded, source, 0, keepdims=False)
        product = jnp.dot(left_op, piece, preferred_element_type=jnp.float32).astype(jnp.bfloat16)
        term_value = jnp.dot(product, right_op.T, preferred_element_type=jnp.float32)
        before = lax.dynamic_index_in_dim(running, target, 0, keepdims=False)
        return lax.dynamic_update_index_in_dim(running, before + term_value, target, 0)

    return lax.fori_loop(0, last_slot, add_block, partial_sum)


def on_any(
    wavefunction, diagonal, left_blocks, right_blocks, block_source, block_target, live_count
):
    devices = lax.axis_size("term")
    position = lax.axis_index("term")
    row_count = wavefunction.shape[1]
    sector_count = wavefunction.shape[0]
    width = wavefunction.shape[2]
    entries = float(sector_count * row_count * devices * width)
    own_count = live_count[0]
    diag_own = diagonal.astype(jnp.float32)
    whole_wave = lax.all_gather(wavefunction, "term", axis=1, tiled=True).astype(jnp.float32)
    scale = jnp.sqrt(jnp.sum(whole_wave * whole_wave) / entries)
    start_whole = whole_wave / scale
    empty_sum = jnp.zeros(start_whole.shape, jnp.float32)
    first_terms = block_loop(
        start_whole.astype(jnp.bfloat16),
        left_blocks,
        right_blocks,
        block_source,
        block_target,
        own_count,
        empty_sum,
    )
    row_start = position * row_count
    whole_diag = lax.all_gather(diagonal, "term", axis=1, tiled=True).astype(jnp.float32)
    first_whole = lax.psum(first_terms, "term") + whole_diag * start_whole
    ritz_value = jnp.sum(start_whole * first_whole) / entries
    correction = (first_whole - ritz_value * start_whole) / jnp.maximum(
        jnp.abs(whole_diag - ritz_value), 1.0
    )
    correlation = jnp.sum(start_whole * correction) / entries
    projected = correction - correlation * start_whole
    second_whole = projected / jnp.sqrt(jnp.sum(projected * projected) / entries)
    first_image = lax.dynamic_slice_in_dim(first_whole, row_start, row_count, 1)
    second_vector = lax.dynamic_slice_in_dim(second_whole, row_start, row_count, 1)
    second_rounded = second_whole.astype(jnp.bfloat16)
    second_terms = block_loop(
        second_rounded, left_blocks, right_blocks, block_source, block_target, own_count, empty_sum
    )
    second_image = (
        lax.psum_scatter(second_terms, "term", scatter_dimension=1, tiled=True)
        + diag_own * second_vector
    )
    return (first_image, second_vector, second_image)


def solution(mesh):
    placed = (
        P("grp", "term", None),
        P("grp", "term", None),
        P(("grp", "term"), None, None),
        P(("grp", "term"), None, None),
        P(("grp", "term")),
        P(("grp", "term")),
        P(("grp", "term")),
    )
    on_device = on_ring if mesh.shape["term"] == 16 else on_any
    return jax.shard_map(
        on_device,
        mesh=mesh,
        in_specs=placed,
        out_specs=(P("grp", "term", None), P("grp", "term", None), P("grp", "term", None)),
        check_vma=False,
    )
```

```python
import functools

import jax
import jax.numpy as jnp
from jax import lax
from jax.experimental import pallas as pl
from jax.experimental.pallas import tpu as pltpu
from jax.sharding import PartitionSpec as P

VMEM = pl.BlockSpec(memory_space=pltpu.VMEM)
SMEM = pl.BlockSpec(memory_space=pltpu.SMEM)
HBM = pl.BlockSpec(memory_space=pltpu.HBM)
PARAMS = pltpu.CompilerParams(vmem_limit_bytes=16 * 1024 * 1024)
FIRST = pltpu.CompilerParams(vmem_limit_bytes=48 * 1024 * 1024)
HALF = 16
GROUP = 2
LANES = 128


def fold(value):
    rows, width = value.shape
    summed = jnp.sum(value.reshape(rows // 8, 8, width), axis=0)
    return sum(summed[:, k * 128 : (k + 1) * 128] for k in range(width // 128))


def down(value):
    return jnp.sum(value, axis=0, keepdims=True)


def halves(rows, width, start=0):
    for h in range(rows // HALF):
        yield h * HALF, slice(start + h * width, start + (h + 1) * width)


def write_lanes(ref, at, lanes):
    whole = jnp.broadcast_to(lanes, (HALF, LANES))
    high = whole.astype(jnp.bfloat16).astype(jnp.float32)
    rest = whole - high
    middle = rest.astype(jnp.bfloat16).astype(jnp.float32)
    low = rest - middle
    row = lax.broadcasted_iota(jnp.int32, whole.shape, 0)
    value = jnp.where(row == 0, high, jnp.where(row == 1, middle, jnp.where(row == 2, low, 0.0)))
    ref[:, at : at + LANES] = value.astype(jnp.bfloat16)


def read_lanes(ref, at):
    return down(ref[:, at : at + LANES].astype(jnp.float32))


def chip_at(place):
    place = lax.rem(place + 8, 8)
    return jnp.where(place < 4, 2 * place, 15 - 2 * place)


def ring_place(me):
    chip, core = me // 2, me % 2
    place = jnp.where(chip % 2 == 0, chip // 2, (15 - chip) // 2)
    return place, core


def ahead(me, distance, half, core=None):
    place, own = ring_place(me)
    core = own if core is None else core
    return chip_at(place + (1 - 2 * core) * distance) * 2 + half


ROUNDS = 3


def sent_devices(me, core):
    devices = []
    for k in range(ROUNDS):
        for half in (core, 1 - core):
            devices.append(ahead(me, ROUNDS - k, half, core))
    return devices + [ahead(me, 4, core, core), ahead(me, 0, core, core)]


def gathered_devices(me):
    core = me % 2
    devices = [ahead(me, 0, core), ahead(me, 0, 1 - core)]
    for k in range(1, ROUNDS + 1):
        devices += [ahead(me, -k, core), ahead(me, -k, 1 - core)]
        devices += [ahead(me, k, 1 - core), ahead(me, k, core)]
    return devices + [ahead(me, 4, core), ahead(me, 4, 1 - core)]


def message_parts(sectors, rows, width):
    for s in range(sectors):
        for row, part in halves(rows, width, s * (rows // HALF) * width):
            yield s, row, part


def message_shape(sectors, rows, width):
    return (HALF, rows // HALF * sectors * width + LANES)


def copy_kernel(in_ref, out_ref):
    out_ref[...] = in_ref[...]


def copied(value):
    return pl.pallas_call(
        copy_kernel,
        in_specs=[VMEM],
        out_specs=VMEM,
        out_shape=jax.ShapeDtypeStruct(value.shape, value.dtype),
        compiler_params=PARAMS,
        cost_estimate=pl.CostEstimate(flops=8 << 30, bytes_accessed=1 << 20, transcendentals=0),
    )(value)


def square_kernel(wave_ref, diag_ref, square_ref):
    square = jnp.zeros((8, 128), jnp.float32)
    for s in range(wave_ref.shape[0]):
        wave = wave_ref[s].astype(jnp.float32)
        square += fold(diag_ref[s].astype(jnp.float32) * wave * wave)
    square_ref[...] = square


def weighted_square(wave, diag):
    return pl.pallas_call(
        square_kernel,
        in_specs=[VMEM, VMEM],
        out_specs=VMEM,
        out_shape=jax.ShapeDtypeStruct((8, 128), jnp.float32),
        compiler_params=PARAMS,
    )(wave, diag)


def blocks_kernel(first, shape, entries, me_ref, ints_ref, *refs):
    sectors, rows, width = shape
    field_refs, refs = refs[:16], refs[16:]
    if first:
        square_ref, *refs = refs
    else:
        scale_ref, wave_ref, correction_ref, *refs = refs
    left_in, right_in, *refs = refs
    total, near_ref, far_ref, dot_ref, out_ref, field, *refs = refs
    slots = left_in.shape[0]
    if first:
        left, right, left_sem, right_sem = refs

        def copies(slot):
            return (
                pltpu.make_async_copy(left_in.at[slot], left.at[slot], left_sem.at[slot]),
                pltpu.make_async_copy(right_in.at[slot], right.at[slot], right_sem.at[slot]),
            )

        for slot in range(GROUP):
            for copy in copies(slot):
                copy.start()
    else:
        left, right = left_in, right_in

    me = me_ref[0]
    core = me % 2

    pieces = []
    for k, owner in enumerate(gathered_devices(me)):
        at = pl.multiple_of(owner * rows, rows)
        if first:
            for s in range(sectors):
                pieces.append((k, (s,), s, pl.ds(at, rows)))
        else:
            for s, row, part in message_parts(sectors, rows, width):
                pieces.append((k, (slice(None), part), s, pl.ds(at + row, HALF)))

    total[...] = jnp.zeros_like(total)
    if first:
        dot = jnp.zeros((8, 128), jnp.float32)
        for k, part, _, _ in pieces:
            value = field_refs[k][part].astype(jnp.float32)
            dot += fold(value * value)
        for slot in range(GROUP, slots):
            for copy in copies(slot):
                copy.start()
        scale = jnp.sqrt(jnp.sum(dot) / entries)
        inverse = 1.0 / scale
        out_ref[...] = jnp.full(out_ref.shape, scale, jnp.float32)
        for k, part, s, at in pieces:
            field[s, at, :] = (field_refs[k][part].astype(jnp.float32) * inverse).astype(jnp.bfloat16)
    else:
        for k, part, s, at in pieces:
            field[s, at, :] = field_refs[k][part]

    used = ints_ref[2 * slots]

    def add_some(step, carry):
        some = [step * GROUP + k for k in range(GROUP)]
        if first:
            for slot in some:
                for copy in copies(slot):
                    copy.wait()

        @pl.when(some[0] < used)
        def _():
            products = [
                jnp.dot(
                    left[slot], field[ints_ref[slot]], preferred_element_type=jnp.float32
                ).astype(jnp.bfloat16)
                for slot in some
            ]
            for slot, product in zip(some, products):
                if slot is not some[0]:
                    product = jnp.where(slot < used, product, jnp.zeros_like(product))
                total[ints_ref[slots + slot]] += lax.dot_general(
                    product,
                    right[slot],
                    (((1,), (1,)), ((), ())),
                    preferred_element_type=jnp.float32,
                )

        return carry

    lax.fori_loop(0, slots // GROUP, add_some, 0)

    dot = jnp.zeros((8, 128), jnp.float32)
    if first:
        for k, part, s, at in pieces:
            dot += fold(total[s, at, :] * field_refs[k][part].astype(jnp.float32))
        dot = dot * inverse + square_ref[...] * inverse * inverse
    else:
        at = message_shape(*shape)[1] - LANES
        lanes = sum(
            ref[:, at : at + LANES].astype(jnp.float32) for ref in field_refs
        )
        along = jnp.sum(lanes) / entries
        out_ref[...] = jnp.full(out_ref.shape, along, jnp.float32)
        inverse = 1.0 / scale_ref[0:1, 0:1]
        for s in range(sectors):
            projected = correction_ref[s] - along * (wave_ref[s].astype(jnp.float32) * inverse)
            dot += fold(projected * projected)
    dot_ref[...] = dot
    lanes = down(dot)
    for k, owner in enumerate(sent_devices(me, 1 - core)):
        at = pl.multiple_of(owner * rows, rows)
        ref = near_ref.at[k] if k < near_ref.shape[0] else far_ref.at[k - near_ref.shape[0]]
        for s, row, part in message_parts(*shape):
            ref[:, part] = total[s, pl.ds(at + row, HALF), :].astype(jnp.bfloat16)
        write_lanes(ref, ref.shape[1] - LANES, lanes)


def apply_blocks(me, ints, fields, own, left, right, shape, first, entries):
    slots, order, width = left.shape
    sectors = shape[0]
    message = message_shape(*shape)
    scratch = []
    if first:
        scratch = [pltpu.VMEM(b.shape, b.dtype) for b in (left, right)]
        scratch += [pltpu.SemaphoreType.DMA((slots,))] * 2
    return pl.pallas_call(
        functools.partial(blocks_kernel, first, shape, entries),
        in_specs=[SMEM, SMEM]
        + [VMEM] * (len(fields) + len(own))
        + [HBM if first else VMEM] * 2,
        out_specs=[VMEM] * 5,
        scratch_shapes=[pltpu.VMEM((sectors, order, width), jnp.bfloat16)] + scratch,
        out_shape=[
            jax.ShapeDtypeStruct((sectors, order, width), jnp.float32),
            jax.ShapeDtypeStruct((2, *message), jnp.bfloat16),
            jax.ShapeDtypeStruct((2 * ROUNDS, *message), jnp.bfloat16),
            jax.ShapeDtypeStruct((8, 128), jnp.float32),
            jax.ShapeDtypeStruct((8, 128), jnp.float32),
        ],
        compiler_params=FIRST if first else PARAMS,
        cost_estimate=pl.CostEstimate(
            flops=4 * slots * order * order * width,
            bytes_accessed=4 * slots * order * order,
            transcendentals=0,
        ),
    )(me, ints, *fields, *own, left, right)


def chain_kernel(shape, k, index, me_ref, total_ref, dot_ref, other_ref, *refs):
    *arrived_refs, out_ref = refs
    _, rows, _ = shape
    me = me_ref[0]
    start = pl.multiple_of(sent_devices(me, me % 2)[k] * rows, rows)
    for s, row, part in message_parts(*shape):
        value = total_ref[s, pl.ds(start + row, HALF), :]
        value += other_ref[index, :, part].astype(jnp.float32)
        for ref in arrived_refs:
            value += ref[:, part].astype(jnp.float32)
        out_ref[:, part] = value.astype(jnp.bfloat16)
    at = out_ref.shape[1] - LANES
    lanes = down(dot_ref[...]) + read_lanes(other_ref.at[index], at)
    for ref in arrived_refs:
        lanes += read_lanes(ref, at)
    write_lanes(out_ref, at, lanes)


def chain(shape, k, index, me, total, dot, other, *arrived):
    return pl.pallas_call(
        functools.partial(chain_kernel, shape, k, index),
        in_specs=[SMEM] + [VMEM] * (3 + len(arrived)),
        out_specs=VMEM,
        out_shape=jax.ShapeDtypeStruct(message_shape(*shape), jnp.bfloat16),
        compiler_params=PARAMS,
    )(me, total, dot, other, *arrived)


def own_terms(shape, sector, me_ref, total_ref, other_ref, _, *arrived_refs):
    start = pl.multiple_of(me_ref[0] * shape[1], shape[1])
    values = []
    for s, row, part in message_parts(*shape):
        if s == sector:
            value = total_ref[s, pl.ds(start + row, HALF), :]
            value += other_ref[other_ref.shape[0] - 1, :, part].astype(jnp.float32)
            for ref in arrived_refs:
                value += ref[:, part].astype(jnp.float32)
            values.append(value)
    return jnp.concatenate(values, axis=0)


def own_scalar(me_ref, total_ref, other_ref, dot_ref, *arrived_refs):
    at = other_ref.shape[2] - LANES
    lanes = down(dot_ref[...]) + read_lanes(other_ref.at[other_ref.shape[0] - 1], at)
    return jnp.sum(lanes + sum(read_lanes(ref, at) for ref in arrived_refs))


def step_kernel(entries, scale_ref, wave_ref, diag_ref, *refs):
    *sums, first_ref, terms_ref, correction_ref, message_ref = refs
    shape = wave_ref.shape
    ritz = own_scalar(*sums) / entries
    inverse = 1.0 / scale_ref[0:1, 0:1]
    dots = jnp.zeros((8, 128), jnp.float32)
    for s in range(shape[0]):
        start = wave_ref[s].astype(jnp.float32) * inverse
        diag = diag_ref[s].astype(jnp.float32)
        terms = own_terms(shape, s, *sums)
        first = terms + diag * start
        correction = (first - ritz * start) / jnp.maximum(jnp.abs(diag - ritz), 1.0)
        first_ref[s] = first
        terms_ref[s] = terms
        correction_ref[s] = correction
        dots += fold(start * correction)
        for t, row, part in message_parts(*shape):
            if t == s:
                message_ref[:, part] = correction[row : row + HALF].astype(jnp.bfloat16)
    write_lanes(message_ref, message_ref.shape[1] - LANES, down(dots))


def davidson_step(scale, wave, diag, sums, entries):
    full = jax.ShapeDtypeStruct(wave.shape, jnp.float32)
    return pl.pallas_call(
        functools.partial(step_kernel, entries),
        in_specs=[VMEM] * 3 + [SMEM] + [VMEM] * (len(sums) - 1),
        out_specs=[VMEM] * 4,
        out_shape=[full, full, full, jax.ShapeDtypeStruct(message_shape(*wave.shape), jnp.bfloat16)],
        compiler_params=PARAMS,
    )(scale, wave, diag, *sums)


def finish_kernel(entries, along_ref, scale_ref, wave_ref, diag_ref, *refs):
    terms_ref, correction_ref, *sums, vector_ref, image_ref = refs
    shape = wave_ref.shape
    along = along_ref[0:1, 0:1]
    norm = jnp.sqrt(jnp.full((1, 1), own_scalar(*sums) / entries, jnp.float32))
    inverse = 1.0 / norm
    start_scale = 1.0 / scale_ref[0:1, 0:1]
    for s in range(shape[0]):
        start = wave_ref[s].astype(jnp.float32) * start_scale
        second = (correction_ref[s] - along * start) * inverse
        vector_ref[s] = second
        image = (own_terms(shape, s, *sums) - along * terms_ref[s]) * inverse
        image_ref[s] = image + diag_ref[s].astype(jnp.float32) * second


def finish(along, scale, wave, diag, terms, correction, sums, entries):
    full = jax.ShapeDtypeStruct(wave.shape, jnp.float32)
    return pl.pallas_call(
        functools.partial(finish_kernel, entries),
        in_specs=[VMEM] * 6 + [SMEM] + [VMEM] * (len(sums) - 1),
        out_specs=[VMEM] * 2,
        out_shape=[full, full],
        compiler_params=PARAMS,
    )(along, scale, wave, diag, terms, correction, *sums)


def flip(value):
    return lax.ppermute(value, "term", [(i, i ^ 1) for i in range(16)])


def hop(value, up=1, down=-1):
    order = [0, 2, 4, 6, 7, 5, 3, 1]
    pairs = []
    for place in range(8):
        for core, step in ((0, up), (1, down)):
            pairs.append((order[place] * 2 + core, order[(place + step) % 8] * 2 + core))
    return lax.ppermute(value, "term", pairs)


def opposite(value):
    return hop(value, 4, 4)


def gather(own, beside=()):
    one, two = own, flip(own)
    across, two = lax.optimization_barrier((own, two))
    pieces = [one, two]
    across = opposite(across)
    results = []
    for k in range(ROUNDS):
        one, two = hop(one), hop(two)
        if k < len(beside):
            results.append(beside[k](*results))
        if k < ROUNDS - 1:
            ready = results[-1:] if beside else []
            two, ready = lax.optimization_barrier((two, ready))
            if ready:
                results[-1] = ready[0]
        pieces += [one, two, flip(one), flip(two)]
    return pieces + [across, flip(across)], results


def scatter(shape, me, total, near, far, dot):
    near = flip(near)
    near, far = lax.optimization_barrier((near, far))
    far = flip(far)
    one = hop(chain(shape, 0, 0, me, total, dot, near))
    two = hop(chain(shape, 1, 1, me, total, dot, near))
    across = opposite(chain(shape, 6, 4, me, total, dot, far))
    for k in (2, 4):
        one = hop(chain(shape, k, k - 2, me, total, dot, far, one))
        if k == 4:
            two, across = lax.optimization_barrier((two, across))
        two = hop(chain(shape, k + 1, k - 1, me, total, dot, far, two))
    return me, total, far, dot, one, flip(two), across


def on_ring(
    wavefunction, diagonal, left_blocks, right_blocks, block_source, block_target, live_count
):
    shape = wavefunction.shape
    sectors, rows, width = shape
    entries = float(sectors * rows * lax.axis_size("term") * width)
    me = lax.axis_index("term").astype(jnp.int32).reshape(1)
    beside = (
        lambda: jnp.concatenate([block_source, block_target, live_count]),
        lambda _: copied(wavefunction),
        lambda _, own: weighted_square(own, diagonal),
    )
    (_, *fields), (ints, own, square) = gather(wavefunction, beside)
    fields = [own, *fields]
    blocks = (left_blocks, right_blocks, shape)
    total, near, far, dot, scale = apply_blocks(me, ints, fields, (square,), *blocks, True, entries)
    first_image, terms, correction, message = davidson_step(
        scale, wavefunction, diagonal, scatter(shape, me, total, near, far, dot), entries
    )
    fields, _ = gather(message)
    own = (scale, wavefunction, correction)
    total, near, far, dot, along = apply_blocks(me, ints, fields, own, *blocks, False, entries)
    second_vector, second_image = finish(
        along, scale, wavefunction, diagonal, terms, correction,
        scatter(shape, me, total, near, far, dot), entries,
    )
    return (first_image, second_vector, second_image)


def block_loop(field_rounded, left_ops, right_ops, sources, targets, last_slot, partial_sum):

    def add_block(slot_index, running):
        left_op = lax.dynamic_index_in_dim(left_ops, slot_index, 0, keepdims=False)
        right_op = lax.dynamic_index_in_dim(right_ops, slot_index, 0, keepdims=False)
        source = lax.dynamic_index_in_dim(sources, slot_index, 0, keepdims=False)
        target = lax.dynamic_index_in_dim(targets, slot_index, 0, keepdims=False)
        piece = lax.dynamic_index_in_dim(field_rounded, source, 0, keepdims=False)
        product = jnp.dot(left_op, piece, preferred_element_type=jnp.float32).astype(jnp.bfloat16)
        term_value = jnp.dot(product, right_op.T, preferred_element_type=jnp.float32)
        before = lax.dynamic_index_in_dim(running, target, 0, keepdims=False)
        return lax.dynamic_update_index_in_dim(running, before + term_value, target, 0)

    return lax.fori_loop(0, last_slot, add_block, partial_sum)


def on_any(
    wavefunction, diagonal, left_blocks, right_blocks, block_source, block_target, live_count
):
    devices = lax.axis_size("term")
    position = lax.axis_index("term")
    row_count = wavefunction.shape[1]
    sector_count = wavefunction.shape[0]
    width = wavefunction.shape[2]
    entries = float(sector_count * row_count * devices * width)
    own_count = live_count[0]
    diag_own = diagonal.astype(jnp.float32)
    whole_wave = lax.all_gather(wavefunction, "term", axis=1, tiled=True).astype(jnp.float32)
    scale = jnp.sqrt(jnp.sum(whole_wave * whole_wave) / entries)
    start_whole = whole_wave / scale
    empty_sum = jnp.zeros(start_whole.shape, jnp.float32)
    first_terms = block_loop(
        start_whole.astype(jnp.bfloat16),
        left_blocks,
        right_blocks,
        block_source,
        block_target,
        own_count,
        empty_sum,
    )
    row_start = position * row_count
    whole_diag = lax.all_gather(diagonal, "term", axis=1, tiled=True).astype(jnp.float32)
    first_whole = lax.psum(first_terms, "term") + whole_diag * start_whole
    ritz_value = jnp.sum(start_whole * first_whole) / entries
    correction = (first_whole - ritz_value * start_whole) / jnp.maximum(
        jnp.abs(whole_diag - ritz_value), 1.0
    )
    correlation = jnp.sum(start_whole * correction) / entries
    projected = correction - correlation * start_whole
    second_whole = projected / jnp.sqrt(jnp.sum(projected * projected) / entries)
    first_image = lax.dynamic_slice_in_dim(first_whole, row_start, row_count, 1)
    second_vector = lax.dynamic_slice_in_dim(second_whole, row_start, row_count, 1)
    second_rounded = second_whole.astype(jnp.bfloat16)
    second_terms = block_loop(
        second_rounded, left_blocks, right_blocks, block_source, block_target, own_count, empty_sum
    )
    second_image = (
        lax.psum_scatter(second_terms, "term", scatter_dimension=1, tiled=True)
        + diag_own * second_vector
    )
    return (first_image, second_vector, second_image)


def solution(mesh):
    placed = (
        P("grp", "term", None),
        P("grp", "term", None),
        P(("grp", "term"), None, None),
        P(("grp", "term"), None, None),
        P(("grp", "term")),
        P(("grp", "term")),
        P(("grp", "term")),
    )
    on_device = on_ring if mesh.shape["term"] == 16 else on_any
    return jax.shard_map(
        on_device,
        mesh=mesh,
        in_specs=placed,
        out_specs=(P("grp", "term", None), P("grp", "term", None), P("grp", "term", None)),
        check_vma=False,
    )
```

```python
import functools

import jax
import jax.numpy as jnp
from jax import lax
from jax.experimental import pallas as pl
from jax.experimental.pallas import tpu as pltpu
from jax.sharding import PartitionSpec as P

VMEM = pl.BlockSpec(memory_space=pltpu.VMEM)
SMEM = pl.BlockSpec(memory_space=pltpu.SMEM)
HBM = pl.BlockSpec(memory_space=pltpu.HBM)
PARAMS = pltpu.CompilerParams(vmem_limit_bytes=16 * 1024 * 1024)
READY_PARAMS = pltpu.CompilerParams(vmem_limit_bytes=48 * 1024 * 1024)
FIRST_PARAMS = pltpu.CompilerParams(vmem_limit_bytes=43 * 1024 * 1024)
HALF = 16
READY = 4
GROUP = 2
LANES = 128


def fold(value):
    rows, width = value.shape
    summed = jnp.sum(value.reshape(rows // 8, 8, width), axis=0)
    return sum(summed[:, k * 128 : (k + 1) * 128] for k in range(width // 128))


def down(value):
    return jnp.sum(value, axis=0, keepdims=True)


def halves(rows, width, start=0):
    for h in range(rows // HALF):
        yield h * HALF, slice(start + h * width, start + (h + 1) * width)


def write_lanes(ref, at, lanes):
    whole = jnp.broadcast_to(lanes, (HALF, LANES))
    high = whole.astype(jnp.bfloat16).astype(jnp.float32)
    rest = whole - high
    middle = rest.astype(jnp.bfloat16).astype(jnp.float32)
    low = rest - middle
    row = lax.broadcasted_iota(jnp.int32, whole.shape, 0)
    value = jnp.where(row == 0, high, jnp.where(row == 1, middle, jnp.where(row == 2, low, 0.0)))
    ref[:, at : at + LANES] = value.astype(jnp.bfloat16)


def read_lanes(ref, at):
    return down(ref[:, at : at + LANES].astype(jnp.float32))


def chip_at(place):
    place = lax.rem(place + 8, 8)
    return jnp.where(place < 4, 2 * place, 15 - 2 * place)


def ring_place(me):
    chip, core = me // 2, me % 2
    place = jnp.where(chip % 2 == 0, chip // 2, (15 - chip) // 2)
    return place, core


def ahead(me, distance, half, core=None):
    place, own = ring_place(me)
    core = own if core is None else core
    return chip_at(place + (1 - 2 * core) * distance) * 2 + half


ROUNDS = 3


def sent_devices(me, core):
    devices = []
    for k in range(ROUNDS):
        for half in (core, 1 - core):
            devices.append(ahead(me, ROUNDS - k, half, core))
    return devices + [ahead(me, 4, core, core), ahead(me, 0, core, core)]


def gathered_devices(me):
    core = me % 2
    devices = [ahead(me, 0, core), ahead(me, 0, 1 - core)]
    for k in range(1, ROUNDS + 1):
        devices += [ahead(me, -k, core), ahead(me, -k, 1 - core)]
        devices += [ahead(me, k, 1 - core), ahead(me, k, core)]
    return devices + [ahead(me, 4, core), ahead(me, 4, 1 - core)]


def message_parts(sectors, rows, width):
    for s in range(sectors):
        for row, part in halves(rows, width, s * (rows // HALF) * width):
            yield s, row, part


def message_shape(sectors, rows, width):
    return (HALF, rows // HALF * sectors * width + LANES)


def copy_kernel(in_ref, out_ref):
    out_ref[...] = in_ref[...]


def copied(value):
    return pl.pallas_call(
        copy_kernel,
        in_specs=[VMEM],
        out_specs=VMEM,
        out_shape=jax.ShapeDtypeStruct(value.shape, value.dtype),
        compiler_params=PARAMS,
        cost_estimate=pl.CostEstimate(flops=8 << 30, bytes_accessed=1 << 20, transcendentals=0),
    )(value)


def ready_kernel(left_in, right_in, _, left, right, left_sem, right_sem):
    copies = [
        pltpu.make_async_copy(left_in.at[pl.ds(0, READY)], left, left_sem),
        pltpu.make_async_copy(right_in.at[pl.ds(0, READY)], right, right_sem),
    ]
    for copy in copies:
        copy.start()
    for copy in copies:
        copy.wait()


def ready_blocks(left, right, after):
    shape = (READY, *left.shape[1:])
    return pl.pallas_call(
        ready_kernel,
        in_specs=[HBM] * 3,
        out_specs=[VMEM] * 2,
        out_shape=[jax.ShapeDtypeStruct(shape, b.dtype) for b in (left, right)],
        scratch_shapes=[pltpu.SemaphoreType.DMA] * 2,
        compiler_params=READY_PARAMS,
        cost_estimate=pl.CostEstimate(flops=2 << 30, bytes_accessed=4 << 20, transcendentals=0),
    )(left, right, after)


def square_kernel(wave_ref, diag_ref, square_ref):
    square = jnp.zeros((8, 128), jnp.float32)
    for s in range(wave_ref.shape[0]):
        wave = wave_ref[s].astype(jnp.float32)
        square += fold(diag_ref[s].astype(jnp.float32) * wave * wave)
    square_ref[...] = square


def weighted_square(wave, diag):
    return pl.pallas_call(
        square_kernel,
        in_specs=[VMEM, VMEM],
        out_specs=VMEM,
        out_shape=jax.ShapeDtypeStruct((8, 128), jnp.float32),
        compiler_params=PARAMS,
    )(wave, diag)


def blocks_kernel(first, shape, entries, me_ref, ints_ref, *refs):
    sectors, rows, width = shape
    field_refs, refs = refs[:16], refs[16:]
    if first:
        square_ref, left_ready, right_ready, *refs = refs
    else:
        scale_ref, wave_ref, correction_ref, *refs = refs
    left_in, right_in, *refs = refs
    total, near_ref, far_ref, dot_ref, out_ref, field, *refs = refs
    slots = left_in.shape[0]
    if first:
        left, right, left_sem, right_sem = refs

        def copies(slot):
            k = slot - READY
            return (
                pltpu.make_async_copy(left_in.at[slot], left.at[k], left_sem.at[k]),
                pltpu.make_async_copy(right_in.at[slot], right.at[k], right_sem.at[k]),
            )

        for slot in range(READY, slots):
            for copy in copies(slot):
                copy.start()
    else:
        left, right = left_in, right_in

    me = me_ref[0]
    core = me % 2

    pieces = []
    for k, owner in enumerate(gathered_devices(me)):
        at = pl.multiple_of(owner * rows, rows)
        if first:
            for s in range(sectors):
                pieces.append((k, (s,), s, pl.ds(at, rows)))
        else:
            for s, row, part in message_parts(sectors, rows, width):
                pieces.append((k, (slice(None), part), s, pl.ds(at + row, HALF)))

    total[...] = jnp.zeros_like(total)
    if first:
        dot = jnp.zeros((8, 128), jnp.float32)
        for k, part, _, _ in pieces:
            value = field_refs[k][part].astype(jnp.float32)
            dot += fold(value * value)
        scale = jnp.sqrt(jnp.sum(dot) / entries)
        inverse = 1.0 / scale
        out_ref[...] = jnp.full(out_ref.shape, scale, jnp.float32)
        for k, part, s, at in pieces:
            field[s, at, :] = (field_refs[k][part].astype(jnp.float32) * inverse).astype(jnp.bfloat16)
    else:
        for k, part, s, at in pieces:
            field[s, at, :] = field_refs[k][part]

    used = ints_ref[2 * slots]

    def add_some(left, right, start, copied_here, step, carry):
        some = [step * GROUP + k for k in range(GROUP)]
        if copied_here:
            for slot in some:
                for copy in copies(slot):
                    copy.wait()

        @pl.when(some[0] < used)
        def _():
            products = [
                jnp.dot(
                    left[slot - start], field[ints_ref[slot]], preferred_element_type=jnp.float32
                ).astype(jnp.bfloat16)
                for slot in some
            ]
            for slot, product in zip(some, products):
                if slot is not some[0]:
                    product = jnp.where(slot < used, product, jnp.zeros_like(product))
                total[ints_ref[slots + slot]] += lax.dot_general(
                    product,
                    right[slot - start],
                    (((1,), (1,)), ((), ())),
                    preferred_element_type=jnp.float32,
                )

        return carry

    if first:
        early = functools.partial(add_some, left_ready, right_ready, 0, False)
        late = functools.partial(add_some, left, right, READY, True)
        lax.fori_loop(0, READY // GROUP, early, 0)
        lax.fori_loop(READY // GROUP, slots // GROUP, late, 0)
    else:
        lax.fori_loop(0, slots // GROUP, functools.partial(add_some, left, right, 0, False), 0)

    dot = jnp.zeros((8, 128), jnp.float32)
    if first:
        for k, part, s, at in pieces:
            dot += fold(total[s, at, :] * field_refs[k][part].astype(jnp.float32))
        dot = dot * inverse + square_ref[...] * inverse * inverse
    else:
        at = message_shape(*shape)[1] - LANES
        lanes = sum(
            ref[:, at : at + LANES].astype(jnp.float32) for ref in field_refs
        )
        along = jnp.sum(lanes) / entries
        out_ref[...] = jnp.full(out_ref.shape, along, jnp.float32)
        inverse = 1.0 / scale_ref[0:1, 0:1]
        for s in range(sectors):
            projected = correction_ref[s] - along * (wave_ref[s].astype(jnp.float32) * inverse)
            dot += fold(projected * projected)
    dot_ref[...] = dot
    lanes = down(dot)
    for k, owner in enumerate(sent_devices(me, 1 - core)):
        at = pl.multiple_of(owner * rows, rows)
        ref = near_ref.at[k] if k < near_ref.shape[0] else far_ref.at[k - near_ref.shape[0]]
        for s, row, part in message_parts(*shape):
            ref[:, part] = total[s, pl.ds(at + row, HALF), :].astype(jnp.bfloat16)
        write_lanes(ref, ref.shape[1] - LANES, lanes)


def apply_blocks(me, ints, fields, own, left, right, shape, first, entries):
    slots, order, width = left.shape
    sectors = shape[0]
    message = message_shape(*shape)
    scratch = []
    if first:
        scratch = [pltpu.VMEM((slots - READY, *b.shape[1:]), b.dtype) for b in (left, right)]
        scratch += [pltpu.SemaphoreType.DMA((slots - READY,))] * 2
    return pl.pallas_call(
        functools.partial(blocks_kernel, first, shape, entries),
        in_specs=[SMEM, SMEM]
        + [VMEM] * (len(fields) + len(own))
        + [HBM if first else VMEM] * 2,
        out_specs=[VMEM] * 5,
        scratch_shapes=[pltpu.VMEM((sectors, order, width), jnp.bfloat16)] + scratch,
        out_shape=[
            jax.ShapeDtypeStruct((sectors, order, width), jnp.float32),
            jax.ShapeDtypeStruct((2, *message), jnp.bfloat16),
            jax.ShapeDtypeStruct((2 * ROUNDS, *message), jnp.bfloat16),
            jax.ShapeDtypeStruct((8, 128), jnp.float32),
            jax.ShapeDtypeStruct((8, 128), jnp.float32),
        ],
        compiler_params=FIRST_PARAMS if first else PARAMS,
        cost_estimate=pl.CostEstimate(
            flops=4 * slots * order * order * width,
            bytes_accessed=4 * slots * order * order,
            transcendentals=0,
        ),
    )(me, ints, *fields, *own, left, right)


def chain_kernel(shape, k, index, me_ref, total_ref, dot_ref, other_ref, *refs):
    *arrived_refs, out_ref = refs
    _, rows, _ = shape
    me = me_ref[0]
    start = pl.multiple_of(sent_devices(me, me % 2)[k] * rows, rows)
    for s, row, part in message_parts(*shape):
        value = total_ref[s, pl.ds(start + row, HALF), :]
        value += other_ref[index, :, part].astype(jnp.float32)
        for ref in arrived_refs:
            value += ref[:, part].astype(jnp.float32)
        out_ref[:, part] = value.astype(jnp.bfloat16)
    at = out_ref.shape[1] - LANES
    lanes = down(dot_ref[...]) + read_lanes(other_ref.at[index], at)
    for ref in arrived_refs:
        lanes += read_lanes(ref, at)
    write_lanes(out_ref, at, lanes)


def chain(shape, k, index, me, total, dot, other, *arrived):
    return pl.pallas_call(
        functools.partial(chain_kernel, shape, k, index),
        in_specs=[SMEM] + [VMEM] * (3 + len(arrived)),
        out_specs=VMEM,
        out_shape=jax.ShapeDtypeStruct(message_shape(*shape), jnp.bfloat16),
        compiler_params=PARAMS,
    )(me, total, dot, other, *arrived)


def own_terms(shape, sector, me_ref, total_ref, other_ref, _, *arrived_refs):
    start = pl.multiple_of(me_ref[0] * shape[1], shape[1])
    values = []
    for s, row, part in message_parts(*shape):
        if s == sector:
            value = total_ref[s, pl.ds(start + row, HALF), :]
            value += other_ref[other_ref.shape[0] - 1, :, part].astype(jnp.float32)
            for ref in arrived_refs:
                value += ref[:, part].astype(jnp.float32)
            values.append(value)
    return jnp.concatenate(values, axis=0)


def own_scalar(me_ref, total_ref, other_ref, dot_ref, *arrived_refs):
    at = other_ref.shape[2] - LANES
    lanes = down(dot_ref[...]) + read_lanes(other_ref.at[other_ref.shape[0] - 1], at)
    return jnp.sum(lanes + sum(read_lanes(ref, at) for ref in arrived_refs))


def step_kernel(entries, scale_ref, wave_ref, diag_ref, *refs):
    *sums, first_ref, terms_ref, correction_ref, message_ref = refs
    shape = wave_ref.shape
    ritz = own_scalar(*sums) / entries
    inverse = 1.0 / scale_ref[0:1, 0:1]
    dots = jnp.zeros((8, 128), jnp.float32)
    for s in range(shape[0]):
        start = wave_ref[s].astype(jnp.float32) * inverse
        diag = diag_ref[s].astype(jnp.float32)
        terms = own_terms(shape, s, *sums)
        first = terms + diag * start
        correction = (first - ritz * start) / jnp.maximum(jnp.abs(diag - ritz), 1.0)
        first_ref[s] = first
        terms_ref[s] = terms
        correction_ref[s] = correction
        dots += fold(start * correction)
        for t, row, part in message_parts(*shape):
            if t == s:
                message_ref[:, part] = correction[row : row + HALF].astype(jnp.bfloat16)
    write_lanes(message_ref, message_ref.shape[1] - LANES, down(dots))


def davidson_step(scale, wave, diag, sums, entries):
    full = jax.ShapeDtypeStruct(wave.shape, jnp.float32)
    return pl.pallas_call(
        functools.partial(step_kernel, entries),
        in_specs=[VMEM] * 3 + [SMEM] + [VMEM] * (len(sums) - 1),
        out_specs=[VMEM] * 4,
        out_shape=[full, full, full, jax.ShapeDtypeStruct(message_shape(*wave.shape), jnp.bfloat16)],
        compiler_params=PARAMS,
    )(scale, wave, diag, *sums)


def finish_kernel(entries, along_ref, scale_ref, wave_ref, diag_ref, *refs):
    terms_ref, correction_ref, *sums, vector_ref, image_ref = refs
    shape = wave_ref.shape
    along = along_ref[0:1, 0:1]
    norm = jnp.sqrt(jnp.full((1, 1), own_scalar(*sums) / entries, jnp.float32))
    inverse = 1.0 / norm
    start_scale = 1.0 / scale_ref[0:1, 0:1]
    for s in range(shape[0]):
        start = wave_ref[s].astype(jnp.float32) * start_scale
        second = (correction_ref[s] - along * start) * inverse
        vector_ref[s] = second
        image = (own_terms(shape, s, *sums) - along * terms_ref[s]) * inverse
        image_ref[s] = image + diag_ref[s].astype(jnp.float32) * second


def finish(along, scale, wave, diag, terms, correction, sums, entries):
    full = jax.ShapeDtypeStruct(wave.shape, jnp.float32)
    return pl.pallas_call(
        functools.partial(finish_kernel, entries),
        in_specs=[VMEM] * 6 + [SMEM] + [VMEM] * (len(sums) - 1),
        out_specs=[VMEM] * 2,
        out_shape=[full, full],
        compiler_params=PARAMS,
    )(along, scale, wave, diag, terms, correction, *sums)


def flip(value):
    return lax.ppermute(value, "term", [(i, i ^ 1) for i in range(16)])


def hop(value, up=1, down=-1):
    order = [0, 2, 4, 6, 7, 5, 3, 1]
    pairs = []
    for place in range(8):
        for core, step in ((0, up), (1, down)):
            pairs.append((order[place] * 2 + core, order[(place + step) % 8] * 2 + core))
    return lax.ppermute(value, "term", pairs)


def opposite(value):
    return hop(value, 4, 4)


def gather(own, beside=(), blocks=()):
    one, two = own, flip(own)
    across, two = lax.optimization_barrier((own, two))
    pieces = [one, two]
    across = opposite(across)
    results = []
    for k in range(ROUNDS):
        one, two = hop(one), hop(two)
        if k < len(beside):
            results.append(beside[k](*results))
        if k < ROUNDS - 1:
            ready = results[-1:] if beside else []
            two, ready = lax.optimization_barrier((two, ready))
            if ready:
                results[-1] = ready[0]
        if k == 1 and blocks:
            blocks = ready_blocks(*blocks, two)
            across, blocks = lax.optimization_barrier((across, blocks))
        pieces += [one, two, flip(one), flip(two)]
    return pieces + [across, flip(across)], results, blocks


def scatter(shape, me, total, near, far, dot):
    near = flip(near)
    near, far = lax.optimization_barrier((near, far))
    far = flip(far)
    one = hop(chain(shape, 0, 0, me, total, dot, near))
    two = hop(chain(shape, 1, 1, me, total, dot, near))
    across = opposite(chain(shape, 6, 4, me, total, dot, far))
    for k in (2, 4):
        one = hop(chain(shape, k, k - 2, me, total, dot, far, one))
        if k == 4:
            two, across = lax.optimization_barrier((two, across))
        two = hop(chain(shape, k + 1, k - 1, me, total, dot, far, two))
    return me, total, far, dot, one, flip(two), across


def on_ring(
    wavefunction, diagonal, left_blocks, right_blocks, block_source, block_target, live_count
):
    shape = wavefunction.shape
    sectors, rows, width = shape
    entries = float(sectors * rows * lax.axis_size("term") * width)
    me = lax.axis_index("term").astype(jnp.int32).reshape(1)
    beside = (
        lambda: jnp.concatenate([block_source, block_target, live_count]),
        lambda _: copied(wavefunction),
        lambda _, own: weighted_square(own, diagonal),
    )
    (_, *fields), (ints, own, square), ready = gather(
        wavefunction, beside, (left_blocks, right_blocks)
    )
    fields = [own, *fields]
    blocks = (left_blocks, right_blocks, shape)
    total, near, far, dot, scale = apply_blocks(
        me, ints, fields, (square, *ready), *blocks, True, entries
    )
    first_image, terms, correction, message = davidson_step(
        scale, wavefunction, diagonal, scatter(shape, me, total, near, far, dot), entries
    )
    fields, *_ = gather(message)
    own = (scale, wavefunction, correction)
    total, near, far, dot, along = apply_blocks(me, ints, fields, own, *blocks, False, entries)
    second_vector, second_image = finish(
        along, scale, wavefunction, diagonal, terms, correction,
        scatter(shape, me, total, near, far, dot), entries,
    )
    return (first_image, second_vector, second_image)


def block_loop(field_rounded, left_ops, right_ops, sources, targets, last_slot, partial_sum):

    def add_block(slot_index, running):
        left_op = lax.dynamic_index_in_dim(left_ops, slot_index, 0, keepdims=False)
        right_op = lax.dynamic_index_in_dim(right_ops, slot_index, 0, keepdims=False)
        source = lax.dynamic_index_in_dim(sources, slot_index, 0, keepdims=False)
        target = lax.dynamic_index_in_dim(targets, slot_index, 0, keepdims=False)
        piece = lax.dynamic_index_in_dim(field_rounded, source, 0, keepdims=False)
        product = jnp.dot(left_op, piece, preferred_element_type=jnp.float32).astype(jnp.bfloat16)
        term_value = jnp.dot(product, right_op.T, preferred_element_type=jnp.float32)
        before = lax.dynamic_index_in_dim(running, target, 0, keepdims=False)
        return lax.dynamic_update_index_in_dim(running, before + term_value, target, 0)

    return lax.fori_loop(0, last_slot, add_block, partial_sum)


def on_any(
    wavefunction, diagonal, left_blocks, right_blocks, block_source, block_target, live_count
):
    devices = lax.axis_size("term")
    position = lax.axis_index("term")
    row_count = wavefunction.shape[1]
    sector_count = wavefunction.shape[0]
    width = wavefunction.shape[2]
    entries = float(sector_count * row_count * devices * width)
    own_count = live_count[0]
    diag_own = diagonal.astype(jnp.float32)
    whole_wave = lax.all_gather(wavefunction, "term", axis=1, tiled=True).astype(jnp.float32)
    scale = jnp.sqrt(jnp.sum(whole_wave * whole_wave) / entries)
    start_whole = whole_wave / scale
    empty_sum = jnp.zeros(start_whole.shape, jnp.float32)
    first_terms = block_loop(
        start_whole.astype(jnp.bfloat16),
        left_blocks,
        right_blocks,
        block_source,
        block_target,
        own_count,
        empty_sum,
    )
    row_start = position * row_count
    whole_diag = lax.all_gather(diagonal, "term", axis=1, tiled=True).astype(jnp.float32)
    first_whole = lax.psum(first_terms, "term") + whole_diag * start_whole
    ritz_value = jnp.sum(start_whole * first_whole) / entries
    correction = (first_whole - ritz_value * start_whole) / jnp.maximum(
        jnp.abs(whole_diag - ritz_value), 1.0
    )
    correlation = jnp.sum(start_whole * correction) / entries
    projected = correction - correlation * start_whole
    second_whole = projected / jnp.sqrt(jnp.sum(projected * projected) / entries)
    first_image = lax.dynamic_slice_in_dim(first_whole, row_start, row_count, 1)
    second_vector = lax.dynamic_slice_in_dim(second_whole, row_start, row_count, 1)
    second_rounded = second_whole.astype(jnp.bfloat16)
    second_terms = block_loop(
        second_rounded, left_blocks, right_blocks, block_source, block_target, own_count, empty_sum
    )
    second_image = (
        lax.psum_scatter(second_terms, "term", scatter_dimension=1, tiled=True)
        + diag_own * second_vector
    )
    return (first_image, second_vector, second_image)


def solution(mesh):
    placed = (
        P("grp", "term", None),
        P("grp", "term", None),
        P(("grp", "term"), None, None),
        P(("grp", "term"), None, None),
        P(("grp", "term")),
        P(("grp", "term")),
        P(("grp", "term")),
    )
    on_device = on_ring if mesh.shape["term"] == 16 else on_any
    return jax.shard_map(
        on_device,
        mesh=mesh,
        in_specs=placed,
        out_specs=(P("grp", "term", None), P("grp", "term", None), P("grp", "term", None)),
        check_vma=False,
    )
```

```python
import functools

import jax
import jax.numpy as jnp
from jax import lax
from jax.experimental import pallas as pl
from jax.experimental.pallas import tpu as pltpu
from jax.sharding import PartitionSpec as P

VMEM = pl.BlockSpec(memory_space=pltpu.VMEM)
SMEM = pl.BlockSpec(memory_space=pltpu.SMEM)
HBM = pl.BlockSpec(memory_space=pltpu.HBM)
PARAMS = pltpu.CompilerParams(vmem_limit_bytes=16 * 1024 * 1024)
READY_PARAMS = pltpu.CompilerParams(vmem_limit_bytes=48 * 1024 * 1024)
FIRST_PARAMS = pltpu.CompilerParams(vmem_limit_bytes=44 * 1024 * 1024)
HALF = 16
READY = 2
GROUP = 2
LANES = 128


def fold(value):
    rows, width = value.shape
    summed = jnp.sum(value.reshape(rows // 8, 8, width), axis=0)
    return sum(summed[:, k * 128 : (k + 1) * 128] for k in range(width // 128))


def down(value):
    return jnp.sum(value, axis=0, keepdims=True)


def halves(rows, width, start=0):
    for h in range(rows // HALF):
        yield h * HALF, slice(start + h * width, start + (h + 1) * width)


def write_lanes(ref, at, lanes):
    whole = jnp.broadcast_to(lanes, (HALF, LANES))
    high = whole.astype(jnp.bfloat16).astype(jnp.float32)
    rest = whole - high
    middle = rest.astype(jnp.bfloat16).astype(jnp.float32)
    low = rest - middle
    row = lax.broadcasted_iota(jnp.int32, whole.shape, 0)
    value = jnp.where(row == 0, high, jnp.where(row == 1, middle, jnp.where(row == 2, low, 0.0)))
    ref[:, at : at + LANES] = value.astype(jnp.bfloat16)


def read_lanes(ref, at):
    return down(ref[:, at : at + LANES].astype(jnp.float32))


def chip_at(place):
    place = lax.rem(place + 8, 8)
    return jnp.where(place < 4, 2 * place, 15 - 2 * place)


def ring_place(me):
    chip, core = me // 2, me % 2
    place = jnp.where(chip % 2 == 0, chip // 2, (15 - chip) // 2)
    return place, core


def ahead(me, distance, half, core=None):
    place, own = ring_place(me)
    core = own if core is None else core
    return chip_at(place + (1 - 2 * core) * distance) * 2 + half


ROUNDS = 3


def sent_devices(me, core):
    devices = []
    for k in range(ROUNDS):
        for half in (core, 1 - core):
            devices.append(ahead(me, ROUNDS - k, half, core))
    return devices + [ahead(me, 4, core, core), ahead(me, 0, core, core)]


def gathered_devices(me):
    core = me % 2
    devices = [ahead(me, 0, core), ahead(me, 0, 1 - core)]
    for k in range(1, ROUNDS + 1):
        devices += [ahead(me, -k, core), ahead(me, -k, 1 - core)]
        devices += [ahead(me, k, 1 - core), ahead(me, k, core)]
    return devices + [ahead(me, 4, core), ahead(me, 4, 1 - core)]


def message_parts(sectors, rows, width):
    for s in range(sectors):
        for row, part in halves(rows, width, s * (rows // HALF) * width):
            yield s, row, part


def message_shape(sectors, rows, width):
    return (HALF, rows // HALF * sectors * width + LANES)


def copy_kernel(in_ref, out_ref):
    out_ref[...] = in_ref[...]


def copied(value):
    return pl.pallas_call(
        copy_kernel,
        in_specs=[VMEM],
        out_specs=VMEM,
        out_shape=jax.ShapeDtypeStruct(value.shape, value.dtype),
        compiler_params=PARAMS,
        cost_estimate=pl.CostEstimate(flops=8 << 30, bytes_accessed=1 << 20, transcendentals=0),
    )(value)


def ready_kernel(left_in, right_in, _, left, right, left_sem, right_sem):
    copies = [
        pltpu.make_async_copy(left_in.at[pl.ds(0, READY)], left, left_sem),
        pltpu.make_async_copy(right_in.at[pl.ds(0, READY)], right, right_sem),
    ]
    for copy in copies:
        copy.start()
    for copy in copies:
        copy.wait()


def ready_blocks(left, right, after):
    shape = (READY, *left.shape[1:])
    return pl.pallas_call(
        ready_kernel,
        in_specs=[HBM] * 3,
        out_specs=[VMEM] * 2,
        out_shape=[jax.ShapeDtypeStruct(shape, b.dtype) for b in (left, right)],
        scratch_shapes=[pltpu.SemaphoreType.DMA] * 2,
        compiler_params=READY_PARAMS,
        cost_estimate=pl.CostEstimate(flops=2 << 30, bytes_accessed=4 << 20, transcendentals=0),
    )(left, right, after)


def square_kernel(wave_ref, diag_ref, square_ref, own_ref):
    own_ref[...] = diag_ref[...]
    square = jnp.zeros((8, 128), jnp.float32)
    for s in range(wave_ref.shape[0]):
        wave = wave_ref[s].astype(jnp.float32)
        square += fold(diag_ref[s].astype(jnp.float32) * wave * wave)
    square_ref[...] = square


def weighted_square(wave, diag):
    return pl.pallas_call(
        square_kernel,
        in_specs=[VMEM, VMEM],
        out_specs=[VMEM, VMEM],
        out_shape=[
            jax.ShapeDtypeStruct((8, 128), jnp.float32),
            jax.ShapeDtypeStruct(diag.shape, diag.dtype),
        ],
        compiler_params=PARAMS,
    )(wave, diag)


def blocks_kernel(first, shape, entries, me_ref, ints_ref, *refs):
    sectors, rows, width = shape
    field_refs, refs = refs[:16], refs[16:]
    if first:
        square_ref, left_ready, right_ready, *refs = refs
    else:
        scale_ref, wave_ref, correction_ref, *refs = refs
    left_in, right_in, *refs = refs
    total, near_ref, far_ref, dot_ref, out_ref, field, *refs = refs
    slots = left_in.shape[0]
    if first:
        left, right, left_sem, right_sem = refs

        def copies(slot):
            k = slot - READY
            return (
                pltpu.make_async_copy(left_in.at[slot], left.at[k], left_sem.at[k]),
                pltpu.make_async_copy(right_in.at[slot], right.at[k], right_sem.at[k]),
            )

        for slot in range(READY, slots):
            for copy in copies(slot):
                copy.start()
    else:
        left, right = left_in, right_in

    me = me_ref[0]
    core = me % 2

    pieces = []
    for k, owner in enumerate(gathered_devices(me)):
        at = pl.multiple_of(owner * rows, rows)
        if first:
            for s in range(sectors):
                pieces.append((k, (s,), s, pl.ds(at, rows)))
        else:
            for s, row, part in message_parts(sectors, rows, width):
                pieces.append((k, (slice(None), part), s, pl.ds(at + row, HALF)))

    total[...] = jnp.zeros_like(total)
    if first:
        dot = jnp.zeros((8, 128), jnp.float32)
        for k, part, _, _ in pieces:
            value = field_refs[k][part].astype(jnp.float32)
            dot += fold(value * value)
        scale = jnp.sqrt(jnp.sum(dot) / entries)
        inverse = 1.0 / scale
        out_ref[...] = jnp.full(out_ref.shape, scale, jnp.float32)
        for k, part, s, at in pieces:
            field[s, at, :] = (field_refs[k][part].astype(jnp.float32) * inverse).astype(jnp.bfloat16)
    else:
        for k, part, s, at in pieces:
            field[s, at, :] = field_refs[k][part]

    used = ints_ref[2 * slots]

    def add_some(left, right, start, copied_here, step, carry):
        some = [step * GROUP + k for k in range(GROUP)]
        if copied_here:
            for slot in some:
                for copy in copies(slot):
                    copy.wait()

        @pl.when(some[0] < used)
        def _():
            products = [
                jnp.dot(
                    left[slot - start], field[ints_ref[slot]], preferred_element_type=jnp.float32
                ).astype(jnp.bfloat16)
                for slot in some
            ]
            for slot, product in zip(some, products):
                if slot is not some[0]:
                    product = jnp.where(slot < used, product, jnp.zeros_like(product))
                total[ints_ref[slots + slot]] += lax.dot_general(
                    product,
                    right[slot - start],
                    (((1,), (1,)), ((), ())),
                    preferred_element_type=jnp.float32,
                )

        return carry

    if first:
        early = functools.partial(add_some, left_ready, right_ready, 0, False)
        late = functools.partial(add_some, left, right, READY, True)
        lax.fori_loop(0, READY // GROUP, early, 0)
        lax.fori_loop(READY // GROUP, slots // GROUP, late, 0)
    else:
        lax.fori_loop(0, slots // GROUP, functools.partial(add_some, left, right, 0, False), 0)

    dot = jnp.zeros((8, 128), jnp.float32)
    if first:
        for k, part, s, at in pieces:
            dot += fold(total[s, at, :] * field_refs[k][part].astype(jnp.float32))
        dot = dot * inverse + square_ref[...] * inverse * inverse
    else:
        at = message_shape(*shape)[1] - LANES
        lanes = sum(
            ref[:, at : at + LANES].astype(jnp.float32) for ref in field_refs
        )
        along = jnp.sum(lanes) / entries
        out_ref[...] = jnp.full(out_ref.shape, along, jnp.float32)
        inverse = 1.0 / scale_ref[0:1, 0:1]
        for s in range(sectors):
            projected = correction_ref[s] - along * (wave_ref[s].astype(jnp.float32) * inverse)
            dot += fold(projected * projected)
    dot_ref[...] = dot
    lanes = down(dot)
    for k, owner in enumerate(sent_devices(me, 1 - core)):
        at = pl.multiple_of(owner * rows, rows)
        ref = near_ref.at[k] if k < near_ref.shape[0] else far_ref.at[k - near_ref.shape[0]]
        for s, row, part in message_parts(*shape):
            ref[:, part] = total[s, pl.ds(at + row, HALF), :].astype(jnp.bfloat16)
        write_lanes(ref, ref.shape[1] - LANES, lanes)


def apply_blocks(me, ints, fields, own, left, right, shape, first, entries):
    slots, order, width = left.shape
    sectors = shape[0]
    message = message_shape(*shape)
    scratch = []
    if first:
        scratch = [pltpu.VMEM((slots - READY, *b.shape[1:]), b.dtype) for b in (left, right)]
        scratch += [pltpu.SemaphoreType.DMA((slots - READY,))] * 2
    return pl.pallas_call(
        functools.partial(blocks_kernel, first, shape, entries),
        in_specs=[SMEM, SMEM]
        + [VMEM] * (len(fields) + len(own))
        + [HBM if first else VMEM] * 2,
        out_specs=[VMEM] * 5,
        scratch_shapes=[pltpu.VMEM((sectors, order, width), jnp.bfloat16)] + scratch,
        out_shape=[
            jax.ShapeDtypeStruct((sectors, order, width), jnp.float32),
            jax.ShapeDtypeStruct((2, *message), jnp.bfloat16),
            jax.ShapeDtypeStruct((2 * ROUNDS, *message), jnp.bfloat16),
            jax.ShapeDtypeStruct((8, 128), jnp.float32),
            jax.ShapeDtypeStruct((8, 128), jnp.float32),
        ],
        compiler_params=FIRST_PARAMS if first else PARAMS,
        cost_estimate=pl.CostEstimate(
            flops=4 * slots * order * order * width,
            bytes_accessed=4 * slots * order * order,
            transcendentals=0,
        ),
    )(me, ints, *fields, *own, left, right)


def chain_kernel(shape, k, index, me_ref, total_ref, dot_ref, other_ref, *refs):
    *arrived_refs, out_ref = refs
    _, rows, _ = shape
    me = me_ref[0]
    start = pl.multiple_of(sent_devices(me, me % 2)[k] * rows, rows)
    for s, row, part in message_parts(*shape):
        value = total_ref[s, pl.ds(start + row, HALF), :]
        value += other_ref[index, :, part].astype(jnp.float32)
        for ref in arrived_refs:
            value += ref[:, part].astype(jnp.float32)
        out_ref[:, part] = value.astype(jnp.bfloat16)
    at = out_ref.shape[1] - LANES
    lanes = down(dot_ref[...]) + read_lanes(other_ref.at[index], at)
    for ref in arrived_refs:
        lanes += read_lanes(ref, at)
    write_lanes(out_ref, at, lanes)


def chain(shape, k, index, me, total, dot, other, *arrived):
    return pl.pallas_call(
        functools.partial(chain_kernel, shape, k, index),
        in_specs=[SMEM] + [VMEM] * (3 + len(arrived)),
        out_specs=VMEM,
        out_shape=jax.ShapeDtypeStruct(message_shape(*shape), jnp.bfloat16),
        compiler_params=PARAMS,
    )(me, total, dot, other, *arrived)


def own_terms(shape, sector, me_ref, total_ref, other_ref, _, *arrived_refs):
    start = pl.multiple_of(me_ref[0] * shape[1], shape[1])
    values = []
    for s, row, part in message_parts(*shape):
        if s == sector:
            value = total_ref[s, pl.ds(start + row, HALF), :]
            value += other_ref[other_ref.shape[0] - 1, :, part].astype(jnp.float32)
            for ref in arrived_refs:
                value += ref[:, part].astype(jnp.float32)
            values.append(value)
    return jnp.concatenate(values, axis=0)


def own_scalar(me_ref, total_ref, other_ref, dot_ref, *arrived_refs):
    at = other_ref.shape[2] - LANES
    lanes = down(dot_ref[...]) + read_lanes(other_ref.at[other_ref.shape[0] - 1], at)
    return jnp.sum(lanes + sum(read_lanes(ref, at) for ref in arrived_refs))


def step_kernel(entries, scale_ref, wave_ref, diag_ref, *refs):
    *sums, first_ref, terms_ref, correction_ref, message_ref = refs
    shape = wave_ref.shape
    ritz = own_scalar(*sums) / entries
    inverse = 1.0 / scale_ref[0:1, 0:1]
    dots = jnp.zeros((8, 128), jnp.float32)
    for s in range(shape[0]):
        start = wave_ref[s].astype(jnp.float32) * inverse
        diag = diag_ref[s].astype(jnp.float32)
        terms = own_terms(shape, s, *sums)
        first = terms + diag * start
        correction = (first - ritz * start) / jnp.maximum(jnp.abs(diag - ritz), 1.0)
        first_ref[s] = first
        terms_ref[s] = terms
        correction_ref[s] = correction
        dots += fold(start * correction)
        for t, row, part in message_parts(*shape):
            if t == s:
                message_ref[:, part] = correction[row : row + HALF].astype(jnp.bfloat16)
    write_lanes(message_ref, message_ref.shape[1] - LANES, down(dots))


def davidson_step(scale, wave, diag, sums, entries):
    full = jax.ShapeDtypeStruct(wave.shape, jnp.float32)
    return pl.pallas_call(
        functools.partial(step_kernel, entries),
        in_specs=[VMEM] * 3 + [SMEM] + [VMEM] * (len(sums) - 1),
        out_specs=[VMEM] * 4,
        out_shape=[full, full, full, jax.ShapeDtypeStruct(message_shape(*wave.shape), jnp.bfloat16)],
        compiler_params=PARAMS,
    )(scale, wave, diag, *sums)


def finish_kernel(entries, along_ref, scale_ref, wave_ref, diag_ref, *refs):
    terms_ref, correction_ref, *sums, vector_ref, image_ref = refs
    shape = wave_ref.shape
    along = along_ref[0:1, 0:1]
    norm = jnp.sqrt(jnp.full((1, 1), own_scalar(*sums) / entries, jnp.float32))
    inverse = 1.0 / norm
    start_scale = 1.0 / scale_ref[0:1, 0:1]
    for s in range(shape[0]):
        start = wave_ref[s].astype(jnp.float32) * start_scale
        second = (correction_ref[s] - along * start) * inverse
        vector_ref[s] = second
        image = (own_terms(shape, s, *sums) - along * terms_ref[s]) * inverse
        image_ref[s] = image + diag_ref[s].astype(jnp.float32) * second


def finish(along, scale, wave, diag, terms, correction, sums, entries):
    full = jax.ShapeDtypeStruct(wave.shape, jnp.float32)
    return pl.pallas_call(
        functools.partial(finish_kernel, entries),
        in_specs=[VMEM] * 6 + [SMEM] + [VMEM] * (len(sums) - 1),
        out_specs=[VMEM] * 2,
        out_shape=[full, full],
        compiler_params=PARAMS,
    )(along, scale, wave, diag, terms, correction, *sums)


def flip(value):
    return lax.ppermute(value, "term", [(i, i ^ 1) for i in range(16)])


def hop(value, up=1, down=-1):
    order = [0, 2, 4, 6, 7, 5, 3, 1]
    pairs = []
    for place in range(8):
        for core, step in ((0, up), (1, down)):
            pairs.append((order[place] * 2 + core, order[(place + step) % 8] * 2 + core))
    return lax.ppermute(value, "term", pairs)


def opposite(value):
    return hop(value, 4, 4)


def gather(own, beside=(), blocks=()):
    one, two = own, flip(own)
    across, two = lax.optimization_barrier((own, two))
    pieces = [one, two]
    across = opposite(across)
    results = []
    for k in range(ROUNDS):
        one, two = hop(one), hop(two)
        if k < len(beside):
            results.append(beside[k](*results))
        if k < ROUNDS - 1:
            ready = results[-1:] if beside else []
            two, ready = lax.optimization_barrier((two, ready))
            if ready:
                results[-1] = ready[0]
        if k == 1 and blocks:
            blocks = ready_blocks(*blocks, two)
            across, blocks = lax.optimization_barrier((across, blocks))
        pieces += [one, two, flip(one), flip(two)]
    return pieces + [across, flip(across)], results, blocks


def scatter(shape, me, total, near, far, dot):
    near = flip(near)
    near, far = lax.optimization_barrier((near, far))
    far = flip(far)
    one = hop(chain(shape, 0, 0, me, total, dot, near))
    two = hop(chain(shape, 1, 1, me, total, dot, near))
    across = opposite(chain(shape, 6, 4, me, total, dot, far))
    for k in (2, 4):
        one = hop(chain(shape, k, k - 2, me, total, dot, far, one))
        if k == 4:
            two, across = lax.optimization_barrier((two, across))
        two = hop(chain(shape, k + 1, k - 1, me, total, dot, far, two))
    return me, total, far, dot, one, flip(two), across


def on_ring(
    wavefunction, diagonal, left_blocks, right_blocks, block_source, block_target, live_count
):
    shape = wavefunction.shape
    sectors, rows, width = shape
    entries = float(sectors * rows * lax.axis_size("term") * width)
    me = lax.axis_index("term").astype(jnp.int32).reshape(1)
    beside = (
        lambda: jnp.concatenate([block_source, block_target, live_count]),
        lambda _: copied(wavefunction),
        lambda _, own: weighted_square(own, diagonal),
    )
    (_, *fields), (ints, wave, (square, diag)), ready = gather(
        wavefunction, beside, (left_blocks, right_blocks)
    )
    fields = [wave, *fields]
    blocks = (left_blocks, right_blocks, shape)
    total, near, far, dot, scale = apply_blocks(
        me, ints, fields, (square, *ready), *blocks, True, entries
    )
    first_image, terms, correction, message = davidson_step(
        scale, wave, diag, scatter(shape, me, total, near, far, dot), entries
    )
    fields, *_ = gather(message)
    own = (scale, wave, correction)
    total, near, far, dot, along = apply_blocks(me, ints, fields, own, *blocks, False, entries)
    second_vector, second_image = finish(
        along, scale, wave, diag, terms, correction,
        scatter(shape, me, total, near, far, dot), entries,
    )
    return (first_image, second_vector, second_image)


def block_loop(field_rounded, left_ops, right_ops, sources, targets, last_slot, partial_sum):

    def add_block(slot_index, running):
        left_op = lax.dynamic_index_in_dim(left_ops, slot_index, 0, keepdims=False)
        right_op = lax.dynamic_index_in_dim(right_ops, slot_index, 0, keepdims=False)
        source = lax.dynamic_index_in_dim(sources, slot_index, 0, keepdims=False)
        target = lax.dynamic_index_in_dim(targets, slot_index, 0, keepdims=False)
        piece = lax.dynamic_index_in_dim(field_rounded, source, 0, keepdims=False)
        product = jnp.dot(left_op, piece, preferred_element_type=jnp.float32).astype(jnp.bfloat16)
        term_value = jnp.dot(product, right_op.T, preferred_element_type=jnp.float32)
        before = lax.dynamic_index_in_dim(running, target, 0, keepdims=False)
        return lax.dynamic_update_index_in_dim(running, before + term_value, target, 0)

    return lax.fori_loop(0, last_slot, add_block, partial_sum)


def on_any(
    wavefunction, diagonal, left_blocks, right_blocks, block_source, block_target, live_count
):
    devices = lax.axis_size("term")
    position = lax.axis_index("term")
    row_count = wavefunction.shape[1]
    sector_count = wavefunction.shape[0]
    width = wavefunction.shape[2]
    entries = float(sector_count * row_count * devices * width)
    own_count = live_count[0]
    diag_own = diagonal.astype(jnp.float32)
    whole_wave = lax.all_gather(wavefunction, "term", axis=1, tiled=True).astype(jnp.float32)
    scale = jnp.sqrt(jnp.sum(whole_wave * whole_wave) / entries)
    start_whole = whole_wave / scale
    empty_sum = jnp.zeros(start_whole.shape, jnp.float32)
    first_terms = block_loop(
        start_whole.astype(jnp.bfloat16),
        left_blocks,
        right_blocks,
        block_source,
        block_target,
        own_count,
        empty_sum,
    )
    row_start = position * row_count
    whole_diag = lax.all_gather(diagonal, "term", axis=1, tiled=True).astype(jnp.float32)
    first_whole = lax.psum(first_terms, "term") + whole_diag * start_whole
    ritz_value = jnp.sum(start_whole * first_whole) / entries
    correction = (first_whole - ritz_value * start_whole) / jnp.maximum(
        jnp.abs(whole_diag - ritz_value), 1.0
    )
    correlation = jnp.sum(start_whole * correction) / entries
    projected = correction - correlation * start_whole
    second_whole = projected / jnp.sqrt(jnp.sum(projected * projected) / entries)
    first_image = lax.dynamic_slice_in_dim(first_whole, row_start, row_count, 1)
    second_vector = lax.dynamic_slice_in_dim(second_whole, row_start, row_count, 1)
    second_rounded = second_whole.astype(jnp.bfloat16)
    second_terms = block_loop(
        second_rounded, left_blocks, right_blocks, block_source, block_target, own_count, empty_sum
    )
    second_image = (
        lax.psum_scatter(second_terms, "term", scatter_dimension=1, tiled=True)
        + diag_own * second_vector
    )
    return (first_image, second_vector, second_image)


def solution(mesh):
    placed = (
        P("grp", "term", None),
        P("grp", "term", None),
        P(("grp", "term"), None, None),
        P(("grp", "term"), None, None),
        P(("grp", "term")),
        P(("grp", "term")),
        P(("grp", "term")),
    )
    on_device = on_ring if mesh.shape["term"] == 16 else on_any
    return jax.shard_map(
        on_device,
        mesh=mesh,
        in_specs=placed,
        out_specs=(P("grp", "term", None), P("grp", "term", None), P("grp", "term", None)),
        check_vma=False,
    )
```

```python
import functools

import jax
import jax.numpy as jnp
from jax import lax
from jax.experimental import pallas as pl
from jax.experimental.pallas import tpu as pltpu
from jax.sharding import PartitionSpec as P

VMEM = pl.BlockSpec(memory_space=pltpu.VMEM)
SMEM = pl.BlockSpec(memory_space=pltpu.SMEM)
HBM = pl.BlockSpec(memory_space=pltpu.HBM)
PARAMS = pltpu.CompilerParams(vmem_limit_bytes=16 * 1024 * 1024)
FIRST = pltpu.CompilerParams(vmem_limit_bytes=48 * 1024 * 1024)
HALF = 16
GROUP = 2
LANES = 128


def fold(value):
    rows, width = value.shape
    summed = jnp.sum(value.reshape(rows // 8, 8, width), axis=0)
    return sum(summed[:, k * 128 : (k + 1) * 128] for k in range(width // 128))


def down(value):
    return jnp.sum(value, axis=0, keepdims=True)


def halves(rows, width, start=0):
    for h in range(rows // HALF):
        yield h * HALF, slice(start + h * width, start + (h + 1) * width)


def write_lanes(ref, at, lanes):
    whole = jnp.broadcast_to(lanes, (HALF, LANES))
    high = whole.astype(jnp.bfloat16).astype(jnp.float32)
    rest = whole - high
    middle = rest.astype(jnp.bfloat16).astype(jnp.float32)
    low = rest - middle
    row = lax.broadcasted_iota(jnp.int32, whole.shape, 0)
    value = jnp.where(row == 0, high, jnp.where(row == 1, middle, jnp.where(row == 2, low, 0.0)))
    ref[:, at : at + LANES] = value.astype(jnp.bfloat16)


def read_lanes(ref, at):
    return down(ref[:, at : at + LANES].astype(jnp.float32))


def chip_at(place):
    place = lax.rem(place + 8, 8)
    return jnp.where(place < 4, 2 * place, 15 - 2 * place)


def ring_place(me):
    chip, core = me // 2, me % 2
    place = jnp.where(chip % 2 == 0, chip // 2, (15 - chip) // 2)
    return place, core


def ahead(me, distance, half, core=None):
    place, own = ring_place(me)
    core = own if core is None else core
    return chip_at(place + (1 - 2 * core) * distance) * 2 + half


ROUNDS = 3


def sent_devices(me, core):
    devices = []
    for k in range(ROUNDS):
        for half in (core, 1 - core):
            devices.append(ahead(me, ROUNDS - k, half, core))
    return devices + [ahead(me, 4, core, core), ahead(me, 0, core, core)]


def gathered_devices(me):
    core = me % 2
    devices = [ahead(me, 0, core), ahead(me, 0, 1 - core)]
    for k in range(1, ROUNDS + 1):
        devices += [ahead(me, -k, core), ahead(me, -k, 1 - core)]
        devices += [ahead(me, k, 1 - core), ahead(me, k, core)]
    return devices + [ahead(me, 4, core), ahead(me, 4, 1 - core)]


def message_parts(sectors, rows, width):
    for s in range(sectors):
        for row, part in halves(rows, width, s * (rows // HALF) * width):
            yield s, row, part


def message_shape(sectors, rows, width):
    return (HALF, rows // HALF * sectors * width + LANES)


def copy_kernel(in_ref, _, out_ref):
    out_ref[...] = in_ref[...]


def copied(value, after):
    return pl.pallas_call(
        copy_kernel,
        in_specs=[VMEM, HBM],
        out_specs=VMEM,
        out_shape=jax.ShapeDtypeStruct(value.shape, value.dtype),
        compiler_params=PARAMS,
        cost_estimate=pl.CostEstimate(flops=8 << 30, bytes_accessed=1 << 20, transcendentals=0),
    )(value, after)


def square_kernel(wave_ref, diag_ref, square_ref):
    square = jnp.zeros((8, 128), jnp.float32)
    for s in range(wave_ref.shape[0]):
        wave = wave_ref[s].astype(jnp.float32)
        square += fold(diag_ref[s].astype(jnp.float32) * wave * wave)
    square_ref[...] = square


def weighted_square(wave, diag):
    return pl.pallas_call(
        square_kernel,
        in_specs=[VMEM, VMEM],
        out_specs=VMEM,
        out_shape=jax.ShapeDtypeStruct((8, 128), jnp.float32),
        compiler_params=PARAMS,
    )(wave, diag)


def blocks_kernel(first, shape, entries, me_ref, ints_ref, *refs):
    sectors, rows, width = shape
    field_refs, refs = refs[:16], refs[16:]
    if first:
        square_ref, *refs = refs
    else:
        scale_ref, wave_ref, correction_ref, *refs = refs
    left_in, right_in, *refs = refs
    total, near_ref, far_ref, dot_ref, out_ref, field, *refs = refs
    slots = left_in.shape[0]
    if first:
        left, right, left_sem, right_sem = refs

        def copies(slot):
            return (
                pltpu.make_async_copy(left_in.at[slot], left.at[slot], left_sem.at[slot]),
                pltpu.make_async_copy(right_in.at[slot], right.at[slot], right_sem.at[slot]),
            )

        for slot in range(GROUP):
            for copy in copies(slot):
                copy.start()
    else:
        left, right = left_in, right_in

    me = me_ref[0]
    core = me % 2

    pieces = []
    for k, owner in enumerate(gathered_devices(me)):
        at = pl.multiple_of(owner * rows, rows)
        if first:
            for s in range(sectors):
                pieces.append((k, (s,), s, pl.ds(at, rows)))
        else:
            for s, row, part in message_parts(sectors, rows, width):
                pieces.append((k, (slice(None), part), s, pl.ds(at + row, HALF)))

    total[...] = jnp.zeros_like(total)
    if first:
        dot = jnp.zeros((8, 128), jnp.float32)
        for k, part, _, _ in pieces:
            value = field_refs[k][part].astype(jnp.float32)
            dot += fold(value * value)
        for slot in range(GROUP, slots):
            for copy in copies(slot):
                copy.start()
        scale = jnp.sqrt(jnp.sum(dot) / entries)
        inverse = 1.0 / scale
        out_ref[...] = jnp.full(out_ref.shape, scale, jnp.float32)
        for k, part, s, at in pieces:
            field[s, at, :] = (field_refs[k][part].astype(jnp.float32) * inverse).astype(jnp.bfloat16)
    else:
        for k, part, s, at in pieces:
            field[s, at, :] = field_refs[k][part]

    used = ints_ref[2 * slots]

    def add_some(step, carry):
        some = [step * GROUP + k for k in range(GROUP)]
        if first:
            for slot in some:
                for copy in copies(slot):
                    copy.wait()

        @pl.when(some[0] < used)
        def _():
            products = [
                jnp.dot(
                    left[slot], field[ints_ref[slot]], preferred_element_type=jnp.float32
                ).astype(jnp.bfloat16)
                for slot in some
            ]
            for slot, product in zip(some, products):
                if slot is not some[0]:
                    product = jnp.where(slot < used, product, jnp.zeros_like(product))
                total[ints_ref[slots + slot]] += lax.dot_general(
                    product,
                    right[slot],
                    (((1,), (1,)), ((), ())),
                    preferred_element_type=jnp.float32,
                )

        return carry

    lax.fori_loop(0, slots // GROUP, add_some, 0)

    dot = jnp.zeros((8, 128), jnp.float32)
    if first:
        for k, part, s, at in pieces:
            dot += fold(total[s, at, :] * field_refs[k][part].astype(jnp.float32))
        dot = dot * inverse + square_ref[...] * inverse * inverse
    else:
        at = message_shape(*shape)[1] - LANES
        lanes = sum(
            ref[:, at : at + LANES].astype(jnp.float32) for ref in field_refs
        )
        along = jnp.sum(lanes) / entries
        out_ref[...] = jnp.full(out_ref.shape, along, jnp.float32)
        inverse = 1.0 / scale_ref[0:1, 0:1]
        for s in range(sectors):
            projected = correction_ref[s] - along * (wave_ref[s].astype(jnp.float32) * inverse)
            dot += fold(projected * projected)
    dot_ref[...] = dot
    lanes = down(dot)
    for k, owner in enumerate(sent_devices(me, 1 - core)):
        at = pl.multiple_of(owner * rows, rows)
        ref = near_ref.at[k] if k < near_ref.shape[0] else far_ref.at[k - near_ref.shape[0]]
        for s, row, part in message_parts(*shape):
            ref[:, part] = total[s, pl.ds(at + row, HALF), :].astype(jnp.bfloat16)
        write_lanes(ref, ref.shape[1] - LANES, lanes)


def apply_blocks(me, ints, fields, own, left, right, shape, first, entries):
    slots, order, width = left.shape
    sectors = shape[0]
    message = message_shape(*shape)
    scratch = []
    if first:
        scratch = [pltpu.VMEM(b.shape, b.dtype) for b in (left, right)]
        scratch += [pltpu.SemaphoreType.DMA((slots,))] * 2
    return pl.pallas_call(
        functools.partial(blocks_kernel, first, shape, entries),
        in_specs=[SMEM, SMEM]
        + [VMEM] * (len(fields) + len(own))
        + [HBM if first else VMEM] * 2,
        out_specs=[VMEM] * 5,
        scratch_shapes=[pltpu.VMEM((sectors, order, width), jnp.bfloat16)] + scratch,
        out_shape=[
            jax.ShapeDtypeStruct((sectors, order, width), jnp.float32),
            jax.ShapeDtypeStruct((2, *message), jnp.bfloat16),
            jax.ShapeDtypeStruct((2 * ROUNDS, *message), jnp.bfloat16),
            jax.ShapeDtypeStruct((8, 128), jnp.float32),
            jax.ShapeDtypeStruct((8, 128), jnp.float32),
        ],
        compiler_params=FIRST if first else PARAMS,
        cost_estimate=pl.CostEstimate(
            flops=4 * slots * order * order * width,
            bytes_accessed=4 * slots * order * order,
            transcendentals=0,
        ),
    )(me, ints, *fields, *own, left, right)


def chain_kernel(shape, k, index, me_ref, total_ref, dot_ref, other_ref, *refs):
    *arrived_refs, out_ref = refs
    _, rows, _ = shape
    me = me_ref[0]
    start = pl.multiple_of(sent_devices(me, me % 2)[k] * rows, rows)
    for s, row, part in message_parts(*shape):
        value = total_ref[s, pl.ds(start + row, HALF), :]
        value += other_ref[index, :, part].astype(jnp.float32)
        for ref in arrived_refs:
            value += ref[:, part].astype(jnp.float32)
        out_ref[:, part] = value.astype(jnp.bfloat16)
    at = out_ref.shape[1] - LANES
    lanes = down(dot_ref[...]) + read_lanes(other_ref.at[index], at)
    for ref in arrived_refs:
        lanes += read_lanes(ref, at)
    write_lanes(out_ref, at, lanes)


def chain(shape, k, index, me, total, dot, other, *arrived):
    return pl.pallas_call(
        functools.partial(chain_kernel, shape, k, index),
        in_specs=[SMEM] + [VMEM] * (3 + len(arrived)),
        out_specs=VMEM,
        out_shape=jax.ShapeDtypeStruct(message_shape(*shape), jnp.bfloat16),
        compiler_params=PARAMS,
    )(me, total, dot, other, *arrived)


def own_terms(shape, sector, me_ref, total_ref, other_ref, _, *arrived_refs):
    start = pl.multiple_of(me_ref[0] * shape[1], shape[1])
    values = []
    for s, row, part in message_parts(*shape):
        if s == sector:
            value = total_ref[s, pl.ds(start + row, HALF), :]
            value += other_ref[other_ref.shape[0] - 1, :, part].astype(jnp.float32)
            for ref in arrived_refs:
                value += ref[:, part].astype(jnp.float32)
            values.append(value)
    return jnp.concatenate(values, axis=0)


def own_scalar(me_ref, total_ref, other_ref, dot_ref, *arrived_refs):
    at = other_ref.shape[2] - LANES
    lanes = down(dot_ref[...]) + read_lanes(other_ref.at[other_ref.shape[0] - 1], at)
    return jnp.sum(lanes + sum(read_lanes(ref, at) for ref in arrived_refs))


def step_kernel(entries, scale_ref, wave_ref, diag_ref, *refs):
    *sums, terms_ref, correction_ref, message_ref = refs
    shape = wave_ref.shape
    ritz = own_scalar(*sums) / entries
    inverse = 1.0 / scale_ref[0:1, 0:1]
    dots = jnp.zeros((8, 128), jnp.float32)
    for s in range(shape[0]):
        start = wave_ref[s].astype(jnp.float32) * inverse
        diag = diag_ref[s].astype(jnp.float32)
        terms = own_terms(shape, s, *sums)
        first = terms + diag * start
        correction = (first - ritz * start) / jnp.maximum(jnp.abs(diag - ritz), 1.0)
        terms_ref[s] = terms
        correction_ref[s] = correction
        dots += fold(start * correction)
        for t, row, part in message_parts(*shape):
            if t == s:
                message_ref[:, part] = correction[row : row + HALF].astype(jnp.bfloat16)
    write_lanes(message_ref, message_ref.shape[1] - LANES, down(dots))


def davidson_step(scale, wave, diag, sums, entries):
    full = jax.ShapeDtypeStruct(wave.shape, jnp.float32)
    return pl.pallas_call(
        functools.partial(step_kernel, entries),
        in_specs=[VMEM] * 3 + [SMEM] + [VMEM] * (len(sums) - 1),
        out_specs=[VMEM] * 3,
        out_shape=[full, full, jax.ShapeDtypeStruct(message_shape(*wave.shape), jnp.bfloat16)],
        compiler_params=PARAMS,
    )(scale, wave, diag, *sums)


def finish_kernel(entries, along_ref, scale_ref, wave_ref, diag_ref, *refs):
    terms_ref, correction_ref, *sums, first_ref, vector_ref, image_ref = refs
    shape = wave_ref.shape
    along = along_ref[0:1, 0:1]
    norm = jnp.sqrt(jnp.full((1, 1), own_scalar(*sums) / entries, jnp.float32))
    inverse = 1.0 / norm
    start_scale = 1.0 / scale_ref[0:1, 0:1]
    for s in range(shape[0]):
        start = wave_ref[s].astype(jnp.float32) * start_scale
        diag = diag_ref[s].astype(jnp.float32)
        first_ref[s] = terms_ref[s] + diag * start
        second = (correction_ref[s] - along * start) * inverse
        vector_ref[s] = second
        image = (own_terms(shape, s, *sums) - along * terms_ref[s]) * inverse
        image_ref[s] = image + diag * second


def finish(along, scale, wave, diag, terms, correction, sums, entries):
    full = jax.ShapeDtypeStruct(wave.shape, jnp.float32)
    return pl.pallas_call(
        functools.partial(finish_kernel, entries),
        in_specs=[VMEM] * 6 + [SMEM] + [VMEM] * (len(sums) - 1),
        out_specs=[VMEM] * 3,
        out_shape=[full] * 3,
        compiler_params=PARAMS,
    )(along, scale, wave, diag, terms, correction, *sums)


def flip(value):
    return lax.ppermute(value, "term", [(i, i ^ 1) for i in range(16)])


def hop(value, up=1, down=-1):
    order = [0, 2, 4, 6, 7, 5, 3, 1]
    pairs = []
    for place in range(8):
        for core, step in ((0, up), (1, down)):
            pairs.append((order[place] * 2 + core, order[(place + step) % 8] * 2 + core))
    return lax.ppermute(value, "term", pairs)


def opposite(value):
    return hop(value, 4, 4)


def gather(own, beside=None):
    one, two = own, flip(own)
    across, two = lax.optimization_barrier((own, two))
    pieces = [one, two]
    across = opposite(across)
    result = None
    for k in range(ROUNDS):
        one, two = hop(one), hop(two)
        pieces += [one, two, flip(one), flip(two)]
        if k == 1 and beside is not None:
            result = beside(two)
            across, result = lax.optimization_barrier((across, result))
    return pieces + [across, flip(across)], result


def scatter(shape, me, total, near, far, dot):
    near = flip(near)
    near, far = lax.optimization_barrier((near, far))
    far = flip(far)
    one = hop(chain(shape, 0, 0, me, total, dot, near))
    two = hop(chain(shape, 1, 1, me, total, dot, near))
    across = opposite(chain(shape, 6, 4, me, total, dot, far))
    for k in (2, 4):
        one = hop(chain(shape, k, k - 2, me, total, dot, far, one))
        if k == 4:
            two, across = lax.optimization_barrier((two, across))
        two = hop(chain(shape, k + 1, k - 1, me, total, dot, far, two))
    return me, total, far, dot, one, flip(two), across


def on_ring(
    wavefunction, diagonal, left_blocks, right_blocks, block_source, block_target, live_count
):
    shape = wavefunction.shape
    sectors, rows, width = shape
    entries = float(sectors * rows * lax.axis_size("term") * width)
    me = lax.axis_index("term").astype(jnp.int32).reshape(1)
    def beside(after):
        ints = jnp.concatenate([block_source, block_target, live_count])
        return ints, copied(wavefunction, after)

    (_, *fields), (ints, wave) = gather(wavefunction, beside)
    fields = [wave, *fields]
    square = weighted_square(wave, diagonal)
    blocks = (left_blocks, right_blocks, shape)
    total, near, far, dot, scale = apply_blocks(me, ints, fields, (square,), *blocks, True, entries)
    terms, correction, message = davidson_step(
        scale, wavefunction, diagonal, scatter(shape, me, total, near, far, dot), entries
    )
    fields, _ = gather(message)
    own = (scale, wavefunction, correction)
    total, near, far, dot, along = apply_blocks(me, ints, fields, own, *blocks, False, entries)
    first_image, second_vector, second_image = finish(
        along, scale, wavefunction, diagonal, terms, correction,
        scatter(shape, me, total, near, far, dot), entries,
    )
    return (first_image, second_vector, second_image)


def block_loop(field_rounded, left_ops, right_ops, sources, targets, last_slot, partial_sum):

    def add_block(slot_index, running):
        left_op = lax.dynamic_index_in_dim(left_ops, slot_index, 0, keepdims=False)
        right_op = lax.dynamic_index_in_dim(right_ops, slot_index, 0, keepdims=False)
        source = lax.dynamic_index_in_dim(sources, slot_index, 0, keepdims=False)
        target = lax.dynamic_index_in_dim(targets, slot_index, 0, keepdims=False)
        piece = lax.dynamic_index_in_dim(field_rounded, source, 0, keepdims=False)
        product = jnp.dot(left_op, piece, preferred_element_type=jnp.float32).astype(jnp.bfloat16)
        term_value = jnp.dot(product, right_op.T, preferred_element_type=jnp.float32)
        before = lax.dynamic_index_in_dim(running, target, 0, keepdims=False)
        return lax.dynamic_update_index_in_dim(running, before + term_value, target, 0)

    return lax.fori_loop(0, last_slot, add_block, partial_sum)


def on_any(
    wavefunction, diagonal, left_blocks, right_blocks, block_source, block_target, live_count
):
    devices = lax.axis_size("term")
    position = lax.axis_index("term")
    row_count = wavefunction.shape[1]
    sector_count = wavefunction.shape[0]
    width = wavefunction.shape[2]
    entries = float(sector_count * row_count * devices * width)
    own_count = live_count[0]
    diag_own = diagonal.astype(jnp.float32)
    whole_wave = lax.all_gather(wavefunction, "term", axis=1, tiled=True).astype(jnp.float32)
    scale = jnp.sqrt(jnp.sum(whole_wave * whole_wave) / entries)
    start_whole = whole_wave / scale
    empty_sum = jnp.zeros(start_whole.shape, jnp.float32)
    first_terms = block_loop(
        start_whole.astype(jnp.bfloat16),
        left_blocks,
        right_blocks,
        block_source,
        block_target,
        own_count,
        empty_sum,
    )
    row_start = position * row_count
    whole_diag = lax.all_gather(diagonal, "term", axis=1, tiled=True).astype(jnp.float32)
    first_whole = lax.psum(first_terms, "term") + whole_diag * start_whole
    ritz_value = jnp.sum(start_whole * first_whole) / entries
    correction = (first_whole - ritz_value * start_whole) / jnp.maximum(
        jnp.abs(whole_diag - ritz_value), 1.0
    )
    correlation = jnp.sum(start_whole * correction) / entries
    projected = correction - correlation * start_whole
    second_whole = projected / jnp.sqrt(jnp.sum(projected * projected) / entries)
    first_image = lax.dynamic_slice_in_dim(first_whole, row_start, row_count, 1)
    second_vector = lax.dynamic_slice_in_dim(second_whole, row_start, row_count, 1)
    second_rounded = second_whole.astype(jnp.bfloat16)
    second_terms = block_loop(
        second_rounded, left_blocks, right_blocks, block_source, block_target, own_count, empty_sum
    )
    second_image = (
        lax.psum_scatter(second_terms, "term", scatter_dimension=1, tiled=True)
        + diag_own * second_vector
    )
    return (first_image, second_vector, second_image)


def solution(mesh):
    placed = (
        P("grp", "term", None),
        P("grp", "term", None),
        P(("grp", "term"), None, None),
        P(("grp", "term"), None, None),
        P(("grp", "term")),
        P(("grp", "term")),
        P(("grp", "term")),
    )
    on_device = on_ring if mesh.shape["term"] == 16 else on_any
    return jax.shard_map(
        on_device,
        mesh=mesh,
        in_specs=placed,
        out_specs=(P("grp", "term", None), P("grp", "term", None), P("grp", "term", None)),
        check_vma=False,
    )
```

```python
import functools

import jax
import jax.numpy as jnp
from jax import lax
from jax.experimental import pallas as pl
from jax.experimental.pallas import tpu as pltpu
from jax.sharding import PartitionSpec as P

VMEM = pl.BlockSpec(memory_space=pltpu.VMEM)
SMEM = pl.BlockSpec(memory_space=pltpu.SMEM)
HBM = pl.BlockSpec(memory_space=pltpu.HBM)
PARAMS = pltpu.CompilerParams(vmem_limit_bytes=16 * 1024 * 1024)
FIRST = pltpu.CompilerParams(vmem_limit_bytes=48 * 1024 * 1024)
HALF = 16
GROUP = 2
LANES = 128


def fold(value):
    rows, width = value.shape
    summed = jnp.sum(value.reshape(rows // 8, 8, width), axis=0)
    return sum(summed[:, k * 128 : (k + 1) * 128] for k in range(width // 128))


def down(value):
    return jnp.sum(value, axis=0, keepdims=True)


def halves(rows, width, start=0):
    for h in range(rows // HALF):
        yield h * HALF, slice(start + h * width, start + (h + 1) * width)


def write_lanes(ref, at, lanes):
    whole = jnp.broadcast_to(lanes, (HALF, LANES))
    high = whole.astype(jnp.bfloat16).astype(jnp.float32)
    rest = whole - high
    middle = rest.astype(jnp.bfloat16).astype(jnp.float32)
    low = rest - middle
    row = lax.broadcasted_iota(jnp.int32, whole.shape, 0)
    value = jnp.where(row == 0, high, jnp.where(row == 1, middle, jnp.where(row == 2, low, 0.0)))
    ref[:, at : at + LANES] = value.astype(jnp.bfloat16)


def read_lanes(ref, at):
    return down(ref[:, at : at + LANES].astype(jnp.float32))


def chip_at(place):
    place = lax.rem(place + 8, 8)
    return jnp.where(place < 4, 2 * place, 15 - 2 * place)


def ring_place(me):
    chip, core = me // 2, me % 2
    place = jnp.where(chip % 2 == 0, chip // 2, (15 - chip) // 2)
    return place, core


def ahead(me, distance, half, core=None):
    place, own = ring_place(me)
    core = own if core is None else core
    return chip_at(place + (1 - 2 * core) * distance) * 2 + half


ROUNDS = 3


def sent_devices(me, core):
    devices = []
    for k in range(ROUNDS):
        for half in (core, 1 - core):
            devices.append(ahead(me, ROUNDS - k, half, core))
    return devices + [ahead(me, 4, core, core), ahead(me, 0, core, core)]


def gathered_devices(me):
    core = me % 2
    devices = [ahead(me, 0, core), ahead(me, 0, 1 - core)]
    for k in range(1, ROUNDS + 1):
        devices += [ahead(me, -k, core), ahead(me, -k, 1 - core)]
        devices += [ahead(me, k, 1 - core), ahead(me, k, core)]
    return devices + [ahead(me, 4, core), ahead(me, 4, 1 - core)]


def message_parts(sectors, rows, width):
    for s in range(sectors):
        for row, part in halves(rows, width, s * (rows // HALF) * width):
            yield s, row, part


def message_shape(sectors, rows, width):
    return (HALF, rows // HALF * sectors * width + LANES)


def copy_kernel(in_ref, _, out_ref):
    out_ref[...] = in_ref[...]


def copied(value, after):
    return pl.pallas_call(
        copy_kernel,
        in_specs=[VMEM, HBM],
        out_specs=VMEM,
        out_shape=jax.ShapeDtypeStruct(value.shape, value.dtype),
        compiler_params=PARAMS,
        cost_estimate=pl.CostEstimate(flops=8 << 30, bytes_accessed=1 << 20, transcendentals=0),
    )(value, after)


def square_kernel(wave_ref, diag_ref, square_ref):
    square = jnp.zeros((8, 128), jnp.float32)
    for s in range(wave_ref.shape[0]):
        wave = wave_ref[s].astype(jnp.float32)
        square += fold(diag_ref[s].astype(jnp.float32) * wave * wave)
    square_ref[...] = square


def weighted_square(wave, diag):
    return pl.pallas_call(
        square_kernel,
        in_specs=[VMEM, VMEM],
        out_specs=VMEM,
        out_shape=jax.ShapeDtypeStruct((8, 128), jnp.float32),
        compiler_params=PARAMS,
    )(wave, diag)


def blocks_kernel(first, shape, entries, me_ref, ints_ref, *refs):
    sectors, rows, width = shape
    field_refs, refs = refs[:16], refs[16:]
    if first:
        square_ref, *refs = refs
    else:
        scale_ref, wave_ref, correction_ref, *refs = refs
    left_in, right_in, *refs = refs
    total, near_ref, far_ref, dot_ref, out_ref, field, *refs = refs
    slots = left_in.shape[0]
    if first:
        left, right, left_sem, right_sem = refs

        def copies(slot):
            return (
                pltpu.make_async_copy(left_in.at[slot], left.at[slot], left_sem.at[slot]),
                pltpu.make_async_copy(right_in.at[slot], right.at[slot], right_sem.at[slot]),
            )

        for slot in range(slots):
            for priority, copy in enumerate(copies(slot)):
                copy.start(priority=priority)
    else:
        left, right = left_in, right_in

    me = me_ref[0]
    core = me % 2

    pieces = []
    for k, owner in enumerate(gathered_devices(me)):
        at = pl.multiple_of(owner * rows, rows)
        if first:
            for s in range(sectors):
                pieces.append((k, (s,), s, pl.ds(at, rows)))
        else:
            for s, row, part in message_parts(sectors, rows, width):
                pieces.append((k, (slice(None), part), s, pl.ds(at + row, HALF)))

    total[...] = jnp.zeros_like(total)
    if first:
        dot = jnp.zeros((8, 128), jnp.float32)
        for k, part, _, _ in pieces:
            value = field_refs[k][part].astype(jnp.float32)
            dot += fold(value * value)
        scale = jnp.sqrt(jnp.sum(dot) / entries)
        inverse = 1.0 / scale
        out_ref[...] = jnp.full(out_ref.shape, scale, jnp.float32)
        for k, part, s, at in pieces:
            field[s, at, :] = (field_refs[k][part].astype(jnp.float32) * inverse).astype(jnp.bfloat16)
    else:
        for k, part, s, at in pieces:
            field[s, at, :] = field_refs[k][part]

    used = ints_ref[2 * slots]

    group = GROUP if first else 2 * GROUP

    def add_some(step, carry):
        some = [step * group + k for k in range(group)]
        if first:
            for slot in some:
                for copy in copies(slot):
                    copy.wait()

        @pl.when(some[0] < used)
        def _():
            products = [
                jnp.dot(
                    left[slot], field[ints_ref[slot]], preferred_element_type=jnp.float32
                ).astype(jnp.bfloat16)
                for slot in some
            ]
            for slot, product in zip(some, products):
                if slot is not some[0]:
                    product = jnp.where(slot < used, product, jnp.zeros_like(product))
                total[ints_ref[slots + slot]] += lax.dot_general(
                    product,
                    right[slot],
                    (((1,), (1,)), ((), ())),
                    preferred_element_type=jnp.float32,
                )

        return carry

    lax.fori_loop(0, slots // group, add_some, 0)

    dot = jnp.zeros((8, 128), jnp.float32)
    if first:
        for k, part, s, at in pieces:
            dot += fold(total[s, at, :] * field_refs[k][part].astype(jnp.float32))
        dot = dot * inverse + square_ref[...] * inverse * inverse
    else:
        at = message_shape(*shape)[1] - LANES
        lanes = sum(
            ref[:, at : at + LANES].astype(jnp.float32) for ref in field_refs
        )
        along = jnp.sum(lanes) / entries
        out_ref[...] = jnp.full(out_ref.shape, along, jnp.float32)
        inverse = 1.0 / scale_ref[0:1, 0:1]
        for s in range(sectors):
            projected = correction_ref[s] - along * (wave_ref[s].astype(jnp.float32) * inverse)
            dot += fold(projected * projected)
    dot_ref[...] = dot
    lanes = down(dot)
    for k, owner in enumerate(sent_devices(me, 1 - core)):
        at = pl.multiple_of(owner * rows, rows)
        ref = near_ref.at[k] if k < near_ref.shape[0] else far_ref.at[k - near_ref.shape[0]]
        for s, row, part in message_parts(*shape):
            ref[:, part] = total[s, pl.ds(at + row, HALF), :].astype(jnp.bfloat16)
        write_lanes(ref, ref.shape[1] - LANES, lanes)


def apply_blocks(me, ints, fields, own, left, right, shape, first, entries):
    slots, order, width = left.shape
    sectors = shape[0]
    message = message_shape(*shape)
    scratch = []
    if first:
        scratch = [pltpu.VMEM(b.shape, b.dtype) for b in (left, right)]
        scratch += [pltpu.SemaphoreType.DMA((slots,))] * 2
    return pl.pallas_call(
        functools.partial(blocks_kernel, first, shape, entries),
        in_specs=[SMEM, SMEM]
        + [VMEM] * (len(fields) + len(own))
        + [HBM if first else VMEM] * 2,
        out_specs=[VMEM] * 5,
        scratch_shapes=[pltpu.VMEM((sectors, order, width), jnp.bfloat16)] + scratch,
        out_shape=[
            jax.ShapeDtypeStruct((sectors, order, width), jnp.float32),
            jax.ShapeDtypeStruct((2, *message), jnp.bfloat16),
            jax.ShapeDtypeStruct((2 * ROUNDS, *message), jnp.bfloat16),
            jax.ShapeDtypeStruct((8, 128), jnp.float32),
            jax.ShapeDtypeStruct((8, 128), jnp.float32),
        ],
        compiler_params=FIRST if first else PARAMS,
        cost_estimate=pl.CostEstimate(
            flops=4 * slots * order * order * width,
            bytes_accessed=4 * slots * order * order,
            transcendentals=0,
        ),
    )(me, ints, *fields, *own, left, right)


def chain_kernel(shape, k, index, me_ref, total_ref, dot_ref, other_ref, *refs):
    *arrived_refs, out_ref = refs
    _, rows, _ = shape
    me = me_ref[0]
    start = pl.multiple_of(sent_devices(me, me % 2)[k] * rows, rows)
    for s, row, part in message_parts(*shape):
        value = total_ref[s, pl.ds(start + row, HALF), :]
        value += other_ref[index, :, part].astype(jnp.float32)
        for ref in arrived_refs:
            value += ref[:, part].astype(jnp.float32)
        out_ref[:, part] = value.astype(jnp.bfloat16)
    at = out_ref.shape[1] - LANES
    lanes = down(dot_ref[...]) + read_lanes(other_ref.at[index], at)
    for ref in arrived_refs:
        lanes += read_lanes(ref, at)
    write_lanes(out_ref, at, lanes)


def chain(shape, k, index, me, total, dot, other, *arrived):
    return pl.pallas_call(
        functools.partial(chain_kernel, shape, k, index),
        in_specs=[SMEM] + [VMEM] * (3 + len(arrived)),
        out_specs=VMEM,
        out_shape=jax.ShapeDtypeStruct(message_shape(*shape), jnp.bfloat16),
        compiler_params=PARAMS,
    )(me, total, dot, other, *arrived)


def own_terms(shape, sector, me_ref, total_ref, other_ref, _, *arrived_refs):
    start = pl.multiple_of(me_ref[0] * shape[1], shape[1])
    values = []
    for s, row, part in message_parts(*shape):
        if s == sector:
            value = total_ref[s, pl.ds(start + row, HALF), :]
            value += other_ref[other_ref.shape[0] - 1, :, part].astype(jnp.float32)
            for ref in arrived_refs:
                value += ref[:, part].astype(jnp.float32)
            values.append(value)
    return jnp.concatenate(values, axis=0)


def own_scalar(me_ref, total_ref, other_ref, dot_ref, *arrived_refs):
    at = other_ref.shape[2] - LANES
    lanes = down(dot_ref[...]) + read_lanes(other_ref.at[other_ref.shape[0] - 1], at)
    return jnp.sum(lanes + sum(read_lanes(ref, at) for ref in arrived_refs))


def step_kernel(entries, scale_ref, wave_ref, diag_ref, *refs):
    *sums, terms_ref, correction_ref, message_ref = refs
    shape = wave_ref.shape
    ritz = own_scalar(*sums) / entries
    inverse = 1.0 / scale_ref[0:1, 0:1]
    dots = jnp.zeros((8, 128), jnp.float32)
    for s in range(shape[0]):
        start = wave_ref[s].astype(jnp.float32) * inverse
        diag = diag_ref[s].astype(jnp.float32)
        terms = own_terms(shape, s, *sums)
        first = terms + diag * start
        correction = (first - ritz * start) / jnp.maximum(jnp.abs(diag - ritz), 1.0)
        terms_ref[s] = terms
        correction_ref[s] = correction
        dots += fold(start * correction)
        for t, row, part in message_parts(*shape):
            if t == s:
                message_ref[:, part] = correction[row : row + HALF].astype(jnp.bfloat16)
    write_lanes(message_ref, message_ref.shape[1] - LANES, down(dots))


def davidson_step(scale, wave, diag, sums, entries):
    full = jax.ShapeDtypeStruct(wave.shape, jnp.float32)
    return pl.pallas_call(
        functools.partial(step_kernel, entries),
        in_specs=[VMEM] * 3 + [SMEM] + [VMEM] * (len(sums) - 1),
        out_specs=[VMEM] * 3,
        out_shape=[full, full, jax.ShapeDtypeStruct(message_shape(*wave.shape), jnp.bfloat16)],
        compiler_params=PARAMS,
    )(scale, wave, diag, *sums)


def finish_kernel(entries, along_ref, scale_ref, wave_ref, diag_ref, *refs):
    terms_ref, correction_ref, *sums, first_ref, vector_ref, image_ref = refs
    shape = wave_ref.shape
    along = along_ref[0:1, 0:1]
    norm = jnp.sqrt(jnp.full((1, 1), own_scalar(*sums) / entries, jnp.float32))
    inverse = 1.0 / norm
    start_scale = 1.0 / scale_ref[0:1, 0:1]
    for s in range(shape[0]):
        start = wave_ref[s].astype(jnp.float32) * start_scale
        diag = diag_ref[s].astype(jnp.float32)
        first_ref[s] = terms_ref[s] + diag * start
        second = (correction_ref[s] - along * start) * inverse
        vector_ref[s] = second
        image = (own_terms(shape, s, *sums) - along * terms_ref[s]) * inverse
        image_ref[s] = image + diag * second


def finish(along, scale, wave, diag, terms, correction, sums, entries):
    full = jax.ShapeDtypeStruct(wave.shape, jnp.float32)
    return pl.pallas_call(
        functools.partial(finish_kernel, entries),
        in_specs=[VMEM] * 6 + [SMEM] + [VMEM] * (len(sums) - 1),
        out_specs=[VMEM] * 3,
        out_shape=[full] * 3,
        compiler_params=PARAMS,
    )(along, scale, wave, diag, terms, correction, *sums)


def flip(value):
    return lax.ppermute(value, "term", [(i, i ^ 1) for i in range(16)])


def hop(value, up=1, down=-1):
    order = [0, 2, 4, 6, 7, 5, 3, 1]
    pairs = []
    for place in range(8):
        for core, step in ((0, up), (1, down)):
            pairs.append((order[place] * 2 + core, order[(place + step) % 8] * 2 + core))
    return lax.ppermute(value, "term", pairs)


def opposite(value):
    return hop(value, 4, 4)


def gather(own, beside=None):
    one, two = own, flip(own)
    across, two = lax.optimization_barrier((own, two))
    pieces = [one, two]
    across = opposite(across)
    result = None
    for k in range(ROUNDS):
        one, two = hop(one), hop(two)
        pieces += [one, two, flip(one), flip(two)]
        if k == 1 and beside is not None:
            result = beside(two)
            across, result = lax.optimization_barrier((across, result))
    return pieces + [across, flip(across)], result


def scatter(shape, me, total, near, far, dot):
    near = flip(near)
    near, far = lax.optimization_barrier((near, far))
    far = flip(far)
    one = hop(chain(shape, 0, 0, me, total, dot, near))
    two = hop(chain(shape, 1, 1, me, total, dot, near))
    across = opposite(chain(shape, 6, 4, me, total, dot, far))
    for k in (2, 4):
        one = hop(chain(shape, k, k - 2, me, total, dot, far, one))
        if k == 4:
            two, across = lax.optimization_barrier((two, across))
        two = hop(chain(shape, k + 1, k - 1, me, total, dot, far, two))
    return me, total, far, dot, one, flip(two), across


def on_ring(
    wavefunction, diagonal, left_blocks, right_blocks, block_source, block_target, live_count
):
    shape = wavefunction.shape
    sectors, rows, width = shape
    entries = float(sectors * rows * lax.axis_size("term") * width)
    me = lax.axis_index("term").astype(jnp.int32).reshape(1)
    def beside(after):
        ints = jnp.concatenate([block_source, block_target, live_count])
        return ints, copied(wavefunction, after)

    (_, *fields), (ints, wave) = gather(wavefunction, beside)
    fields = [wave, *fields]
    square = weighted_square(wave, diagonal)
    blocks = (left_blocks, right_blocks, shape)
    total, near, far, dot, scale = apply_blocks(me, ints, fields, (square,), *blocks, True, entries)
    terms, correction, message = davidson_step(
        scale, wavefunction, diagonal, scatter(shape, me, total, near, far, dot), entries
    )
    fields, _ = gather(message)
    own = (scale, wavefunction, correction)
    total, near, far, dot, along = apply_blocks(me, ints, fields, own, *blocks, False, entries)
    first_image, second_vector, second_image = finish(
        along, scale, wavefunction, diagonal, terms, correction,
        scatter(shape, me, total, near, far, dot), entries,
    )
    return (first_image, second_vector, second_image)


def block_loop(field_rounded, left_ops, right_ops, sources, targets, last_slot, partial_sum):

    def add_block(slot_index, running):
        left_op = lax.dynamic_index_in_dim(left_ops, slot_index, 0, keepdims=False)
        right_op = lax.dynamic_index_in_dim(right_ops, slot_index, 0, keepdims=False)
        source = lax.dynamic_index_in_dim(sources, slot_index, 0, keepdims=False)
        target = lax.dynamic_index_in_dim(targets, slot_index, 0, keepdims=False)
        piece = lax.dynamic_index_in_dim(field_rounded, source, 0, keepdims=False)
        product = jnp.dot(left_op, piece, preferred_element_type=jnp.float32).astype(jnp.bfloat16)
        term_value = jnp.dot(product, right_op.T, preferred_element_type=jnp.float32)
        before = lax.dynamic_index_in_dim(running, target, 0, keepdims=False)
        return lax.dynamic_update_index_in_dim(running, before + term_value, target, 0)

    return lax.fori_loop(0, last_slot, add_block, partial_sum)


def on_any(
    wavefunction, diagonal, left_blocks, right_blocks, block_source, block_target, live_count
):
    devices = lax.axis_size("term")
    position = lax.axis_index("term")
    row_count = wavefunction.shape[1]
    sector_count = wavefunction.shape[0]
    width = wavefunction.shape[2]
    entries = float(sector_count * row_count * devices * width)
    own_count = live_count[0]
    diag_own = diagonal.astype(jnp.float32)
    whole_wave = lax.all_gather(wavefunction, "term", axis=1, tiled=True).astype(jnp.float32)
    scale = jnp.sqrt(jnp.sum(whole_wave * whole_wave) / entries)
    start_whole = whole_wave / scale
    empty_sum = jnp.zeros(start_whole.shape, jnp.float32)
    first_terms = block_loop(
        start_whole.astype(jnp.bfloat16),
        left_blocks,
        right_blocks,
        block_source,
        block_target,
        own_count,
        empty_sum,
    )
    row_start = position * row_count
    whole_diag = lax.all_gather(diagonal, "term", axis=1, tiled=True).astype(jnp.float32)
    first_whole = lax.psum(first_terms, "term") + whole_diag * start_whole
    ritz_value = jnp.sum(start_whole * first_whole) / entries
    correction = (first_whole - ritz_value * start_whole) / jnp.maximum(
        jnp.abs(whole_diag - ritz_value), 1.0
    )
    correlation = jnp.sum(start_whole * correction) / entries
    projected = correction - correlation * start_whole
    second_whole = projected / jnp.sqrt(jnp.sum(projected * projected) / entries)
    first_image = lax.dynamic_slice_in_dim(first_whole, row_start, row_count, 1)
    second_vector = lax.dynamic_slice_in_dim(second_whole, row_start, row_count, 1)
    second_rounded = second_whole.astype(jnp.bfloat16)
    second_terms = block_loop(
        second_rounded, left_blocks, right_blocks, block_source, block_target, own_count, empty_sum
    )
    second_image = (
        lax.psum_scatter(second_terms, "term", scatter_dimension=1, tiled=True)
        + diag_own * second_vector
    )
    return (first_image, second_vector, second_image)


def solution(mesh):
    placed = (
        P("grp", "term", None),
        P("grp", "term", None),
        P(("grp", "term"), None, None),
        P(("grp", "term"), None, None),
        P(("grp", "term")),
        P(("grp", "term")),
        P(("grp", "term")),
    )
    on_device = on_ring if mesh.shape["term"] == 16 else on_any
    return jax.shard_map(
        on_device,
        mesh=mesh,
        in_specs=placed,
        out_specs=(P("grp", "term", None), P("grp", "term", None), P("grp", "term", None)),
        check_vma=False,
    )
```

```python
import functools

import jax
import jax.numpy as jnp
from jax import lax
from jax.experimental import pallas as pl
from jax.experimental.pallas import tpu as pltpu
from jax.sharding import PartitionSpec as P

VMEM = pl.BlockSpec(memory_space=pltpu.VMEM)
SMEM = pl.BlockSpec(memory_space=pltpu.SMEM)
HBM = pl.BlockSpec(memory_space=pltpu.HBM)
PARAMS = pltpu.CompilerParams(vmem_limit_bytes=16 * 1024 * 1024)
FIRST = pltpu.CompilerParams(vmem_limit_bytes=48 * 1024 * 1024)
HALF = 16
GROUP = 2
LANES = 128


def fold(value):
    rows, width = value.shape
    summed = jnp.sum(value.reshape(rows // 8, 8, width), axis=0)
    return sum(summed[:, k * 128 : (k + 1) * 128] for k in range(width // 128))


def down(value):
    return jnp.sum(value, axis=0, keepdims=True)


def halves(rows, width, start=0):
    for h in range(rows // HALF):
        yield h * HALF, slice(start + h * width, start + (h + 1) * width)


def write_lanes(ref, at, lanes):
    whole = jnp.broadcast_to(lanes, (HALF, LANES))
    high = whole.astype(jnp.bfloat16).astype(jnp.float32)
    rest = whole - high
    middle = rest.astype(jnp.bfloat16).astype(jnp.float32)
    low = rest - middle
    row = lax.broadcasted_iota(jnp.int32, whole.shape, 0)
    value = jnp.where(row == 0, high, jnp.where(row == 1, middle, jnp.where(row == 2, low, 0.0)))
    ref[:, at : at + LANES] = value.astype(jnp.bfloat16)


def read_lanes(ref, at):
    return down(ref[:, at : at + LANES].astype(jnp.float32))


def chip_at(place):
    place = lax.rem(place + 8, 8)
    return jnp.where(place < 4, 2 * place, 15 - 2 * place)


def ring_place(me):
    chip, core = me // 2, me % 2
    place = jnp.where(chip % 2 == 0, chip // 2, (15 - chip) // 2)
    return place, core


def ahead(me, distance, half, core=None):
    place, own = ring_place(me)
    core = own if core is None else core
    return chip_at(place + (1 - 2 * core) * distance) * 2 + half


ROUNDS = 3


def sent_devices(me, core):
    devices = []
    for k in range(ROUNDS):
        for half in (core, 1 - core):
            devices.append(ahead(me, ROUNDS - k, half, core))
    return devices + [ahead(me, 4, core, core), ahead(me, 0, core, core)]


def gathered_devices(me):
    core = me % 2
    devices = [ahead(me, 0, core), ahead(me, 0, 1 - core)]
    for k in range(1, ROUNDS + 1):
        devices += [ahead(me, -k, core), ahead(me, -k, 1 - core)]
        devices += [ahead(me, k, 1 - core), ahead(me, k, core)]
    return devices + [ahead(me, 4, core), ahead(me, 4, 1 - core)]


def message_parts(sectors, rows, width):
    for s in range(sectors):
        for row, part in halves(rows, width, s * (rows // HALF) * width):
            yield s, row, part


def message_shape(sectors, rows, width):
    return (HALF, rows // HALF * sectors * width + LANES)


def copy_kernel(in_ref, _, out_ref):
    out_ref[...] = in_ref[...]


def copied(value, after):
    return pl.pallas_call(
        copy_kernel,
        in_specs=[VMEM, HBM],
        out_specs=VMEM,
        out_shape=jax.ShapeDtypeStruct(value.shape, value.dtype),
        compiler_params=PARAMS,
        cost_estimate=pl.CostEstimate(flops=8 << 30, bytes_accessed=1 << 20, transcendentals=0),
    )(value, after)


def square_kernel(wave_ref, diag_ref, square_ref):
    square = jnp.zeros((8, 128), jnp.float32)
    for s in range(wave_ref.shape[0]):
        wave = wave_ref[s].astype(jnp.float32)
        square += fold(diag_ref[s].astype(jnp.float32) * wave * wave)
    square_ref[...] = square


def weighted_square(wave, diag):
    return pl.pallas_call(
        square_kernel,
        in_specs=[VMEM, VMEM],
        out_specs=VMEM,
        out_shape=jax.ShapeDtypeStruct((8, 128), jnp.float32),
        compiler_params=PARAMS,
    )(wave, diag)


def blocks_kernel(first, shape, entries, me_ref, ints_ref, *refs):
    sectors, rows, width = shape
    field_refs, refs = refs[:16], refs[16:]
    if first:
        square_ref, *refs = refs
    else:
        scale_ref, wave_ref, correction_ref, *refs = refs
    left_in, right_in, *refs = refs
    total, near_ref, far_ref, dot_ref, out_ref, field, *refs = refs
    slots = left_in.shape[0]
    if first:
        left, right, left_sem, right_sem = refs

        def copies(slot):
            return (
                pltpu.make_async_copy(left_in.at[slot], left.at[slot], left_sem.at[slot]),
                pltpu.make_async_copy(right_in.at[slot], right.at[slot], right_sem.at[slot]),
            )

        for slot in range(GROUP):
            for copy in copies(slot):
                copy.start()
    else:
        left, right = left_in, right_in

    me = me_ref[0]
    core = me % 2

    pieces = []
    for k, owner in enumerate(gathered_devices(me)):
        at = pl.multiple_of(owner * rows, rows)
        if first:
            for s in range(sectors):
                pieces.append((k, (s,), s, pl.ds(at, rows)))
        else:
            for s, row, part in message_parts(sectors, rows, width):
                pieces.append((k, (slice(None), part), s, pl.ds(at + row, HALF)))

    total[...] = jnp.zeros_like(total)
    if first:
        dot = jnp.zeros((8, 128), jnp.float32)
        for k, part, _, _ in pieces:
            value = field_refs[k][part].astype(jnp.float32)
            dot += fold(value * value)
        for slot in range(GROUP, slots):
            for copy in copies(slot):
                copy.start()
        scale = jnp.sqrt(jnp.sum(dot) / entries)
        inverse = 1.0 / scale
        out_ref[...] = jnp.full(out_ref.shape, scale, jnp.float32)
        for k, part, s, at in pieces:
            field[s, at, :] = (field_refs[k][part].astype(jnp.float32) * inverse).astype(jnp.bfloat16)
    else:
        for k, part, s, at in pieces:
            field[s, at, :] = field_refs[k][part]

    used = ints_ref[2 * slots]

    group = GROUP if first else 2 * GROUP

    def add_some(step, carry):
        some = [step * group + k for k in range(group)]
        if first:
            for slot in some:
                for copy in copies(slot):
                    copy.wait()

        @pl.when(some[0] < used)
        def _():
            products = [
                jnp.dot(
                    left[slot], field[ints_ref[slot]], preferred_element_type=jnp.float32
                ).astype(jnp.bfloat16)
                for slot in some
            ]
            for slot, product in zip(some, products):
                if slot is not some[0]:
                    product = jnp.where(slot < used, product, jnp.zeros_like(product))
                total[ints_ref[slots + slot]] += lax.dot_general(
                    product,
                    right[slot],
                    (((1,), (1,)), ((), ())),
                    preferred_element_type=jnp.float32,
                )

        return carry

    lax.fori_loop(0, slots // group, add_some, 0)

    dot = jnp.zeros((8, 128), jnp.float32)
    if first:
        for k, part, s, at in pieces:
            dot += fold(total[s, at, :] * field_refs[k][part].astype(jnp.float32))
        dot = dot * inverse + square_ref[...] * inverse * inverse
    else:
        at = message_shape(*shape)[1] - LANES
        lanes = sum(
            ref[:, at : at + LANES].astype(jnp.float32) for ref in field_refs
        )
        along = jnp.sum(lanes) / entries
        out_ref[...] = jnp.full(out_ref.shape, along, jnp.float32)
        inverse = 1.0 / scale_ref[0:1, 0:1]
        for s in range(sectors):
            projected = correction_ref[s] - along * (wave_ref[s].astype(jnp.float32) * inverse)
            dot += fold(projected * projected)
    dot_ref[...] = dot
    lanes = down(dot)
    for k, owner in enumerate(sent_devices(me, 1 - core)):
        at = pl.multiple_of(owner * rows, rows)
        ref = near_ref.at[k] if k < near_ref.shape[0] else far_ref.at[k - near_ref.shape[0]]
        for s, row, part in message_parts(*shape):
            ref[:, part] = total[s, pl.ds(at + row, HALF), :].astype(jnp.bfloat16)
        write_lanes(ref, ref.shape[1] - LANES, lanes)


def apply_blocks(me, ints, fields, own, left, right, shape, first, entries):
    slots, order, width = left.shape
    sectors = shape[0]
    message = message_shape(*shape)
    scratch = []
    if first:
        scratch = [pltpu.VMEM(b.shape, b.dtype) for b in (left, right)]
        scratch += [pltpu.SemaphoreType.DMA((slots,))] * 2
    return pl.pallas_call(
        functools.partial(blocks_kernel, first, shape, entries),
        in_specs=[SMEM, SMEM]
        + [VMEM] * (len(fields) + len(own))
        + [HBM if first else VMEM] * 2,
        out_specs=[VMEM] * 5,
        scratch_shapes=[pltpu.VMEM((sectors, order, width), jnp.bfloat16)] + scratch,
        out_shape=[
            jax.ShapeDtypeStruct((sectors, order, width), jnp.float32),
            jax.ShapeDtypeStruct((2, *message), jnp.bfloat16),
            jax.ShapeDtypeStruct((2 * ROUNDS, *message), jnp.bfloat16),
            jax.ShapeDtypeStruct((8, 128), jnp.float32),
            jax.ShapeDtypeStruct((8, 128), jnp.float32),
        ],
        compiler_params=FIRST if first else PARAMS,
        cost_estimate=pl.CostEstimate(
            flops=4 * slots * order * order * width,
            bytes_accessed=4 * slots * order * order,
            transcendentals=0,
        ),
    )(me, ints, *fields, *own, left, right)


def chain_kernel(shape, k, index, me_ref, total_ref, dot_ref, other_ref, *refs):
    *arrived_refs, out_ref = refs
    _, rows, _ = shape
    me = me_ref[0]
    start = pl.multiple_of(sent_devices(me, me % 2)[k] * rows, rows)
    for s, row, part in message_parts(*shape):
        value = total_ref[s, pl.ds(start + row, HALF), :]
        value += other_ref[index, :, part].astype(jnp.float32)
        for ref in arrived_refs:
            value += ref[:, part].astype(jnp.float32)
        out_ref[:, part] = value.astype(jnp.bfloat16)
    at = out_ref.shape[1] - LANES
    lanes = down(dot_ref[...]) + read_lanes(other_ref.at[index], at)
    for ref in arrived_refs:
        lanes += read_lanes(ref, at)
    write_lanes(out_ref, at, lanes)


def chain(shape, k, index, me, total, dot, other, *arrived):
    return pl.pallas_call(
        functools.partial(chain_kernel, shape, k, index),
        in_specs=[SMEM] + [VMEM] * (3 + len(arrived)),
        out_specs=VMEM,
        out_shape=jax.ShapeDtypeStruct(message_shape(*shape), jnp.bfloat16),
        compiler_params=PARAMS,
    )(me, total, dot, other, *arrived)


def own_terms(shape, sector, me_ref, total_ref, other_ref, _, *arrived_refs):
    start = pl.multiple_of(me_ref[0] * shape[1], shape[1])
    values = []
    for s, row, part in message_parts(*shape):
        if s == sector:
            value = total_ref[s, pl.ds(start + row, HALF), :]
            value += other_ref[other_ref.shape[0] - 1, :, part].astype(jnp.float32)
            for ref in arrived_refs:
                value += ref[:, part].astype(jnp.float32)
            values.append(value)
    return jnp.concatenate(values, axis=0)


def own_scalar(me_ref, total_ref, other_ref, dot_ref, *arrived_refs):
    at = other_ref.shape[2] - LANES
    lanes = down(dot_ref[...]) + read_lanes(other_ref.at[other_ref.shape[0] - 1], at)
    return jnp.sum(lanes + sum(read_lanes(ref, at) for ref in arrived_refs))


def step_kernel(entries, scale_ref, wave_ref, diag_ref, *refs):
    *sums, terms_ref, correction_ref, message_ref = refs
    shape = wave_ref.shape
    ritz = own_scalar(*sums) / entries
    inverse = 1.0 / scale_ref[0:1, 0:1]
    dots = jnp.zeros((8, 128), jnp.float32)
    for s in range(shape[0]):
        start = wave_ref[s].astype(jnp.float32) * inverse
        diag = diag_ref[s].astype(jnp.float32)
        terms = own_terms(shape, s, *sums)
        first = terms + diag * start
        correction = (first - ritz * start) / jnp.maximum(jnp.abs(diag - ritz), 1.0)
        terms_ref[s] = terms
        correction_ref[s] = correction
        dots += fold(start * correction)
        for t, row, part in message_parts(*shape):
            if t == s:
                message_ref[:, part] = correction[row : row + HALF].astype(jnp.bfloat16)
    write_lanes(message_ref, message_ref.shape[1] - LANES, down(dots))


def davidson_step(scale, wave, diag, sums, entries):
    full = jax.ShapeDtypeStruct(wave.shape, jnp.float32)
    return pl.pallas_call(
        functools.partial(step_kernel, entries),
        in_specs=[VMEM] * 3 + [SMEM] + [VMEM] * (len(sums) - 1),
        out_specs=[VMEM] * 3,
        out_shape=[full, full, jax.ShapeDtypeStruct(message_shape(*wave.shape), jnp.bfloat16)],
        compiler_params=PARAMS,
    )(scale, wave, diag, *sums)


def finish_kernel(entries, along_ref, scale_ref, wave_ref, diag_ref, *refs):
    terms_ref, correction_ref, *sums, first_ref, vector_ref, image_ref = refs
    shape = wave_ref.shape
    along = along_ref[0:1, 0:1]
    norm = jnp.sqrt(jnp.full((1, 1), own_scalar(*sums) / entries, jnp.float32))
    inverse = 1.0 / norm
    start_scale = 1.0 / scale_ref[0:1, 0:1]
    for s in range(shape[0]):
        start = wave_ref[s].astype(jnp.float32) * start_scale
        diag = diag_ref[s].astype(jnp.float32)
        first_ref[s] = terms_ref[s] + diag * start
        second = (correction_ref[s] - along * start) * inverse
        vector_ref[s] = second
        image = (own_terms(shape, s, *sums) - along * terms_ref[s]) * inverse
        image_ref[s] = image + diag * second


def finish(along, scale, wave, diag, terms, correction, sums, entries):
    full = jax.ShapeDtypeStruct(wave.shape, jnp.float32)
    return pl.pallas_call(
        functools.partial(finish_kernel, entries),
        in_specs=[VMEM] * 6 + [SMEM] + [VMEM] * (len(sums) - 1),
        out_specs=[VMEM] * 3,
        out_shape=[full] * 3,
        compiler_params=PARAMS,
    )(along, scale, wave, diag, terms, correction, *sums)


def flip(value):
    return lax.ppermute(value, "term", [(i, i ^ 1) for i in range(16)])


def hop(value, up=1, down=-1):
    order = [0, 2, 4, 6, 7, 5, 3, 1]
    pairs = []
    for place in range(8):
        for core, step in ((0, up), (1, down)):
            pairs.append((order[place] * 2 + core, order[(place + step) % 8] * 2 + core))
    return lax.ppermute(value, "term", pairs)


def opposite(value):
    return hop(value, 4, 4)


def gather(own, beside=None):
    one, two = own, flip(own)
    across, two = lax.optimization_barrier((own, two))
    pieces = [one, two]
    across = opposite(across)
    result = None
    for k in range(ROUNDS):
        one, two = hop(one), hop(two)
        pieces += [one, two, flip(one), flip(two)]
        if k == 1 and beside is not None:
            result = beside(two)
            across, result = lax.optimization_barrier((across, result))
    return pieces + [across, flip(across)], result


def scatter(shape, me, total, near, far, dot):
    near = flip(near)
    near, far = lax.optimization_barrier((near, far))
    far = flip(far)
    one = hop(chain(shape, 0, 0, me, total, dot, near))
    two = hop(chain(shape, 1, 1, me, total, dot, near))
    across = opposite(chain(shape, 6, 4, me, total, dot, far))
    for k in (2, 4):
        one = hop(chain(shape, k, k - 2, me, total, dot, far, one))
        if k == 4:
            two, across = lax.optimization_barrier((two, across))
        two = hop(chain(shape, k + 1, k - 1, me, total, dot, far, two))
    return me, total, far, dot, one, flip(two), across


def on_ring(
    wavefunction, diagonal, left_blocks, right_blocks, block_source, block_target, live_count
):
    shape = wavefunction.shape
    sectors, rows, width = shape
    entries = float(sectors * rows * lax.axis_size("term") * width)
    me = lax.axis_index("term").astype(jnp.int32).reshape(1)

    def beside(after):
        ints = jnp.concatenate([block_source, block_target, live_count])
        return ints, copied(wavefunction, after)

    (_, *fields), (ints, wave) = gather(wavefunction, beside)
    fields = [wave, *fields]
    square = weighted_square(wave, diagonal)
    blocks = (left_blocks, right_blocks, shape)
    total, near, far, dot, scale = apply_blocks(me, ints, fields, (square,), *blocks, True, entries)
    terms, correction, message = davidson_step(
        scale, wavefunction, diagonal, scatter(shape, me, total, near, far, dot), entries
    )
    fields, _ = gather(message)
    own = (scale, wavefunction, correction)
    total, near, far, dot, along = apply_blocks(me, ints, fields, own, *blocks, False, entries)
    first_image, second_vector, second_image = finish(
        along, scale, wavefunction, diagonal, terms, correction,
        scatter(shape, me, total, near, far, dot), entries,
    )
    return (first_image, second_vector, second_image)


def block_loop(field_rounded, left_ops, right_ops, sources, targets, last_slot, partial_sum):

    def add_block(slot_index, running):
        left_op = lax.dynamic_index_in_dim(left_ops, slot_index, 0, keepdims=False)
        right_op = lax.dynamic_index_in_dim(right_ops, slot_index, 0, keepdims=False)
        source = lax.dynamic_index_in_dim(sources, slot_index, 0, keepdims=False)
        target = lax.dynamic_index_in_dim(targets, slot_index, 0, keepdims=False)
        piece = lax.dynamic_index_in_dim(field_rounded, source, 0, keepdims=False)
        product = jnp.dot(left_op, piece, preferred_element_type=jnp.float32).astype(jnp.bfloat16)
        term_value = jnp.dot(product, right_op.T, preferred_element_type=jnp.float32)
        before = lax.dynamic_index_in_dim(running, target, 0, keepdims=False)
        return lax.dynamic_update_index_in_dim(running, before + term_value, target, 0)

    return lax.fori_loop(0, last_slot, add_block, partial_sum)


def on_any(
    wavefunction, diagonal, left_blocks, right_blocks, block_source, block_target, live_count
):
    devices = lax.axis_size("term")
    position = lax.axis_index("term")
    row_count = wavefunction.shape[1]
    sector_count = wavefunction.shape[0]
    width = wavefunction.shape[2]
    entries = float(sector_count * row_count * devices * width)
    own_count = live_count[0]
    diag_own = diagonal.astype(jnp.float32)
    whole_wave = lax.all_gather(wavefunction, "term", axis=1, tiled=True).astype(jnp.float32)
    scale = jnp.sqrt(jnp.sum(whole_wave * whole_wave) / entries)
    start_whole = whole_wave / scale
    empty_sum = jnp.zeros(start_whole.shape, jnp.float32)
    first_terms = block_loop(
        start_whole.astype(jnp.bfloat16),
        left_blocks,
        right_blocks,
        block_source,
        block_target,
        own_count,
        empty_sum,
    )
    row_start = position * row_count
    whole_diag = lax.all_gather(diagonal, "term", axis=1, tiled=True).astype(jnp.float32)
    first_whole = lax.psum(first_terms, "term") + whole_diag * start_whole
    ritz_value = jnp.sum(start_whole * first_whole) / entries
    correction = (first_whole - ritz_value * start_whole) / jnp.maximum(
        jnp.abs(whole_diag - ritz_value), 1.0
    )
    correlation = jnp.sum(start_whole * correction) / entries
    projected = correction - correlation * start_whole
    second_whole = projected / jnp.sqrt(jnp.sum(projected * projected) / entries)
    first_image = lax.dynamic_slice_in_dim(first_whole, row_start, row_count, 1)
    second_vector = lax.dynamic_slice_in_dim(second_whole, row_start, row_count, 1)
    second_rounded = second_whole.astype(jnp.bfloat16)
    second_terms = block_loop(
        second_rounded, left_blocks, right_blocks, block_source, block_target, own_count, empty_sum
    )
    second_image = (
        lax.psum_scatter(second_terms, "term", scatter_dimension=1, tiled=True)
        + diag_own * second_vector
    )
    return (first_image, second_vector, second_image)


def solution(mesh):
    placed = (
        P("grp", "term", None),
        P("grp", "term", None),
        P(("grp", "term"), None, None),
        P(("grp", "term"), None, None),
        P(("grp", "term")),
        P(("grp", "term")),
        P(("grp", "term")),
    )
    on_device = on_ring if mesh.shape["term"] == 16 else on_any
    return jax.shard_map(
        on_device,
        mesh=mesh,
        in_specs=placed,
        out_specs=(P("grp", "term", None), P("grp", "term", None), P("grp", "term", None)),
        check_vma=False,
    )
```
